32 devices in a mesh: pts: 8 (over y, x, core), top: 4 (over z).
Axes of the slice: x: 2, y: 2, z: 4, core: 2. Of those that a mesh axis runs over, the one named last changes fastest.
Arguments:
- local_pos: float32 [3, 32768], P(None, ('pts', 'top')), may hold values from -1 to 1
- densities: float32 [8, 32768], P(None, ('pts', 'top')), may hold values from -6 to 6
- morton_slot: int32 [32768], P(('pts', 'top')), may hold values from 0 to 32767, as said below
- slot_leaf: int32 [32768], P(('pts', 'top')), may hold values from 0 to 4095, as said below
- uc2e: float32 [152, 152], replicated, may hold values from -0.5 to 0.5
- m2m: float32 [184832], replicated, may hold values from -0.15625 to 0.15625
- m2l_ops: bfloat16 [7300864], replicated, may hold values from -0.02734375 to 0.02734375
- dc2e: float32 [152, 152], replicated, may hold values from -0.5 to 0.5
- lattice: float32 [152, 152], replicated, may hold values from -0.5 to 0.5
- l2l: float32 [184832], replicated, may hold values from -0.5 to 0.5
Outputs:
- potentials: float32 [8, 32768], P(None, ('pts', 'top'))
The draws below stay inside these ranges and needn't reach their ends.
Inputs may be any that keep to these rules, and one draw needn't show every extreme that they name: `morton_slot`: every slot 0 to 32767 appears once. The points of one device go to at most 64 slots of any one device of the Morton layout (slot // 1024). `slot_leaf`: Non-decreasing. The leaves of the 4096 slots of one owner (slot // 4096) lie in at most 128 consecutive boxes of level 3 (leaf // 8).
All inputs are finite; a program needn't handle non-finite values.
Results may differ from the reference program's by a relative error of at most 0.003.
Values may be sent and summed in bfloat16 or wider, within the bound.
No kernel may reach another device: no remote copies, remote signals or barrier semaphores. Data moves between devices by JAX's collectives and lax.ppermute only.
A program may use at most 192 MiB of HBM per device.

```python
import math
import jax
import jax.numpy as jnp
import numpy as np
from jax import lax

PTS_DEV = 1024
LEVEL = 3
EDGE = 6
DENS = 8
OFFSETS = 316
COEF = 152
BOXES4 = 512
LEAVES = 4096
POINTS = 32768
BOX_CAP = 128
N_PTS = 8
N_TOP = 4
DEVICES = 32


def draw_slot_leaf(key, part):
    owners = N_PTS
    mean_boxes = BOXES4 // owners
    key_perm, key_pair, key_flip, key_edge, key_leaf = jax.random.split(key, 5)
    owner_order = jax.random.permutation(key_perm, owners)
    shifts = jax.random.randint(key_pair, (owners // 2,), 0, mean_boxes).astype(jnp.int32)
    shifts = shifts.at[0].set(mean_boxes - 1)
    flip_vals = jax.random.randint(key_flip, (owners // 2,), 0, 2).astype(jnp.int32)
    flip_vals = flip_vals.at[0].set(jnp.where(owner_order[0] == owners - 1, 1, 0))
    upper_own = jnp.where(flip_vals == 0, owner_order[0::2], owner_order[1::2])
    lower_own = jnp.where(flip_vals == 0, owner_order[1::2], owner_order[0::2])
    counts = jnp.zeros((owners,), jnp.int32).at[upper_own].add(mean_boxes + shifts).at[lower_own].add(mean_boxes - shifts)
    box_first = jnp.concatenate([jnp.zeros((1,), jnp.int32), jnp.cumsum(counts)[:-1].astype(jnp.int32)])
    edge_vals = jax.random.randint(key_edge, (owners,), 1, 8).astype(jnp.int32).at[0].set(0)
    leaf_first = 8 * box_first + edge_vals
    leaf_end = jnp.concatenate([leaf_first[1:], jnp.full((1,), LEAVES, jnp.int32)])
    span_len = leaf_end - leaf_first
    per_owner = POINTS // owners
    offsets = jax.random.randint(key_leaf, (owners, per_owner), 0, span_len[:, None]).astype(jnp.int32)
    leaves = jnp.sort(leaf_first[:, None] + offsets, axis=1)
    leaves = leaves.at[:, 0].set(leaf_first).at[:, per_owner - 1].set(leaf_end - 1)
    return leaves.reshape(-1).astype(jnp.int32)


def draw_morton_slot(key, part):
    devices = DEVICES
    mean_send = PTS_DEV // devices
    key_perm, key_pair, key_dest, key_slot, key_body = jax.random.split(key, 5)
    block_order = jax.random.permutation(key_perm, devices)
    shifts = jax.random.randint(key_pair, (devices // 2,), 0, mean_send + 1).astype(jnp.int32)
    shifts = shifts.at[0].set(mean_send)
    size_vals = jnp.zeros((devices,), jnp.int32).at[block_order[0::2]].add(mean_send + shifts).at[block_order[1::2]].add(mean_send - shifts)
    bounds = jnp.cumsum(size_vals).astype(jnp.int32)
    rank_vals = jnp.arange(PTS_DEV, dtype=jnp.int32)
    block_of = jnp.sum((rank_vals[:, None] >= bounds[None, :]).astype(jnp.int32), axis=1)
    dest_shift = jax.random.permutation(key_dest, devices).astype(jnp.int32)
    slot_keys = jax.random.split(key_slot, devices)
    slot_perm = jax.vmap(lambda one_key: jax.random.permutation(one_key, PTS_DEV))(slot_keys).astype(jnp.int32)
    source = (dest_shift[:, None] + block_of[None, :]) % devices
    slot_value = jnp.arange(devices, dtype=jnp.int32)[:, None] * PTS_DEV + slot_perm
    tiebreak = jax.random.permutation(key_body, POINTS).astype(jnp.int32).reshape(devices, PTS_DEV)
    score_vals = (source * POINTS + tiebreak).reshape(-1)
    body_order = jnp.argsort(score_vals, stable=True)
    return slot_value.reshape(-1)[body_order].astype(jnp.int32)


def level_of(stream_key, shape, cuts, smallest, top_value):
    gain, own = 1.0, jax.random.fold_in(stream_key, 6)
    for position, parts in cuts:
        steps = jnp.exp(jax.random.uniform(jax.random.fold_in(own, position), (parts,), jnp.float32, smallest / len(cuts), top_value / len(cuts)))
        gain = gain * jnp.repeat(steps, shape[position] // parts).reshape([-1 if axis == position else 1 for axis in range(len(shape))])
    return gain


def bell_draw(rng, extent, scale, reach, pieces=(), kind=jnp.bfloat16):
    values = scale * jax.random.normal(rng, extent, jnp.float32)
    if pieces:
        values = values * level_of(rng, extent, pieces, -0.22, 0.18)
    return jnp.clip(values, -reach, reach).astype(kind)


def setup_inputs(seed: int = 0) -> dict:
    streams_of = jax.random.split(jax.random.key(seed), 11)
    local_pos = jnp.clip(jax.random.uniform(streams_of[0], (3, POINTS), jnp.float32, -1.0, 1.0) * level_of(streams_of[0], (3, POINTS), ((1, 32),), -0.4, 0.0), -1.0, 1.0)
    densities = bell_draw(streams_of[1], (DENS, POINTS), 1.0, 6.0, ((1, 32),), jnp.float32)
    morton_slot = draw_morton_slot(jax.random.fold_in(streams_of[10], 71), 0)
    slot_leaf = draw_slot_leaf(jax.random.fold_in(streams_of[10], 71), 0)
    uc2e = bell_draw(streams_of[4], (COEF, COEF), COEF ** -0.5, 0.5, (), jnp.float32)
    m2m = bell_draw(streams_of[5], (8 * COEF * COEF,), (8 * COEF) ** -0.5, 0.15625, (), jnp.float32)
    m2l_ops = bell_draw(streams_of[6], (COEF * OFFSETS * COEF,), (OFFSETS * COEF) ** -0.5, 0.02734375)
    dc2e = bell_draw(streams_of[7], (COEF, COEF), COEF ** -0.5, 0.5, (), jnp.float32)
    lattice = bell_draw(streams_of[8], (COEF, COEF), COEF ** -0.5, 0.5, (), jnp.float32)
    l2l = bell_draw(streams_of[9], (8 * COEF * COEF,), COEF ** -0.5, 0.5, (), jnp.float32)
    return dict(local_pos=local_pos, densities=densities, morton_slot=morton_slot, slot_leaf=slot_leaf, uc2e=uc2e, m2m=m2m, m2l_ops=m2l_ops, dc2e=dc2e, lattice=lattice, l2l=l2l)


def surface_table():
    grid_vals = np.linspace(-1.0, 1.0, EDGE)
    points_list = []
    for index_a in range(EDGE):
        for index_b in range(EDGE):
            for index_c in range(EDGE):
                if min(index_a, index_b, index_c) == 0 or max(index_a, index_b, index_c) == EDGE - 1:
                    points_list.append([grid_vals[index_a], grid_vals[index_b], grid_vals[index_c]])
    return np.array(points_list, dtype=np.float32).T

def offset_table():
    points_list = []
    for shift_x in range(-3, 4):
        for shift_y in range(-3, 4):
            for shift_z in range(-3, 4):
                if max(abs(shift_x), abs(shift_y), abs(shift_z)) >= 2:
                    points_list.append([shift_x, shift_y, shift_z])
    return np.array(points_list, dtype=np.int32)

def morton_decode(number, bit_count):
    coord_x = jnp.zeros_like(number)
    coord_y = jnp.zeros_like(number)
    coord_z = jnp.zeros_like(number)
    for level_idx in range(bit_count):
        digit_val = number // 8 ** level_idx % 8
        coord_x = coord_x + digit_val // 4 * 2 ** level_idx
        coord_y = coord_y + digit_val // 2 % 2 * 2 ** level_idx
        coord_z = coord_z + digit_val % 2 * 2 ** level_idx
    return (coord_x, coord_y, coord_z)

def morton_encode(coord_x, coord_y, coord_z, bit_count):
    number = jnp.zeros_like(coord_x)
    for level_idx in range(bit_count):
        digit_val = coord_x // 2 ** level_idx % 2 * 4 + coord_y // 2 ** level_idx % 2 * 2 + coord_z // 2 ** level_idx % 2
        number = number + digit_val * 8 ** level_idx
    return number

def source_boxes(targets):
    side_len = 2 ** LEVEL
    coord_x, coord_y, coord_z = morton_decode(targets, LEVEL)
    shift_table = jnp.asarray(offset_table())
    return morton_encode((coord_x[None, :] + shift_table[:, 0:1]) % side_len, (coord_y[None, :] + shift_table[:, 1:2]) % side_len, (coord_z[None, :] + shift_table[:, 2:3]) % side_len, LEVEL).astype(jnp.int32)

def kernel_tile(local_pos):
    surface = surface_table()
    squared = jnp.zeros((local_pos.shape[1], surface.shape[1]), jnp.float32)
    for dim_index in range(3):
        spacing = 1.25 * jnp.asarray(surface[dim_index])[None, :] - local_pos[dim_index][:, None]
        squared = squared + spacing * spacing
    return 1.0 / (4.0 * math.pi * jnp.sqrt(squared))

def upward(level_mult, m2m):
    current = level_mult
    for level_idx in range(LEVEL):
        parents = current.shape[2] // 8
        current = jnp.einsum('oce,ekpo->ckp', m2m, current.reshape(current.shape[0], current.shape[1], parents, 8), precision=lax.Precision.HIGHEST)
    return current

def downward(root_local, l2l, levels):
    current = root_local
    for level_idx in range(levels):
        current = jnp.einsum('oce,ekp->ckpo', l2l, current, precision=lax.Precision.HIGHEST)
        current = current.reshape(current.shape[0], current.shape[1], -1)
    return current

def reference(local_pos, densities, morton_slot, slot_leaf, uc2e, m2m, m2l_ops, dc2e, lattice, l2l):
    m2m = m2m.reshape(8, COEF, COEF)
    l2l = l2l.reshape(8, COEF, COEF)
    m2l_ops = m2l_ops.reshape(COEF, OFFSETS, COEF)
    own_pts = PTS_DEV * N_TOP
    inverse = jnp.zeros((POINTS,), jnp.int32).at[morton_slot].set(jnp.arange(POINTS, dtype=jnp.int32))
    sorted_pos = local_pos[:, inverse]
    sorted_dens = densities[:, inverse]
    owner_pos = sorted_pos.reshape(3, N_PTS, own_pts).transpose(1, 0, 2)
    owner_dens = sorted_dens.reshape(DENS, N_PTS, own_pts).transpose(1, 0, 2)
    owner_leaf = slot_leaf.reshape(N_PTS, own_pts)

    def owner_partial(packed):
        pos_block, dens_block, leaf_block = packed
        first_box = (leaf_block[0] // 8).astype(jnp.int32)
        kernel = kernel_tile(pos_block)
        contrib = (dens_block.T[:, :, None] * kernel[:, None, :]).reshape(own_pts, DENS * COEF)
        checks = jax.ops.segment_sum(contrib, (leaf_block - 8 * first_box).astype(jnp.int32), num_segments=8 * BOX_CAP)
        checks = checks.reshape(BOX_CAP, 8, DENS, COEF)
        leaf_mult = jnp.einsum('ef,bokf->boke', uc2e, checks, precision=lax.Precision.HIGHEST)
        partial_value = jnp.einsum('oce,boke->ckb', m2m, leaf_mult, precision=lax.Precision.HIGHEST)
        rounded = lax.optimization_barrier(partial_value.astype(jnp.bfloat16)).astype(jnp.float32)
        return (rounded, first_box)
    partials, first_boxes = lax.map(owner_partial, (owner_pos, owner_dens, owner_leaf))
    box_ids = (first_boxes[:, None] + jnp.arange(BOX_CAP, dtype=jnp.int32)[None, :]).astype(jnp.int32)
    spread = partials.transpose(1, 2, 0, 3).reshape(COEF, DENS, N_PTS * BOX_CAP)
    level4 = jnp.zeros((COEF, DENS, BOXES4), jnp.float32).at[:, :, box_ids.reshape(-1)].add(spread, mode='drop')
    level4_low = level4.astype(jnp.bfloat16)
    root_mult = upward(level4, m2m)
    root_local = jnp.einsum('ce,ekp->ckp', lattice, root_mult, precision=lax.Precision.HIGHEST)
    lattice4 = downward(root_local, l2l, LEVEL)
    ops_wide = m2l_ops.astype(jnp.float32)
    low_wide = level4_low.astype(jnp.float32)
    block_len = math.gcd(BOXES4, 32)

    def m2l_block(targets):
        sources = source_boxes(targets)
        return jnp.einsum('cds,skdt->ckt', ops_wide, low_wide[:, :, sources], precision=lax.Precision.HIGHEST)
    target_blocks = jnp.arange(BOXES4, dtype=jnp.int32).reshape(-1, block_len)
    checks4 = lax.map(m2l_block, target_blocks)
    checks4 = checks4.transpose(1, 2, 0, 3).reshape(COEF, DENS, BOXES4)
    locals4 = jnp.einsum('cd,dkt->ckt', dc2e, checks4, precision=lax.Precision.HIGHEST) + lattice4
    leaf_local = jnp.einsum('oce,ekb->ckbo', l2l, locals4, precision=lax.Precision.HIGHEST).reshape(COEF, DENS, LEAVES)

    def owner_potential(packed):
        pos_block, leaf_block = packed
        kernel = kernel_tile(pos_block)
        return jnp.einsum('sc,cks->ks', kernel, leaf_local[:, :, leaf_block], precision=lax.Precision.HIGHEST)
    owner_pot = lax.map(owner_potential, (owner_pos, owner_leaf))
    sorted_pot = owner_pot.transpose(1, 0, 2).reshape(DENS, POINTS)
    return sorted_pot[:, morton_slot]
```

```python
import functools
import math

import jax
import jax.numpy as jnp
import numpy as np
from jax import lax
from jax.experimental import pallas as pl
from jax.experimental.pallas import tpu as pltpu
from jax.sharding import PartitionSpec as P

LEVEL = 3
EDGE = 6
DENS = 8
SIDE = 2**LEVEL
BOXES4 = SIDE**3
PLANE = SIDE * SIDE
LANE = 128
REACH = 3
SHIFTS = list(range(-REACH, REACH + 1))
OUTER = [s for s in SHIFTS if abs(s) >= 2]
INNER = [s for s in SHIFTS if abs(s) < 2]
bf16 = jnp.bfloat16
f32 = jnp.float32
NN = (((1,), (0,)), ((), ()))
NT = (((1,), (1,)), ((), ()))


def up(value, multiple):
    return -(-value // multiple) * multiple


def surface_table():
    grid_vals = np.linspace(-1.0, 1.0, EDGE)
    points_list = []
    for a in range(EDGE):
        for b in range(EDGE):
            for c in range(EDGE):
                if min(a, b, c) == 0 or max(a, b, c) == EDGE - 1:
                    points_list.append([grid_vals[a], grid_vals[b], grid_vals[c]])
    return np.array(points_list, dtype=np.float32).T


COEF = surface_table().shape[1]
OFFSETS = (2 * REACH + 1) ** 3 - 27
CPAD = up(COEF, 32)


def blocks():
    out, position = [], 0
    for dx in SHIFTS:
        for dy in SHIFTS:
            count = sum(max(abs(dx), abs(dy), abs(dz)) >= 2 for dz in SHIFTS)
            out.append((dx, dy, position, count))
            position += count
    return out


def dot(a, b, dims=NN):
    return lax.dot_general(a, b, dims, preferred_element_type=f32)


def split(value):
    high = value.astype(bf16)
    return high, (value - high.astype(f32)).astype(bf16)


def dot3(a, b, dims=NN):
    return dot(a[0], b[0], dims) + dot(a[1], b[0], dims) + dot(a[0], b[1], dims)


def call(kernel, out_shape, mib, flops, bytes_accessed=1 << 20, **kw):
    return pl.pallas_call(
        kernel,
        out_shape=out_shape,
        compiler_params=pltpu.CompilerParams(vmem_limit_bytes=mib << 20),
        cost_estimate=pl.CostEstimate(
            flops=flops, bytes_accessed=bytes_accessed, transcendentals=0
        ),
        **kw,
    )


VMEM = pl.BlockSpec(memory_space=pltpu.VMEM)
SMEM = pl.BlockSpec(memory_space=pltpu.SMEM)
ANY = pl.BlockSpec(memory_space=pl.ANY)


HG = 4 * OFFSETS * COEF // LANE
KT = up(up(OFFSETS * COEF, LANE) // LANE, 8)
WFULL = up(7 * COEF, LANE)
WIN = up(4 * COEF, LANE)
NG = COEF // 8
STEPS = -(-NG // 4)
ROWS = 16 * STEPS
CHUNK = up(HG + 15, 16)
TAIL = 32
STRIDE = 17


def relayout_kernel(nrows, half_ref, f_hbm, tail_hbm, oa, ob, oc, inb, fbuf, tbuf, tb16, sem):
    step = pl.program_id(0)
    half = half_ref[0]
    end16 = nrows // 16 * 16

    def start_row(st, g):
        return jnp.minimum(4 * st + g, NG - 1) * (2 * HG) + half * HG

    def start(st, slot):
        for g in range(4):
            row = pl.multiple_of(start_row(st, g) // 16 * 16, 16)
            pltpu.make_async_copy(
                f_hbm.at[pl.ds(row, CHUNK - TAIL)],
                inb.at[slot, g, pl.ds(0, CHUNK - TAIL)],
                sem.at[slot, g, 0],
            ).start()
            last = row + CHUNK > end16

            @pl.when(jnp.logical_not(last))
            def _():
                pltpu.make_async_copy(
                    f_hbm.at[pl.ds(pl.multiple_of(row + CHUNK - TAIL, 16), TAIL)],
                    inb.at[slot, g, pl.ds(CHUNK - TAIL, TAIL)],
                    sem.at[slot, g, 1],
                ).start()

            @pl.when(last)
            def _():
                pltpu.make_async_copy(
                    tail_hbm, inb.at[slot, g, pl.ds(CHUNK - TAIL, TAIL)], sem.at[slot, g, 1]
                ).start()

    def wait(slot):
        for g in range(4):
            pltpu.make_async_copy(
                f_hbm.at[pl.ds(0, CHUNK - TAIL)],
                inb.at[slot, g, pl.ds(0, CHUNK - TAIL)],
                sem.at[slot, g, 0],
            ).wait()
            pltpu.make_async_copy(
                tail_hbm, inb.at[slot, g, pl.ds(CHUNK - TAIL, TAIL)], sem.at[slot, g, 1]
            ).wait()

    slot = lax.rem(step, 2)

    @pl.when(step == 0)
    def _():
        fbuf[...] = jnp.zeros_like(fbuf)
        start(0, 0)

    @pl.when(step + 1 < STEPS)
    def _():
        start(step + 1, 1 - slot)

    wait(slot)
    lane = lax.broadcasted_iota(jnp.int32, (8, LANE), 1)
    for g in range(4):
        fbuf[g, 0:CHUNK] = inb[slot, g].astype(f32)
    for g in range(4):
        row = start_row(step, g)
        off = row - row // 16 * 16
        for e in range(4):
            first = OFFSETS * COEF * e
            phase = first % LANE

            @pl.loop(0, KT // 8, unroll=KT // 8)
            def _(n):
                base = off + first // LANE + 8 * n
                value = fbuf[g, pl.ds(base, 8), :]
                if phase:
                    after = fbuf[g, pl.ds(base + 1, 8), :]
                    value = pltpu.roll(jnp.where(lane >= phase, value, after), LANE - phase, 1)
                tbuf[pl.ds(8 * n * STRIDE + 4 * g + e, 8, stride=STRIDE), :] = value

    @pl.loop(0, KT, unroll=8)
    def _(k):
        tb16[k] = tbuf[pl.ds(k * STRIDE, 16), :].astype(bf16)

    for dx, dy, d0, count in blocks():
        tile0, phase = divmod(d0 * COEF, LANE)
        if dy in OUTER:
            ref = oa.at[dx + REACH, OUTER.index(dy)]
        elif dx in OUTER:
            ref = ob.at[OUTER.index(dx), INNER.index(dy)]
        else:
            ref = oc.at[INNER.index(dx), INNER.index(dy)]
        for t in range(up(count * COEF, LANE) // LANE):
            value = tb16[tile0 + t]
            if phase:
                after = tb16[min(tile0 + t + 1, KT - 1)]
                value = jnp.concatenate([value[:, phase:], after[:, :phase]], axis=1)
            ref[:, t * LANE : (t + 1) * LANE] = value


def relayout(flat, half):
    nrows = flat.shape[0] // LANE
    rows = flat.reshape(nrows, LANE)
    tail = rows[nrows // 16 * 16 :]
    tail = jnp.pad(tail, ((0, TAIL - tail.shape[0]), (0, 0)))
    shapes = ((7, 4, ROWS, WFULL), (4, 3, ROWS, WFULL), (3, 3, ROWS, WIN))
    return call(
        functools.partial(relayout_kernel, nrows),
        tuple(jax.ShapeDtypeStruct(s, bf16) for s in shapes),
        58,
        1 << 20,
        16 << 20,
        grid_spec=pltpu.PrefetchScalarGridSpec(
            num_scalar_prefetch=1,
            grid=(STEPS,),
            in_specs=[ANY, ANY],
            out_specs=tuple(
                pl.BlockSpec((s[0], s[1], 16, s[3]), lambda i, h: (0, 0, i, 0)) for s in shapes
            ),
            scratch_shapes=[
                pltpu.VMEM((2, 4, CHUNK, LANE), bf16),
                pltpu.VMEM((4, CHUNK + 16, LANE), f32),
                pltpu.VMEM((KT * STRIDE, LANE), f32),
                pltpu.VMEM((KT, 16, LANE), bf16),
                pltpu.SemaphoreType.DMA((2, 4, 2)),
            ],
        ),
    )(half, rows, tail)


def route_kernel(own, cap, n_top, pos, dens, slot, out):
    points = pos.shape[1]
    owners = out.shape[0]
    slots = slot[...]
    owner = slots // own
    inside = slots - owner * own
    hit = owner == lax.broadcasted_iota(jnp.int32, (owners, points), 0)
    hit = jnp.where(hit, 1.0, 0.0)
    hit16 = hit.astype(bf16)
    row = lax.broadcasted_iota(jnp.int32, (LANE, LANE), 0)
    col = lax.broadcasted_iota(jnp.int32, (LANE, LANE), 1)
    before = jnp.where(row < col, 1.0, 0.0).astype(bf16)
    every = jnp.ones((LANE, LANE), bf16)
    total = jnp.zeros((owners, LANE), f32)
    ranks = []
    for t in range(points // LANE):
        part = hit16[:, t * LANE : (t + 1) * LANE]
        ranks.append(total + dot(part, before))
        total = total + dot(part, every)
    rank = jnp.sum(hit * jnp.concatenate(ranks, axis=1), axis=0, keepdims=True)
    entry = owner * cap + rank.astype(jnp.int32)
    inside_hi = inside // 64
    value = jnp.concatenate([pos[...], dens[...]], axis=0)
    width = value.shape[0]
    high, low = split(value)
    ones = jnp.ones((1, points), f32)
    high = jnp.concatenate(
        [high.astype(f32), inside_hi.astype(f32), (inside - 64 * inside_hi).astype(f32), ones]
        + [jnp.zeros((16 - width - 3, points), f32)],
        axis=0,
    )
    low = jnp.concatenate([low.astype(f32), jnp.zeros((16 - width, points), f32)], axis=0)
    payload = jnp.concatenate([high, low], axis=0).astype(bf16)
    block = max(cap, LANE)
    for o in range(owners * cap // block):
        there = entry == o * block + lax.broadcasted_iota(jnp.int32, (block, points), 0)
        there = jnp.where(there, 1.0, 0.0).astype(bf16)
        got = dot(payload, there, NT)
        value = got[0:width] + got[16 : 16 + width]
        where = got[width : width + 1] * 64.0 + got[width + 1 : width + 2]
        valid = got[width + 2 : width + 3]
        per = DENS // n_top
        for q in range(n_top):
            rows = [value[0:3], where, valid, value[3 + per * q : 3 + per * (q + 1)]]
            rows.append(jnp.zeros((8 - 5 - per, block), f32))
            packed = jnp.concatenate([r for r in rows if r.shape[0]], axis=0)
            for i in range(block // cap):
                out[o * (block // cap) + i, q] = packed[:, i * cap : (i + 1) * cap]


def octant_product(pos, octant, surf, oper_hi, oper_lo):
    squared = None
    for d in range(3):
        spacing = surf[d] - pos[d : d + 1]
        squared = spacing * spacing if squared is None else squared + spacing * spacing
    value = lax.rsqrt(squared)
    value = jnp.concatenate([value, jnp.zeros((CPAD - COEF, value.shape[1]), f32)], axis=0)
    high, low = split(value)
    low = low.astype(f32)
    high = high.astype(f32)
    his = [jnp.where(octant == o, high, 0.0).astype(bf16) for o in range(8)]
    los = [jnp.where(octant == o, low, 0.0).astype(bf16) for o in range(8)]
    return dot3(
        (oper_hi, oper_lo), (jnp.concatenate(his, axis=0), jnp.concatenate(los, axis=0))
    )


def look_up(index, table):
    rows = table.shape[1]
    width = index.shape[1]
    at_row = index // LANE
    at_lane = index - at_row * LANE
    there = at_row == lax.broadcasted_iota(jnp.int32, (rows, width), 0)
    got = dot(table, jnp.where(there, 1.0, 0.0).astype(bf16))
    mine = at_lane == lax.broadcasted_iota(jnp.int32, (LANE, width), 0)
    first = jnp.sum(jnp.where(mine, got[0:LANE], 0.0), axis=0, keepdims=True)
    second = jnp.sum(jnp.where(mine, got[LANE : 2 * LANE], 0.0), axis=0, keepdims=True)
    return first, second


PB = 256


def upward_kernel(own, box_cap, flip_ref, got, table, surf, w_hi, w_lo, out, buf):
    sources, _, cap = got.shape
    wide = up(cap, LANE)
    flip = flip_ref[0]
    buf[...] = jnp.zeros_like(buf)

    def place(s, offset):
        value = got[s]
        count = jnp.sum(value[4:5]).astype(jnp.int32)
        value = jnp.concatenate([value, jnp.zeros((8, wide + LANE - cap), f32)], axis=1)
        tile = offset // LANE
        value = pltpu.roll(value, offset - tile * LANE, 1)
        place_at = pl.ds(pl.multiple_of(tile * LANE, LANE), wide + LANE)
        buf[:, place_at] = buf[:, place_at] + value
        return offset + count

    lax.fori_loop(0, sources, place, jnp.int32(0), unroll=4)
    out_rows = out.shape[1]

    def block(j, total):
        value = buf[:, pl.ds(pl.multiple_of(j * PB, PB), PB)]
        index = value[3:4].astype(jnp.int32) ^ flip
        box, octant = look_up(index, table[...])
        field = split(octant_product(value[0:3], octant, surf, w_hi[...], w_lo[...]))
        rows = []
        at = lax.broadcasted_iota(jnp.int32, (box_cap, PB), 0).astype(f32)
        for k in range(out_rows // box_cap):
            rows.append(jnp.where(box == at, value[5 + k : 6 + k], 0.0))
        return total + dot3(field, split(jnp.concatenate(rows, axis=0)), NT)

    total = lax.fori_loop(0, own // PB, block, jnp.zeros((COEF, out_rows), f32))
    out[...] = total.astype(bf16)


def morton_place(box):
    place = jnp.zeros_like(box)
    for b in range(LEVEL):
        digit = box >> (3 * b)
        place = place + ((((digit >> 2) & 1) << (2 * LEVEL + b)))
        place = place + ((((digit >> 1) & 1) << (LEVEL + b)) + ((digit & 1) << b))
    return place


def target_kernel(flip_ref, pos, slot, table, surf, w_hi, w_lo, field, place):
    flip = flip_ref[0]
    count = pos.shape[1]

    @pl.loop(0, count // PB)
    def _(j):
        at = pl.ds(pl.multiple_of(j * PB, PB), PB)
        index = slot[:, at].astype(jnp.int32) ^ flip
        high, low = look_up(index, table[...])
        leaf = (high * 64.0 + low).astype(jnp.int32)
        octant = leaf & 7
        field[:, at] = octant_product(
            pos[:, at], octant, surf, w_hi[...], w_lo[...]
        )
        place[:, at] = morton_place(leaf >> 3)


def translate_kernel(slabs, x0_ref, ids, part, oa, ob, oc, out, xs, xin, acc, ma, mb, mc, sem):
    copies = []
    for i, (src, dst) in enumerate(((oa, ma), (ob, mb), (oc, mc))):
        for j in range(src.shape[0]):
            copies.append(pltpu.make_async_copy(src.at[j], dst.at[j], sem.at[i, j]))
            copies[-1].start()
    x0 = x0_ref[0]
    dens = part.shape[0]
    place = morton_place(ids[...])
    place = (((place >> 6) - x0 + REACH) & 7) * 64 + (place & 63)
    place = jnp.where((ids[...] >= 0) & (ids[...] < BOXES4), place, -1)
    at = lax.broadcasted_iota(jnp.int32, (BOXES4, ids.shape[1]), 0)
    there = jnp.where(at == place, 1.0, 0.0).astype(bf16)
    columns = dens * PLANE
    for k in range(dens):
        low = dot(there, part[k], NT)
        low = low.astype(bf16).astype(f32)
        for s in range(7 + slabs - 1):
            slab = low[s * PLANE : (s + 1) * PLANE].reshape(SIDE, SIDE, COEF)
            shifted = {}
            for dz in SHIFTS:
                if dz == 0:
                    moved = slab
                else:
                    cut = dz % SIDE
                    moved = jnp.concatenate([slab[:, cut:], slab[:, :cut]], axis=1)
                shifted[dz] = moved.reshape(PLANE, COEF)
            rows = pl.ds(s * columns + k * PLANE, PLANE)
            pad = [jnp.zeros((PLANE, WFULL - 7 * COEF), f32)]
            xs[rows, :] = jnp.concatenate([shifted[z] for z in SHIFTS] + pad, axis=1).astype(bf16)
            pad = [jnp.zeros((PLANE, WIN - 4 * COEF), f32)]
            xin[rows, :] = jnp.concatenate([shifted[z] for z in OUTER] + pad, axis=1).astype(bf16)
    for c in copies:
        c.wait()
    n_out = len(OUTER) * ROWS
    n_in = len(INNER) * ROWS
    for i, dx in enumerate(SHIFTS):
        rows = pl.ds(i * columns, slabs * columns)
        source = xs[rows, :]
        outer = dot(ma[i].reshape(n_out, WFULL), source, NT)
        if dx in OUTER:
            inner = dot(mb[OUTER.index(dx)].reshape(n_in, WFULL), source, NT)
        else:
            inner = dot(mc[INNER.index(dx)].reshape(n_in, WIN), xin[rows, :], NT)
        if i == 0:
            acc[0:n_out] = outer
            acc[n_out : n_out + n_in] = inner
        else:
            acc[0:n_out] += outer
            acc[n_out : n_out + n_in] += inner
    lane = lax.broadcasted_iota(jnp.int32, (ROWS, LANE), 1)
    for t in range(slabs * columns // LANE):
        total = jnp.zeros((ROWS, LANE), f32)
        for i, dy in enumerate(OUTER + INNER):
            value = acc[i * ROWS : (i + 1) * ROWS, t * LANE : (t + 1) * LANE]
            by = SIDE * (dy % SIDE)
            if by:
                near = pltpu.roll(value, LANE - by, 1)
                far = pltpu.roll(value, PLANE - by, 1)
                value = jnp.where((lane & (PLANE - 1)) < PLANE - by, near, far)
            total = total + value
        out[:, t * LANE : (t + 1) * LANE] = total.astype(out.dtype)


def coarse_kernel(ids, part, m2m_hi, m2m_lo, lat_hi, lat_lo, l2l_hi, l2l_lo, out):
    dens = part.shape[0]
    box = ids[...]
    place = ((box & 7) << 6) + (box & 56) + (box >> 6)
    place = jnp.where((box >= 0) & (box < BOXES4), place, -1)
    at = lax.broadcasted_iota(jnp.int32, (BOXES4, ids.shape[1]), 0)
    there = jnp.where(at == place, 1.0, 0.0).astype(bf16)
    level = [dot(there, part[k], NT) for k in range(dens)]

    def oper(hi, lo, o):
        return hi[o], lo[o]

    for _ in range(LEVEL):
        count = level[0].shape[0] // 8
        total = None
        for o in range(8):
            rows = jnp.concatenate([v[o * count : (o + 1) * count] for v in level], axis=0)
            term = dot3(split(rows), oper(m2m_hi, m2m_lo, o), NT)
            total = term if total is None else total + term
        level = [total[k * count : (k + 1) * count] for k in range(dens)]
    rows = jnp.concatenate(level, axis=0)
    rows = dot3(split(rows), (lat_hi[...], lat_lo[...]), NT)
    level = [rows[k : k + 1] for k in range(dens)]
    for _ in range(LEVEL):
        count = level[0].shape[0]
        rows = split(jnp.concatenate(level, axis=0))
        children = [dot3(rows, oper(l2l_hi, l2l_lo, o), NT) for o in range(8)]
        level = [
            jnp.concatenate([c[k * count : (k + 1) * count] for c in children], axis=0)
            for k in range(dens)
        ]
    at = lax.broadcasted_iota(jnp.int32, (BOXES4, BOXES4), 1)
    row = lax.broadcasted_iota(jnp.int32, (BOXES4, BOXES4), 0)
    number = ((row & 7) << 6) + (row & 56) + (row >> 6)
    move = jnp.where(at == morton_place(number), 1.0, 0.0).astype(bf16)
    for k in range(dens):
        high, low = split(level[k])
        turned = (((0,), (0,)), ((), ()))
        out[k] = dot(high, move, turned) + dot(low, move, turned)


def evaluate_kernel(slabs, me_ref, *refs):
    n = SIDE // slabs
    checks = refs[: 2 * n]
    d_hi, d_lo, lattice, field, place, out, stack = refs[2 * n :]
    core = me_ref[0]
    group = me_ref[1]
    dens = lattice.shape[0]
    lane = lax.broadcasted_iota(jnp.int32, (COEF, LANE), 1)
    mine = jnp.concatenate([d_hi[core], d_lo[core]], axis=0)
    other = jnp.concatenate([d_hi[1 - core], d_lo[1 - core]], axis=0)
    for m in range(n):
        value = dot(mine, checks[2 * m][...]) + dot(other, checks[2 * m + 1][...])
        value = value[0:COEF] + value[COEF : 2 * COEF]
        if slabs == 2:
            a, b = value[:, 0:LANE], value[:, LANE : 2 * LANE]
            half = LANE // 2
            pieces = [
                jnp.where(lane < half, a, pltpu.roll(b, half, 1)),
                jnp.where(lane < half, pltpu.roll(a, half, 1), b),
            ]
        else:
            pieces = [value[:, k * PLANE : (k + 1) * PLANE] for k in range(dens)]
        width = slabs * PLANE
        for k in range(dens):
            at = m ^ group
            if width % LANE == 0:
                base = lattice[k, :, pl.ds(pl.multiple_of(at * width, width), width)]
            else:
                pair = lattice[k, :, pl.ds(pl.multiple_of(at // 2 * LANE, LANE), LANE)]
                base = jnp.where(at % 2 == 0, pair[:, :width], pair[:, width:])
            high, low = split(pieces[k] + base)
            rows = pl.ds(k * CPAD, COEF)
            stack[rows, m * width : (m + 1) * width] = high.astype(f32)
            rows = pl.ds((dens + k) * CPAD, COEF)
            stack[rows, m * width : (m + 1) * width] = low.astype(f32)
    local = stack[...].astype(bf16)

    @pl.loop(0, place.shape[1] // PB)
    def _(j):
        at = pl.ds(pl.multiple_of(j * PB, PB), PB)
        want = place[:, at] ^ (group * (slabs * PLANE))
        there = want == lax.broadcasted_iota(jnp.int32, (BOXES4, PB), 0)
        got = dot(local, jnp.where(there, 1.0, 0.0).astype(bf16))
        mine = field[:, at]
        rows = []
        for k in range(dens):
            value = got[k * CPAD : k * CPAD + COEF]
            value = value + got[(dens + k) * CPAD : (dens + k) * CPAD + COEF]
            rows.append(jnp.sum(value * mine, axis=0, keepdims=True))
        out[:, at] = jnp.concatenate(rows, axis=0)


def shifts_of(axis, value, distances):
    size = lax.axis_size(axis)
    return [
        value if m == 0 else lax.ppermute(value, axis, [(i, i ^ m) for i in range(size)])
        for m in distances
    ]


def split_oper(value):
    high = lax.reduce_precision(value, 8, 7)
    return high.astype(bf16), (value - high).astype(bf16)


def per_device(
    local_pos, densities, morton_slot, slot_leaf, uc2e, m2m, m2l_ops, dc2e, lattice, l2l
):
    n_pts = lax.axis_size("pts")
    n_top = lax.axis_size("top")
    me = lax.axis_index("pts")
    top = lax.axis_index("top")
    points = local_pos.shape[1]
    own = points * n_top
    cap = 2 * points // n_pts
    box_cap = 2 * BOXES4 // n_pts
    dens = DENS // n_top
    slabs = max(1, 2 * SIDE // n_pts)
    coef = uc2e.shape[0]
    scalar = lambda *v: jnp.stack([jnp.asarray(x, jnp.int32) for x in v])

    slot_row = morton_slot.reshape(1, points)
    outgoing = call(
        functools.partial(route_kernel, own, cap, n_top),
        jax.ShapeDtypeStruct((n_pts, n_top, 8, cap), f32),
        32,
        1 << 27,
        in_specs=[VMEM] * 3,
        out_specs=VMEM,
    )(local_pos, densities, slot_row)
    outgoing = outgoing.reshape(n_pts * n_top, 8, cap)
    incoming = lax.all_to_all(outgoing, ("pts", "top"), split_axis=0, concat_axis=0, tiled=True)

    shared = jnp.concatenate(
        [
            local_pos,
            morton_slot.astype(f32).reshape(1, points),
            slot_leaf.astype(f32).reshape(1, points),
        ],
        axis=0,
    )
    shared = shifts_of("top", shared, range(n_top))
    leaves = jnp.stack([s[4] for s in shared])
    row_pos = jnp.concatenate([s[0:3] for s in shared], axis=1)
    row_slot = jnp.concatenate([s[3:4] for s in shared], axis=1)
    all_leaves = jnp.stack(shifts_of("pts", leaves, range(n_pts)))
    firsts = (jnp.min(all_leaves, axis=(1, 2)).astype(jnp.int32)) // 8
    box_ids = (firsts[:, None] + jnp.arange(box_cap, dtype=jnp.int32)[None, :]).reshape(1, -1)

    oa, ob, oc = relayout(m2l_ops, scalar(me & 1))
    m2m = m2m.reshape(8, coef, coef)
    l2l = l2l.reshape(8, coef, coef)
    scale = 1.0 / (4.0 * math.pi)
    high = lax.Precision.HIGHEST
    w_up = jnp.einsum("ocf,fe->coe", m2m, uc2e * scale, precision=high)
    pad = ((0, 0), (0, 0), (0, CPAD - coef))
    w_up = split_oper(jnp.pad(w_up, pad).reshape(coef, 8 * CPAD))
    w_down = jnp.transpose(l2l * scale, (2, 0, 1))
    w_down = split_oper(jnp.pad(w_down, pad).reshape(coef, 8 * CPAD))
    surf = jnp.asarray(np.repeat((np.float32(1.25) * surface_table())[:, :, None], PB, axis=2))

    table = leaves.reshape(own // LANE, LANE).T.astype(jnp.int32)
    table = jnp.concatenate([table // 8 - firsts[0], table % 8], axis=0).astype(bf16)
    partial = call(
        functools.partial(upward_kernel, own, box_cap),
        jax.ShapeDtypeStruct((coef, dens * box_cap), bf16),
        32,
        8 << 30,
        in_specs=[SMEM] + [VMEM] * 5,
        out_specs=VMEM,
        scratch_shapes=[pltpu.VMEM((8, up(own + up(cap, LANE) + LANE, PB)), f32)],
    )(scalar(top * points), incoming, table, surf, *w_up)
    parts = shifts_of("pts", partial, range(n_pts))
    part = jnp.stack(
        [
            jnp.concatenate([v[:, k * box_cap : (k + 1) * box_cap] for v in parts], axis=1)
            for k in range(dens)
        ]
    )

    table = all_leaves.reshape(-1, LANE).T.astype(jnp.int32)
    table = jnp.concatenate([table // 64, table % 64], axis=0).astype(bf16)
    field, place = call(
        target_kernel,
        (
            jax.ShapeDtypeStruct((coef, own), f32),
            jax.ShapeDtypeStruct((1, own), jnp.int32),
        ),
        32,
        6 << 30,
        in_specs=[SMEM] + [VMEM] * 6,
        out_specs=(VMEM, VMEM),
    )(scalar(me * own + top * points), row_pos, row_slot, table, surf, *w_down)

    columns = dens * PLANE
    x0 = (me // 2 * 2) * SIDE // n_pts
    checks = call(
        functools.partial(translate_kernel, slabs),
        jax.ShapeDtypeStruct((ROWS, slabs * columns), bf16),
        56,
        8 << 30,
        in_specs=[SMEM, VMEM, VMEM, ANY, ANY, ANY],
        out_specs=VMEM,
        scratch_shapes=[
            pltpu.VMEM(((7 + slabs - 1) * columns, WFULL), bf16),
            pltpu.VMEM(((7 + slabs - 1) * columns, WIN), bf16),
            pltpu.VMEM((7 * ROWS, slabs * columns), f32),
            pltpu.VMEM(oa.shape, bf16),
            pltpu.VMEM(ob.shape, bf16),
            pltpu.VMEM(oc.shape, bf16),
            pltpu.SemaphoreType.DMA((3, 7)),
        ],
    )(scalar(x0), box_ids, part, oa, ob, oc)
    step = n_pts // SIDE * slabs
    distances = [step * m + c for m in range(SIDE // slabs) for c in range(2)]
    gathered = shifts_of("pts", checks, distances)

    lattice4 = call(
        coarse_kernel,
        jax.ShapeDtypeStruct((dens, coef, BOXES4), f32),
        32,
        4 << 30,
        in_specs=[VMEM] * 8,
        out_specs=VMEM,
    )(box_ids, part, *split_oper(m2m), *split_oper(lattice), *split_oper(l2l))

    halves = dc2e.reshape(coef, NG, 2, 4).transpose(2, 0, 1, 3).reshape(2, coef, 4 * NG)
    halves = split_oper(jnp.pad(halves, ((0, 0), (0, 0), (0, ROWS - 4 * NG))))
    reply = call(
        functools.partial(evaluate_kernel, slabs),
        jax.ShapeDtypeStruct((dens, own), f32),
        32,
        4 << 30,
        in_specs=[SMEM] + [VMEM] * (len(gathered) + 5),
        out_specs=VMEM,
        scratch_shapes=[pltpu.VMEM((2 * dens * CPAD, BOXES4), f32)],
    )(scalar(me & 1, me // step), *gathered, *halves, lattice4, field, place)
    reply = reply.reshape(dens, n_top, points)
    answers = []
    for m in range(n_top):
        value = reply[:, m]
        if m:
            value = lax.ppermute(value, "top", [(i, i ^ m) for i in range(n_top)])
        answers.append(value)
    answers = jnp.stack(answers)
    order = jnp.arange(n_top, dtype=jnp.int32) ^ top
    picked = sum(
        jnp.where(order[:, None, None, None] == m, answers[m][None], 0.0) for m in range(n_top)
    )
    return picked.reshape(DENS, points)


def solution(mesh):
    split_all = P(None, ("pts", "top"))
    placed = (split_all, split_all, P(("pts", "top")), P(("pts", "top"))) + (P(),) * 6
    return jax.shard_map(
        per_device, mesh=mesh, in_specs=placed, out_specs=split_all, check_vma=False
    )
```

```python
import functools
import math

import jax
import jax.numpy as jnp
import numpy as np
from jax import lax
from jax.experimental import pallas as pl
from jax.experimental.pallas import tpu as pltpu
from jax.sharding import PartitionSpec as P

LEVEL = 3
EDGE = 6
DENS = 8
SIDE = 2**LEVEL
BOXES4 = SIDE**3
PLANE = SIDE * SIDE
LANE = 128
REACH = 3
SHIFTS = list(range(-REACH, REACH + 1))
OUTER = [s for s in SHIFTS if abs(s) >= 2]
INNER = [s for s in SHIFTS if abs(s) < 2]
bf16 = jnp.bfloat16
f32 = jnp.float32
NN = (((1,), (0,)), ((), ()))
NT = (((1,), (1,)), ((), ()))


def up(value, multiple):
    return -(-value // multiple) * multiple


def surface_table():
    grid_vals = np.linspace(-1.0, 1.0, EDGE)
    points_list = []
    for a in range(EDGE):
        for b in range(EDGE):
            for c in range(EDGE):
                if min(a, b, c) == 0 or max(a, b, c) == EDGE - 1:
                    points_list.append([grid_vals[a], grid_vals[b], grid_vals[c]])
    return np.array(points_list, dtype=np.float32).T


COEF = surface_table().shape[1]
OFFSETS = (2 * REACH + 1) ** 3 - 27
CPAD = up(COEF, 32)


def blocks():
    out, position = [], 0
    for dx in SHIFTS:
        for dy in SHIFTS:
            count = sum(max(abs(dx), abs(dy), abs(dz)) >= 2 for dz in SHIFTS)
            out.append((dx, dy, position, count))
            position += count
    return out


def dot(a, b, dims=NN):
    return lax.dot_general(a, b, dims, preferred_element_type=f32)


def split(value):
    high = value.astype(bf16)
    return high, (value - high.astype(f32)).astype(bf16)


def dot3(a, b, dims=NN):
    return dot(a[0], b[0], dims) + dot(a[1], b[0], dims) + dot(a[0], b[1], dims)


def dot3_rows(a, b, dims=NN):
    rows = a[0].shape[0]
    both = jnp.concatenate([x.astype(f32) for x in a], axis=0).astype(bf16)
    both = dot(both, b[0], dims)
    return both[0:rows] + both[rows : 2 * rows] + dot(a[0], b[1], dims)


def call(kernel, out_shape, mib, flops, bytes_accessed=1 << 20, **kw):
    return pl.pallas_call(
        kernel,
        out_shape=out_shape,
        compiler_params=pltpu.CompilerParams(vmem_limit_bytes=mib << 20),
        cost_estimate=pl.CostEstimate(
            flops=flops, bytes_accessed=bytes_accessed, transcendentals=0
        ),
        **kw,
    )


VMEM = pl.BlockSpec(memory_space=pltpu.VMEM)
SMEM = pl.BlockSpec(memory_space=pltpu.SMEM)
ANY = pl.BlockSpec(memory_space=pl.ANY)


HG = 4 * OFFSETS * COEF // LANE
KT = up(up(OFFSETS * COEF, LANE) // LANE, 8)
WFULL = up(7 * COEF, LANE)
WIN = up(4 * COEF, LANE)
NG = COEF // 8
STEPS = -(-NG // 4)
ROWS = 16 * STEPS
CHUNK = up(HG + 15, 16)
TAIL = 32
STRIDE = 17


def relayout_kernel(nrows, me_ref, f_hbm, tail_ref, oa, ob, oc, inb, fbuf, tbuf, tb16, sem):
    step = pl.program_id(0)
    half = me_ref[0] & 1
    end16 = nrows // 16 * 16

    def start_row(st, g):
        return jnp.minimum(4 * st + g, NG - 1) * (2 * HG) + half * HG

    def start(st, slot):
        for g in range(4):
            row = pl.multiple_of(start_row(st, g) // 16 * 16, 16)
            pltpu.make_async_copy(
                f_hbm.at[pl.ds(row, CHUNK - TAIL)],
                inb.at[slot, g, pl.ds(0, CHUNK - TAIL)],
                sem.at[slot, g, 0],
            ).start()
            last = row + CHUNK > end16

            @pl.when(jnp.logical_not(last))
            def _():
                pltpu.make_async_copy(
                    f_hbm.at[pl.ds(pl.multiple_of(row + CHUNK - TAIL, 16), TAIL)],
                    inb.at[slot, g, pl.ds(CHUNK - TAIL, TAIL)],
                    sem.at[slot, g, 1],
                ).start()


    def wait(st, slot):
        for g in range(4):
            row = pl.multiple_of(start_row(st, g) // 16 * 16, 16)
            pltpu.make_async_copy(
                f_hbm.at[pl.ds(row, CHUNK - TAIL)],
                inb.at[slot, g, pl.ds(0, CHUNK - TAIL)],
                sem.at[slot, g, 0],
            ).wait()
            last = row + CHUNK > end16

            @pl.when(jnp.logical_not(last))
            def _():
                pltpu.make_async_copy(
                    f_hbm.at[pl.ds(pl.multiple_of(row + CHUNK - TAIL, 16), TAIL)],
                    inb.at[slot, g, pl.ds(CHUNK - TAIL, TAIL)],
                    sem.at[slot, g, 1],
                ).wait()

            @pl.when(last)
            def _():
                row16 = lax.broadcasted_iota(jnp.int32, (16, LANE), 0)
                tail = jnp.where(row16 < nrows - end16, tail_ref[...].astype(f32), 0.0)
                inb[slot, g, CHUNK - TAIL : CHUNK - TAIL + 16] = tail.astype(bf16)

    slot = lax.rem(step, 2)

    @pl.when(step == 0)
    def _():
        fbuf[...] = jnp.zeros_like(fbuf)
        start(0, 0)

    @pl.when(step + 1 < STEPS)
    def _():
        start(step + 1, 1 - slot)

    wait(step, slot)
    lane = lax.broadcasted_iota(jnp.int32, (8, LANE), 1)
    for g in range(4):
        fbuf[g, 0:CHUNK] = inb[slot, g].astype(f32)
    for g in range(4):
        row = start_row(step, g)
        off = row - row // 16 * 16
        for e in range(4):
            first = OFFSETS * COEF * e
            phase = first % LANE

            @pl.loop(0, KT // 8, unroll=KT // 8)
            def _(n):
                base = off + first // LANE + 8 * n
                value = fbuf[g, pl.ds(base, 8), :]
                if phase:
                    after = fbuf[g, pl.ds(base + 1, 8), :]
                    value = pltpu.roll(jnp.where(lane >= phase, value, after), LANE - phase, 1)
                tbuf[pl.ds(8 * n * STRIDE + 4 * g + e, 8, stride=STRIDE), :] = value

    @pl.loop(0, KT, unroll=8)
    def _(k):
        tb16[k] = tbuf[pl.ds(k * STRIDE, 16), :].astype(bf16)

    for dx, dy, d0, count in blocks():
        tile0, phase = divmod(d0 * COEF, LANE)
        if dy in OUTER:
            ref = oa.at[dx + REACH, OUTER.index(dy)]
        elif dx in OUTER:
            ref = ob.at[OUTER.index(dx), INNER.index(dy)]
        else:
            ref = oc.at[INNER.index(dx), INNER.index(dy)]
        for t in range(up(count * COEF, LANE) // LANE):
            value = tb16[tile0 + t]
            if phase:
                after = tb16[min(tile0 + t + 1, KT - 1)]
                value = jnp.concatenate([value[:, phase:], after[:, :phase]], axis=1)
            ref[:, t * LANE : (t + 1) * LANE] = value


def relayout(flat, me):
    nrows = flat.shape[0] // LANE
    rows = flat.reshape(nrows, LANE)
    shapes = ((7, 4, ROWS, WFULL), (4, 3, ROWS, WFULL), (3, 3, ROWS, WIN))
    return call(
        functools.partial(relayout_kernel, nrows),
        tuple(jax.ShapeDtypeStruct(s, bf16) for s in shapes),
        58,
        1 << 20,
        16 << 20,
        grid_spec=pltpu.PrefetchScalarGridSpec(
            num_scalar_prefetch=1,
            grid=(STEPS,),
            in_specs=[ANY, pl.BlockSpec((16, LANE), lambda i, h: (nrows // 16, 0))],
            out_specs=tuple(
                pl.BlockSpec((s[0], s[1], 16, s[3]), lambda i, h: (0, 0, i, 0)) for s in shapes
            ),
            scratch_shapes=[
                pltpu.VMEM((2, 4, CHUNK, LANE), bf16),
                pltpu.VMEM((4, CHUNK + 16, LANE), f32),
                pltpu.VMEM((KT * STRIDE, LANE), f32),
                pltpu.VMEM((KT, 16, LANE), bf16),
                pltpu.SemaphoreType.DMA((2, 4, 2)),
            ],
        ),
    )(me, rows, rows)


GROUP = 16


def square(flat, out):
    per = GROUP * COEF // LANE
    groups = flat.shape[0] // per
    lane = lax.broadcasted_iota(jnp.int32, (groups, LANE), 1)
    for r in range(GROUP):
        first, phase = divmod(r * COEF, LANE)
        got = []
        for t in range(3):
            row = min(first + t, per - 1)
            got.append(flat[pl.ds(row, groups, stride=per), :])
        for t in range(2):
            value = got[t]
            if phase:
                value = jnp.where(lane >= phase, got[t], got[t + 1])
                value = pltpu.roll(value, LANE - phase, 1)
            out[t, pl.ds(r, groups, stride=GROUP), :] = value


def operators_kernel(
    m2m, l2l, uc2e, dc2e, lattice, w_up, w_down, m2m_hi, m2m_lo, l2l_hi, l2l_lo, lat_hi, lat_lo,
    d_hi, d_lo, rows
):
    scale = 1.0 / (4.0 * math.pi)
    lat_hi[...], lat_lo[...] = split(lattice[...])
    first = split(uc2e[...] * scale)

    def stack(pieces, out):
        blank = jnp.zeros((COEF, CPAD - COEF), f32)
        wide = jnp.concatenate([x for p in pieces for x in (p, blank)], axis=1)
        high, low = split(wide)
        out[0:COEF] = high
        out[COEF : 2 * COEF] = low

    def matrix(o):
        at = slice(o * COEF, (o + 1) * COEF)
        return jnp.concatenate([rows[0, at], rows[1, at, 0 : COEF - LANE]], axis=1)

    square(m2m, rows)
    pieces = []
    for o in range(8):
        high, low = split(matrix(o))
        m2m_hi[o], m2m_lo[o] = high, low
        pieces.append(dot3((high, low), first))
    stack(pieces, w_up)
    square(l2l, rows)
    pieces = []
    for o in range(8):
        value = matrix(o)
        l2l_hi[o], l2l_lo[o] = split(value)
        pieces.append(jnp.transpose(value) * scale)
    stack(pieces, w_down)
    high, low = split(dc2e[...])
    i = lax.broadcasted_iota(jnp.int32, (COEF, ROWS), 0)
    r = lax.broadcasted_iota(jnp.int32, (COEF, ROWS), 1)
    for h in range(2):
        here = (i == (r >> 2) * 8 + 4 * h + (r & 3)) & (r < 4 * NG)
        here = jnp.where(here, 1.0, 0.0).astype(bf16)
        d_hi[h] = dot(high, here).astype(bf16)
        d_lo[h] = dot(low, here).astype(bf16)


def route_kernel(own, cap, n_top, pos, dens, slot, leaf, out, shared):
    points = pos.shape[1]
    owners = out.shape[0]
    slots = slot[...]
    shared[0:3] = pos[...]
    shared[3:4] = slots.astype(f32)
    owner = slots // own
    inside = slots - owner * own
    hit = owner == lax.broadcasted_iota(jnp.int32, (owners, points), 0)
    hit = jnp.where(hit, 1.0, 0.0)
    hit16 = hit.astype(bf16)
    row = lax.broadcasted_iota(jnp.int32, (LANE, LANE), 0)
    col = lax.broadcasted_iota(jnp.int32, (LANE, LANE), 1)
    before = jnp.where(row < col, 1.0, 0.0).astype(bf16)
    every = jnp.ones((LANE, LANE), bf16)
    total = jnp.zeros((owners, LANE), f32)
    ranks = []
    for t in range(points // LANE):
        part = hit16[:, t * LANE : (t + 1) * LANE]
        ranks.append(total + dot(part, before))
        total = total + dot(part, every)
    rank = jnp.sum(hit * jnp.concatenate(ranks, axis=1), axis=0, keepdims=True)
    entry = owner * cap + rank.astype(jnp.int32)
    inside_hi = inside // 64
    value = jnp.concatenate([pos[...], dens[...]], axis=0)
    width = value.shape[0]
    high, low = split(value)
    ones = jnp.ones((1, points), f32)
    high = jnp.concatenate(
        [high.astype(f32), inside_hi.astype(f32), (inside - 64 * inside_hi).astype(f32), ones]
        + [jnp.zeros((16 - width - 3, points), f32)],
        axis=0,
    )
    low = jnp.concatenate([low.astype(f32), jnp.zeros((16 - width, points), f32)], axis=0)
    payload = jnp.concatenate([high, low], axis=0).astype(bf16)
    block = max(cap, LANE)
    per = DENS // n_top
    leaves = leaf[...].astype(f32)
    if leaves.shape[1] < cap:
        leaves = jnp.concatenate(
            [leaves, jnp.zeros((leaves.shape[0], cap - leaves.shape[1]), f32)], axis=1
        )
    for o in range(owners * cap // block):
        there = entry == o * block + lax.broadcasted_iota(jnp.int32, (block, points), 0)
        there = jnp.where(there, 1.0, 0.0).astype(bf16)
        got = dot(payload, there, NT)
        value = got[0:width] + got[16 : 16 + width]
        where = got[width : width + 1] * 64.0 + got[width + 1 : width + 2]
        valid = got[width + 2 : width + 3]
        for q in range(n_top):
            rows = [value[0:3], where, valid, value[3 + per * q : 3 + per * (q + 1)]]
            rows.append(jnp.zeros((8 - 5 - per, block), f32))
            packed = jnp.concatenate([r for r in rows if r.shape[0]], axis=0)
            for i in range(block // cap):
                at = o * (block // cap) + i
                out[at, q, 0:8] = packed[:, i * cap : (i + 1) * cap]
                out[at, q, 8:] = leaves


def octant_product(pos, octant, surf, oper):
    squared = None
    for d in range(3):
        spacing = surf[d] - pos[d : d + 1]
        squared = spacing * spacing if squared is None else squared + spacing * spacing
    value = lax.rsqrt(squared)
    value = jnp.concatenate([value, jnp.zeros((CPAD - COEF, value.shape[1]), f32)], axis=0)
    high, low = split(value)
    masks = [jnp.where(octant == o, 1.0, 0.0).astype(bf16) for o in range(8)]
    got = dot(oper[...], jnp.concatenate([high * m for m in masks], axis=0))
    got = got[0:COEF] + got[COEF : 2 * COEF]
    return got + dot(oper[0:COEF], jnp.concatenate([low * m for m in masks], axis=0))


TURNED = (((0,), (0,)), ((), ()))


def look_up(index, first, second):
    rows, lanes = first.shape
    width = index.shape[1]
    at_row = index // lanes
    at_lane = index - at_row * lanes
    there = at_row == lax.broadcasted_iota(jnp.int32, (rows, width), 0)
    there = jnp.where(there, 1.0, 0.0).astype(bf16)
    mine = at_lane == lax.broadcasted_iota(jnp.int32, (lanes, width), 0)
    out = []
    for table in (first, second):
        got = dot(table, there, TURNED)
        out.append(jnp.sum(jnp.where(mine, got, 0.0), axis=0, keepdims=True))
    return out


PB = 256


def fill_surface(surf, column):
    for d in range(3):
        surf[d] = jnp.broadcast_to(column[:, d : d + 1], surf.shape[1:])


def upward_kernel(n_top, own, box_cap, me_ref, got, column, oper, out, ids, buf, surf):
    sources, _, cap = got.shape
    lanes = min(cap, LANE)
    wide = up(cap, LANE)
    me = me_ref[0]
    buf[...] = jnp.zeros_like(buf)
    fill_surface(surf, column)

    def place(s, offset):
        value = got[s, 0:8]
        count = jnp.sum(value[4:5]).astype(jnp.int32)
        value = jnp.concatenate([value, jnp.zeros((8, wide + LANE - cap), f32)], axis=1)
        tile = offset // LANE
        value = pltpu.roll(value, offset - tile * LANE, 1)
        place_at = pl.ds(pl.multiple_of(tile * LANE, LANE), wide + LANE)
        buf[:, place_at] = buf[:, place_at] + value
        return offset + count

    lax.fori_loop(0, sources, place, jnp.int32(0), unroll=4)
    out_rows = out.shape[1]
    firsts = []
    at = lax.broadcasted_iota(jnp.int32, (1, box_cap), 1)
    for m in range(sources // n_top):
        leaf = got[(me ^ m) * n_top, 8:9, 0:1].astype(jnp.int32)
        firsts.append((leaf >> 3) + at)
    ids[...] = jnp.concatenate(firsts, axis=1)
    leaf = got[pl.ds(me * n_top, n_top), 8:, 0:lanes].reshape(own // lanes, lanes)
    leaf = leaf.astype(jnp.int32)
    first = got[me * n_top, 8:9, 0:1].astype(jnp.int32) >> 3
    boxes = ((leaf >> 3) - first).astype(f32).astype(bf16)
    octants = (leaf & 7).astype(f32).astype(bf16)

    def block(j, total):
        value = buf[:, pl.ds(pl.multiple_of(j * PB, PB), PB)]
        box, octant = look_up(value[3:4].astype(jnp.int32), boxes, octants)
        high, low = split(octant_product(value[0:3], octant, surf, oper))
        rows = []
        at = lax.broadcasted_iota(jnp.int32, (box_cap, PB), 0).astype(f32)
        for k in range(out_rows // box_cap):
            rows.append(jnp.where(box == at, value[5 + k : 6 + k], 0.0))
        a_high, a_low = split(jnp.concatenate(rows, axis=0))
        both = dot(jnp.concatenate([high, low], axis=0), a_high, NT)
        return total + both[0:COEF] + both[COEF : 2 * COEF] + dot(high, a_low, NT)

    total = lax.fori_loop(0, own // PB, block, jnp.zeros((COEF, out_rows), f32))
    out[...] = total.astype(bf16)


def morton_place(box):
    place = jnp.zeros_like(box)
    for b in range(LEVEL):
        digit = box >> (3 * b)
        place = place + ((((digit >> 2) & 1) << (2 * LEVEL + b)))
        place = place + ((((digit >> 1) & 1) << (LEVEL + b)) + ((digit & 1) << b))
    return place


def target_kernel(n_top, got, *refs):
    shared = refs[:n_top]
    column, oper, field, place, surf = refs[n_top:]
    fill_surface(surf, column)
    lanes = min(got.shape[2], LANE)
    leaf = got[:, 8:, 0:lanes].reshape(-1, lanes).astype(jnp.int32)
    boxes = (leaf >> 6).astype(f32).astype(bf16)
    rest = (leaf & 63).astype(f32).astype(bf16)
    points = shared[0].shape[1]
    for m in range(n_top):
        source = shared[m]

        @pl.loop(0, points // PB)
        def _(j):
            at = pl.ds(pl.multiple_of(j * PB, PB), PB)
            value = source[:, at]
            high, low = look_up(value[3:4].astype(jnp.int32), boxes, rest)
            leaf = (high * 64.0 + low).astype(jnp.int32)
            to = pl.ds(pl.multiple_of(m * points + j * PB, PB), PB)
            field[:, to] = octant_product(value[0:3], leaf & 7, surf, oper)
            place[:, to] = morton_place(leaf >> 3)


def all_parts(parts, k, dens):
    width = parts[0].shape[1] // dens
    return jnp.concatenate([p[:, k * width : (k + 1) * width] for p in parts], axis=1)


def translate_kernel(slabs, dens, me_ref, ids, *refs):
    parts = refs[:-11]
    oa, ob, oc, out, xs, xin, acc, ma, mb, mc, sem = refs[-11:]
    copies = []
    for i, (src, dst) in enumerate(((oa, ma), (ob, mb), (oc, mc))):
        for j in range(src.shape[0]):
            copies.append(pltpu.make_async_copy(src.at[j], dst.at[j], sem.at[i, j]))
            copies[-1].start()
    x0 = (me_ref[0] // 2 * 2) * SIDE // len(parts)
    place = morton_place(ids[...])
    place = (((place >> 6) - x0 + REACH) & 7) * 64 + (place & 63)
    place = jnp.where((ids[...] >= 0) & (ids[...] < BOXES4), place, -1)
    at = lax.broadcasted_iota(jnp.int32, (BOXES4, ids.shape[1]), 0)
    there = jnp.where(at == place, 1.0, 0.0).astype(bf16)
    columns = dens * PLANE
    for k in range(dens):
        low = dot(there, all_parts(parts, k, dens), NT)
        low = low.astype(bf16).astype(f32)
        for s in range(7 + slabs - 1):
            slab = low[s * PLANE : (s + 1) * PLANE].reshape(SIDE, SIDE, COEF)
            shifted = {}
            for dz in SHIFTS:
                if dz == 0:
                    moved = slab
                else:
                    cut = dz % SIDE
                    moved = jnp.concatenate([slab[:, cut:], slab[:, :cut]], axis=1)
                shifted[dz] = moved.reshape(PLANE, COEF)
            rows = pl.ds(s * columns + k * PLANE, PLANE)
            pad = [jnp.zeros((PLANE, WFULL - 7 * COEF), f32)]
            xs[rows, :] = jnp.concatenate([shifted[z] for z in SHIFTS] + pad, axis=1).astype(bf16)
            pad = [jnp.zeros((PLANE, WIN - 4 * COEF), f32)]
            xin[rows, :] = jnp.concatenate([shifted[z] for z in OUTER] + pad, axis=1).astype(bf16)
    for c in copies:
        c.wait()
    n_out = len(OUTER) * ROWS
    n_in = len(INNER) * ROWS
    for i, dx in enumerate(SHIFTS):
        rows = pl.ds(i * columns, slabs * columns)
        source = xs[rows, :]
        outer = dot(ma[i].reshape(n_out, WFULL), source, NT)
        if dx in OUTER:
            inner = dot(mb[OUTER.index(dx)].reshape(n_in, WFULL), source, NT)
        else:
            inner = dot(mc[INNER.index(dx)].reshape(n_in, WIN), xin[rows, :], NT)
        if i == 0:
            acc[0:n_out] = outer
            acc[n_out : n_out + n_in] = inner
        else:
            acc[0:n_out] += outer
            acc[n_out : n_out + n_in] += inner
    lane = lax.broadcasted_iota(jnp.int32, (ROWS, LANE), 1)
    for t in range(slabs * columns // LANE):
        total = jnp.zeros((ROWS, LANE), f32)
        for i, dy in enumerate(OUTER + INNER):
            value = acc[i * ROWS : (i + 1) * ROWS, t * LANE : (t + 1) * LANE]
            by = SIDE * (dy % SIDE)
            if by:
                near = pltpu.roll(value, LANE - by, 1)
                far = pltpu.roll(value, PLANE - by, 1)
                value = jnp.where((lane & (PLANE - 1)) < PLANE - by, near, far)
            total = total + value
        out[:, t * LANE : (t + 1) * LANE] = total.astype(out.dtype)


def coarse_kernel(ids, *refs):
    parts = refs[:-7]
    m2m_hi, m2m_lo, lat_hi, lat_lo, l2l_hi, l2l_lo, out = refs[-7:]
    dens = out.shape[0]
    box = ids[...]
    place = ((box & 7) << 6) + (box & 56) + (box >> 6)
    place = jnp.where((box >= 0) & (box < BOXES4), place, -1)
    at = lax.broadcasted_iota(jnp.int32, (BOXES4, ids.shape[1]), 0)
    there = jnp.where(at == place, 1.0, 0.0).astype(bf16)
    level = [dot(there, all_parts(parts, k, dens), NT) for k in range(dens)]

    def oper(hi, lo, o):
        return hi[o], lo[o]

    for _ in range(LEVEL):
        count = level[0].shape[0] // 8
        total = None
        for o in range(8):
            rows = jnp.concatenate([v[o * count : (o + 1) * count] for v in level], axis=0)
            term = dot3_rows(split(rows), oper(m2m_hi, m2m_lo, o), NT)
            total = term if total is None else total + term
        level = [total[k * count : (k + 1) * count] for k in range(dens)]
    rows = jnp.concatenate(level, axis=0)
    rows = dot3(split(rows), (lat_hi[...], lat_lo[...]), NT)
    level = [rows[k : k + 1] for k in range(dens)]
    for _ in range(LEVEL):
        count = level[0].shape[0]
        rows = split(jnp.concatenate(level, axis=0))
        children = [dot3_rows(rows, oper(l2l_hi, l2l_lo, o), NT) for o in range(8)]
        level = [
            jnp.concatenate([c[k * count : (k + 1) * count] for c in children], axis=0)
            for k in range(dens)
        ]
    at = lax.broadcasted_iota(jnp.int32, (BOXES4, BOXES4), 1)
    row = lax.broadcasted_iota(jnp.int32, (BOXES4, BOXES4), 0)
    number = ((row & 7) << 6) + (row & 56) + (row >> 6)
    move = jnp.where(at == morton_place(number), 1.0, 0.0).astype(bf16)
    for k in range(dens):
        high, low = split(level[k])
        out[k] = dot(high, move, TURNED) + dot(low, move, TURNED)


def evaluate_kernel(slabs, step, me_ref, *refs):
    n = SIDE // slabs
    checks = refs[: 2 * n]
    d_hi, d_lo, lattice, field, place, out, stack = refs[2 * n :]
    core = me_ref[0] & 1
    group = me_ref[0] // step
    dens = lattice.shape[0]
    points = out.shape[2]
    lane = lax.broadcasted_iota(jnp.int32, (COEF, LANE), 1)
    mine = jnp.concatenate([d_hi[core], d_lo[core]], axis=0)
    other = jnp.concatenate([d_hi[1 - core], d_lo[1 - core]], axis=0)
    for m in range(n):
        value = dot(mine, checks[2 * m][...]) + dot(other, checks[2 * m + 1][...])
        value = value[0:COEF] + value[COEF : 2 * COEF]
        if slabs == 2:
            a, b = value[:, 0:LANE], value[:, LANE : 2 * LANE]
            half = LANE // 2
            pieces = [
                jnp.where(lane < half, a, pltpu.roll(b, half, 1)),
                jnp.where(lane < half, pltpu.roll(a, half, 1), b),
            ]
        else:
            pieces = [value[:, k * PLANE : (k + 1) * PLANE] for k in range(dens)]
        width = slabs * PLANE
        for k in range(dens):
            at = m ^ group
            if width % LANE == 0:
                base = lattice[k, :, pl.ds(pl.multiple_of(at * width, width), width)]
            else:
                pair = lattice[k, :, pl.ds(pl.multiple_of(at // 2 * LANE, LANE), LANE)]
                base = jnp.where(at % 2 == 0, pair[:, :width], pair[:, width:])
            high, low = split(pieces[k] + base)
            rows = pl.ds(k * CPAD, COEF)
            stack[rows, m * width : (m + 1) * width] = high.astype(f32)
            rows = pl.ds((dens + k) * CPAD, COEF)
            stack[rows, m * width : (m + 1) * width] = low.astype(f32)
    local = stack[...].astype(bf16)

    @pl.loop(0, place.shape[1] // PB)
    def _(j):
        at = pl.ds(pl.multiple_of(j * PB, PB), PB)
        m = j // (points // PB)
        to = pl.ds(pl.multiple_of((j - m * (points // PB)) * PB, PB), PB)
        want = place[:, at] ^ (group * (slabs * PLANE))
        there = want == lax.broadcasted_iota(jnp.int32, (BOXES4, PB), 0)
        got = dot(local, jnp.where(there, 1.0, 0.0).astype(bf16))
        mine = field[:, at]
        rows = []
        for k in range(dens):
            value = got[k * CPAD : k * CPAD + COEF]
            value = value + got[(dens + k) * CPAD : (dens + k) * CPAD + COEF]
            rows.append(jnp.sum(value * mine, axis=0, keepdims=True))
        out[m, :, to] = jnp.concatenate(rows, axis=0)


def shift_by(axis, value, distance):
    size = lax.axis_size(axis)
    return lax.ppermute(value, axis, [(i, i ^ distance) for i in range(size)])


def gather_by(value, distances):
    got = {m: shift_by("pts", value, m) if m else value for m in distances if m % 2 == 0}
    got.update({m + 1: shift_by("pts", got[m], 1) for m in list(got) if m + 1 in distances})
    return [got[m] for m in distances]


def per_device(
    local_pos, densities, morton_slot, slot_leaf, uc2e, m2m, m2l_ops, dc2e, lattice, l2l
):
    n_pts = lax.axis_size("pts")
    n_top = lax.axis_size("top")
    top = lax.axis_index("top")
    me = lax.axis_index("pts").astype(jnp.int32).reshape(1)
    points = local_pos.shape[1]
    own = points * n_top
    cap = 2 * points // n_pts
    lanes = min(cap, LANE)
    box_cap = 2 * BOXES4 // n_pts
    dens = DENS // n_top
    slabs = max(1, 2 * SIDE // n_pts)
    coef = uc2e.shape[0]

    def shape(*dims, dtype=bf16):
        return jax.ShapeDtypeStruct(dims, dtype)

    rows = 8 + points // lanes
    outgoing, shared = call(
        functools.partial(route_kernel, own, cap, n_top),
        (shape(n_pts, n_top, rows, cap, dtype=f32), shape(4, points, dtype=f32)),
        32,
        1 << 27,
        in_specs=[VMEM] * 4,
        out_specs=(VMEM, VMEM),
    )(
        local_pos,
        densities,
        morton_slot.reshape(1, points),
        slot_leaf.reshape(points // lanes, lanes),
    )
    outgoing = outgoing.reshape(n_pts * n_top, rows, cap)
    incoming = lax.all_to_all(outgoing, ("pts", "top"), split_axis=0, concat_axis=0, tiled=True)

    shared = [shift_by("top", shared, m) if m else shared for m in range(n_top)]
    flat = (-1, LANE)
    two = 2 * coef
    square_shape = shape(8, coef, coef)
    w_up, w_down, *coarse_ops = call(
        operators_kernel,
        (shape(two, 8 * CPAD), shape(two, 8 * CPAD))
        + (square_shape,) * 4
        + (shape(coef, coef),) * 2
        + (shape(2, coef, ROWS),) * 2,
        32,
        1 << 30,
        in_specs=[VMEM] * 5,
        out_specs=(VMEM,) * 10,
        scratch_shapes=[pltpu.VMEM((2, 8 * coef, LANE), f32)],
    )(m2m.reshape(flat), l2l.reshape(flat), uc2e, dc2e, lattice)
    coarse_ops, halves = coarse_ops[:6], coarse_ops[6:]
    m2m_hi, m2m_lo, l2l_hi, l2l_lo, lat_hi, lat_lo = coarse_ops
    oa, ob, oc = relayout(m2l_ops, me)
    column = jnp.asarray(
        np.pad((np.float32(1.25) * surface_table()).T, ((0, 0), (0, LANE - 3)))
    )

    surf = pltpu.VMEM((3, coef, PB), f32)
    partial, ids = call(
        functools.partial(upward_kernel, n_top, own, box_cap),
        (shape(coef, dens * box_cap), shape(1, n_pts * box_cap, dtype=jnp.int32)),
        32,
        8 << 30,
        in_specs=[SMEM] + [VMEM] * 3,
        out_specs=(VMEM, VMEM),
        scratch_shapes=[pltpu.VMEM((8, up(own + up(cap, LANE) + LANE, PB)), f32), surf],
    )(me, incoming, column, w_up)
    parts = gather_by(partial, range(n_pts))

    field, place = call(
        functools.partial(target_kernel, n_top),
        (shape(coef, own, dtype=f32), shape(1, own, dtype=jnp.int32)),
        32,
        6 << 30,
        in_specs=[VMEM] * (n_top + 3),
        out_specs=(VMEM, VMEM),
        scratch_shapes=[surf],
    )(incoming, *shared, column, w_down)

    columns = dens * PLANE
    checks = call(
        functools.partial(translate_kernel, slabs, dens),
        shape(ROWS, slabs * columns),
        56,
        8 << 30,
        in_specs=[SMEM] + [VMEM] * (1 + n_pts) + [ANY] * 3,
        out_specs=VMEM,
        scratch_shapes=[
            pltpu.VMEM(((7 + slabs - 1) * columns, WFULL), bf16),
            pltpu.VMEM(((7 + slabs - 1) * columns, WIN), bf16),
            pltpu.VMEM((7 * ROWS, slabs * columns), f32),
            pltpu.VMEM(oa.shape, bf16),
            pltpu.VMEM(ob.shape, bf16),
            pltpu.VMEM(oc.shape, bf16),
            pltpu.SemaphoreType.DMA((3, 7)),
        ],
    )(me, ids, *parts, oa, ob, oc)
    step = n_pts // SIDE * slabs
    gathered = gather_by(checks, [step * m + c for m in range(SIDE // slabs) for c in range(2)])

    lattice4 = call(
        coarse_kernel,
        shape(dens, coef, BOXES4, dtype=f32),
        32,
        4 << 30,
        in_specs=[VMEM] * (n_pts + 7),
        out_specs=VMEM,
    )(ids, *parts, m2m_hi, m2m_lo, lat_hi, lat_lo, l2l_hi, l2l_lo)

    reply = call(
        functools.partial(evaluate_kernel, slabs, step),
        shape(n_top, dens, points, dtype=f32),
        32,
        4 << 30,
        in_specs=[SMEM] + [VMEM] * (len(gathered) + 5),
        out_specs=VMEM,
        scratch_shapes=[pltpu.VMEM((2 * dens * CPAD, BOXES4), f32)],
    )(me, *gathered, *halves, lattice4, field, place)
    answers = [shift_by("top", reply[m], m) if m else reply[m] for m in range(n_top)]
    order = jnp.arange(n_top, dtype=jnp.int32) ^ top
    picked = sum(
        jnp.where(order[:, None, None] == m, answers[m][None], 0.0) for m in range(n_top)
    )
    return picked.reshape(DENS, points)


def solution(mesh):
    split_all = P(None, ("pts", "top"))
    placed = (split_all, split_all, P(("pts", "top")), P(("pts", "top"))) + (P(),) * 6
    return jax.shard_map(
        per_device, mesh=mesh, in_specs=placed, out_specs=split_all, check_vma=False
    )
```

```python
import functools
import math

import jax
import jax.numpy as jnp
import numpy as np
from jax import lax
from jax.experimental import pallas as pl
from jax.experimental.pallas import tpu as pltpu
from jax.sharding import PartitionSpec as P

LEVEL = 3
EDGE = 6
DENS = 8
SIDE = 2**LEVEL
BOXES4 = SIDE**3
PLANE = SIDE * SIDE
LANE = 128
REACH = 3
SHIFTS = list(range(-REACH, REACH + 1))
OUTER = [s for s in SHIFTS if abs(s) >= 2]
INNER = [s for s in SHIFTS if abs(s) < 2]
bf16 = jnp.bfloat16
f32 = jnp.float32
NN = (((1,), (0,)), ((), ()))
NT = (((1,), (1,)), ((), ()))


def up(value, multiple):
    return -(-value // multiple) * multiple


def surface_table():
    grid_vals = np.linspace(-1.0, 1.0, EDGE)
    points_list = []
    for a in range(EDGE):
        for b in range(EDGE):
            for c in range(EDGE):
                if min(a, b, c) == 0 or max(a, b, c) == EDGE - 1:
                    points_list.append([grid_vals[a], grid_vals[b], grid_vals[c]])
    return np.array(points_list, dtype=np.float32).T


COEF = surface_table().shape[1]
OFFSETS = (2 * REACH + 1) ** 3 - 27
FEATURES = 4
PB = 256
STRIP = 16
GRANT = 58
CPAD = up(COEF, 32)


def column_table():
    surface = 1.25 * surface_table().astype(np.float64)
    grid = np.linspace(-0.9, 0.9, 10)
    points = np.stack(np.meshgrid(grid, grid, grid, indexing="ij")).reshape(3, -1)
    values = 1.0 / np.sqrt(((surface[:, :, None] - points[:, None, :]) ** 2).sum(axis=0))
    scale = (points**2).sum(axis=1)
    out = np.zeros((surface.shape[1], LANE), np.float32)
    out[:, 0:3] = (np.float32(1.25) * surface_table()).T
    out[:, 8] = values.mean(axis=1)
    out[:, 9:12] = values @ points.T / scale
    return out


def blocks():
    out, position = [], 0
    for dx in SHIFTS:
        for dy in SHIFTS:
            count = sum(max(abs(dx), abs(dy), abs(dz)) >= 2 for dz in SHIFTS)
            out.append((dx, dy, position, count))
            position += count
    return out


def dot(a, b, dims=NN):
    return lax.dot_general(a, b, dims, preferred_element_type=f32)


def split(value):
    high = value.astype(bf16)
    return high, (value - high.astype(f32)).astype(bf16)


def dot3(a, b, dims=NN):
    return dot(a[0], b[0], dims) + dot(a[1], b[0], dims) + dot(a[0], b[1], dims)


def dot3_rows(a, b, dims=NN):
    rows = a[0].shape[0]
    both = jnp.concatenate([x.astype(f32) for x in a], axis=0).astype(bf16)
    both = dot(both, b[0], dims)
    return both[0:rows] + both[rows : 2 * rows] + dot(a[0], b[1], dims)


def call(kernel, out_shape, mib, flops, bytes_accessed=1 << 20, **kw):
    return pl.pallas_call(
        kernel,
        out_shape=out_shape,
        compiler_params=pltpu.CompilerParams(vmem_limit_bytes=mib << 20),
        cost_estimate=pl.CostEstimate(
            flops=flops, bytes_accessed=bytes_accessed, transcendentals=0
        ),
        **kw,
    )


VMEM = pl.BlockSpec(memory_space=pltpu.VMEM)
WHOLE = pl.BlockSpec()
SMEM = pl.BlockSpec(memory_space=pltpu.SMEM)
ANY = pl.BlockSpec(memory_space=pl.ANY)


HG = 4 * OFFSETS * COEF // LANE
KT = up(up(OFFSETS * COEF, LANE) // LANE, 8)
WFULL = up(7 * COEF, LANE)
WIN = up(4 * COEF, LANE)
NG = COEF // 8
STEPS = -(-NG // 4)
ROWS = 16 * STEPS
CHUNK = up(HG + 15, 16)
TAIL = 32
STRIDE = 17


def relayout_kernel(nrows, me_ref, f_hbm, tail_ref, oa, ob, oc, inb, fbuf, tbuf, tb16, sem):
    step = pl.program_id(0)
    half = me_ref[0] & 1
    end16 = nrows // 16 * 16

    def start_row(st, g):
        return jnp.minimum(4 * st + g, NG - 1) * (2 * HG) + half * HG

    def start(st, slot):
        for g in range(4):
            row = pl.multiple_of(start_row(st, g) // 16 * 16, 16)
            pltpu.make_async_copy(
                f_hbm.at[pl.ds(row, CHUNK - TAIL)],
                inb.at[slot, g, pl.ds(0, CHUNK - TAIL)],
                sem.at[slot, g, 0],
            ).start()
            last = row + CHUNK > end16

            @pl.when(jnp.logical_not(last))
            def _():
                pltpu.make_async_copy(
                    f_hbm.at[pl.ds(pl.multiple_of(row + CHUNK - TAIL, 16), TAIL)],
                    inb.at[slot, g, pl.ds(CHUNK - TAIL, TAIL)],
                    sem.at[slot, g, 1],
                ).start()


    def wait(st, slot):
        for g in range(4):
            row = pl.multiple_of(start_row(st, g) // 16 * 16, 16)
            pltpu.make_async_copy(
                f_hbm.at[pl.ds(row, CHUNK - TAIL)],
                inb.at[slot, g, pl.ds(0, CHUNK - TAIL)],
                sem.at[slot, g, 0],
            ).wait()
            last = row + CHUNK > end16

            @pl.when(jnp.logical_not(last))
            def _():
                pltpu.make_async_copy(
                    f_hbm.at[pl.ds(pl.multiple_of(row + CHUNK - TAIL, 16), TAIL)],
                    inb.at[slot, g, pl.ds(CHUNK - TAIL, TAIL)],
                    sem.at[slot, g, 1],
                ).wait()

            @pl.when(last)
            def _():
                row16 = lax.broadcasted_iota(jnp.int32, (16, LANE), 0)
                tail = jnp.where(row16 < nrows - end16, tail_ref[...].astype(f32), 0.0)
                inb[slot, g, CHUNK - TAIL : CHUNK - TAIL + 16] = tail.astype(bf16)

    slot = lax.rem(step, 2)

    @pl.when(step == 0)
    def _():
        fbuf[...] = jnp.zeros_like(fbuf)
        start(0, 0)

    @pl.when(step + 1 < STEPS)
    def _():
        start(step + 1, 1 - slot)

    wait(step, slot)
    lane = lax.broadcasted_iota(jnp.int32, (8, LANE), 1)
    for g in range(4):
        fbuf[g, 0:CHUNK] = inb[slot, g].astype(f32)
    for g in range(4):
        row = start_row(step, g)
        off = row - row // 16 * 16
        for e in range(4):
            first = OFFSETS * COEF * e
            phase = first % LANE

            @pl.loop(0, KT // 8, unroll=KT // 8)
            def _(n):
                base = off + first // LANE + 8 * n
                value = fbuf[g, pl.ds(base, 8), :]
                if phase:
                    after = fbuf[g, pl.ds(base + 1, 8), :]
                    value = pltpu.roll(jnp.where(lane >= phase, value, after), LANE - phase, 1)
                tbuf[pl.ds(8 * n * STRIDE + 4 * g + e, 8, stride=STRIDE), :] = value

    @pl.loop(0, KT, unroll=8)
    def _(k):
        tb16[k] = tbuf[pl.ds(k * STRIDE, 16), :].astype(bf16)

    for dx, dy, d0, count in blocks():
        tile0, phase = divmod(d0 * COEF, LANE)
        if dy in OUTER:
            ref = oa.at[dx + REACH, OUTER.index(dy)]
        elif dx in OUTER:
            ref = ob.at[OUTER.index(dx), INNER.index(dy)]
        else:
            ref = oc.at[INNER.index(dx), INNER.index(dy)]
        for t in range(up(count * COEF, LANE) // LANE):
            value = tb16[tile0 + t]
            if phase:
                after = tb16[min(tile0 + t + 1, KT - 1)]
                value = jnp.concatenate([value[:, phase:], after[:, :phase]], axis=1)
            ref[:, t * LANE : (t + 1) * LANE] = value


def relayout(flat, me):
    nrows = flat.shape[0] // LANE
    rows = flat.reshape(nrows, LANE)
    shapes = ((7, 4, ROWS, WFULL), (4, 3, ROWS, WFULL), (3, 3, ROWS, WIN))
    return call(
        functools.partial(relayout_kernel, nrows),
        tuple(jax.ShapeDtypeStruct(s, bf16) for s in shapes),
        GRANT,
        1 << 20,
        16 << 20,
        grid_spec=pltpu.PrefetchScalarGridSpec(
            num_scalar_prefetch=1,
            grid=(STEPS,),
            in_specs=[ANY, pl.BlockSpec((16, LANE), lambda i, h: (nrows // 16, 0))],
            out_specs=tuple(
                pl.BlockSpec((s[0], s[1], 16, s[3]), lambda i, h: (0, 0, i, 0)) for s in shapes
            ),
            scratch_shapes=[
                pltpu.VMEM((2, 4, CHUNK, LANE), bf16),
                pltpu.VMEM((4, CHUNK + 16, LANE), f32),
                pltpu.VMEM((KT * STRIDE, LANE), f32),
                pltpu.VMEM((KT, 16, LANE), bf16),
                pltpu.SemaphoreType.DMA((2, 4, 2)),
            ],
        ),
    )(me, rows, rows)


GROUP = 16


def square(flat, out):
    per = GROUP * COEF // LANE
    groups = flat.shape[0] // per
    lane = lax.broadcasted_iota(jnp.int32, (groups, LANE), 1)
    for r in range(GROUP):
        first, phase = divmod(r * COEF, LANE)
        got = []
        for t in range(3):
            row = min(first + t, per - 1)
            got.append(flat[pl.ds(row, groups, stride=per), :])
        for t in range(2):
            value = got[t]
            if phase:
                value = jnp.where(lane >= phase, got[t], got[t + 1])
                value = pltpu.roll(value, LANE - phase, 1)
            out[t, pl.ds(r, groups, stride=GROUP), :] = value


def operators_kernel(
    m2m, l2l, uc2e, dc2e, lattice, column, w_both, m2m_hi, m2m_lo, l2l_hi, l2l_lo, lat_hi, lat_lo,
    d_hi, d_lo, rows
):
    scale = 1.0 / (4.0 * math.pi)
    lat_hi[...], lat_lo[...] = split(lattice[...])
    first = split(uc2e[...] * scale)

    plane = split(column[...])

    def stack(pieces, first):
        wide = []
        for piece in pieces:
            high, low = split(dot3(split(piece), plane)[:, 8 : 8 + FEATURES])
            wide += [piece, high.astype(f32), low.astype(f32)]
            wide.append(jnp.zeros((COEF, CPAD - COEF - 2 * FEATURES), f32))
        wide = jnp.concatenate([w for w in wide if w.shape[1]], axis=1).astype(bf16)
        w_both[first : first + COEF] = wide

    def matrix(o):
        at = slice(o * COEF, (o + 1) * COEF)
        return jnp.concatenate([rows[0, at], rows[1, at, 0 : COEF - LANE]], axis=1)

    square(m2m, rows)
    pieces = []
    for o in range(8):
        high, low = split(matrix(o))
        m2m_hi[o], m2m_lo[o] = high, low
        pieces.append(dot3((high, low), first))
    stack(pieces, 0)
    square(l2l, rows)
    pieces = []
    for o in range(8):
        value = matrix(o)
        l2l_hi[o], l2l_lo[o] = split(value)
        pieces.append(jnp.transpose(value) * scale)
    stack(pieces, COEF)
    high, low = split(dc2e[...])
    i = lax.broadcasted_iota(jnp.int32, (COEF, ROWS), 0)
    r = lax.broadcasted_iota(jnp.int32, (COEF, ROWS), 1)
    for h in range(2):
        here = (i == (r >> 2) * 8 + 4 * h + (r & 3)) & (r < 4 * NG)
        here = jnp.where(here, 1.0, 0.0).astype(bf16)
        d_hi[h] = dot(high, here).astype(bf16)
        d_lo[h] = dot(low, here).astype(bf16)


def route_kernel(own, cap, n_top, pos, dens, slot, out, entries):
    points = pos.shape[1]
    owners = out.shape[0]
    slots = slot[...]
    owner = slots // own
    inside = slots - owner * own
    hit = owner == lax.broadcasted_iota(jnp.int32, (owners, points), 0)
    hit = jnp.where(hit, 1.0, 0.0)
    hit16 = hit.astype(bf16)
    row = lax.broadcasted_iota(jnp.int32, (LANE, LANE), 0)
    col = lax.broadcasted_iota(jnp.int32, (LANE, LANE), 1)
    before = jnp.where(row < col, 1.0, 0.0).astype(bf16)
    every = jnp.ones((LANE, LANE), bf16)
    total = jnp.zeros((owners, LANE), f32)
    ranks = []
    for t in range(points // LANE):
        part = hit16[:, t * LANE : (t + 1) * LANE]
        ranks.append(total + dot(part, before))
        total = total + dot(part, every)
    rank = jnp.sum(hit * jnp.concatenate(ranks, axis=1), axis=0, keepdims=True)
    entry = owner * cap + rank.astype(jnp.int32)
    entries[...] = entry
    inside_hi = inside // 64
    value = jnp.concatenate([pos[...], dens[...]], axis=0)
    width = value.shape[0]
    high, low = split(value)
    ones = jnp.ones((1, points), f32)
    high = jnp.concatenate(
        [high.astype(f32), inside_hi.astype(f32), (inside - 64 * inside_hi).astype(f32), ones]
        + [jnp.zeros((16 - width - 3, points), f32)],
        axis=0,
    )
    low = jnp.concatenate([low.astype(f32), jnp.zeros((16 - width, points), f32)], axis=0)
    payload = jnp.concatenate([high, low], axis=0).astype(bf16)
    block = max(cap, LANE)
    per = DENS // n_top
    for o in range(owners * cap // block):
        there = entry == o * block + lax.broadcasted_iota(jnp.int32, (block, points), 0)
        there = jnp.where(there, 1.0, 0.0).astype(bf16)
        got = dot(payload, there, NT)
        value = got[0:width] + got[16 : 16 + width]
        where = got[width : width + 1] * 64.0 + got[width + 1 : width + 2]
        valid = got[width + 2 : width + 3]
        for q in range(n_top):
            rows = [value[0:3], where, valid, value[3 + per * q : 3 + per * (q + 1)]]
            rows.append(jnp.zeros((8 - 5 - per, block), f32))
            packed = jnp.concatenate([r for r in rows if r.shape[0]], axis=0)
            for i in range(block // cap):
                at = o * (block // cap) + i
                out[at, q] = packed[:, i * cap : (i + 1) * cap]


def restore_kernel(got, entries, out):
    devices, per, cap = got.shape
    n_top = out.shape[0] // per
    points = out.shape[1]
    block = max(cap, PB)
    total = jnp.zeros((2 * out.shape[0], points), f32)
    for o in range(devices // n_top * cap // block):
        count = block // cap
        value = []
        for q in range(n_top):
            pieces = [got[(o * count + i) * n_top + q] for i in range(count)]
            value.append(jnp.concatenate(pieces, axis=1))
        high, low = split(jnp.concatenate(value, axis=0))
        both = jnp.concatenate([high.astype(f32), low.astype(f32)], axis=0).astype(bf16)
        at = o * block + lax.broadcasted_iota(jnp.int32, (block, points), 0)
        total = total + dot(both, jnp.where(entries[...] == at, 1.0, 0.0).astype(bf16))
    out[...] = total[0 : out.shape[0]] + total[out.shape[0] :]


def octant_product(pos, octant, surf, oper):
    squared = None
    for d in range(3):
        spacing = surf[d] - pos[d : d + 1]
        squared = spacing * spacing if squared is None else squared + spacing * spacing
    value = lax.rsqrt(squared)
    round_pos = pos.astype(bf16).astype(f32)
    value = value - surf[3]
    for d in range(3):
        value = value - surf[4 + d] * round_pos[d : d + 1]
    features = [jnp.ones_like(round_pos[0:1]), round_pos]
    blank = jnp.zeros((CPAD - COEF - 2 * FEATURES, value.shape[1]), f32)
    value = [value] + features + features + [blank]
    value = jnp.concatenate([v for v in value if v.shape[0]], axis=0).astype(bf16)
    masks = [jnp.where(octant == o, 1.0, 0.0).astype(bf16) for o in range(8)]
    return dot(oper[...], jnp.concatenate([value * m for m in masks], axis=0))


TURNED = (((0,), (0,)), ((), ()))


def look_up(index, table):
    lanes, rows = table.shape[0] // 2, table.shape[1]
    width = index.shape[1]
    at_row = index // lanes
    at_lane = index - at_row * lanes
    there = at_row == lax.broadcasted_iota(jnp.int32, (rows, width), 0)
    got = dot(table, jnp.where(there, 1.0, 0.0).astype(bf16))
    mine = at_lane == lax.broadcasted_iota(jnp.int32, (lanes, width), 0)
    first = jnp.sum(jnp.where(mine, got[0:lanes], 0.0), axis=0, keepdims=True)
    return first, jnp.sum(jnp.where(mine, got[lanes:], 0.0), axis=0, keepdims=True)


def fill_surface(surf, column):
    for i, lane in enumerate((0, 1, 2, 8, 9, 10, 11)):
        surf[i] = jnp.broadcast_to(column[:, lane : lane + 1], surf.shape[1:])


def morton_place(box):
    place = jnp.zeros_like(box)
    for b in range(LEVEL):
        digit = box >> (3 * b)
        place = place + ((((digit >> 2) & 1) << (2 * LEVEL + b)))
        place = place + ((((digit >> 1) & 1) << (LEVEL + b)) + ((digit & 1) << b))
    return place


def points_kernel(n_top, box_cap, me_ref, got, *refs):
    leaves = refs[:n_top]
    column, oper, out, field, place, offsets, buf, surf = refs[n_top:]
    sources, _, cap = got.shape
    own = field.shape[1]
    wide = up(cap, LANE)
    flip = me_ref[1] * (own // n_top)
    buf[...] = jnp.zeros_like(buf)
    fill_surface(surf, column)

    def put(i, offset):
        values = [got[i * STRIP + s] for s in range(STRIP)]
        counts = [jnp.sum(v[4:5]).astype(jnp.int32) for v in values]
        for s, (value, count) in enumerate(zip(values, counts)):
            offsets[i * STRIP + s] = offset
            value = jnp.concatenate([value, jnp.zeros((8, wide + LANE - cap), f32)], axis=1)
            tile = offset // LANE
            value = pltpu.roll(value, offset - tile * LANE, 1)
            at = pl.ds(pl.multiple_of(tile * LANE, LANE), wide + LANE)
            buf[:, at] = buf[:, at] + value
            offset = offset + count
        return offset

    lax.fori_loop(0, sources // STRIP, put, jnp.int32(0))
    leaf = jnp.concatenate([v[...] for v in leaves], axis=0)
    low = jnp.min(jnp.min(leaf.astype(f32), axis=1, keepdims=True), axis=0, keepdims=True)
    first = low.astype(jnp.int32) >> 3
    table = jnp.concatenate([(leaf >> 3) - first, leaf & 7], axis=1).astype(f32)
    table = jnp.transpose(table).astype(bf16)
    out_rows = out.shape[1]

    def block(j, total):
        to = pl.ds(pl.multiple_of(j * PB, PB), PB)
        value = buf[:, to]
        box, octant = look_up(value[3:4].astype(jnp.int32) ^ flip, table)
        place[:, to] = morton_place(first + box.astype(jnp.int32))
        both = octant_product(value[0:3], octant, surf, oper)
        field[:, to] = both[COEF : 2 * COEF]
        high, low = split(both[0:COEF])
        rows = []
        at = lax.broadcasted_iota(jnp.int32, (box_cap, PB), 0).astype(f32)
        for k in range(out_rows // box_cap):
            rows.append(jnp.where(box == at, value[5 + k : 6 + k], 0.0))
        a_high, a_low = split(jnp.concatenate(rows, axis=0))
        both = dot(jnp.concatenate([high, low], axis=0), a_high, NT)
        return total + both[0:COEF] + both[COEF : 2 * COEF] + dot(high, a_low, NT)

    total = lax.fori_loop(0, own // PB, block, jnp.zeros((COEF, out_rows), f32), unroll=2)
    digits = jnp.concatenate([first >> 3, first & 7], axis=0).astype(f32)
    digits = jnp.broadcast_to(digits, (2, out_rows))
    blank = jnp.zeros((out.shape[0] - COEF - 2, out_rows), f32)
    out[...] = jnp.concatenate([total, digits, blank], axis=0).astype(bf16)


def box_ids(parts, dens):
    ids = []
    for part in parts:
        digits = part[COEF : COEF + 8, 0:1].astype(f32).astype(jnp.int32)
        first = digits[0:1] * 8 + digits[1:2]
        at = lax.broadcasted_iota(jnp.int32, (1, part.shape[1] // dens), 1)
        ids.append(first + at)
    return jnp.concatenate(ids, axis=1)


def all_parts(parts, k, dens):
    width = parts[0].shape[1] // dens
    return jnp.concatenate([p[0:COEF, k * width : (k + 1) * width] for p in parts], axis=1)


def translate_kernel(slabs, dens, me_ref, *refs):
    parts = refs[:-11]
    oa, ob, oc, out, xs, xin, acc, ma, mb, mc, sem = refs[-11:]
    copies = []
    for i, (src, dst) in enumerate(((oa, ma), (ob, mb), (oc, mc))):
        for j in range(src.shape[0]):
            copies.append(pltpu.make_async_copy(src.at[j], dst.at[j], sem.at[i, j]))
            copies[-1].start()
    x0 = (me_ref[0] // 2 * 2) * SIDE // len(parts)
    ids = box_ids(parts, dens)
    place = morton_place(ids)
    place = (((place >> 6) - x0 + REACH) & 7) * 64 + (place & 63)
    place = jnp.where(ids < BOXES4, place, -1)
    at = lax.broadcasted_iota(jnp.int32, (BOXES4, ids.shape[1]), 0)
    there = jnp.where(at == place, 1.0, 0.0).astype(bf16)
    columns = dens * PLANE
    for k in range(dens):
        low = dot(there, all_parts(parts, k, dens), NT)
        low = low.astype(bf16).astype(f32)
        for s in range(7 + slabs - 1):
            slab = low[s * PLANE : (s + 1) * PLANE].reshape(SIDE, SIDE, COEF)
            shifted = {}
            for dz in SHIFTS:
                if dz == 0:
                    moved = slab
                else:
                    cut = dz % SIDE
                    moved = jnp.concatenate([slab[:, cut:], slab[:, :cut]], axis=1)
                shifted[dz] = moved.reshape(PLANE, COEF)
            rows = pl.ds(s * columns + k * PLANE, PLANE)
            pad = [jnp.zeros((PLANE, WFULL - 7 * COEF), f32)]
            xs[rows, :] = jnp.concatenate([shifted[z] for z in SHIFTS] + pad, axis=1).astype(bf16)
            pad = [jnp.zeros((PLANE, WIN - 4 * COEF), f32)]
            xin[rows, :] = jnp.concatenate([shifted[z] for z in OUTER] + pad, axis=1).astype(bf16)
    for c in copies:
        c.wait()
    n_out = len(OUTER) * ROWS
    n_in = len(INNER) * ROWS
    for i, dx in enumerate(SHIFTS):
        rows = pl.ds(i * columns, slabs * columns)
        source = xs[rows, :]
        outer = dot(ma[i].reshape(n_out, WFULL), source, NT)
        if dx in OUTER:
            inner = dot(mb[OUTER.index(dx)].reshape(n_in, WFULL), source, NT)
        else:
            inner = dot(mc[INNER.index(dx)].reshape(n_in, WIN), xin[rows, :], NT)
        if i == 0:
            acc[0:n_out] = outer
            acc[n_out : n_out + n_in] = inner
        else:
            acc[0:n_out] += outer
            acc[n_out : n_out + n_in] += inner
    lane = lax.broadcasted_iota(jnp.int32, (ROWS, LANE), 1)
    for t in range(slabs * columns // LANE):
        total = jnp.zeros((ROWS, LANE), f32)
        for i, dy in enumerate(OUTER + INNER):
            value = acc[i * ROWS : (i + 1) * ROWS, t * LANE : (t + 1) * LANE]
            by = SIDE * (dy % SIDE)
            if by:
                near = pltpu.roll(value, LANE - by, 1)
                far = pltpu.roll(value, PLANE - by, 1)
                value = jnp.where((lane & (PLANE - 1)) < PLANE - by, near, far)
            total = total + value
        out[:, t * LANE : (t + 1) * LANE] = total.astype(out.dtype)


def coarse_kernel(*refs):
    parts = refs[:-7]
    m2m_hi, m2m_lo, lat_hi, lat_lo, l2l_hi, l2l_lo, out = refs[-7:]
    dens = out.shape[0]
    box = ids = box_ids(parts, dens)
    place = ((box & 7) << 6) + (box & 56) + (box >> 6)
    place = jnp.where(box < BOXES4, place, -1)
    at = lax.broadcasted_iota(jnp.int32, (BOXES4, ids.shape[1]), 0)
    there = jnp.where(at == place, 1.0, 0.0).astype(bf16)
    level = [dot(there, all_parts(parts, k, dens), NT) for k in range(dens)]

    def oper(hi, lo, o):
        return hi[o], lo[o]

    for _ in range(LEVEL):
        count = level[0].shape[0] // 8
        total = None
        for o in range(8):
            rows = jnp.concatenate([v[o * count : (o + 1) * count] for v in level], axis=0)
            term = dot3_rows(split(rows), oper(m2m_hi, m2m_lo, o), NT)
            total = term if total is None else total + term
        level = [total[k * count : (k + 1) * count] for k in range(dens)]
    rows = jnp.concatenate(level, axis=0)
    rows = dot3(split(rows), (lat_hi[...], lat_lo[...]), NT)
    level = [rows[k : k + 1] for k in range(dens)]
    for _ in range(LEVEL):
        count = level[0].shape[0]
        rows = split(jnp.concatenate(level, axis=0))
        children = [dot3_rows(rows, oper(l2l_hi, l2l_lo, o), NT) for o in range(8)]
        level = [
            jnp.concatenate([c[k * count : (k + 1) * count] for c in children], axis=0)
            for k in range(dens)
        ]
    at = lax.broadcasted_iota(jnp.int32, (BOXES4, BOXES4), 1)
    row = lax.broadcasted_iota(jnp.int32, (BOXES4, BOXES4), 0)
    number = ((row & 7) << 6) + (row & 56) + (row >> 6)
    move = jnp.where(at == morton_place(number), 1.0, 0.0).astype(bf16)
    for k in range(dens):
        high, low = split(level[k])
        out[k] = dot(high, move, TURNED) + dot(low, move, TURNED)


def evaluate_kernel(slabs, step, me_ref, *refs):
    n = SIDE // slabs
    checks = refs[: 2 * n]
    d_hi, d_lo, lattice, field, place, offsets, out, stack, found = refs[2 * n :]
    core = me_ref[0] & 1
    group = me_ref[0] // step
    dens = lattice.shape[0]
    lane = lax.broadcasted_iota(jnp.int32, (COEF, LANE), 1)
    mine = jnp.concatenate([d_hi[core], d_lo[core]], axis=0)
    other = jnp.concatenate([d_hi[1 - core], d_lo[1 - core]], axis=0)
    for m in range(n):
        value = dot(mine, checks[2 * m][...]) + dot(other, checks[2 * m + 1][...])
        value = value[0:COEF] + value[COEF : 2 * COEF]
        if slabs == 2:
            a, b = value[:, 0:LANE], value[:, LANE : 2 * LANE]
            half = LANE // 2
            pieces = [
                jnp.where(lane < half, a, pltpu.roll(b, half, 1)),
                jnp.where(lane < half, pltpu.roll(a, half, 1), b),
            ]
        else:
            pieces = [value[:, k * PLANE : (k + 1) * PLANE] for k in range(dens)]
        width = slabs * PLANE
        for k in range(dens):
            at = m ^ group
            if width % LANE == 0:
                base = lattice[k, :, pl.ds(pl.multiple_of(at * width, width), width)]
            else:
                pair = lattice[k, :, pl.ds(pl.multiple_of(at // 2 * LANE, LANE), LANE)]
                base = jnp.where(at % 2 == 0, pair[:, :width], pair[:, width:])
            high, low = split(pieces[k] + base)
            rows = pl.ds(k * CPAD, COEF)
            stack[rows, m * width : (m + 1) * width] = high.astype(f32)
            rows = pl.ds((dens + k) * CPAD, COEF)
            stack[rows, m * width : (m + 1) * width] = low.astype(f32)
    found[:, place.shape[1] :] = jnp.zeros((8, found.shape[1] - place.shape[1]), f32)
    local = stack[...].astype(bf16)

    @pl.loop(0, place.shape[1] // PB)
    def _(j):
        at = pl.ds(pl.multiple_of(j * PB, PB), PB)
        want = place[:, at] ^ (group * (slabs * PLANE))
        there = want == lax.broadcasted_iota(jnp.int32, (BOXES4, PB), 0)
        got = dot(local, jnp.where(there, 1.0, 0.0).astype(bf16))
        mine = field[:, at]
        rows = []
        for k in range(dens):
            value = got[k * CPAD : k * CPAD + COEF]
            value = value + got[(dens + k) * CPAD : (dens + k) * CPAD + COEF]
            rows.append(jnp.sum(value * mine, axis=0, keepdims=True))
        rows.append(jnp.zeros((8 - dens, PB), f32))
        found[:, at] = jnp.concatenate(rows, axis=0)

    sources, _, cap = out.shape
    wide = up(cap, LANE) + LANE

    @pl.loop(0, sources // STRIP)
    def _(i):
        for s in range(STRIP):
            offset = offsets[i * STRIP + s]
            tile = offset // LANE
            value = found[:, pl.ds(pl.multiple_of(tile * LANE, LANE), wide)]
            value = pltpu.roll(value, wide - (offset - tile * LANE), 1)
            out[i * STRIP + s] = value[0:dens, 0:cap]


def shift_by(axis, value, distance):
    size = lax.axis_size(axis)
    return lax.ppermute(value, axis, [(i, i ^ distance) for i in range(size)])


def gather_by(value, distances):
    got = {m: shift_by("pts", value, m) if m else value for m in distances if m % 2 == 0}
    got.update({m + 1: shift_by("pts", got[m], 1) for m in list(got) if m + 1 in distances})
    return [got[m] for m in distances]


def per_device(
    local_pos, densities, morton_slot, slot_leaf, uc2e, m2m, m2l_ops, dc2e, lattice, l2l
):
    n_pts = lax.axis_size("pts")
    n_top = lax.axis_size("top")
    me = jnp.stack([lax.axis_index("pts"), lax.axis_index("top")]).astype(jnp.int32)
    points = local_pos.shape[1]
    own = points * n_top
    cap = 2 * points // n_pts
    box_cap = 2 * BOXES4 // n_pts
    dens = DENS // n_top
    slabs = max(1, 2 * SIDE // n_pts)
    coef = uc2e.shape[0]
    sources = n_pts * n_top

    def shape(*dims, dtype=bf16):
        return jax.ShapeDtypeStruct(dims, dtype)

    outgoing, entries = call(
        functools.partial(route_kernel, own, cap, n_top),
        (shape(n_pts, n_top, 8, cap, dtype=f32), shape(1, points, dtype=jnp.int32)),
        GRANT,
        1 << 27,
        in_specs=[WHOLE] * 3,
        out_specs=(WHOLE, WHOLE),
    )(local_pos, densities, morton_slot.reshape(1, points))
    outgoing = outgoing.reshape(sources, 8, cap)
    incoming = lax.all_to_all(outgoing, ("pts", "top"), split_axis=0, concat_axis=0, tiled=True)

    leaf = slot_leaf.reshape(points // LANE, LANE)
    leaves = [shift_by("top", leaf, m) if m else leaf for m in range(n_top)]
    flat = (-1, LANE)
    column = jnp.asarray(column_table())
    square_shape = shape(8, coef, coef)
    w_both, *coarse_ops = call(
        operators_kernel,
        (shape(2 * coef, 8 * CPAD),)
        + (square_shape,) * 4
        + (shape(coef, coef),) * 2
        + (shape(2, coef, ROWS),) * 2,
        GRANT,
        1 << 30,
        in_specs=[WHOLE] * 6,
        out_specs=(WHOLE,) * 9,
        scratch_shapes=[pltpu.VMEM((2, 8 * coef, LANE), f32)],
    )(m2m.reshape(flat), l2l.reshape(flat), uc2e, dc2e, lattice, column)
    coarse_ops, halves = coarse_ops[:6], coarse_ops[6:]
    m2m_hi, m2m_lo, l2l_hi, l2l_lo, lat_hi, lat_lo = coarse_ops
    oa, ob, oc = relayout(m2l_ops, me)
    incoming, oa, ob, oc = lax.optimization_barrier((incoming, oa, ob, oc))

    partial, field, place, offsets = call(
        functools.partial(points_kernel, n_top, box_cap),
        (
            shape(up(coef + 2, 16), dens * box_cap),
            shape(coef, own, dtype=f32),
            shape(1, own, dtype=jnp.int32),
            shape(sources, dtype=jnp.int32),
        ),
        GRANT,
        8 << 30,
        in_specs=[SMEM] + [WHOLE] * (n_top + 3),
        out_specs=(WHOLE, WHOLE, WHOLE, SMEM),
        scratch_shapes=[
            pltpu.VMEM((8, up(own + up(cap, LANE) + LANE, PB)), f32),
            pltpu.VMEM((3 + FEATURES, coef, PB), f32),
        ],
    )(me, incoming, *leaves, column, w_both)
    parts = gather_by(partial, range(n_pts))

    columns = dens * PLANE
    checks = call(
        functools.partial(translate_kernel, slabs, dens),
        shape(ROWS, slabs * columns),
        GRANT,
        8 << 30,
        in_specs=[SMEM] + [WHOLE] * n_pts + [ANY] * 3,
        out_specs=WHOLE,
        scratch_shapes=[
            pltpu.VMEM(((7 + slabs - 1) * columns, WFULL), bf16),
            pltpu.VMEM(((7 + slabs - 1) * columns, WIN), bf16),
            pltpu.VMEM((7 * ROWS, slabs * columns), f32),
            pltpu.VMEM(oa.shape, bf16),
            pltpu.VMEM(ob.shape, bf16),
            pltpu.VMEM(oc.shape, bf16),
            pltpu.SemaphoreType.DMA((3, 7)),
        ],
    )(me, *parts, oa, ob, oc)
    step = n_pts // SIDE * slabs
    gathered = gather_by(checks, [step * m + c for m in range(SIDE // slabs) for c in range(2)])

    lattice4 = call(
        coarse_kernel,
        shape(dens, coef, BOXES4, dtype=f32),
        GRANT,
        4 << 30,
        in_specs=[WHOLE] * (n_pts + 6),
        out_specs=WHOLE,
    )(*parts, m2m_hi, m2m_lo, lat_hi, lat_lo, l2l_hi, l2l_lo)

    reply = call(
        functools.partial(evaluate_kernel, slabs, step),
        shape(sources, dens, cap, dtype=f32),
        GRANT,
        4 << 30,
        in_specs=[SMEM] + [WHOLE] * (len(gathered) + 5) + [SMEM],
        out_specs=WHOLE,
        scratch_shapes=[
            pltpu.VMEM((2 * dens * CPAD, BOXES4), f32),
            pltpu.VMEM((8, own + up(cap, LANE) + LANE), f32),
        ],
    )(me, *gathered, *halves, lattice4, field, place, offsets)
    returned = lax.all_to_all(reply, ("pts", "top"), split_axis=0, concat_axis=0, tiled=True)
    return call(
        restore_kernel,
        shape(DENS, points, dtype=f32),
        GRANT,
        1 << 28,
        in_specs=[WHOLE] * 2,
        out_specs=WHOLE,
    )(returned, entries)


def solution(mesh):
    split_all = P(None, ("pts", "top"))
    placed = (split_all, split_all, P(("pts", "top")), P(("pts", "top"))) + (P(),) * 6
    return jax.shard_map(
        per_device, mesh=mesh, in_specs=placed, out_specs=split_all, check_vma=False
    )
```

```python
import functools
import math

import jax
import jax.numpy as jnp
import numpy as np
from jax import lax
from jax.experimental import pallas as pl
from jax.experimental.pallas import tpu as pltpu
from jax.sharding import PartitionSpec as P

LEVEL = 3
EDGE = 6
DENS = 8
SIDE = 2**LEVEL
BOXES4 = SIDE**3
PLANE = SIDE * SIDE
LANE = 128
REACH = 3
SHIFTS = list(range(-REACH, REACH + 1))
OUTER = [s for s in SHIFTS if abs(s) >= 2]
INNER = [s for s in SHIFTS if abs(s) < 2]
bf16 = jnp.bfloat16
f32 = jnp.float32
NN = (((1,), (0,)), ((), ()))
NT = (((1,), (1,)), ((), ()))


def up(value, multiple):
    return -(-value // multiple) * multiple


def surface_table():
    grid_vals = np.linspace(-1.0, 1.0, EDGE)
    points_list = []
    for a in range(EDGE):
        for b in range(EDGE):
            for c in range(EDGE):
                if min(a, b, c) == 0 or max(a, b, c) == EDGE - 1:
                    points_list.append([grid_vals[a], grid_vals[b], grid_vals[c]])
    return np.array(points_list, dtype=np.float32).T


COEF = surface_table().shape[1]
OFFSETS = (2 * REACH + 1) ** 3 - 27
FEATURES = 4
PB = 256
STRIP = 16
GRANT = 58
CPAD = up(COEF, 32)


def column_table():
    surface = 1.25 * surface_table().astype(np.float64)
    grid = np.linspace(-0.9, 0.9, 10)
    points = np.stack(np.meshgrid(grid, grid, grid, indexing="ij")).reshape(3, -1)
    values = 1.0 / np.sqrt(((surface[:, :, None] - points[:, None, :]) ** 2).sum(axis=0))
    scale = (points**2).sum(axis=1)
    out = np.zeros((surface.shape[1], LANE), np.float32)
    out[:, 0:3] = (np.float32(1.25) * surface_table()).T
    out[:, 8] = values.mean(axis=1)
    out[:, 9:12] = values @ points.T / scale
    return out


def blocks():
    out, position = [], 0
    for dx in SHIFTS:
        for dy in SHIFTS:
            count = sum(max(abs(dx), abs(dy), abs(dz)) >= 2 for dz in SHIFTS)
            out.append((dx, dy, position, count))
            position += count
    return out


def dot(a, b, dims=NN):
    return lax.dot_general(a, b, dims, preferred_element_type=f32)


def split(value):
    high = value.astype(bf16)
    return high, (value - high.astype(f32)).astype(bf16)


def dot3(a, b, dims=NN):
    return dot(a[0], b[0], dims) + dot(a[1], b[0], dims) + dot(a[0], b[1], dims)


def dot3_rows(a, b, dims=NN):
    rows = a[0].shape[0]
    both = jnp.concatenate([x.astype(f32) for x in a], axis=0).astype(bf16)
    both = dot(both, b[0], dims)
    return both[0:rows] + both[rows : 2 * rows] + dot(a[0], b[1], dims)


def call(kernel, out_shape, mib, flops, bytes_accessed=1 << 20, **kw):
    return pl.pallas_call(
        kernel,
        out_shape=out_shape,
        compiler_params=pltpu.CompilerParams(vmem_limit_bytes=mib << 20),
        cost_estimate=pl.CostEstimate(
            flops=flops, bytes_accessed=bytes_accessed, transcendentals=0
        ),
        **kw,
    )


VMEM = pl.BlockSpec(memory_space=pltpu.VMEM)
WHOLE = pl.BlockSpec()
SMEM = pl.BlockSpec(memory_space=pltpu.SMEM)
ANY = pl.BlockSpec(memory_space=pl.ANY)


HG = 4 * OFFSETS * COEF // LANE
KT = up(up(OFFSETS * COEF, LANE) // LANE, 8)
WFULL = up(7 * COEF, LANE)
WIN = up(4 * COEF, LANE)
NG = COEF // 8
STEPS = -(-NG // 4)
ROWS = 16 * STEPS
CHUNK = up(HG + 15, 16)
TAIL = 32
EARLY = 3
STRIDE = 17
PIECES = ((4, 7, WFULL), (3, 4, WFULL), (3, 3, WIN))


def relayout_kernel(nrows, step0, steps, me_ref, f_hbm, tail_ref, oa, ob, oc, inb, fbuf, tbuf, tb16, sem):
    step = pl.program_id(0)
    half = me_ref[0] & 1
    end16 = nrows // 16 * 16

    def start_row(st, g):
        return jnp.minimum(4 * (st + step0) + g, NG - 1) * (2 * HG) + half * HG

    def start(st, slot):
        for g in range(4):
            row = pl.multiple_of(start_row(st, g) // 16 * 16, 16)
            pltpu.make_async_copy(
                f_hbm.at[pl.ds(row, CHUNK - TAIL)],
                inb.at[slot, g, pl.ds(0, CHUNK - TAIL)],
                sem.at[slot, g, 0],
            ).start()
            last = row + CHUNK > end16

            @pl.when(jnp.logical_not(last))
            def _():
                pltpu.make_async_copy(
                    f_hbm.at[pl.ds(pl.multiple_of(row + CHUNK - TAIL, 16), TAIL)],
                    inb.at[slot, g, pl.ds(CHUNK - TAIL, TAIL)],
                    sem.at[slot, g, 1],
                ).start()


    def wait(st, slot):
        for g in range(4):
            row = pl.multiple_of(start_row(st, g) // 16 * 16, 16)
            pltpu.make_async_copy(
                f_hbm.at[pl.ds(row, CHUNK - TAIL)],
                inb.at[slot, g, pl.ds(0, CHUNK - TAIL)],
                sem.at[slot, g, 0],
            ).wait()
            last = row + CHUNK > end16

            @pl.when(jnp.logical_not(last))
            def _():
                pltpu.make_async_copy(
                    f_hbm.at[pl.ds(pl.multiple_of(row + CHUNK - TAIL, 16), TAIL)],
                    inb.at[slot, g, pl.ds(CHUNK - TAIL, TAIL)],
                    sem.at[slot, g, 1],
                ).wait()

            @pl.when(last)
            def _():
                row16 = lax.broadcasted_iota(jnp.int32, (16, LANE), 0)
                tail = jnp.where(row16 < nrows - end16, tail_ref[...].astype(f32), 0.0)
                inb[slot, g, CHUNK - TAIL : CHUNK - TAIL + 16] = tail.astype(bf16)

    slot = lax.rem(step, 2)

    @pl.when(step == 0)
    def _():
        fbuf[...] = jnp.zeros_like(fbuf)
        start(0, 0)

    @pl.when(step + 1 < steps)
    def _():
        start(step + 1, 1 - slot)

    wait(step, slot)
    lane = lax.broadcasted_iota(jnp.int32, (8, LANE), 1)
    for g in range(4):
        fbuf[g, 0:CHUNK] = inb[slot, g].astype(f32)
    for g in range(4):
        row = start_row(step, g)
        off = row - row // 16 * 16
        for e in range(4):
            first = OFFSETS * COEF * e
            phase = first % LANE

            @pl.loop(0, KT // 8, unroll=KT // 8)
            def _(n):
                base = off + first // LANE + 8 * n
                value = fbuf[g, pl.ds(base, 8), :]
                if phase:
                    after = fbuf[g, pl.ds(base + 1, 8), :]
                    value = pltpu.roll(jnp.where(lane >= phase, value, after), LANE - phase, 1)
                tbuf[pl.ds(8 * n * STRIDE + 4 * g + e, 8, stride=STRIDE), :] = value

    @pl.loop(0, KT, unroll=8)
    def _(k):
        tb16[k] = tbuf[pl.ds(k * STRIDE, 16), :].astype(bf16)

    for dx, dy, d0, count in blocks():
        tile0, phase = divmod(d0 * COEF, LANE)
        if dx in OUTER:
            ref = oa.at[OUTER.index(dx), (OUTER + INNER).index(dy)]
        elif dy in OUTER:
            ref = ob.at[INNER.index(dx), OUTER.index(dy)]
        else:
            ref = oc.at[INNER.index(dx), INNER.index(dy)]
        for t in range(up(count * COEF, LANE) // LANE):
            value = tb16[tile0 + t]
            if phase:
                after = tb16[min(tile0 + t + 1, KT - 1)]
                value = jnp.concatenate([value[:, phase:], after[:, :phase]], axis=1)
            ref[:, t * LANE : (t + 1) * LANE] = value


def relayout(flat, me, step0, steps):
    nrows = flat.shape[0] // LANE
    rows = flat.reshape(nrows, LANE)
    shapes = tuple((a, b, 16 * steps, c) for a, b, c in PIECES)
    return call(
        functools.partial(relayout_kernel, nrows, step0, steps),
        tuple(jax.ShapeDtypeStruct(s, bf16) for s in shapes),
        GRANT,
        1 << 20,
        steps << 21,
        grid_spec=pltpu.PrefetchScalarGridSpec(
            num_scalar_prefetch=1,
            grid=(steps,),
            in_specs=[ANY, pl.BlockSpec((16, LANE), lambda i, h: (nrows // 16, 0))],
            out_specs=tuple(
                pl.BlockSpec((s[0], s[1], 16, s[3]), lambda i, h: (0, 0, i, 0)) for s in shapes
            ),
            scratch_shapes=[
                pltpu.VMEM((2, 4, CHUNK, LANE), bf16),
                pltpu.VMEM((4, CHUNK + 16, LANE), f32),
                pltpu.VMEM((KT * STRIDE, LANE), f32),
                pltpu.VMEM((KT, 16, LANE), bf16),
                pltpu.SemaphoreType.DMA((2, 4, 2)),
            ],
        ),
    )(me, rows, rows)


GROUP = 16


def square(flat, out):
    per = GROUP * COEF // LANE
    groups = flat.shape[0] // per
    lane = lax.broadcasted_iota(jnp.int32, (groups, LANE), 1)
    for r in range(GROUP):
        first, phase = divmod(r * COEF, LANE)
        got = []
        for t in range(3):
            row = min(first + t, per - 1)
            got.append(flat[pl.ds(row, groups, stride=per), :])
        for t in range(2):
            value = got[t]
            if phase:
                value = jnp.where(lane >= phase, got[t], got[t + 1])
                value = pltpu.roll(value, LANE - phase, 1)
            out[t, pl.ds(r, groups, stride=GROUP), :] = value


def operators_kernel(
    m2m, l2l, uc2e, dc2e, lattice, column, w_both, m2m_hi, m2m_lo, l2l_hi, l2l_lo, lat_hi, lat_lo,
    d_hi, d_lo, rows
):
    scale = 1.0 / (4.0 * math.pi)
    lat_hi[...], lat_lo[...] = split(lattice[...])
    first = split(uc2e[...] * scale)

    plane = split(column[...])

    def stack(pieces, first):
        wide = []
        for piece in pieces:
            high, low = split(dot3(split(piece), plane)[:, 8 : 8 + FEATURES])
            wide += [piece, high.astype(f32), low.astype(f32)]
            wide.append(jnp.zeros((COEF, CPAD - COEF - 2 * FEATURES), f32))
        wide = jnp.concatenate([w for w in wide if w.shape[1]], axis=1).astype(bf16)
        w_both[first : first + COEF] = wide

    def matrix(o):
        at = slice(o * COEF, (o + 1) * COEF)
        return jnp.concatenate([rows[0, at], rows[1, at, 0 : COEF - LANE]], axis=1)

    square(m2m, rows)
    pieces = []
    for o in range(8):
        high, low = split(matrix(o))
        m2m_hi[o], m2m_lo[o] = high, low
        pieces.append(dot3((high, low), first))
    stack(pieces, 0)
    square(l2l, rows)
    pieces = []
    for o in range(8):
        value = matrix(o)
        l2l_hi[o], l2l_lo[o] = split(value)
        pieces.append(jnp.transpose(value) * scale)
    stack(pieces, COEF)
    high, low = split(dc2e[...])
    i = lax.broadcasted_iota(jnp.int32, (COEF, ROWS), 0)
    r = lax.broadcasted_iota(jnp.int32, (COEF, ROWS), 1)
    for h in range(2):
        here = (i == (r >> 2) * 8 + 4 * h + (r & 3)) & (r < 4 * NG)
        here = jnp.where(here, 1.0, 0.0).astype(bf16)
        d_hi[h] = dot(high, here).astype(bf16)
        d_lo[h] = dot(low, here).astype(bf16)


def route_kernel(own, cap, n_top, pos, dens, slot, leaf, out, entries):
    points = pos.shape[1]
    owners = out.shape[0]
    slots = slot[...]
    owner = slots // own
    inside = slots - owner * own
    hit = owner == lax.broadcasted_iota(jnp.int32, (owners, points), 0)
    hit = jnp.where(hit, 1.0, 0.0)
    hit16 = hit.astype(bf16)
    row = lax.broadcasted_iota(jnp.int32, (LANE, LANE), 0)
    col = lax.broadcasted_iota(jnp.int32, (LANE, LANE), 1)
    before = jnp.where(row < col, 1.0, 0.0).astype(bf16)
    every = jnp.ones((LANE, LANE), bf16)
    total = jnp.zeros((owners, LANE), f32)
    ranks = []
    for t in range(points // LANE):
        part = hit16[:, t * LANE : (t + 1) * LANE]
        ranks.append(total + dot(part, before))
        total = total + dot(part, every)
    rank = jnp.sum(hit * jnp.concatenate(ranks, axis=1), axis=0, keepdims=True)
    entry = owner * cap + rank.astype(jnp.int32)
    entries[...] = entry
    inside_hi = inside // 64
    value = jnp.concatenate([pos[...], dens[...]], axis=0)
    width = value.shape[0]
    high, low = split(value)
    ones = jnp.ones((1, points), f32)
    high = jnp.concatenate(
        [high.astype(f32), inside_hi.astype(f32), (inside - 64 * inside_hi).astype(f32), ones]
        + [jnp.zeros((16 - width - 3, points), f32)],
        axis=0,
    )
    low = jnp.concatenate([low.astype(f32), jnp.zeros((16 - width, points), f32)], axis=0)
    payload = jnp.concatenate([high, low], axis=0).astype(bf16)
    block = max(cap, LANE)
    per = DENS // n_top
    leaves = leaf[...].astype(f32)
    if leaves.shape[1] < cap:
        blank = jnp.zeros((leaves.shape[0], cap - leaves.shape[1]), f32)
        leaves = jnp.concatenate([leaves, blank], axis=1)
    for o in range(owners * cap // block):
        there = entry == o * block + lax.broadcasted_iota(jnp.int32, (block, points), 0)
        there = jnp.where(there, 1.0, 0.0).astype(bf16)
        got = dot(payload, there, NT)
        value = got[0:width] + got[16 : 16 + width]
        where = got[width : width + 1] * 64.0 + got[width + 1 : width + 2]
        valid = got[width + 2 : width + 3]
        for q in range(n_top):
            rows = [value[0:3], where, valid, value[3 + per * q : 3 + per * (q + 1)]]
            rows.append(jnp.zeros((8 - 5 - per, block), f32))
            packed = jnp.concatenate([r for r in rows if r.shape[0]], axis=0)
            for i in range(block // cap):
                at = o * (block // cap) + i
                out[at, q, 0:8] = packed[:, i * cap : (i + 1) * cap]
                out[at, q, 8:] = leaves


def restore_kernel(n_top, got, entries, out):
    devices = got.shape[0]
    per = out.shape[0] // n_top
    cap = got.shape[2] // per
    points = out.shape[1]
    block = max(cap, PB)
    total = jnp.zeros((2 * out.shape[0], points), f32)
    for o in range(devices // n_top * cap // block):
        count = block // cap
        value = []
        for q in range(n_top):
            for k in range(per):
                pieces = []
                for i in range(count):
                    row = (o * count + i) * n_top + q
                    pieces.append(got[row, :, k * cap : (k + 1) * cap])
                value.append(jnp.concatenate(pieces, axis=1))
        high, low = split(jnp.concatenate(value, axis=0))
        both = jnp.concatenate([high.astype(f32), low.astype(f32)], axis=0).astype(bf16)
        at = o * block + lax.broadcasted_iota(jnp.int32, (block, points), 0)
        total = total + dot(both, jnp.where(entries[...] == at, 1.0, 0.0).astype(bf16))
    out[...] = total[0 : out.shape[0]] + total[out.shape[0] :]


def octant_product(pos, octant, surf, oper):
    squared = None
    for d in range(3):
        spacing = surf[d] - pos[d : d + 1]
        squared = spacing * spacing if squared is None else squared + spacing * spacing
    value = lax.rsqrt(squared)
    round_pos = pos.astype(bf16).astype(f32)
    value = value - surf[3]
    for d in range(3):
        value = value - surf[4 + d] * round_pos[d : d + 1]
    features = [jnp.ones_like(round_pos[0:1]), round_pos]
    blank = jnp.zeros((CPAD - COEF - 2 * FEATURES, value.shape[1]), f32)
    value = [value] + features + features + [blank]
    value = jnp.concatenate([v for v in value if v.shape[0]], axis=0).astype(bf16)
    masks = [jnp.where(octant == o, 1.0, 0.0).astype(bf16) for o in range(8)]
    return dot(oper[...], jnp.concatenate([value * m for m in masks], axis=0))


TURNED = (((0,), (0,)), ((), ()))


def look_up(index, table):
    lanes, rows = table.shape[0] // 2, table.shape[1]
    width = index.shape[1]
    at_row = index // lanes
    at_lane = index - at_row * lanes
    there = at_row == lax.broadcasted_iota(jnp.int32, (rows, width), 0)
    got = dot(table, jnp.where(there, 1.0, 0.0).astype(bf16))
    mine = at_lane == lax.broadcasted_iota(jnp.int32, (lanes, width), 0)
    first = jnp.sum(jnp.where(mine, got[0:lanes], 0.0), axis=0, keepdims=True)
    return first, jnp.sum(jnp.where(mine, got[lanes:], 0.0), axis=0, keepdims=True)


def fill_surface(surf, column):
    for i, lane in enumerate((0, 1, 2, 8, 9, 10, 11)):
        surf[i] = jnp.broadcast_to(column[:, lane : lane + 1], surf.shape[1:])


def morton_place(box):
    place = jnp.zeros_like(box)
    for b in range(LEVEL):
        digit = box >> (3 * b)
        place = place + ((((digit >> 2) & 1) << (2 * LEVEL + b)))
        place = place + ((((digit >> 1) & 1) << (LEVEL + b)) + ((digit & 1) << b))
    return place


def points_kernel(n_top, box_cap, me_ref, got, *refs):
    column, oper_hbm, out, field, place, offsets, buf, surf, oper, sem = refs
    fetch = pltpu.make_async_copy(oper_hbm, oper, sem)
    fetch.start()
    sources, _, cap = got.shape
    lanes = min(cap, LANE)
    own = field.shape[1]
    wide = up(cap, LANE)
    me = me_ref[0]
    buf[...] = jnp.zeros_like(buf)
    fill_surface(surf, column)

    def put(i, offset):
        values = [got[i * STRIP + s, 0:8] for s in range(STRIP)]
        counts = [jnp.sum(v[4:5]).astype(jnp.int32) for v in values]
        for s, (value, count) in enumerate(zip(values, counts)):
            offsets[i * STRIP + s] = offset
            value = jnp.concatenate([value, jnp.zeros((8, wide + LANE - cap), f32)], axis=1)
            tile = offset // LANE
            value = pltpu.roll(value, offset - tile * LANE, 1)
            at = pl.ds(pl.multiple_of(tile * LANE, LANE), wide + LANE)
            buf[:, at] = buf[:, at] + value
            offset = offset + count
        return offset

    lax.fori_loop(0, sources // STRIP, put, jnp.int32(0))
    leaf = got[pl.ds(me * n_top, n_top), 8:, 0:lanes].reshape(own // lanes, lanes)
    leaf = leaf.astype(jnp.int32)
    first = got[me * n_top, 8:9, 0:1].astype(jnp.int32) >> 3
    offsets[sources] = jnp.sum(got[me * n_top, 8:9, 0:1]).astype(jnp.int32) >> 3
    fetch.wait()
    table = jnp.concatenate([(leaf >> 3) - first, leaf & 7], axis=1).astype(f32)
    table = jnp.transpose(table).astype(bf16)
    out_rows = out.shape[1]

    def block(j, total):
        to = pl.ds(pl.multiple_of(j * PB, PB), PB)
        value = buf[:, to]
        box, octant = look_up(value[3:4].astype(jnp.int32), table)
        place[:, to] = box.astype(jnp.int32)
        both = octant_product(value[0:3], octant, surf, oper)
        field[:, to] = both[COEF : 2 * COEF]
        high, low = split(both[0:COEF])
        rows = []
        at = lax.broadcasted_iota(jnp.int32, (box_cap, PB), 0).astype(f32)
        for k in range(out_rows // box_cap):
            rows.append(jnp.where(box == at, value[5 + k : 6 + k], 0.0))
        a_high, a_low = split(jnp.concatenate(rows, axis=0))
        both = dot(jnp.concatenate([high, low], axis=0), a_high, NT)
        return total + both[0:COEF] + both[COEF : 2 * COEF] + dot(high, a_low, NT)

    total = lax.fori_loop(0, own // PB, block, jnp.zeros((COEF, out_rows), f32), unroll=2)
    digits = jnp.concatenate([first >> 3, first & 7], axis=0).astype(f32)
    digits = jnp.broadcast_to(digits, (2, out_rows))
    blank = jnp.zeros((out.shape[0] - COEF - 2, out_rows), f32)
    out[...] = jnp.concatenate([total, digits, blank], axis=0).astype(bf16)


def box_ids(parts, dens):
    ids = []
    for part in parts:
        digits = part[COEF : COEF + 8, 0:1].astype(f32).astype(jnp.int32)
        first = digits[0:1] * 8 + digits[1:2]
        at = lax.broadcasted_iota(jnp.int32, (1, part.shape[1] // dens), 1)
        ids.append(first + at)
    return jnp.concatenate(ids, axis=1)


def all_parts(parts, k, dens):
    width = parts[0].shape[1] // dens
    return jnp.concatenate([p[0:COEF, k * width : (k + 1) * width] for p in parts], axis=1)


def translate_kernel(slabs, dens, me_ref, *refs):
    parts = refs[:-14]
    pieces = refs[-14:-8]
    out, xs, xin, acc, ma, mb, mc, sem = refs[-8:]
    copies = []
    for j in range(4):
        row = 0
        for h in range(2):
            for i, dst in enumerate((ma, mb, mc)):
                src = pieces[3 * h + i]
                if j < src.shape[0]:
                    rows = pl.ds(row, src.shape[2])
                    copy = pltpu.make_async_copy(src.at[j], dst.at[j, :, rows], sem.at[h, i, j])
                    copy.start()
                    copies.append(copy)
            row += pieces[3 * h].shape[2]
    x0 = (me_ref[0] // 2 * 2) * SIDE // len(parts)
    ids = box_ids(parts, dens)
    place = morton_place(ids)
    place = (((place >> 6) - x0 + REACH) & 7) * 64 + (place & 63)
    place = jnp.where(ids < BOXES4, place, -1)
    at = lax.broadcasted_iota(jnp.int32, (BOXES4, ids.shape[1]), 0)
    there = jnp.where(at == place, 1.0, 0.0).astype(bf16)
    columns = dens * PLANE
    for k in range(dens):
        low = dot(there, all_parts(parts, k, dens), NT)
        low = low.astype(bf16).astype(f32)
        for s in range(7 + slabs - 1):
            slab = low[s * PLANE : (s + 1) * PLANE].reshape(SIDE, SIDE, COEF)
            shifted = {}
            for dz in SHIFTS:
                if dz == 0:
                    moved = slab
                else:
                    cut = dz % SIDE
                    moved = jnp.concatenate([slab[:, cut:], slab[:, :cut]], axis=1)
                shifted[dz] = moved.reshape(PLANE, COEF)
            rows = pl.ds(s * columns + k * PLANE, PLANE)
            pad = [jnp.zeros((PLANE, WFULL - 7 * COEF), f32)]
            xs[rows, :] = jnp.concatenate([shifted[z] for z in SHIFTS] + pad, axis=1).astype(bf16)
            pad = [jnp.zeros((PLANE, WIN - 4 * COEF), f32)]
            xin[rows, :] = jnp.concatenate([shifted[z] for z in OUTER] + pad, axis=1).astype(bf16)
    for c in copies:
        c.wait()
    n_out = len(OUTER) * ROWS
    n_all = len(SHIFTS) * ROWS
    for i, dx in enumerate(OUTER + INNER):
        rows = pl.ds((dx + REACH) * columns, slabs * columns)
        source = xs[rows, :]
        if dx in OUTER:
            term = dot(ma[OUTER.index(dx)].reshape(n_all, WFULL), source, NT)
            if i == 0:
                acc[...] = term
            else:
                acc[...] += term
        else:
            acc[0:n_out] += dot(mb[INNER.index(dx)].reshape(n_out, WFULL), source, NT)
            inner = mc[INNER.index(dx)].reshape(n_all - n_out, WIN)
            acc[n_out:n_all] += dot(inner, xin[rows, :], NT)
    lane = lax.broadcasted_iota(jnp.int32, (ROWS, LANE), 1)
    for t in range(slabs * columns // LANE):
        total = jnp.zeros((ROWS, LANE), f32)
        for i, dy in enumerate(OUTER + INNER):
            value = acc[i * ROWS : (i + 1) * ROWS, t * LANE : (t + 1) * LANE]
            by = SIDE * (dy % SIDE)
            if by:
                near = pltpu.roll(value, LANE - by, 1)
                far = pltpu.roll(value, PLANE - by, 1)
                value = jnp.where((lane & (PLANE - 1)) < PLANE - by, near, far)
            total = total + value
        out[:, t * LANE : (t + 1) * LANE] = total.astype(out.dtype)


def coarse_kernel(*refs):
    parts = refs[:-14]
    out = refs[-8]
    m2m_hi, m2m_lo, lat_hi, lat_lo, l2l_hi, l2l_lo, sem = refs[-7:]
    copies = []
    for i in range(6):
        copies.append(pltpu.make_async_copy(refs[-14 + i], refs[-7 + i], sem.at[i]))
        copies[-1].start()
    dens = out.shape[0]
    box = ids = box_ids(parts, dens)
    place = ((box & 7) << 6) + (box & 56) + (box >> 6)
    place = jnp.where(box < BOXES4, place, -1)
    at = lax.broadcasted_iota(jnp.int32, (BOXES4, ids.shape[1]), 0)
    there = jnp.where(at == place, 1.0, 0.0).astype(bf16)
    level = [dot(there, all_parts(parts, k, dens), NT) for k in range(dens)]

    for copy in copies:
        copy.wait()

    def oper(hi, lo, o):
        return hi[o], lo[o]

    for _ in range(LEVEL):
        count = level[0].shape[0] // 8
        total = None
        for o in range(8):
            rows = jnp.concatenate([v[o * count : (o + 1) * count] for v in level], axis=0)
            term = dot3_rows(split(rows), oper(m2m_hi, m2m_lo, o), NT)
            total = term if total is None else total + term
        level = [total[k * count : (k + 1) * count] for k in range(dens)]
    rows = jnp.concatenate(level, axis=0)
    rows = dot3(split(rows), (lat_hi[...], lat_lo[...]), NT)
    level = [rows[k : k + 1] for k in range(dens)]
    for _ in range(LEVEL):
        count = level[0].shape[0]
        rows = split(jnp.concatenate(level, axis=0))
        children = [dot3_rows(rows, oper(l2l_hi, l2l_lo, o), NT) for o in range(8)]
        level = [
            jnp.concatenate([c[k * count : (k + 1) * count] for c in children], axis=0)
            for k in range(dens)
        ]
    at = lax.broadcasted_iota(jnp.int32, (BOXES4, BOXES4), 1)
    row = lax.broadcasted_iota(jnp.int32, (BOXES4, BOXES4), 0)
    number = ((row & 7) << 6) + (row & 56) + (row >> 6)
    move = jnp.where(at == morton_place(number), 1.0, 0.0).astype(bf16)
    for k in range(dens):
        high, low = split(level[k])
        out[k] = dot(high, move, TURNED) + dot(low, move, TURNED)


def evaluate_kernel(slabs, step, window, me_ref, *refs):
    n = SIDE // slabs
    checks = refs[: 2 * n]
    d_hi, d_lo, lattice, field_hbm, place, offsets, out, stack, found, field, sem = refs[2 * n :]
    fetch = pltpu.make_async_copy(field_hbm, field, sem)
    fetch.start()
    core = me_ref[0] & 1
    group = me_ref[0] // step
    dens = lattice.shape[0]
    sources, cap = out.shape[0], out.shape[2] // dens
    lane = lax.broadcasted_iota(jnp.int32, (COEF, LANE), 1)
    mine = jnp.concatenate([d_hi[core], d_lo[core]], axis=0)
    other = jnp.concatenate([d_hi[1 - core], d_lo[1 - core]], axis=0)
    for m in range(n):
        value = dot(mine, checks[2 * m][...]) + dot(other, checks[2 * m + 1][...])
        value = value[0:COEF] + value[COEF : 2 * COEF]
        if slabs == 2:
            a, b = value[:, 0:LANE], value[:, LANE : 2 * LANE]
            half = LANE // 2
            pieces = [
                jnp.where(lane < half, a, pltpu.roll(b, half, 1)),
                jnp.where(lane < half, pltpu.roll(a, half, 1), b),
            ]
        else:
            pieces = [value[:, k * PLANE : (k + 1) * PLANE] for k in range(dens)]
        width = slabs * PLANE
        for k in range(dens):
            at = m ^ group
            if width % LANE == 0:
                base = lattice[k, :, pl.ds(pl.multiple_of(at * width, width), width)]
            else:
                pair = lattice[k, :, pl.ds(pl.multiple_of(at // 2 * LANE, LANE), LANE)]
                base = jnp.where(at % 2 == 0, pair[:, :width], pair[:, width:])
            high, low = split(pieces[k] + base)
            rows = pl.ds(k * CPAD, COEF)
            stack[rows, m * width : (m + 1) * width] = high.astype(f32)
            rows = pl.ds((dens + k) * CPAD, COEF)
            stack[rows, m * width : (m + 1) * width] = low.astype(f32)
    box = offsets[sources] + lax.broadcasted_iota(jnp.int32, (1, window), 1)
    want = morton_place(box) ^ (group * (slabs * PLANE))
    want = jnp.where(box < BOXES4, want, -1)
    pick = want == lax.broadcasted_iota(jnp.int32, (BOXES4, window), 0)
    pick = jnp.where(pick, 1.0, 0.0).astype(bf16)
    half = dens * CPAD
    local = jnp.concatenate(
        [dot(stack[h * half : (h + 1) * half].astype(bf16), pick) for h in range(2)], axis=1
    ).astype(bf16)
    found[:, place.shape[1] :] = jnp.zeros((8, found.shape[1] - place.shape[1]), f32)
    fetch.wait()

    def block(j, carry):
        at = pl.ds(pl.multiple_of(j * PB, PB), PB)
        there = place[:, at] == lax.broadcasted_iota(jnp.int32, (window, PB), 0)
        there = jnp.where(there, 1.0, 0.0)
        there = jnp.concatenate([there, there], axis=0).astype(bf16)
        got = dot(local, there)
        mine = field[:, at]
        rows = []
        for k in range(dens):
            value = got[k * CPAD : k * CPAD + COEF]
            rows.append(jnp.sum(value * mine, axis=0, keepdims=True))
        rows.append(jnp.zeros((8 - dens, PB), f32))
        found[:, at] = jnp.concatenate(rows, axis=0)
        return carry

    lax.fori_loop(0, place.shape[1] // PB, block, 0, unroll=2)

    wide = up(cap, LANE) + LANE

    @pl.loop(0, sources // STRIP)
    def _(i):
        for s in range(STRIP):
            offset = offsets[i * STRIP + s]
            tile = offset // LANE
            value = found[:, pl.ds(pl.multiple_of(tile * LANE, LANE), wide)]
            value = pltpu.roll(value, wide - (offset - tile * LANE), 1)
            for k in range(dens):
                out[i * STRIP + s, :, k * cap : (k + 1) * cap] = value[k : k + 1, 0:cap]


def shift_by(axis, value, distance):
    size = lax.axis_size(axis)
    return lax.ppermute(value, axis, [(i, i ^ distance) for i in range(size)])


def gather_by(value, distances, beside):
    got = {m: shift_by("pts", value, m) if m else value for m in distances if m % 2 == 0}
    got, beside = lax.optimization_barrier((got, beside))
    got.update({m + 1: shift_by("pts", got[m], 1) for m in list(got) if m + 1 in distances})
    return [got[m] for m in distances], beside


def per_device(
    local_pos, densities, morton_slot, slot_leaf, uc2e, m2m, m2l_ops, dc2e, lattice, l2l
):
    n_pts = lax.axis_size("pts")
    n_top = lax.axis_size("top")
    me = jnp.stack([lax.axis_index("pts"), lax.axis_index("top")]).astype(jnp.int32)
    points = local_pos.shape[1]
    own = points * n_top
    cap = 2 * points // n_pts
    box_cap = 2 * BOXES4 // n_pts
    dens = DENS // n_top
    slabs = max(1, 2 * SIDE // n_pts)
    coef = uc2e.shape[0]
    sources = n_pts * n_top
    lanes = min(cap, LANE)
    rows = 8 + points // lanes

    def shape(*dims, dtype=bf16):
        return jax.ShapeDtypeStruct(dims, dtype)

    outgoing, entries = call(
        functools.partial(route_kernel, own, cap, n_top),
        (shape(n_pts, n_top, rows, cap, dtype=f32), shape(1, points, dtype=jnp.int32)),
        GRANT,
        1 << 27,
        in_specs=[WHOLE] * 4,
        out_specs=(WHOLE, WHOLE),
    )(
        local_pos,
        densities,
        morton_slot.reshape(1, points),
        slot_leaf.reshape(points // lanes, lanes),
    )
    outgoing = outgoing.reshape(sources, rows, cap)
    incoming = lax.all_to_all(outgoing, ("pts", "top"), split_axis=0, concat_axis=0, tiled=True)

    flat = (-1, LANE)
    column = jnp.asarray(column_table())
    square_shape = shape(8, coef, coef)
    w_both, *coarse_ops = call(
        operators_kernel,
        (shape(2 * coef, 8 * CPAD),)
        + (square_shape,) * 4
        + (shape(coef, coef),) * 2
        + (shape(2, coef, ROWS),) * 2,
        GRANT,
        1 << 30,
        in_specs=[WHOLE] * 6,
        out_specs=(WHOLE,) * 9,
        scratch_shapes=[pltpu.VMEM((2, 8 * coef, LANE), f32)],
    )(m2m.reshape(flat), l2l.reshape(flat), uc2e, dc2e, lattice, column)
    coarse_ops, halves = coarse_ops[:6], coarse_ops[6:]
    m2m_hi, m2m_lo, l2l_hi, l2l_lo, lat_hi, lat_lo = coarse_ops
    coarse_ops = (m2m_hi, m2m_lo, lat_hi, lat_lo, l2l_hi, l2l_lo)
    first = relayout(m2l_ops, me, 0, EARLY)
    incoming, first = lax.optimization_barrier((incoming, first))

    partial, field, place, offsets = call(
        functools.partial(points_kernel, n_top, box_cap),
        (
            shape(up(coef + 2, 16), dens * box_cap),
            shape(coef, own, dtype=f32),
            shape(1, own, dtype=jnp.int32),
            shape(sources + 1, dtype=jnp.int32),
        ),
        GRANT,
        8 << 30,
        in_specs=[SMEM] + [WHOLE] * 2 + [ANY],
        out_specs=(WHOLE, WHOLE, WHOLE, SMEM),
        scratch_shapes=[
            pltpu.VMEM((8, up(own + up(cap, LANE) + LANE, PB)), f32),
            pltpu.VMEM((3 + FEATURES, coef, PB), f32),
            pltpu.VMEM(w_both.shape, bf16),
            pltpu.SemaphoreType.DMA,
        ],
    )(me, incoming, column, w_both)
    later, flat_ops = lax.optimization_barrier((partial, m2l_ops))
    rest = relayout(flat_ops, me, EARLY, STEPS - EARLY)
    parts, rest = gather_by(later, range(n_pts), rest)

    columns = dens * PLANE
    checks = call(
        functools.partial(translate_kernel, slabs, dens),
        shape(ROWS, slabs * columns),
        GRANT,
        8 << 30,
        in_specs=[SMEM] + [WHOLE] * n_pts + [ANY] * 6,
        out_specs=WHOLE,
        scratch_shapes=[
            pltpu.VMEM(((7 + slabs - 1) * columns, WFULL), bf16),
            pltpu.VMEM(((7 + slabs - 1) * columns, WIN), bf16),
            pltpu.VMEM((7 * ROWS, slabs * columns), f32),
            *[pltpu.VMEM((a, b, ROWS, c), bf16) for a, b, c in PIECES],
            pltpu.SemaphoreType.DMA((2, 3, 4)),
        ],
    )(me, *parts, *first, *rest)
    lattice4 = call(
        coarse_kernel,
        shape(dens, coef, BOXES4, dtype=f32),
        GRANT,
        4 << 30,
        in_specs=[WHOLE] * n_pts + [ANY] * 6,
        out_specs=WHOLE,
        scratch_shapes=[pltpu.VMEM(v.shape, bf16) for v in coarse_ops]
        + [pltpu.SemaphoreType.DMA((6,))],
    )(*parts, *coarse_ops)

    step = n_pts // SIDE * slabs
    distances = [step * m + c for m in range(SIDE // slabs) for c in range(2)]
    gathered, lattice4 = gather_by(checks, distances, lattice4)

    reply = call(
        functools.partial(evaluate_kernel, slabs, step, box_cap),
        shape(sources, 1, dens * cap, dtype=f32),
        GRANT,
        4 << 30,
        in_specs=[SMEM] + [WHOLE] * (len(gathered) + 3) + [ANY, WHOLE, SMEM],
        out_specs=WHOLE,
        scratch_shapes=[
            pltpu.VMEM((2 * dens * CPAD, BOXES4), f32),
            pltpu.VMEM((8, own + up(cap, LANE) + LANE), f32),
            pltpu.VMEM(field.shape, f32),
            pltpu.SemaphoreType.DMA,
        ],
    )(me, *gathered, *halves, lattice4, field, place, offsets)
    returned = lax.all_to_all(reply, ("pts", "top"), split_axis=0, concat_axis=0, tiled=True)
    return call(
        functools.partial(restore_kernel, n_top),
        shape(DENS, points, dtype=f32),
        GRANT,
        1 << 28,
        in_specs=[WHOLE] * 2,
        out_specs=WHOLE,
    )(returned, entries)


def solution(mesh):
    split_all = P(None, ("pts", "top"))
    placed = (split_all, split_all, P(("pts", "top")), P(("pts", "top"))) + (P(),) * 6
    return jax.shard_map(
        per_device, mesh=mesh, in_specs=placed, out_specs=split_all, check_vma=False
    )
```

```python
import functools
import math

import jax
import jax.numpy as jnp
import numpy as np
from jax import lax
from jax.experimental import pallas as pl
from jax.experimental.pallas import tpu as pltpu
from jax.sharding import PartitionSpec as P

LEVEL = 3
EDGE = 6
DENS = 8
SIDE = 2**LEVEL
BOXES4 = SIDE**3
PLANE = SIDE * SIDE
LANE = 128
REACH = 3
SHIFTS = list(range(-REACH, REACH + 1))
OUTER = [s for s in SHIFTS if abs(s) >= 2]
INNER = [s for s in SHIFTS if abs(s) < 2]
bf16 = jnp.bfloat16
f32 = jnp.float32
NN = (((1,), (0,)), ((), ()))
NT = (((1,), (1,)), ((), ()))


def up(value, multiple):
    return -(-value // multiple) * multiple


def surface_table():
    grid_vals = np.linspace(-1.0, 1.0, EDGE)
    points_list = []
    for a in range(EDGE):
        for b in range(EDGE):
            for c in range(EDGE):
                if min(a, b, c) == 0 or max(a, b, c) == EDGE - 1:
                    points_list.append([grid_vals[a], grid_vals[b], grid_vals[c]])
    return np.array(points_list, dtype=np.float32).T


COEF = surface_table().shape[1]
OFFSETS = (2 * REACH + 1) ** 3 - 27
FEATURES = 4
PB = 256
STRIP = 16
GRANT = 28
GRANT_FIRST = 60
GRANT_EARLY = 52
GRANT_LATER = 49
CPAD = up(COEF, 32)


def column_table():
    surface = 1.25 * surface_table().astype(np.float64)
    grid = np.linspace(-0.9, 0.9, 10)
    points = np.stack(np.meshgrid(grid, grid, grid, indexing="ij")).reshape(3, -1)
    values = 1.0 / np.sqrt(((surface[:, :, None] - points[:, None, :]) ** 2).sum(axis=0))
    scale = (points**2).sum(axis=1)
    out = np.zeros((surface.shape[1], LANE), np.float32)
    out[:, 0:3] = (np.float32(1.25) * surface_table()).T
    out[:, 8] = values.mean(axis=1)
    out[:, 9:12] = values @ points.T / scale
    return out


def blocks():
    out, position = [], 0
    for dx in SHIFTS:
        for dy in SHIFTS:
            count = sum(max(abs(dx), abs(dy), abs(dz)) >= 2 for dz in SHIFTS)
            out.append((dx, dy, position, count))
            position += count
    return out


def dot(a, b, dims=NN):
    return lax.dot_general(a, b, dims, preferred_element_type=f32)


def split(value):
    high = value.astype(bf16)
    return high, (value - high.astype(f32)).astype(bf16)


def dot3(a, b, dims=NN):
    return dot(a[0], b[0], dims) + dot(a[1], b[0], dims) + dot(a[0], b[1], dims)


def dot3_rows(a, b, dims=NN):
    rows = a[0].shape[0]
    both = jnp.concatenate([x.astype(f32) for x in a], axis=0).astype(bf16)
    both = dot(both, b[0], dims)
    return both[0:rows] + both[rows : 2 * rows] + dot(a[0], b[1], dims)


def call(kernel, out_shape, mib, flops, bytes_accessed=1 << 20, **kw):
    return pl.pallas_call(
        kernel,
        out_shape=out_shape,
        compiler_params=pltpu.CompilerParams(vmem_limit_bytes=mib << 20),
        cost_estimate=pl.CostEstimate(
            flops=flops, bytes_accessed=bytes_accessed, transcendentals=0
        ),
        **kw,
    )


SMEM = pl.BlockSpec(memory_space=pltpu.SMEM)
VMEM = pl.BlockSpec(memory_space=pltpu.VMEM)
HBM = pl.BlockSpec(memory_space=pltpu.HBM)

class Buffers:
    def __init__(self, scalars, ins, outs, moved, sources, targets, sem_in, sem_out):
        self.scalars, self.ins, self.outs, self.targets = scalars, ins, outs, targets
        self.sem_out = sem_out
        self.coming, self.going, self.waited = {}, {}, set()
        for i in moved:
            self.coming[i] = pltpu.make_async_copy(sources[i], ins[i], sem_in.at[i])
            self.coming[i].start()

    def wait(self, *which):
        for i in which:
            if i in self.coming and i not in self.waited:
                self.waited.add(i)
                self.coming[i].wait()

    def send(self, *which):
        for i in which:
            if i not in self.going:
                copy = pltpu.make_async_copy(self.outs[i], self.targets[i], self.sem_out.at[i])
                copy.start()
                self.going[i] = copy


def run(kernel, scalars, ins, outs, flops, scratch=(), late=(), here=(), stays=(), numbers=(), grant=GRANT):
    n_s, n_i, n_o, n_n = len(scalars), len(ins), len(outs), len(numbers)
    moved_in = [i for i in range(n_i) if i not in here]
    moved_out = [i for i in range(n_o) if i not in stays]

    def body(*refs):
        refs = list(refs)
        take = lambda count: [refs.pop(0) for _ in range(count)]
        given, sources, targets, counts = take(n_s), take(n_i), take(n_o), take(n_n)
        in_refs, out_refs = list(sources), list(targets)
        for i in moved_in:
            in_refs[i] = refs.pop(0)
        for i in moved_out:
            out_refs[i] = refs.pop(0)
        io = Buffers(given, in_refs, out_refs, moved_in, sources, targets, *take(2))
        io.wait(*[i for i in moved_in if i not in late])
        kernel(io, *counts, *refs)
        io.wait(*moved_in)
        io.send(*moved_out)
        for i in moved_out:
            io.going[i].wait()

    return call(
        body,
        tuple(outs) + tuple(numbers),
        grant,
        flops,
        in_specs=[SMEM] * n_s + [VMEM if i in here else HBM for i in range(n_i)],
        out_specs=tuple(VMEM if i in stays else HBM for i in range(n_o)) + (SMEM,) * n_n,
        scratch_shapes=[pltpu.VMEM(ins[i].shape, ins[i].dtype) for i in moved_in]
        + [pltpu.VMEM(outs[i].shape, outs[i].dtype) for i in moved_out]
        + [pltpu.SemaphoreType.DMA((max(n, 1),)) for n in (n_i, n_o)]
        + list(scratch),
    )(*scalars, *ins)


HG = 4 * OFFSETS * COEF // LANE
KT = up(up(OFFSETS * COEF, LANE) // LANE, 8)
WFULL = up(7 * COEF, LANE)
WIN = up(4 * COEF, LANE)
NG = COEF // 8
STEPS = -(-NG // 4)
ROWS = 16 * STEPS
CHUNK = up(HG + 15, 16)
TAIL = 32
EARLY = 3
STRIDE = 17
PIECES = ((4, 7, WFULL), (3, 4, WFULL), (3, 3, WIN))


def relayout_kernel(nrows, step0, steps, me_ref, f_hbm, tail_ref, oa, ob, oc, inb, fbuf, tbuf, tb16, sem):
    step = pl.program_id(0)
    half = me_ref[0] & 1
    end16 = nrows // 16 * 16

    def start_row(st, g):
        return jnp.minimum(4 * (st + step0) + g, NG - 1) * (2 * HG) + half * HG

    def start(st, slot):
        for g in range(4):
            row = pl.multiple_of(start_row(st, g) // 16 * 16, 16)
            pltpu.make_async_copy(
                f_hbm.at[pl.ds(row, CHUNK - TAIL)],
                inb.at[slot, g, pl.ds(0, CHUNK - TAIL)],
                sem.at[slot, g, 0],
            ).start()
            last = row + CHUNK > end16

            @pl.when(jnp.logical_not(last))
            def _():
                pltpu.make_async_copy(
                    f_hbm.at[pl.ds(pl.multiple_of(row + CHUNK - TAIL, 16), TAIL)],
                    inb.at[slot, g, pl.ds(CHUNK - TAIL, TAIL)],
                    sem.at[slot, g, 1],
                ).start()


    def wait(st, slot):
        for g in range(4):
            row = pl.multiple_of(start_row(st, g) // 16 * 16, 16)
            pltpu.make_async_copy(
                f_hbm.at[pl.ds(row, CHUNK - TAIL)],
                inb.at[slot, g, pl.ds(0, CHUNK - TAIL)],
                sem.at[slot, g, 0],
            ).wait()
            last = row + CHUNK > end16

            @pl.when(jnp.logical_not(last))
            def _():
                pltpu.make_async_copy(
                    f_hbm.at[pl.ds(pl.multiple_of(row + CHUNK - TAIL, 16), TAIL)],
                    inb.at[slot, g, pl.ds(CHUNK - TAIL, TAIL)],
                    sem.at[slot, g, 1],
                ).wait()

            @pl.when(last)
            def _():
                row16 = lax.broadcasted_iota(jnp.int32, (16, LANE), 0)
                tail = jnp.where(row16 < nrows - end16, tail_ref[...].astype(f32), 0.0)
                inb[slot, g, CHUNK - TAIL : CHUNK - TAIL + 16] = tail.astype(bf16)

    slot = lax.rem(step, 2)

    @pl.when(step == 0)
    def _():
        fbuf[...] = jnp.zeros_like(fbuf)
        start(0, 0)

    @pl.when(step + 1 < steps)
    def _():
        start(step + 1, 1 - slot)

    wait(step, slot)
    lane = lax.broadcasted_iota(jnp.int32, (8, LANE), 1)
    for g in range(4):
        fbuf[g, 0:CHUNK] = inb[slot, g].astype(f32)
    for g in range(4):
        row = start_row(step, g)
        off = row - row // 16 * 16
        for e in range(4):
            first = OFFSETS * COEF * e
            phase = first % LANE

            @pl.loop(0, KT // 8, unroll=KT // 8)
            def _(n):
                base = off + first // LANE + 8 * n
                value = fbuf[g, pl.ds(base, 8), :]
                if phase:
                    after = fbuf[g, pl.ds(base + 1, 8), :]
                    value = pltpu.roll(jnp.where(lane >= phase, value, after), LANE - phase, 1)
                tbuf[pl.ds(8 * n * STRIDE + 4 * g + e, 8, stride=STRIDE), :] = value

    @pl.loop(0, KT, unroll=8)
    def _(k):
        tb16[k] = tbuf[pl.ds(k * STRIDE, 16), :].astype(bf16)

    here = pl.ds(pl.multiple_of(step * 16, 16), 16)
    for dx, dy, d0, count in blocks():
        tile0, phase = divmod(d0 * COEF, LANE)
        if dx in OUTER:
            ref = oa.at[OUTER.index(dx), (OUTER + INNER).index(dy)]
        elif dy in OUTER:
            ref = ob.at[INNER.index(dx), OUTER.index(dy)]
        else:
            ref = oc.at[INNER.index(dx), INNER.index(dy)]
        for t in range(up(count * COEF, LANE) // LANE):
            value = tb16[tile0 + t]
            if phase:
                after = tb16[min(tile0 + t + 1, KT - 1)]
                value = jnp.concatenate([value[:, phase:], after[:, :phase]], axis=1)
            ref[here, t * LANE : (t + 1) * LANE] = value


def relayout(flat, me, step0, steps, grant):
    nrows = flat.shape[0] // LANE
    rows = flat.reshape(nrows, LANE)
    shapes = tuple((a, b, 16 * steps, c) for a, b, c in PIECES)
    return call(
        functools.partial(relayout_kernel, nrows, step0, steps),
        tuple(jax.ShapeDtypeStruct(s, bf16) for s in shapes),
        grant,
        1 << 20,
        steps << 21,
        grid_spec=pltpu.PrefetchScalarGridSpec(
            num_scalar_prefetch=1,
            grid=(steps,),
            in_specs=[HBM, pl.BlockSpec((16, LANE), lambda i, h: (nrows // 16, 0))],
            out_specs=(VMEM,) * len(shapes),
            scratch_shapes=[
                pltpu.VMEM((2, 4, CHUNK, LANE), bf16),
                pltpu.VMEM((4, CHUNK + 16, LANE), f32),
                pltpu.VMEM((KT * STRIDE, LANE), f32),
                pltpu.VMEM((KT, 16, LANE), bf16),
                pltpu.SemaphoreType.DMA((2, 4, 2)),
            ],
        ),
    )(me, rows, rows)


GROUP = 16


def square(flat, out):
    per = GROUP * COEF // LANE
    groups = flat.shape[0] // per
    lane = lax.broadcasted_iota(jnp.int32, (groups, LANE), 1)
    for r in range(GROUP):
        first, phase = divmod(r * COEF, LANE)
        got = []
        for t in range(3):
            row = min(first + t, per - 1)
            got.append(flat[pl.ds(row, groups, stride=per), :])
        for t in range(2):
            value = got[t]
            if phase:
                value = jnp.where(lane >= phase, got[t], got[t + 1])
                value = pltpu.roll(value, LANE - phase, 1)
            out[t, pl.ds(r, groups, stride=GROUP), :] = value


def operators_kernel(io, rows):
    m2m, l2l, uc2e, dc2e, lattice, column = io.ins
    w_both, coarse, d_hi, d_lo = io.outs
    scale = 1.0 / (4.0 * math.pi)
    coarse[32], coarse[33] = split(lattice[...])
    first = split(uc2e[...] * scale)

    plane = split(column[...])

    def stack(pieces, first):
        wide = []
        for piece in pieces:
            high, low = split(dot3(split(piece), plane)[:, 8 : 8 + FEATURES])
            wide += [piece, high.astype(f32), low.astype(f32)]
            wide.append(jnp.zeros((COEF, CPAD - COEF - 2 * FEATURES), f32))
        wide = jnp.concatenate([w for w in wide if w.shape[1]], axis=1).astype(bf16)
        w_both[first : first + COEF] = wide

    def matrix(o):
        at = slice(o * COEF, (o + 1) * COEF)
        return jnp.concatenate([rows[0, at], rows[1, at, 0 : COEF - LANE]], axis=1)

    io.wait(0)
    square(m2m, rows)
    pieces = []
    for o in range(8):
        high, low = split(matrix(o))
        coarse[o], coarse[8 + o] = high, low
        pieces.append(dot3((high, low), first))
    stack(pieces, 0)
    io.wait(1)
    square(l2l, rows)
    pieces = []
    for o in range(8):
        value = matrix(o)
        coarse[16 + o], coarse[24 + o] = split(value)
        pieces.append(jnp.transpose(value) * scale)
    stack(pieces, COEF)
    high, low = split(dc2e[...])
    i = lax.broadcasted_iota(jnp.int32, (COEF, ROWS), 0)
    r = lax.broadcasted_iota(jnp.int32, (COEF, ROWS), 1)
    for h in range(2):
        here = (i == (r >> 2) * 8 + 4 * h + (r & 3)) & (r < 4 * NG)
        here = jnp.where(here, 1.0, 0.0).astype(bf16)
        d_hi[h] = dot(high, here).astype(bf16)
        d_lo[h] = dot(low, here).astype(bf16)


def route_kernel(own, cap, n_top, io):
    pos, dens, slot, leaf = io.ins
    out, entries = io.outs
    points = pos.shape[1]
    owners = out.shape[0]
    slots = slot[...]
    owner = slots // own
    inside = slots - owner * own
    hit = owner == lax.broadcasted_iota(jnp.int32, (owners, points), 0)
    hit = jnp.where(hit, 1.0, 0.0)
    hit16 = hit.astype(bf16)
    row = lax.broadcasted_iota(jnp.int32, (LANE, LANE), 0)
    col = lax.broadcasted_iota(jnp.int32, (LANE, LANE), 1)
    before = jnp.where(row < col, 1.0, 0.0).astype(bf16)
    every = jnp.ones((LANE, LANE), bf16)
    total = jnp.zeros((owners, LANE), f32)
    ranks = []
    for t in range(points // LANE):
        part = hit16[:, t * LANE : (t + 1) * LANE]
        ranks.append(total + dot(part, before))
        total = total + dot(part, every)
    rank = jnp.sum(hit * jnp.concatenate(ranks, axis=1), axis=0, keepdims=True)
    entry = owner * cap + rank.astype(jnp.int32)
    entries[...] = entry
    inside_hi = inside // 64
    value = jnp.concatenate([pos[...], dens[...]], axis=0)
    width = value.shape[0]
    high, low = split(value)
    ones = jnp.ones((1, points), f32)
    high = jnp.concatenate(
        [high.astype(f32), inside_hi.astype(f32), (inside - 64 * inside_hi).astype(f32), ones]
        + [jnp.zeros((16 - width - 3, points), f32)],
        axis=0,
    )
    low = jnp.concatenate([low.astype(f32), jnp.zeros((16 - width, points), f32)], axis=0)
    payload = jnp.concatenate([high, low], axis=0).astype(bf16)
    block = max(cap, LANE)
    per = DENS // n_top
    leaves = leaf[...].astype(f32)
    if leaves.shape[1] < cap:
        blank = jnp.zeros((leaves.shape[0], cap - leaves.shape[1]), f32)
        leaves = jnp.concatenate([leaves, blank], axis=1)
    for o in range(owners * cap // block):
        there = entry == o * block + lax.broadcasted_iota(jnp.int32, (block, points), 0)
        there = jnp.where(there, 1.0, 0.0).astype(bf16)
        got = dot(payload, there, NT)
        value = got[0:width] + got[16 : 16 + width]
        where = got[width : width + 1] * 64.0 + got[width + 1 : width + 2]
        valid = got[width + 2 : width + 3]
        for q in range(n_top):
            rows = [value[0:3], where, valid, value[3 + per * q : 3 + per * (q + 1)]]
            rows.append(jnp.zeros((8 - 5 - per, block), f32))
            packed = jnp.concatenate([r for r in rows if r.shape[0]], axis=0)
            for i in range(block // cap):
                at = o * (block // cap) + i
                out[at, q, 0:8] = packed[:, i * cap : (i + 1) * cap]
                out[at, q, 8:] = leaves


def restore_kernel(n_top, io):
    got, entries = io.ins
    out = io.outs[0]
    devices = got.shape[0]
    per = out.shape[0] // n_top
    cap = got.shape[2] // per
    points = out.shape[1]
    block = max(cap, PB)
    total = jnp.zeros((2 * out.shape[0], points), f32)
    for o in range(devices // n_top * cap // block):
        count = block // cap
        value = []
        for q in range(n_top):
            for k in range(per):
                pieces = []
                for i in range(count):
                    row = (o * count + i) * n_top + q
                    pieces.append(got[row, :, k * cap : (k + 1) * cap])
                value.append(jnp.concatenate(pieces, axis=1))
        high, low = split(jnp.concatenate(value, axis=0))
        both = jnp.concatenate([high.astype(f32), low.astype(f32)], axis=0).astype(bf16)
        at = o * block + lax.broadcasted_iota(jnp.int32, (block, points), 0)
        total = total + dot(both, jnp.where(entries[...] == at, 1.0, 0.0).astype(bf16))
    out[...] = total[0 : out.shape[0]] + total[out.shape[0] :]


def octant_product(pos, octant, surf, oper):
    squared = None
    for d in range(3):
        spacing = surf[d] - pos[d : d + 1]
        squared = spacing * spacing if squared is None else squared + spacing * spacing
    value = lax.rsqrt(squared)
    round_pos = pos.astype(bf16).astype(f32)
    value = value - surf[3]
    for d in range(3):
        value = value - surf[4 + d] * round_pos[d : d + 1]
    features = [jnp.ones_like(round_pos[0:1]), round_pos]
    blank = jnp.zeros((CPAD - COEF - 2 * FEATURES, value.shape[1]), f32)
    value = [value] + features + features + [blank]
    value = jnp.concatenate([v for v in value if v.shape[0]], axis=0).astype(bf16)
    masks = [jnp.where(octant == o, 1.0, 0.0).astype(bf16) for o in range(8)]
    return dot(oper[...], jnp.concatenate([value * m for m in masks], axis=0))


TURNED = (((0,), (0,)), ((), ()))


def look_up(index, table):
    lanes, rows = table.shape[0] // 2, table.shape[1]
    width = index.shape[1]
    at_row = index // lanes
    at_lane = index - at_row * lanes
    there = at_row == lax.broadcasted_iota(jnp.int32, (rows, width), 0)
    got = dot(table, jnp.where(there, 1.0, 0.0).astype(bf16))
    mine = at_lane == lax.broadcasted_iota(jnp.int32, (lanes, width), 0)
    first = jnp.sum(jnp.where(mine, got[0:lanes], 0.0), axis=0, keepdims=True)
    return first, jnp.sum(jnp.where(mine, got[lanes:], 0.0), axis=0, keepdims=True)


def fill_surface(surf, column):
    for i, lane in enumerate((0, 1, 2, 8, 9, 10, 11)):
        surf[i] = jnp.broadcast_to(column[:, lane : lane + 1], surf.shape[1:])


def morton_place(box):
    place = jnp.zeros_like(box)
    for b in range(LEVEL):
        digit = box >> (3 * b)
        place = place + ((((digit >> 2) & 1) << (2 * LEVEL + b)))
        place = place + ((((digit >> 1) & 1) << (LEVEL + b)) + ((digit & 1) << b))
    return place


def points_kernel(n_top, box_cap, io, offsets, buf, surf):
    got, column, oper = io.ins
    out, field, place = io.outs
    sources, _, cap = got.shape
    lanes = min(cap, LANE)
    own = field.shape[1]
    wide = up(cap, LANE)
    me = io.scalars[0][0]
    buf[...] = jnp.zeros_like(buf)
    fill_surface(surf, column)
    io.wait(0)

    def put(i, offset):
        values = [got[i * STRIP + s, 0:8] for s in range(STRIP)]
        counts = [jnp.sum(v[4:5]).astype(jnp.int32) for v in values]
        for s, (value, count) in enumerate(zip(values, counts)):
            offsets[i * STRIP + s] = offset
            value = jnp.concatenate([value, jnp.zeros((8, wide + LANE - cap), f32)], axis=1)
            tile = offset // LANE
            value = pltpu.roll(value, offset - tile * LANE, 1)
            at = pl.ds(pl.multiple_of(tile * LANE, LANE), wide + LANE)
            buf[:, at] = buf[:, at] + value
            offset = offset + count
        return offset

    lax.fori_loop(0, sources // STRIP, put, jnp.int32(0))
    leaf = got[pl.ds(me * n_top, n_top), 8:, 0:lanes].reshape(own // lanes, lanes)
    leaf = leaf.astype(jnp.int32)
    first = got[me * n_top, 8:9, 0:1].astype(jnp.int32) >> 3
    offsets[sources] = jnp.sum(got[me * n_top, 8:9, 0:1]).astype(jnp.int32) >> 3
    io.wait(2)
    table = jnp.concatenate([(leaf >> 3) - first, leaf & 7], axis=1).astype(f32)
    table = jnp.transpose(table).astype(bf16)
    out_rows = out.shape[1]

    def block(j, total):
        to = pl.ds(pl.multiple_of(j * PB, PB), PB)
        value = buf[:, to]
        box, octant = look_up(value[3:4].astype(jnp.int32), table)
        place[:, to] = box.astype(jnp.int32)
        both = octant_product(value[0:3], octant, surf, oper)
        field[:, to] = both[COEF : 2 * COEF]
        high, low = split(both[0:COEF])
        rows = []
        at = lax.broadcasted_iota(jnp.int32, (box_cap, PB), 0).astype(f32)
        for k in range(out_rows // box_cap):
            rows.append(jnp.where(box == at, value[5 + k : 6 + k], 0.0))
        a_high, a_low = split(jnp.concatenate(rows, axis=0))
        both = dot(jnp.concatenate([high, low], axis=0), a_high, NT)
        return total + both[0:COEF] + both[COEF : 2 * COEF] + dot(high, a_low, NT)

    total = lax.fori_loop(0, own // PB, block, jnp.zeros((COEF, out_rows), f32), unroll=2)
    digits = jnp.concatenate([first >> 3, first & 7], axis=0).astype(f32)
    digits = jnp.broadcast_to(digits, (2, out_rows))
    blank = jnp.zeros((out.shape[0] - COEF - 2, out_rows), f32)
    out[...] = jnp.concatenate([total, digits, blank], axis=0).astype(bf16)
    io.send(0)


def box_ids(parts, dens):
    ids = []
    for part in parts:
        digits = part[COEF : COEF + 8, 0:1].astype(f32).astype(jnp.int32)
        first = digits[0:1] * 8 + digits[1:2]
        at = lax.broadcasted_iota(jnp.int32, (1, part.shape[1] // dens), 1)
        ids.append(first + at)
    return jnp.concatenate(ids, axis=1)


def all_parts(parts, k, dens):
    width = parts[0].shape[1] // dens
    return jnp.concatenate([p[0:COEF, k * width : (k + 1) * width] for p in parts], axis=1)


def translate_kernel(slabs, dens, io, xs, xin, acc):
    parts = io.ins[:-6]
    first, rest = io.ins[-6:-3], io.ins[-3:]
    out = io.outs[0]
    x0 = (io.scalars[0][0] // 2 * 2) * SIDE // len(parts)
    ids = box_ids(parts, dens)
    place = morton_place(ids)
    place = (((place >> 6) - x0 + REACH) & 7) * 64 + (place & 63)
    place = jnp.where(ids < BOXES4, place, -1)
    at = lax.broadcasted_iota(jnp.int32, (BOXES4, ids.shape[1]), 0)
    there = jnp.where(at == place, 1.0, 0.0).astype(bf16)
    columns = dens * PLANE
    for k in range(dens):
        low = dot(there, all_parts(parts, k, dens), NT)
        low = low.astype(bf16).astype(f32)
        for s in range(7 + slabs - 1):
            slab = low[s * PLANE : (s + 1) * PLANE].reshape(SIDE, SIDE, COEF)
            shifted = {}
            for dz in SHIFTS:
                if dz == 0:
                    moved = slab
                else:
                    cut = dz % SIDE
                    moved = jnp.concatenate([slab[:, cut:], slab[:, :cut]], axis=1)
                shifted[dz] = moved.reshape(PLANE, COEF)
            rows = pl.ds(s * columns + k * PLANE, PLANE)
            pad = [jnp.zeros((PLANE, WFULL - 7 * COEF), f32)]
            xs[rows, :] = jnp.concatenate([shifted[z] for z in SHIFTS] + pad, axis=1).astype(bf16)
            pad = [jnp.zeros((PLANE, WIN - 4 * COEF), f32)]
            xin[rows, :] = jnp.concatenate([shifted[z] for z in OUTER] + pad, axis=1).astype(bf16)

    def rows_of(i, j):
        value = jnp.concatenate([first[i][j], rest[i][j]], axis=1)
        return value.reshape(-1, value.shape[2])

    n_out = len(OUTER) * ROWS
    n_all = len(SHIFTS) * ROWS
    for i, dx in enumerate(OUTER + INNER):
        rows = pl.ds((dx + REACH) * columns, slabs * columns)
        source = xs[rows, :]
        if dx in OUTER:
            term = dot(rows_of(0, OUTER.index(dx)), source, NT)
            if i == 0:
                acc[...] = term
            else:
                acc[...] += term
        else:
            acc[0:n_out] += dot(rows_of(1, INNER.index(dx)), source, NT)
            acc[n_out:n_all] += dot(rows_of(2, INNER.index(dx)), xin[rows, :], NT)
    lane = lax.broadcasted_iota(jnp.int32, (ROWS, LANE), 1)
    for t in range(slabs * columns // LANE):
        total = jnp.zeros((ROWS, LANE), f32)
        for i, dy in enumerate(OUTER + INNER):
            value = acc[i * ROWS : (i + 1) * ROWS, t * LANE : (t + 1) * LANE]
            by = SIDE * (dy % SIDE)
            if by:
                near = pltpu.roll(value, LANE - by, 1)
                far = pltpu.roll(value, PLANE - by, 1)
                value = jnp.where((lane & (PLANE - 1)) < PLANE - by, near, far)
            total = total + value
        out[:, t * LANE : (t + 1) * LANE] = total.astype(out.dtype)


def coarse_kernel(io):
    out = io.outs[0]
    parts = io.ins[:-1]
    opers = io.ins[-1]
    dens = out.shape[0]
    box = ids = box_ids(parts, dens)
    place = ((box & 7) << 6) + (box & 56) + (box >> 6)
    place = jnp.where(box < BOXES4, place, -1)
    at = lax.broadcasted_iota(jnp.int32, (BOXES4, ids.shape[1]), 0)
    there = jnp.where(at == place, 1.0, 0.0).astype(bf16)
    level = [dot(there, all_parts(parts, k, dens), NT) for k in range(dens)]

    io.wait(*range(len(io.ins)))

    for _ in range(LEVEL):
        count = level[0].shape[0] // 8
        total = None
        for o in range(8):
            rows = jnp.concatenate([v[o * count : (o + 1) * count] for v in level], axis=0)
            term = dot3_rows(split(rows), (opers[o], opers[8 + o]), NT)
            total = term if total is None else total + term
        level = [total[k * count : (k + 1) * count] for k in range(dens)]
    rows = jnp.concatenate(level, axis=0)
    rows = dot3(split(rows), (opers[32], opers[33]), NT)
    level = [rows[k : k + 1] for k in range(dens)]
    for _ in range(LEVEL):
        count = level[0].shape[0]
        rows = split(jnp.concatenate(level, axis=0))
        children = [dot3_rows(rows, (opers[16 + o], opers[24 + o]), NT) for o in range(8)]
        level = [
            jnp.concatenate([c[k * count : (k + 1) * count] for c in children], axis=0)
            for k in range(dens)
        ]
    at = lax.broadcasted_iota(jnp.int32, (1, BOXES4), 1)
    number = jnp.zeros_like(at)
    for b in range(LEVEL):
        digit = ((at >> (2 * LEVEL + b)) & 1) * 4 + ((at >> (LEVEL + b)) & 1) * 2 + ((at >> b) & 1)
        number = number + (digit << (3 * (LEVEL - 1 - b)))
    row = lax.broadcasted_iota(jnp.int32, (BOXES4, BOXES4), 0)
    move = jnp.where(row == number, 1.0, 0.0).astype(bf16)
    for k in range(dens):
        high, low = split(level[k])
        out[k] = dot(high, move, TURNED) + dot(low, move, TURNED)


def evaluate_kernel(slabs, step, window, io, stack, found):
    n = SIDE // slabs
    checks = io.ins[: 2 * n]
    d_hi, d_lo, lattice, place, field = io.ins[2 * n :]
    offsets = io.scalars[1]
    out = io.outs[0]
    core = io.scalars[0][0] & 1
    group = io.scalars[0][0] // step
    dens = lattice.shape[0]
    sources, cap = out.shape[0], out.shape[2] // dens
    lane = lax.broadcasted_iota(jnp.int32, (COEF, LANE), 1)
    mine = jnp.concatenate([d_hi[core], d_lo[core]], axis=0)
    other = jnp.concatenate([d_hi[1 - core], d_lo[1 - core]], axis=0)
    for m in range(n):
        value = dot(mine, checks[2 * m][...]) + dot(other, checks[2 * m + 1][...])
        value = value[0:COEF] + value[COEF : 2 * COEF]
        if slabs == 2:
            a, b = value[:, 0:LANE], value[:, LANE : 2 * LANE]
            half = LANE // 2
            pieces = [
                jnp.where(lane < half, a, pltpu.roll(b, half, 1)),
                jnp.where(lane < half, pltpu.roll(a, half, 1), b),
            ]
        else:
            pieces = [value[:, k * PLANE : (k + 1) * PLANE] for k in range(dens)]
        width = slabs * PLANE
        for k in range(dens):
            at = m ^ group
            if width % LANE == 0:
                base = lattice[k, :, pl.ds(pl.multiple_of(at * width, width), width)]
            else:
                pair = lattice[k, :, pl.ds(pl.multiple_of(at // 2 * LANE, LANE), LANE)]
                base = jnp.where(at % 2 == 0, pair[:, :width], pair[:, width:])
            high, low = split(pieces[k] + base)
            rows = pl.ds(k * CPAD, COEF)
            stack[rows, m * width : (m + 1) * width] = high.astype(f32)
            rows = pl.ds((dens + k) * CPAD, COEF)
            stack[rows, m * width : (m + 1) * width] = low.astype(f32)
    box = offsets[sources] + lax.broadcasted_iota(jnp.int32, (1, window), 1)
    want = morton_place(box) ^ (group * (slabs * PLANE))
    want = jnp.where(box < BOXES4, want, -1)
    pick = want == lax.broadcasted_iota(jnp.int32, (BOXES4, window), 0)
    pick = jnp.where(pick, 1.0, 0.0).astype(bf16)
    half = dens * CPAD
    local = jnp.concatenate(
        [dot(stack[h * half : (h + 1) * half].astype(bf16), pick) for h in range(2)], axis=1
    ).astype(bf16)
    found[:, place.shape[1] :] = jnp.zeros((8, found.shape[1] - place.shape[1]), f32)
    io.wait(*range(len(io.ins)))

    def block(j, carry):
        at = pl.ds(pl.multiple_of(j * PB, PB), PB)
        there = place[:, at] == lax.broadcasted_iota(jnp.int32, (window, PB), 0)
        there = jnp.where(there, 1.0, 0.0)
        there = jnp.concatenate([there, there], axis=0).astype(bf16)
        got = dot(local, there)
        mine = field[:, at]
        rows = []
        for k in range(dens):
            value = got[k * CPAD : k * CPAD + COEF]
            rows.append(jnp.sum(value * mine, axis=0, keepdims=True))
        rows.append(jnp.zeros((8 - dens, PB), f32))
        found[:, at] = jnp.concatenate(rows, axis=0)
        return carry

    lax.fori_loop(0, place.shape[1] // PB, block, 0, unroll=2)

    wide = up(cap, LANE) + LANE

    @pl.loop(0, sources // STRIP)
    def _(i):
        for s in range(STRIP):
            offset = offsets[i * STRIP + s]
            tile = offset // LANE
            value = found[:, pl.ds(pl.multiple_of(tile * LANE, LANE), wide)]
            value = pltpu.roll(value, wide - (offset - tile * LANE), 1)
            for k in range(dens):
                out[i * STRIP + s, :, k * cap : (k + 1) * cap] = value[k : k + 1, 0:cap]


def shift_by(axis, value, distance):
    size = lax.axis_size(axis)
    return lax.ppermute(value, axis, [(i, i ^ distance) for i in range(size)])


def gather_by(value, distances, beside):
    got = {m: shift_by("pts", value, m) if m else value for m in distances if m % 2 == 0}
    got, beside = lax.optimization_barrier((got, beside))
    got.update({m + 1: shift_by("pts", got[m], 1) for m in list(got) if m + 1 in distances})
    return [got[m] for m in distances], beside


def per_device(
    local_pos, densities, morton_slot, slot_leaf, uc2e, m2m, m2l_ops, dc2e, lattice, l2l
):
    n_pts = lax.axis_size("pts")
    n_top = lax.axis_size("top")
    me = jnp.stack([lax.axis_index("pts"), lax.axis_index("top")]).astype(jnp.int32)
    points = local_pos.shape[1]
    own = points * n_top
    cap = 2 * points // n_pts
    box_cap = 2 * BOXES4 // n_pts
    dens = DENS // n_top
    slabs = max(1, 2 * SIDE // n_pts)
    coef = uc2e.shape[0]
    sources = n_pts * n_top
    lanes = min(cap, LANE)
    rows = 8 + points // lanes

    def shape(*dims, dtype=bf16):
        return jax.ShapeDtypeStruct(dims, dtype)

    outgoing, entries = run(
        functools.partial(route_kernel, own, cap, n_top),
        [],
        [
            local_pos,
            densities,
            morton_slot.reshape(1, points),
            slot_leaf.reshape(points // lanes, lanes),
        ],
        [shape(n_pts, n_top, rows, cap, dtype=f32), shape(1, points, dtype=jnp.int32)],
        1 << 27,
        stays=(1,),
        grant=GRANT_FIRST,
    )
    outgoing = outgoing.reshape(sources, rows, cap)
    incoming = lax.all_to_all(outgoing, ("pts", "top"), split_axis=0, concat_axis=0, tiled=True)

    flat = (-1, LANE)
    column = jnp.asarray(column_table())
    w_both, opers, *halves = run(
        operators_kernel,
        [],
        [m2m.reshape(flat), l2l.reshape(flat), uc2e, dc2e, lattice, column],
        [shape(2 * coef, 8 * CPAD), shape(34, coef, coef)] + [shape(2, coef, ROWS)] * 2,
        1 << 30,
        late=(0, 1),
        stays=range(4),
        scratch=[pltpu.VMEM((2, 8 * coef, LANE), f32)],
    )
    first = relayout(m2l_ops, me, 0, EARLY, GRANT_EARLY)
    incoming, first = lax.optimization_barrier((incoming, first))

    partial, field, place, offsets = run(
        functools.partial(points_kernel, n_top, box_cap),
        [me],
        [incoming, column, w_both],
        [
            shape(up(coef + 2, 16), dens * box_cap),
            shape(coef, own, dtype=f32),
            shape(1, own, dtype=jnp.int32),
        ],
        8 << 30,
        late=(0,),
        here=(2,),
        stays=(1, 2),
        numbers=[shape(sources + 1, dtype=jnp.int32)],
        scratch=[
            pltpu.VMEM((8, up(own + up(cap, LANE) + LANE, PB)), f32),
            pltpu.VMEM((3 + FEATURES, coef, PB), f32),
        ],
    )
    later, flat_ops = lax.optimization_barrier((partial, m2l_ops))
    rest = relayout(flat_ops, me, EARLY, STEPS - EARLY, GRANT_LATER)
    parts, rest = gather_by(later, range(n_pts), rest)

    columns = dens * PLANE
    (checks,) = run(
        functools.partial(translate_kernel, slabs, dens),
        [me],
        [*parts, *first, *rest],
        [shape(ROWS, slabs * columns)],
        8 << 30,
        here=range(n_pts, n_pts + 6),
        scratch=[
            pltpu.VMEM(((7 + slabs - 1) * columns, WFULL), bf16),
            pltpu.VMEM(((7 + slabs - 1) * columns, WIN), bf16),
            pltpu.VMEM((7 * ROWS, slabs * columns), f32),
        ],
    )
    (lattice4,) = run(
        coarse_kernel,
        [],
        [*parts, opers],
        [shape(dens, coef, BOXES4, dtype=f32)],
        4 << 30,
        here=(n_pts,),
        stays=(0,),
    )
    step = n_pts // SIDE * slabs
    distances = [step * m + c for m in range(SIDE // slabs) for c in range(2)]
    gathered, lattice4 = gather_by(checks, distances, lattice4)

    (reply,) = run(
        functools.partial(evaluate_kernel, slabs, step, box_cap),
        [me, offsets],
        [*gathered, *halves, lattice4, place, field],
        [shape(sources, 1, dens * cap, dtype=f32)],
        4 << 30,
        here=range(len(gathered), len(gathered) + 5),
        scratch=[
            pltpu.VMEM((2 * dens * CPAD, BOXES4), f32),
            pltpu.VMEM((8, own + up(cap, LANE) + LANE), f32),
        ],
    )
    returned = lax.all_to_all(reply, ("pts", "top"), split_axis=0, concat_axis=0, tiled=True)
    (out,) = run(
        functools.partial(restore_kernel, n_top),
        [],
        [returned, entries],
        [shape(DENS, points, dtype=f32)],
        1 << 28,
        here=(1,),
    )
    return out


def solution(mesh):
    split_all = P(None, ("pts", "top"))
    placed = (split_all, split_all, P(("pts", "top")), P(("pts", "top"))) + (P(),) * 6
    return jax.shard_map(
        per_device, mesh=mesh, in_specs=placed, out_specs=split_all, check_vma=False
    )
```

```python
import functools
import math

import jax
import jax.numpy as jnp
import numpy as np
from jax import lax
from jax.experimental import pallas as pl
from jax.experimental.pallas import tpu as pltpu
from jax.sharding import PartitionSpec as P

LEVEL = 3
EDGE = 6
DENS = 8
SIDE = 2**LEVEL
BOXES4 = SIDE**3
PLANE = SIDE * SIDE
LANE = 128
REACH = 3
SHIFTS = list(range(-REACH, REACH + 1))
OUTER = [s for s in SHIFTS if abs(s) >= 2]
INNER = [s for s in SHIFTS if abs(s) < 2]
bf16 = jnp.bfloat16
f32 = jnp.float32
NN = (((1,), (0,)), ((), ()))
NT = (((1,), (1,)), ((), ()))


def up(value, multiple):
    return -(-value // multiple) * multiple


def surface_table():
    grid_vals = np.linspace(-1.0, 1.0, EDGE)
    points_list = []
    for a in range(EDGE):
        for b in range(EDGE):
            for c in range(EDGE):
                if min(a, b, c) == 0 or max(a, b, c) == EDGE - 1:
                    points_list.append([grid_vals[a], grid_vals[b], grid_vals[c]])
    return np.array(points_list, dtype=np.float32).T


COEF = surface_table().shape[1]
OFFSETS = (2 * REACH + 1) ** 3 - 27
FEATURES = 4
PB = 256
STRIP = 16
GRANT = 28
GRANT_FIRST = 60
GRANT_EARLY = 52
GRANT_LATER = 49
CPAD = up(COEF, 32)


def column_table():
    surface = 1.25 * surface_table().astype(np.float64)
    grid = np.linspace(-0.9, 0.9, 10)
    points = np.stack(np.meshgrid(grid, grid, grid, indexing="ij")).reshape(3, -1)
    values = 1.0 / np.sqrt(((surface[:, :, None] - points[:, None, :]) ** 2).sum(axis=0))
    scale = (points**2).sum(axis=1)
    out = np.zeros((surface.shape[1], LANE), np.float32)
    out[:, 0:3] = (np.float32(1.25) * surface_table()).T
    out[:, 8] = values.mean(axis=1)
    out[:, 9:12] = values @ points.T / scale
    return out


def blocks():
    out, position = [], 0
    for dx in SHIFTS:
        for dy in SHIFTS:
            count = sum(max(abs(dx), abs(dy), abs(dz)) >= 2 for dz in SHIFTS)
            out.append((dx, dy, position, count))
            position += count
    return out


def dot(a, b, dims=NN):
    return lax.dot_general(a, b, dims, preferred_element_type=f32)


def split(value):
    high = value.astype(bf16)
    return high, (value - high.astype(f32)).astype(bf16)


def dot3(a, b, dims=NN):
    return dot(a[0], b[0], dims) + dot(a[1], b[0], dims) + dot(a[0], b[1], dims)


def dot3_rows(a, b, dims=NN):
    rows = a[0].shape[0]
    both = jnp.concatenate([x.astype(f32) for x in a], axis=0).astype(bf16)
    both = dot(both, b[0], dims)
    return both[0:rows] + both[rows : 2 * rows] + dot(a[0], b[1], dims)


def call(kernel, out_shape, mib, flops, bytes_accessed=1 << 20, **kw):
    return pl.pallas_call(
        kernel,
        out_shape=out_shape,
        compiler_params=pltpu.CompilerParams(vmem_limit_bytes=mib << 20),
        cost_estimate=pl.CostEstimate(
            flops=flops, bytes_accessed=bytes_accessed, transcendentals=0
        ),
        **kw,
    )


SMEM = pl.BlockSpec(memory_space=pltpu.SMEM)
VMEM = pl.BlockSpec(memory_space=pltpu.VMEM)
HBM = pl.BlockSpec(memory_space=pltpu.HBM)

class Buffers:
    def __init__(self, scalars, ins, outs, moved, sources, targets, sem_in, sem_out):
        self.scalars, self.ins, self.outs, self.targets = scalars, ins, outs, targets
        self.sem_out = sem_out
        self.coming, self.going, self.waited = {}, {}, set()
        for i in moved:
            self.coming[i] = pltpu.make_async_copy(sources[i], ins[i], sem_in.at[i])
            self.coming[i].start()

    def wait(self, *which):
        for i in which:
            if i in self.coming and i not in self.waited:
                self.waited.add(i)
                self.coming[i].wait()

    def send(self, *which):
        for i in which:
            if i not in self.going:
                copy = pltpu.make_async_copy(self.outs[i], self.targets[i], self.sem_out.at[i])
                copy.start()
                self.going[i] = copy


def run(kernel, scalars, ins, outs, flops, scratch=(), late=(), here=(), stays=(), numbers=(), grant=GRANT):
    n_s, n_i, n_o, n_n = len(scalars), len(ins), len(outs), len(numbers)
    moved_in = [i for i in range(n_i) if i not in here]
    moved_out = [i for i in range(n_o) if i not in stays]

    def body(*refs):
        refs = list(refs)
        take = lambda count: [refs.pop(0) for _ in range(count)]
        given, sources, targets, counts = take(n_s), take(n_i), take(n_o), take(n_n)
        in_refs, out_refs = list(sources), list(targets)
        for i in moved_in:
            in_refs[i] = refs.pop(0)
        for i in moved_out:
            out_refs[i] = refs.pop(0)
        io = Buffers(given, in_refs, out_refs, moved_in, sources, targets, *take(2))
        io.wait(*[i for i in moved_in if i not in late])
        kernel(io, *counts, *refs)
        io.wait(*moved_in)
        io.send(*moved_out)
        for i in moved_out:
            io.going[i].wait()

    return call(
        body,
        tuple(outs) + tuple(numbers),
        grant,
        flops,
        in_specs=[SMEM] * n_s + [VMEM if i in here else HBM for i in range(n_i)],
        out_specs=tuple(VMEM if i in stays else HBM for i in range(n_o)) + (SMEM,) * n_n,
        scratch_shapes=[pltpu.VMEM(ins[i].shape, ins[i].dtype) for i in moved_in]
        + [pltpu.VMEM(outs[i].shape, outs[i].dtype) for i in moved_out]
        + [pltpu.SemaphoreType.DMA((max(n, 1),)) for n in (n_i, n_o)]
        + list(scratch),
    )(*scalars, *ins)


HG = 4 * OFFSETS * COEF // LANE
KT = up(up(OFFSETS * COEF, LANE) // LANE, 8)
WFULL = up(7 * COEF, LANE)
WIN = up(4 * COEF, LANE)
NG = COEF // 8
STEPS = -(-NG // 4)
ROWS = 16 * STEPS
CHUNK = up(HG + 15, 16)
TAIL = 32
EARLY = 3
STRIDE = 17
PIECES = ((4, 7, WFULL), (3, 4, WFULL), (3, 3, WIN))


def relayout_kernel(nrows, step0, steps, me_ref, f_hbm, tail_ref, oa, ob, oc, inb, fbuf, tbuf, sem):
    step = pl.program_id(0)
    half = me_ref[0] & 1
    end16 = nrows // 16 * 16

    def start_row(st, g):
        return jnp.minimum(4 * (st + step0) + g, NG - 1) * (2 * HG) + half * HG

    def start(st, slot):
        for g in range(4):
            row = pl.multiple_of(start_row(st, g) // 16 * 16, 16)
            pltpu.make_async_copy(
                f_hbm.at[pl.ds(row, CHUNK - TAIL)],
                inb.at[slot, g, pl.ds(0, CHUNK - TAIL)],
                sem.at[slot, g, 0],
            ).start()
            last = row + CHUNK > end16

            @pl.when(jnp.logical_not(last))
            def _():
                pltpu.make_async_copy(
                    f_hbm.at[pl.ds(pl.multiple_of(row + CHUNK - TAIL, 16), TAIL)],
                    inb.at[slot, g, pl.ds(CHUNK - TAIL, TAIL)],
                    sem.at[slot, g, 1],
                ).start()


    def wait(st, slot):
        for g in range(4):
            row = pl.multiple_of(start_row(st, g) // 16 * 16, 16)
            pltpu.make_async_copy(
                f_hbm.at[pl.ds(row, CHUNK - TAIL)],
                inb.at[slot, g, pl.ds(0, CHUNK - TAIL)],
                sem.at[slot, g, 0],
            ).wait()
            last = row + CHUNK > end16

            @pl.when(jnp.logical_not(last))
            def _():
                pltpu.make_async_copy(
                    f_hbm.at[pl.ds(pl.multiple_of(row + CHUNK - TAIL, 16), TAIL)],
                    inb.at[slot, g, pl.ds(CHUNK - TAIL, TAIL)],
                    sem.at[slot, g, 1],
                ).wait()

            @pl.when(last)
            def _():
                row16 = lax.broadcasted_iota(jnp.int32, (16, LANE), 0)
                tail = jnp.where(row16 < nrows - end16, tail_ref[...].astype(f32), 0.0)
                inb[slot, g, CHUNK - TAIL : CHUNK - TAIL + 16] = tail.astype(bf16)

    slot = step

    @pl.when(step == 0)
    def _():
        fbuf[...] = jnp.zeros_like(fbuf)
        inb[:, :, CHUNK - 16 :] = jnp.zeros_like(inb[:, :, CHUNK - 16 :])
        for st in range(steps):
            start(st, st)

    wait(step, slot)
    lane = lax.broadcasted_iota(jnp.int32, (8, LANE), 1)
    for g in range(4):
        fbuf[g, 0:CHUNK] = inb[slot, g].astype(f32)
    for g in range(4):
        row = start_row(step, g)
        off = row - row // 16 * 16
        for e in range(4):
            first = OFFSETS * COEF * e
            phase = first % LANE

            @pl.loop(0, KT // 8, unroll=KT // 8)
            def _(n):
                base = off + first // LANE + 8 * n
                value = fbuf[g, pl.ds(base, 8), :]
                if phase:
                    after = fbuf[g, pl.ds(base + 1, 8), :]
                    value = pltpu.roll(jnp.where(lane >= phase, value, after), LANE - phase, 1)
                tbuf[pl.ds(8 * n * STRIDE + 4 * g + e, 8, stride=STRIDE), :] = value

    packed = {}

    def tile(k):
        if k not in packed:
            packed[k] = tbuf[k * STRIDE : k * STRIDE + 16, :].astype(bf16)
        return packed[k]

    lane16 = lax.broadcasted_iota(jnp.int32, (16, LANE), 1)
    here = pl.ds(pl.multiple_of(step * 16, 16), 16)
    for dx, dy, d0, count in blocks():
        tile0, phase = divmod(d0 * COEF, LANE)
        if dx in OUTER:
            ref = oa.at[OUTER.index(dx), (OUTER + INNER).index(dy)]
        elif dy in OUTER:
            ref = ob.at[INNER.index(dx), OUTER.index(dy)]
        else:
            ref = oc.at[INNER.index(dx), INNER.index(dy)]
        for t in range(up(count * COEF, LANE) // LANE):
            value = tile(tile0 + t)
            if phase:
                after = tile(min(tile0 + t + 1, KT - 1))
                value = pltpu.roll(jnp.where(lane16 >= phase, value, after), LANE - phase, 1)
            ref[here, t * LANE : (t + 1) * LANE] = value


def relayout(flat, me, step0, steps, grant):
    nrows = flat.shape[0] // LANE
    rows = flat.reshape(nrows, LANE)
    shapes = tuple((a, b, 16 * steps, c) for a, b, c in PIECES)
    return call(
        functools.partial(relayout_kernel, nrows, step0, steps),
        tuple(jax.ShapeDtypeStruct(s, bf16) for s in shapes),
        grant,
        1 << 20,
        steps << 21,
        grid_spec=pltpu.PrefetchScalarGridSpec(
            num_scalar_prefetch=1,
            grid=(steps,),
            in_specs=[HBM, pl.BlockSpec((16, LANE), lambda i, h: (nrows // 16, 0))],
            out_specs=(VMEM,) * len(shapes),
            scratch_shapes=[
                pltpu.VMEM((steps, 4, CHUNK, LANE), bf16),
                pltpu.VMEM((4, CHUNK + 16, LANE), f32),
                pltpu.VMEM((KT * STRIDE, LANE), f32),
                pltpu.SemaphoreType.DMA((steps, 4, 2)),
            ],
        ),
    )(me, rows, rows)


GROUP = 16


def square(flat, out):
    per = GROUP * COEF // LANE
    groups = flat.shape[0] // per
    lane = lax.broadcasted_iota(jnp.int32, (groups, LANE), 1)
    for r in range(GROUP):
        first, phase = divmod(r * COEF, LANE)
        got = []
        for t in range(3):
            row = min(first + t, per - 1)
            got.append(flat[pl.ds(row, groups, stride=per), :])
        for t in range(2):
            value = got[t]
            if phase:
                value = jnp.where(lane >= phase, got[t], got[t + 1])
                value = pltpu.roll(value, LANE - phase, 1)
            out[t, pl.ds(r, groups, stride=GROUP), :] = value


def operators_kernel(io, rows):
    m2m, l2l, uc2e, dc2e, lattice, column = io.ins
    w_both, coarse, d_hi, d_lo = io.outs
    scale = 1.0 / (4.0 * math.pi)
    coarse[32], coarse[33] = split(lattice[...])
    first = split(uc2e[...] * scale)

    plane = split(column[...])

    def stack(pieces, first):
        wide = []
        for piece in pieces:
            high, low = split(dot3(split(piece), plane)[:, 8 : 8 + FEATURES])
            wide += [piece, high.astype(f32), low.astype(f32)]
            wide.append(jnp.zeros((COEF, CPAD - COEF - 2 * FEATURES), f32))
        wide = jnp.concatenate([w for w in wide if w.shape[1]], axis=1).astype(bf16)
        w_both[first : first + COEF] = wide

    def matrix(o):
        at = slice(o * COEF, (o + 1) * COEF)
        return jnp.concatenate([rows[0, at], rows[1, at, 0 : COEF - LANE]], axis=1)

    io.wait(0)
    square(m2m, rows)
    pieces = []
    for o in range(8):
        high, low = split(matrix(o))
        coarse[o], coarse[8 + o] = high, low
        pieces.append(dot3((high, low), first))
    stack(pieces, 0)
    io.wait(1)
    square(l2l, rows)
    pieces = []
    for o in range(8):
        value = matrix(o)
        coarse[16 + o], coarse[24 + o] = split(value)
        pieces.append(jnp.transpose(value) * scale)
    stack(pieces, COEF)
    high, low = split(dc2e[...])
    i = lax.broadcasted_iota(jnp.int32, (COEF, ROWS), 0)
    r = lax.broadcasted_iota(jnp.int32, (COEF, ROWS), 1)
    for h in range(2):
        here = (i == (r >> 2) * 8 + 4 * h + (r & 3)) & (r < 4 * NG)
        here = jnp.where(here, 1.0, 0.0).astype(bf16)
        d_hi[h] = dot(high, here).astype(bf16)
        d_lo[h] = dot(low, here).astype(bf16)


def route_kernel(own, cap, n_top, io):
    pos, dens, slot, leaf = io.ins
    out, entries = io.outs
    points = pos.shape[1]
    owners = out.shape[0]
    slots = slot[...]
    owner = slots // own
    inside = slots - owner * own
    hit = owner == lax.broadcasted_iota(jnp.int32, (owners, points), 0)
    hit = jnp.where(hit, 1.0, 0.0)
    hit16 = hit.astype(bf16)
    row = lax.broadcasted_iota(jnp.int32, (LANE, LANE), 0)
    col = lax.broadcasted_iota(jnp.int32, (LANE, LANE), 1)
    before = jnp.where(row < col, 1.0, 0.0).astype(bf16)
    every = jnp.ones((LANE, LANE), bf16)
    total = jnp.zeros((owners, LANE), f32)
    ranks = []
    for t in range(points // LANE):
        part = hit16[:, t * LANE : (t + 1) * LANE]
        ranks.append(total + dot(part, before))
        total = total + dot(part, every)
    rank = jnp.sum(hit * jnp.concatenate(ranks, axis=1), axis=0, keepdims=True)
    entry = owner * cap + rank.astype(jnp.int32)
    entries[...] = entry
    inside_hi = inside // 64
    value = jnp.concatenate([pos[...], dens[...]], axis=0)
    width = value.shape[0]
    high, low = split(value)
    ones = jnp.ones((1, points), f32)
    high = jnp.concatenate(
        [high.astype(f32), inside_hi.astype(f32), (inside - 64 * inside_hi).astype(f32), ones]
        + [jnp.zeros((16 - width - 3, points), f32)],
        axis=0,
    )
    low = jnp.concatenate([low.astype(f32), jnp.zeros((16 - width, points), f32)], axis=0)
    payload = jnp.concatenate([high, low], axis=0).astype(bf16)
    block = max(cap, LANE)
    per = DENS // n_top
    leaves = leaf[...].astype(f32)
    if leaves.shape[1] < cap:
        blank = jnp.zeros((leaves.shape[0], cap - leaves.shape[1]), f32)
        leaves = jnp.concatenate([leaves, blank], axis=1)
    for o in range(owners * cap // block):
        there = entry == o * block + lax.broadcasted_iota(jnp.int32, (block, points), 0)
        there = jnp.where(there, 1.0, 0.0).astype(bf16)
        got = dot(payload, there, NT)
        value = got[0:width] + got[16 : 16 + width]
        where = got[width : width + 1] * 64.0 + got[width + 1 : width + 2]
        valid = got[width + 2 : width + 3]
        for q in range(n_top):
            rows = [value[0:3], where, valid, value[3 + per * q : 3 + per * (q + 1)]]
            rows.append(jnp.zeros((8 - 5 - per, block), f32))
            packed = jnp.concatenate([r for r in rows if r.shape[0]], axis=0)
            for i in range(block // cap):
                at = o * (block // cap) + i
                out[at, q, 0:8] = packed[:, i * cap : (i + 1) * cap]
                out[at, q, 8:] = leaves


def restore_kernel(n_top, io):
    got, entries = io.ins
    out = io.outs[0]
    devices = got.shape[0]
    per = out.shape[0] // n_top
    cap = got.shape[2] // per
    points = out.shape[1]
    block = max(cap, PB)
    total = jnp.zeros((2 * out.shape[0], points), f32)
    for o in range(devices // n_top * cap // block):
        count = block // cap
        value = []
        for q in range(n_top):
            for k in range(per):
                pieces = []
                for i in range(count):
                    row = (o * count + i) * n_top + q
                    pieces.append(got[row, :, k * cap : (k + 1) * cap])
                value.append(jnp.concatenate(pieces, axis=1))
        high, low = split(jnp.concatenate(value, axis=0))
        both = jnp.concatenate([high.astype(f32), low.astype(f32)], axis=0).astype(bf16)
        at = o * block + lax.broadcasted_iota(jnp.int32, (block, points), 0)
        total = total + dot(both, jnp.where(entries[...] == at, 1.0, 0.0).astype(bf16))
    out[...] = total[0 : out.shape[0]] + total[out.shape[0] :]


def octant_product(pos, octant, surf, oper):
    squared = None
    for d in range(3):
        spacing = surf[d] - pos[d : d + 1]
        squared = spacing * spacing if squared is None else squared + spacing * spacing
    value = lax.rsqrt(squared)
    round_pos = pos.astype(bf16).astype(f32)
    value = value - surf[3]
    for d in range(3):
        value = value - surf[4 + d] * round_pos[d : d + 1]
    features = [jnp.ones_like(round_pos[0:1]), round_pos]
    blank = jnp.zeros((CPAD - COEF - 2 * FEATURES, value.shape[1]), f32)
    value = [value] + features + features + [blank]
    value = jnp.concatenate([v for v in value if v.shape[0]], axis=0).astype(bf16)
    masks = [jnp.where(octant == o, 1.0, 0.0).astype(bf16) for o in range(8)]
    return dot(oper[...], jnp.concatenate([value * m for m in masks], axis=0))


TURNED = (((0,), (0,)), ((), ()))


def look_up(index, table):
    lanes, rows = table.shape[0] // 2, table.shape[1]
    width = index.shape[1]
    at_row = index // lanes
    at_lane = index - at_row * lanes
    there = at_row == lax.broadcasted_iota(jnp.int32, (rows, width), 0)
    got = dot(table, jnp.where(there, 1.0, 0.0).astype(bf16))
    mine = at_lane == lax.broadcasted_iota(jnp.int32, (lanes, width), 0)
    first = jnp.sum(jnp.where(mine, got[0:lanes], 0.0), axis=0, keepdims=True)
    return first, jnp.sum(jnp.where(mine, got[lanes:], 0.0), axis=0, keepdims=True)


def fill_surface(surf, column):
    for i, lane in enumerate((0, 1, 2, 8, 9, 10, 11)):
        surf[i] = jnp.broadcast_to(column[:, lane : lane + 1], surf.shape[1:])


def morton_place(box):
    place = jnp.zeros_like(box)
    for b in range(LEVEL):
        digit = box >> (3 * b)
        place = place + ((((digit >> 2) & 1) << (2 * LEVEL + b)))
        place = place + ((((digit >> 1) & 1) << (LEVEL + b)) + ((digit & 1) << b))
    return place


def points_kernel(n_top, box_cap, io, offsets, buf, surf):
    got, column, oper = io.ins
    out, field, place = io.outs
    sources, _, cap = got.shape
    lanes = min(cap, LANE)
    own = field.shape[1]
    wide = up(cap, LANE)
    me = io.scalars[0][0]
    buf[...] = jnp.zeros_like(buf)
    fill_surface(surf, column)
    io.wait(0)

    def put(i, offset):
        values = [got[i * STRIP + s, 0:8] for s in range(STRIP)]
        counts = [jnp.sum(v[4:5]).astype(jnp.int32) for v in values]
        for s, (value, count) in enumerate(zip(values, counts)):
            offsets[i * STRIP + s] = offset
            value = jnp.concatenate([value, jnp.zeros((8, wide + LANE - cap), f32)], axis=1)
            tile = offset // LANE
            value = pltpu.roll(value, offset - tile * LANE, 1)
            at = pl.ds(pl.multiple_of(tile * LANE, LANE), wide + LANE)
            buf[:, at] = buf[:, at] + value
            offset = offset + count
        return offset

    lax.fori_loop(0, sources // STRIP, put, jnp.int32(0))
    leaf = got[pl.ds(me * n_top, n_top), 8:, 0:lanes].reshape(own // lanes, lanes)
    leaf = leaf.astype(jnp.int32)
    first = got[me * n_top, 8:9, 0:1].astype(jnp.int32) >> 3
    offsets[sources] = jnp.sum(got[me * n_top, 8:9, 0:1]).astype(jnp.int32) >> 3
    io.wait(2)
    table = jnp.concatenate([(leaf >> 3) - first, leaf & 7], axis=1).astype(f32)
    table = jnp.transpose(table).astype(bf16)
    out_rows = out.shape[1]

    def block(j, total):
        to = pl.ds(pl.multiple_of(j * PB, PB), PB)
        value = buf[:, to]
        box, octant = look_up(value[3:4].astype(jnp.int32), table)
        place[:, to] = box.astype(jnp.int32)
        both = octant_product(value[0:3], octant, surf, oper)
        field[:, to] = both[COEF : 2 * COEF]
        high, low = split(both[0:COEF])
        rows = []
        at = lax.broadcasted_iota(jnp.int32, (box_cap, PB), 0).astype(f32)
        for k in range(out_rows // box_cap):
            rows.append(jnp.where(box == at, value[5 + k : 6 + k], 0.0))
        a_high, a_low = split(jnp.concatenate(rows, axis=0))
        both = dot(jnp.concatenate([high, low], axis=0), a_high, NT)
        return total + both[0:COEF] + both[COEF : 2 * COEF] + dot(high, a_low, NT)

    total = lax.fori_loop(0, own // PB, block, jnp.zeros((COEF, out_rows), f32), unroll=2)
    digits = jnp.concatenate([first >> 3, first & 7], axis=0).astype(f32)
    digits = jnp.broadcast_to(digits, (2, out_rows))
    blank = jnp.zeros((out.shape[0] - COEF - 2, out_rows), f32)
    out[...] = jnp.concatenate([total, digits, blank], axis=0).astype(bf16)
    io.send(0)


def box_ids(parts, dens):
    ids = []
    for part in parts:
        digits = part[COEF : COEF + 8, 0:1].astype(f32).astype(jnp.int32)
        first = digits[0:1] * 8 + digits[1:2]
        at = lax.broadcasted_iota(jnp.int32, (1, part.shape[1] // dens), 1)
        ids.append(first + at)
    return jnp.concatenate(ids, axis=1)


def all_parts(parts, k, dens):
    width = parts[0].shape[1] // dens
    return jnp.concatenate([p[0:COEF, k * width : (k + 1) * width] for p in parts], axis=1)


def translate_kernel(slabs, dens, io, xs, xin, acc):
    parts = io.ins[:-6]
    first, rest = io.ins[-6:-3], io.ins[-3:]
    out = io.outs[0]
    x0 = (io.scalars[0][0] // 2 * 2) * SIDE // len(parts)
    ids = box_ids(parts, dens)
    place = morton_place(ids)
    place = (((place >> 6) - x0 + REACH) & 7) * 64 + (place & 63)
    place = jnp.where(ids < BOXES4, place, -1)
    at = lax.broadcasted_iota(jnp.int32, (BOXES4, ids.shape[1]), 0)
    there = jnp.where(at == place, 1.0, 0.0).astype(bf16)
    columns = dens * PLANE
    for k in range(dens):
        low = dot(there, all_parts(parts, k, dens), NT)
        low = low.astype(bf16).astype(f32)
        for s in range(7 + slabs - 1):
            slab = low[s * PLANE : (s + 1) * PLANE].reshape(SIDE, SIDE, COEF)
            shifted = {}
            for dz in SHIFTS:
                if dz == 0:
                    moved = slab
                else:
                    cut = dz % SIDE
                    moved = jnp.concatenate([slab[:, cut:], slab[:, :cut]], axis=1)
                shifted[dz] = moved.reshape(PLANE, COEF)
            rows = pl.ds(s * columns + k * PLANE, PLANE)
            pad = [jnp.zeros((PLANE, WFULL - 7 * COEF), f32)]
            xs[rows, :] = jnp.concatenate([shifted[z] for z in SHIFTS] + pad, axis=1).astype(bf16)
            pad = [jnp.zeros((PLANE, WIN - 4 * COEF), f32)]
            xin[rows, :] = jnp.concatenate([shifted[z] for z in OUTER] + pad, axis=1).astype(bf16)

    def rows_of(i, j):
        value = jnp.concatenate([first[i][j], rest[i][j]], axis=1)
        return value.reshape(-1, value.shape[2])

    n_out = len(OUTER) * ROWS
    n_all = len(SHIFTS) * ROWS
    for i, dx in enumerate(OUTER + INNER):
        rows = pl.ds((dx + REACH) * columns, slabs * columns)
        source = xs[rows, :]
        if dx in OUTER:
            term = dot(rows_of(0, OUTER.index(dx)), source, NT)
            if i == 0:
                acc[...] = term
            else:
                acc[...] += term
        else:
            acc[0:n_out] += dot(rows_of(1, INNER.index(dx)), source, NT)
            acc[n_out:n_all] += dot(rows_of(2, INNER.index(dx)), xin[rows, :], NT)
    lane = lax.broadcasted_iota(jnp.int32, (ROWS, LANE), 1)
    for t in range(slabs * columns // LANE):
        total = jnp.zeros((ROWS, LANE), f32)
        for i, dy in enumerate(OUTER + INNER):
            value = acc[i * ROWS : (i + 1) * ROWS, t * LANE : (t + 1) * LANE]
            by = SIDE * (dy % SIDE)
            if by:
                near = pltpu.roll(value, LANE - by, 1)
                far = pltpu.roll(value, PLANE - by, 1)
                value = jnp.where((lane & (PLANE - 1)) < PLANE - by, near, far)
            total = total + value
        out[:, t * LANE : (t + 1) * LANE] = total.astype(out.dtype)


def coarse_kernel(io):
    out = io.outs[0]
    parts = io.ins[:-1]
    opers = io.ins[-1]
    dens = out.shape[0]
    box = ids = box_ids(parts, dens)
    place = ((box & 7) << 6) + (box & 56) + (box >> 6)
    place = jnp.where(box < BOXES4, place, -1)
    at = lax.broadcasted_iota(jnp.int32, (BOXES4, ids.shape[1]), 0)
    there = jnp.where(at == place, 1.0, 0.0).astype(bf16)
    level = [dot(there, all_parts(parts, k, dens), NT) for k in range(dens)]

    io.wait(*range(len(io.ins)))

    for _ in range(LEVEL):
        count = level[0].shape[0] // 8
        total = None
        for o in range(8):
            rows = jnp.concatenate([v[o * count : (o + 1) * count] for v in level], axis=0)
            term = dot3_rows(split(rows), (opers[o], opers[8 + o]), NT)
            total = term if total is None else total + term
        level = [total[k * count : (k + 1) * count] for k in range(dens)]
    rows = jnp.concatenate(level, axis=0)
    rows = dot3(split(rows), (opers[32], opers[33]), NT)
    level = [rows[k : k + 1] for k in range(dens)]
    for _ in range(LEVEL):
        count = level[0].shape[0]
        rows = split(jnp.concatenate(level, axis=0))
        children = [dot3_rows(rows, (opers[16 + o], opers[24 + o]), NT) for o in range(8)]
        level = [
            jnp.concatenate([c[k * count : (k + 1) * count] for c in children], axis=0)
            for k in range(dens)
        ]
    at = lax.broadcasted_iota(jnp.int32, (1, BOXES4), 1)
    number = jnp.zeros_like(at)
    for b in range(LEVEL):
        digit = ((at >> (2 * LEVEL + b)) & 1) * 4 + ((at >> (LEVEL + b)) & 1) * 2 + ((at >> b) & 1)
        number = number + (digit << (3 * (LEVEL - 1 - b)))
    row = lax.broadcasted_iota(jnp.int32, (BOXES4, BOXES4), 0)
    move = jnp.where(row == number, 1.0, 0.0).astype(bf16)
    for k in range(dens):
        high, low = split(level[k])
        out[k] = dot(high, move, TURNED) + dot(low, move, TURNED)


def evaluate_kernel(slabs, step, window, io, stack, found):
    n = SIDE // slabs
    checks = io.ins[: 2 * n]
    d_hi, d_lo, lattice, place, field = io.ins[2 * n :]
    offsets = io.scalars[1]
    out = io.outs[0]
    core = io.scalars[0][0] & 1
    group = io.scalars[0][0] // step
    dens = lattice.shape[0]
    sources, cap = out.shape[0], out.shape[2] // dens
    lane = lax.broadcasted_iota(jnp.int32, (COEF, LANE), 1)
    mine = jnp.concatenate([d_hi[core], d_lo[core]], axis=0)
    other = jnp.concatenate([d_hi[1 - core], d_lo[1 - core]], axis=0)
    for m in range(n):
        value = dot(mine, checks[2 * m][...]) + dot(other, checks[2 * m + 1][...])
        value = value[0:COEF] + value[COEF : 2 * COEF]
        if slabs == 2:
            a, b = value[:, 0:LANE], value[:, LANE : 2 * LANE]
            half = LANE // 2
            pieces = [
                jnp.where(lane < half, a, pltpu.roll(b, half, 1)),
                jnp.where(lane < half, pltpu.roll(a, half, 1), b),
            ]
        else:
            pieces = [value[:, k * PLANE : (k + 1) * PLANE] for k in range(dens)]
        width = slabs * PLANE
        for k in range(dens):
            at = m ^ group
            if width % LANE == 0:
                base = lattice[k, :, pl.ds(pl.multiple_of(at * width, width), width)]
            else:
                pair = lattice[k, :, pl.ds(pl.multiple_of(at // 2 * LANE, LANE), LANE)]
                base = jnp.where(at % 2 == 0, pair[:, :width], pair[:, width:])
            high, low = split(pieces[k] + base)
            rows = pl.ds(k * CPAD, COEF)
            stack[rows, m * width : (m + 1) * width] = high.astype(f32)
            rows = pl.ds((dens + k) * CPAD, COEF)
            stack[rows, m * width : (m + 1) * width] = low.astype(f32)
    box = offsets[sources] + lax.broadcasted_iota(jnp.int32, (1, window), 1)
    want = morton_place(box) ^ (group * (slabs * PLANE))
    want = jnp.where(box < BOXES4, want, -1)
    pick = want == lax.broadcasted_iota(jnp.int32, (BOXES4, window), 0)
    pick = jnp.where(pick, 1.0, 0.0).astype(bf16)
    half = dens * CPAD
    local = jnp.concatenate(
        [dot(stack[h * half : (h + 1) * half].astype(bf16), pick) for h in range(2)], axis=1
    ).astype(bf16)
    found[:, place.shape[1] :] = jnp.zeros((8, found.shape[1] - place.shape[1]), f32)
    io.wait(*range(len(io.ins)))

    def block(j, carry):
        at = pl.ds(pl.multiple_of(j * PB, PB), PB)
        there = place[:, at] == lax.broadcasted_iota(jnp.int32, (window, PB), 0)
        there = jnp.where(there, 1.0, 0.0)
        there = jnp.concatenate([there, there], axis=0).astype(bf16)
        got = dot(local, there)
        mine = field[:, at]
        rows = []
        for k in range(dens):
            value = got[k * CPAD : k * CPAD + COEF]
            rows.append(jnp.sum(value * mine, axis=0, keepdims=True))
        rows.append(jnp.zeros((8 - dens, PB), f32))
        found[:, at] = jnp.concatenate(rows, axis=0)
        return carry

    lax.fori_loop(0, place.shape[1] // PB, block, 0, unroll=2)

    wide = up(cap, LANE) + LANE

    @pl.loop(0, sources // STRIP)
    def _(i):
        for s in range(STRIP):
            offset = offsets[i * STRIP + s]
            tile = offset // LANE
            value = found[:, pl.ds(pl.multiple_of(tile * LANE, LANE), wide)]
            value = pltpu.roll(value, wide - (offset - tile * LANE), 1)
            for k in range(dens):
                out[i * STRIP + s, :, k * cap : (k + 1) * cap] = value[k : k + 1, 0:cap]


def shift_by(axis, value, distance):
    size = lax.axis_size(axis)
    return lax.ppermute(value, axis, [(i, i ^ distance) for i in range(size)])


def gather_by(value, distances, beside):
    got = {m: shift_by("pts", value, m) if m else value for m in distances if m % 2 == 0}
    got, beside = lax.optimization_barrier((got, beside))
    got.update({m + 1: shift_by("pts", got[m], 1) for m in list(got) if m + 1 in distances})
    return [got[m] for m in distances], beside


def per_device(
    local_pos, densities, morton_slot, slot_leaf, uc2e, m2m, m2l_ops, dc2e, lattice, l2l
):
    n_pts = lax.axis_size("pts")
    n_top = lax.axis_size("top")
    me = jnp.stack([lax.axis_index("pts"), lax.axis_index("top")]).astype(jnp.int32)
    points = local_pos.shape[1]
    own = points * n_top
    cap = 2 * points // n_pts
    box_cap = 2 * BOXES4 // n_pts
    dens = DENS // n_top
    slabs = max(1, 2 * SIDE // n_pts)
    coef = uc2e.shape[0]
    sources = n_pts * n_top
    lanes = min(cap, LANE)
    rows = 8 + points // lanes

    def shape(*dims, dtype=bf16):
        return jax.ShapeDtypeStruct(dims, dtype)

    outgoing, entries = run(
        functools.partial(route_kernel, own, cap, n_top),
        [],
        [
            local_pos,
            densities,
            morton_slot.reshape(1, points),
            slot_leaf.reshape(points // lanes, lanes),
        ],
        [shape(n_pts, n_top, rows, cap, dtype=f32), shape(1, points, dtype=jnp.int32)],
        1 << 27,
        stays=(1,),
        grant=GRANT_FIRST,
    )
    outgoing = outgoing.reshape(sources, rows, cap)
    incoming = lax.all_to_all(outgoing, ("pts", "top"), split_axis=0, concat_axis=0, tiled=True)

    flat = (-1, LANE)
    column = jnp.asarray(column_table())
    w_both, opers, *halves = run(
        operators_kernel,
        [],
        [m2m.reshape(flat), l2l.reshape(flat), uc2e, dc2e, lattice, column],
        [shape(2 * coef, 8 * CPAD), shape(34, coef, coef)] + [shape(2, coef, ROWS)] * 2,
        1 << 30,
        late=(0, 1),
        stays=range(4),
        scratch=[pltpu.VMEM((2, 8 * coef, LANE), f32)],
    )
    first = relayout(m2l_ops, me, 0, EARLY, GRANT_EARLY)
    incoming, first = lax.optimization_barrier((incoming, first))

    partial, field, place, offsets = run(
        functools.partial(points_kernel, n_top, box_cap),
        [me],
        [incoming, column, w_both],
        [
            shape(up(coef + 2, 16), dens * box_cap),
            shape(coef, own, dtype=f32),
            shape(1, own, dtype=jnp.int32),
        ],
        8 << 30,
        late=(0,),
        here=(2,),
        stays=(1, 2),
        numbers=[shape(sources + 1, dtype=jnp.int32)],
        scratch=[
            pltpu.VMEM((8, up(own + up(cap, LANE) + LANE, PB)), f32),
            pltpu.VMEM((3 + FEATURES, coef, PB), f32),
        ],
    )
    later, flat_ops = lax.optimization_barrier((partial, m2l_ops))
    rest = relayout(flat_ops, me, EARLY, STEPS - EARLY, GRANT_LATER)
    parts, rest = gather_by(later, range(n_pts), rest)

    columns = dens * PLANE
    (checks,) = run(
        functools.partial(translate_kernel, slabs, dens),
        [me],
        [*parts, *first, *rest],
        [shape(ROWS, slabs * columns)],
        8 << 30,
        here=range(n_pts, n_pts + 6),
        scratch=[
            pltpu.VMEM(((7 + slabs - 1) * columns, WFULL), bf16),
            pltpu.VMEM(((7 + slabs - 1) * columns, WIN), bf16),
            pltpu.VMEM((7 * ROWS, slabs * columns), f32),
        ],
    )
    (lattice4,) = run(
        coarse_kernel,
        [],
        [*parts, opers],
        [shape(dens, coef, BOXES4, dtype=f32)],
        4 << 30,
        here=(n_pts,),
        stays=(0,),
    )
    step = n_pts // SIDE * slabs
    distances = [step * m + c for m in range(SIDE // slabs) for c in range(2)]
    gathered, lattice4 = gather_by(checks, distances, lattice4)

    (reply,) = run(
        functools.partial(evaluate_kernel, slabs, step, box_cap),
        [me, offsets],
        [*gathered, *halves, lattice4, place, field],
        [shape(sources, 1, dens * cap, dtype=f32)],
        4 << 30,
        here=range(len(gathered), len(gathered) + 5),
        scratch=[
            pltpu.VMEM((2 * dens * CPAD, BOXES4), f32),
            pltpu.VMEM((8, own + up(cap, LANE) + LANE), f32),
        ],
    )
    returned = lax.all_to_all(reply, ("pts", "top"), split_axis=0, concat_axis=0, tiled=True)
    (out,) = run(
        functools.partial(restore_kernel, n_top),
        [],
        [returned, entries],
        [shape(DENS, points, dtype=f32)],
        1 << 28,
        here=(1,),
    )
    return out


def solution(mesh):
    split_all = P(None, ("pts", "top"))
    placed = (split_all, split_all, P(("pts", "top")), P(("pts", "top"))) + (P(),) * 6
    return jax.shard_map(
        per_device, mesh=mesh, in_specs=placed, out_specs=split_all, check_vma=False
    )
```

```python
import functools
import math

import jax
import jax.numpy as jnp
import numpy as np
from jax import lax
from jax.experimental import pallas as pl
from jax.experimental.pallas import tpu as pltpu
from jax.sharding import PartitionSpec as P

LEVEL = 3
EDGE = 6
DENS = 8
SIDE = 2**LEVEL
BOXES4 = SIDE**3
PLANE = SIDE * SIDE
LANE = 128
REACH = 3
SHIFTS = list(range(-REACH, REACH + 1))
OUTER = [s for s in SHIFTS if abs(s) >= 2]
INNER = [s for s in SHIFTS if abs(s) < 2]
bf16 = jnp.bfloat16
f32 = jnp.float32
NN = (((1,), (0,)), ((), ()))
NT = (((1,), (1,)), ((), ()))


def up(value, multiple):
    return -(-value // multiple) * multiple


def surface_table():
    grid_vals = np.linspace(-1.0, 1.0, EDGE)
    points_list = []
    for a in range(EDGE):
        for b in range(EDGE):
            for c in range(EDGE):
                if min(a, b, c) == 0 or max(a, b, c) == EDGE - 1:
                    points_list.append([grid_vals[a], grid_vals[b], grid_vals[c]])
    return np.array(points_list, dtype=np.float32).T


COEF = surface_table().shape[1]
OFFSETS = (2 * REACH + 1) ** 3 - 27
FEATURES = 4
PB = 256
STRIP = 16
UNROLL_FIND, UNROLL_APPLY, UNROLL_GATHER = 16, 8, 8
GRANT = 28
GRANT_FIRST = 60
GRANT_EARLY = 52
GRANT_LATER = 49
CPAD = up(COEF, 32)


def column_table():
    surface = 1.25 * surface_table().astype(np.float64)
    grid = np.linspace(-0.9, 0.9, 10)
    points = np.stack(np.meshgrid(grid, grid, grid, indexing="ij")).reshape(3, -1)
    values = 1.0 / np.sqrt(((surface[:, :, None] - points[:, None, :]) ** 2).sum(axis=0))
    scale = (points**2).sum(axis=1)
    out = np.zeros((surface.shape[1], LANE), np.float32)
    out[:, 0:3] = (np.float32(1.25) * surface_table()).T
    out[:, 8] = values.mean(axis=1)
    out[:, 9:12] = values @ points.T / scale
    return out


def blocks():
    out, position = [], 0
    for dx in SHIFTS:
        for dy in SHIFTS:
            count = sum(max(abs(dx), abs(dy), abs(dz)) >= 2 for dz in SHIFTS)
            out.append((dx, dy, position, count))
            position += count
    return out


def dot(a, b, dims=NN):
    return lax.dot_general(a, b, dims, preferred_element_type=f32)


def split(value):
    high = value.astype(bf16)
    return high, (value - high.astype(f32)).astype(bf16)


def dot3(a, b, dims=NN):
    return dot(a[0], b[0], dims) + dot(a[1], b[0], dims) + dot(a[0], b[1], dims)


def dot3_rows(a, b, dims=NN):
    rows = a[0].shape[0]
    both = jnp.concatenate([x.astype(f32) for x in a], axis=0).astype(bf16)
    both = dot(both, b[0], dims)
    return both[0:rows] + both[rows : 2 * rows] + dot(a[0], b[1], dims)


def call(kernel, out_shape, mib, flops, bytes_accessed=1 << 20, **kw):
    return pl.pallas_call(
        kernel,
        out_shape=out_shape,
        compiler_params=pltpu.CompilerParams(vmem_limit_bytes=mib << 20),
        cost_estimate=pl.CostEstimate(
            flops=flops, bytes_accessed=bytes_accessed, transcendentals=0
        ),
        **kw,
    )


SMEM = pl.BlockSpec(memory_space=pltpu.SMEM)
VMEM = pl.BlockSpec(memory_space=pltpu.VMEM)
HBM = pl.BlockSpec(memory_space=pltpu.HBM)

class Buffers:
    def __init__(self, scalars, ins, outs, moved, sources, targets, sem_in, sem_out):
        self.scalars, self.ins, self.outs, self.targets = scalars, ins, outs, targets
        self.sem_out = sem_out
        self.coming, self.going, self.waited = {}, {}, set()
        for i in moved:
            self.coming[i] = pltpu.make_async_copy(sources[i], ins[i], sem_in.at[i])
            self.coming[i].start()

    def wait(self, *which):
        for i in which:
            if i in self.coming and i not in self.waited:
                self.waited.add(i)
                self.coming[i].wait()

    def send(self, *which):
        for i in which:
            if i not in self.going:
                copy = pltpu.make_async_copy(self.outs[i], self.targets[i], self.sem_out.at[i])
                copy.start()
                self.going[i] = copy


def run(kernel, scalars, ins, outs, flops, scratch=(), late=(), here=(), stays=(), numbers=(), grant=GRANT):
    n_s, n_i, n_o, n_n = len(scalars), len(ins), len(outs), len(numbers)
    moved_in = [i for i in range(n_i) if i not in here]
    moved_out = [i for i in range(n_o) if i not in stays]

    def body(*refs):
        refs = list(refs)
        take = lambda count: [refs.pop(0) for _ in range(count)]
        given, sources, targets, counts = take(n_s), take(n_i), take(n_o), take(n_n)
        in_refs, out_refs = list(sources), list(targets)
        for i in moved_in:
            in_refs[i] = refs.pop(0)
        for i in moved_out:
            out_refs[i] = refs.pop(0)
        io = Buffers(given, in_refs, out_refs, moved_in, sources, targets, *take(2))
        io.wait(*[i for i in moved_in if i not in late])
        kernel(io, *counts, *refs)
        io.wait(*moved_in)
        io.send(*moved_out)
        for i in moved_out:
            io.going[i].wait()

    return call(
        body,
        tuple(outs) + tuple(numbers),
        grant,
        flops,
        in_specs=[SMEM] * n_s + [VMEM if i in here else HBM for i in range(n_i)],
        out_specs=tuple(VMEM if i in stays else HBM for i in range(n_o)) + (SMEM,) * n_n,
        scratch_shapes=[pltpu.VMEM(ins[i].shape, ins[i].dtype) for i in moved_in]
        + [pltpu.VMEM(outs[i].shape, outs[i].dtype) for i in moved_out]
        + [pltpu.SemaphoreType.DMA((max(n, 1),)) for n in (n_i, n_o)]
        + list(scratch),
    )(*scalars, *ins)


HG = 4 * OFFSETS * COEF // LANE
KT = up(up(OFFSETS * COEF, LANE) // LANE, 8)
WFULL = up(7 * COEF, LANE)
WIN = up(4 * COEF, LANE)
NG = COEF // 8
STEPS = -(-NG // 4)
ROWS = 16 * STEPS
CHUNK = up(HG + 15, 16)
TAIL = 32
EARLY = 3
STRIDE = 17
PIECES = ((4, 7, WFULL), (3, 4, WFULL), (3, 3, WIN))


def relayout_kernel(nrows, step0, steps, me_ref, f_hbm, tail_ref, oa, ob, oc, inb, fbuf, tbuf, sem):
    step = pl.program_id(0)
    half = me_ref[0] & 1
    end16 = nrows // 16 * 16

    def start_row(st, g):
        return jnp.minimum(4 * (st + step0) + g, NG - 1) * (2 * HG) + half * HG

    def start(st, slot):
        for g in range(4):
            row = pl.multiple_of(start_row(st, g) // 16 * 16, 16)
            pltpu.make_async_copy(
                f_hbm.at[pl.ds(row, CHUNK - TAIL)],
                inb.at[slot, g, pl.ds(0, CHUNK - TAIL)],
                sem.at[slot, g, 0],
            ).start()
            last = row + CHUNK > end16

            @pl.when(jnp.logical_not(last))
            def _():
                pltpu.make_async_copy(
                    f_hbm.at[pl.ds(pl.multiple_of(row + CHUNK - TAIL, 16), TAIL)],
                    inb.at[slot, g, pl.ds(CHUNK - TAIL, TAIL)],
                    sem.at[slot, g, 1],
                ).start()


    def wait(st, slot):
        for g in range(4):
            row = pl.multiple_of(start_row(st, g) // 16 * 16, 16)
            pltpu.make_async_copy(
                f_hbm.at[pl.ds(row, CHUNK - TAIL)],
                inb.at[slot, g, pl.ds(0, CHUNK - TAIL)],
                sem.at[slot, g, 0],
            ).wait()
            last = row + CHUNK > end16

            @pl.when(jnp.logical_not(last))
            def _():
                pltpu.make_async_copy(
                    f_hbm.at[pl.ds(pl.multiple_of(row + CHUNK - TAIL, 16), TAIL)],
                    inb.at[slot, g, pl.ds(CHUNK - TAIL, TAIL)],
                    sem.at[slot, g, 1],
                ).wait()

            @pl.when(last)
            def _():
                row16 = lax.broadcasted_iota(jnp.int32, (16, LANE), 0)
                tail = jnp.where(row16 < nrows - end16, tail_ref[...].astype(f32), 0.0)
                inb[slot, g, CHUNK - TAIL : CHUNK - TAIL + 16] = tail.astype(bf16)

    slot = step

    @pl.when(step == 0)
    def _():
        fbuf[...] = jnp.zeros_like(fbuf)
        inb[:, :, CHUNK - 16 :] = jnp.zeros_like(inb[:, :, CHUNK - 16 :])
        for st in range(steps):
            start(st, st)

    wait(step, slot)
    lane = lax.broadcasted_iota(jnp.int32, (8, LANE), 1)
    for g in range(4):
        fbuf[g, 0:CHUNK] = inb[slot, g].astype(f32)
    for g in range(4):
        row = start_row(step, g)
        off = row - row // 16 * 16
        for e in range(4):
            first = OFFSETS * COEF * e
            phase = first % LANE

            @pl.loop(0, KT // 8, unroll=KT // 8)
            def _(n):
                base = off + first // LANE + 8 * n
                value = fbuf[g, pl.ds(base, 8), :]
                if phase:
                    after = fbuf[g, pl.ds(base + 1, 8), :]
                    value = pltpu.roll(jnp.where(lane >= phase, value, after), LANE - phase, 1)
                tbuf[pl.ds(8 * n * STRIDE + 4 * g + e, 8, stride=STRIDE), :] = value

    packed = {}

    def tile(k):
        if k not in packed:
            packed[k] = tbuf[k * STRIDE : k * STRIDE + 16, :].astype(bf16)
        return packed[k]

    lane16 = lax.broadcasted_iota(jnp.int32, (16, LANE), 1)
    here = pl.ds(pl.multiple_of(step * 16, 16), 16)
    for dx, dy, d0, count in blocks():
        tile0, phase = divmod(d0 * COEF, LANE)
        if dx in OUTER:
            ref = oa.at[OUTER.index(dx), (OUTER + INNER).index(dy)]
        elif dy in OUTER:
            ref = ob.at[INNER.index(dx), OUTER.index(dy)]
        else:
            ref = oc.at[INNER.index(dx), INNER.index(dy)]
        for t in range(up(count * COEF, LANE) // LANE):
            value = tile(tile0 + t)
            if phase:
                after = tile(min(tile0 + t + 1, KT - 1))
                value = pltpu.roll(jnp.where(lane16 >= phase, value, after), LANE - phase, 1)
            ref[here, t * LANE : (t + 1) * LANE] = value


def relayout(flat, me, step0, steps, grant):
    nrows = flat.shape[0] // LANE
    rows = flat.reshape(nrows, LANE)
    shapes = tuple((a, b, 16 * steps, c) for a, b, c in PIECES)
    return call(
        functools.partial(relayout_kernel, nrows, step0, steps),
        tuple(jax.ShapeDtypeStruct(s, bf16) for s in shapes),
        grant,
        1 << 20,
        steps << 21,
        grid_spec=pltpu.PrefetchScalarGridSpec(
            num_scalar_prefetch=1,
            grid=(steps,),
            in_specs=[HBM, pl.BlockSpec((16, LANE), lambda i, h: (nrows // 16, 0))],
            out_specs=(VMEM,) * len(shapes),
            scratch_shapes=[
                pltpu.VMEM((steps, 4, CHUNK, LANE), bf16),
                pltpu.VMEM((4, CHUNK + 16, LANE), f32),
                pltpu.VMEM((KT * STRIDE, LANE), f32),
                pltpu.SemaphoreType.DMA((steps, 4, 2)),
            ],
        ),
    )(me, rows, rows)


GROUP = 16


def square(flat, out):
    per = GROUP * COEF // LANE
    groups = flat.shape[0] // per
    lane = lax.broadcasted_iota(jnp.int32, (groups, LANE), 1)
    for r in range(GROUP):
        first, phase = divmod(r * COEF, LANE)
        got = []
        for t in range(3):
            row = min(first + t, per - 1)
            got.append(flat[pl.ds(row, groups, stride=per), :])
        for t in range(2):
            value = got[t]
            if phase:
                value = jnp.where(lane >= phase, got[t], got[t + 1])
                value = pltpu.roll(value, LANE - phase, 1)
            out[t, pl.ds(r, groups, stride=GROUP), :] = value


def operators_kernel(io, rows):
    m2m, l2l, uc2e, dc2e, lattice, column = io.ins
    w_both, coarse, d_hi, d_lo = io.outs
    scale = 1.0 / (4.0 * math.pi)
    coarse[32], coarse[33] = split(lattice[...])
    first = split(uc2e[...] * scale)

    plane = split(column[...])

    def side_by_side(pieces):
        wide = []
        for piece in pieces:
            high, low = split(dot3(split(piece), plane)[:, 8 : 8 + FEATURES])
            wide += [piece, high.astype(f32), low.astype(f32)]
            wide.append(jnp.zeros((COEF, CPAD - COEF - 2 * FEATURES), f32))
        return jnp.concatenate([w for w in wide if w.shape[1]], axis=1)

    def matrix(o):
        at = slice(o * COEF, (o + 1) * COEF)
        return jnp.concatenate([rows[0, at], rows[1, at, 0 : COEF - LANE]], axis=1)

    io.wait(0)
    square(m2m, rows)
    pieces = []
    for o in range(8):
        high, low = split(matrix(o))
        coarse[o], coarse[8 + o] = high, low
        pieces.append(dot3((high, low), first))
    upward = side_by_side(pieces)
    io.wait(1)
    square(l2l, rows)
    pieces = []
    for o in range(8):
        value = matrix(o)
        coarse[16 + o], coarse[24 + o] = split(value)
        pieces.append(jnp.transpose(value) * scale)
    w_both[...] = jnp.concatenate([upward, side_by_side(pieces)], axis=0).astype(bf16)
    high, low = split(dc2e[...])
    i = lax.broadcasted_iota(jnp.int32, (COEF, ROWS), 0)
    r = lax.broadcasted_iota(jnp.int32, (COEF, ROWS), 1)
    for h in range(2):
        here = (i == (r >> 2) * 8 + 4 * h + (r & 3)) & (r < 4 * NG)
        here = jnp.where(here, 1.0, 0.0).astype(bf16)
        d_hi[h] = dot(high, here).astype(bf16)
        d_lo[h] = dot(low, here).astype(bf16)


def route_kernel(own, cap, n_top, io):
    pos, dens, slot, leaf = io.ins
    out, entries = io.outs
    points = pos.shape[1]
    owners = out.shape[0]
    slots = slot[...]
    owner = slots // own
    inside = slots - owner * own
    hit = owner == lax.broadcasted_iota(jnp.int32, (owners, points), 0)
    hit = jnp.where(hit, 1.0, 0.0)
    hit16 = hit.astype(bf16)
    row = lax.broadcasted_iota(jnp.int32, (LANE, LANE), 0)
    col = lax.broadcasted_iota(jnp.int32, (LANE, LANE), 1)
    before = jnp.where(row < col, 1.0, 0.0).astype(bf16)
    every = jnp.ones((LANE, LANE), bf16)
    total = jnp.zeros((owners, LANE), f32)
    ranks = []
    for t in range(points // LANE):
        part = hit16[:, t * LANE : (t + 1) * LANE]
        ranks.append(total + dot(part, before))
        total = total + dot(part, every)
    rank = jnp.sum(hit * jnp.concatenate(ranks, axis=1), axis=0, keepdims=True)
    entry = owner * cap + rank.astype(jnp.int32)
    entries[...] = entry
    inside_hi = inside // 64
    value = jnp.concatenate([pos[...], dens[...]], axis=0)
    width = value.shape[0]
    high, low = split(value)
    ones = jnp.ones((1, points), f32)
    high = jnp.concatenate(
        [high.astype(f32), inside_hi.astype(f32), (inside - 64 * inside_hi).astype(f32), ones]
        + [jnp.zeros((16 - width - 3, points), f32)],
        axis=0,
    )
    low = jnp.concatenate([low.astype(f32), jnp.zeros((16 - width, points), f32)], axis=0)
    payload = jnp.concatenate([high, low], axis=0).astype(bf16)
    block = max(cap, LANE)
    per = DENS // n_top
    leaves = leaf[...].astype(f32)
    if leaves.shape[1] < cap:
        blank = jnp.zeros((leaves.shape[0], cap - leaves.shape[1]), f32)
        leaves = jnp.concatenate([leaves, blank], axis=1)
    for o in range(owners * cap // block):
        there = entry == o * block + lax.broadcasted_iota(jnp.int32, (block, points), 0)
        there = jnp.where(there, 1.0, 0.0).astype(bf16)
        got = dot(payload, there, NT)
        value = got[0:width] + got[16 : 16 + width]
        where = got[width : width + 1] * 64.0 + got[width + 1 : width + 2]
        valid = got[width + 2 : width + 3]
        for q in range(n_top):
            rows = [value[0:3], where, valid, value[3 + per * q : 3 + per * (q + 1)]]
            rows.append(jnp.zeros((8 - 5 - per, block), f32))
            packed = jnp.concatenate([r for r in rows if r.shape[0]], axis=0)
            for i in range(block // cap):
                at = o * (block // cap) + i
                out[at, q, 0:8] = packed[:, i * cap : (i + 1) * cap]
                out[at, q, 8:] = leaves


def restore_kernel(n_top, io):
    got, entries = io.ins
    out = io.outs[0]
    devices = got.shape[0]
    per = out.shape[0] // n_top
    cap = got.shape[2] // per
    points = out.shape[1]
    block = max(cap, PB)
    total = jnp.zeros((2 * out.shape[0], points), f32)
    for o in range(devices // n_top * cap // block):
        count = block // cap
        value = []
        for q in range(n_top):
            for k in range(per):
                pieces = []
                for i in range(count):
                    row = (o * count + i) * n_top + q
                    pieces.append(got[row, :, k * cap : (k + 1) * cap])
                value.append(jnp.concatenate(pieces, axis=1))
        high, low = split(jnp.concatenate(value, axis=0))
        both = jnp.concatenate([high.astype(f32), low.astype(f32)], axis=0).astype(bf16)
        at = o * block + lax.broadcasted_iota(jnp.int32, (block, points), 0)
        total = total + dot(both, jnp.where(entries[...] == at, 1.0, 0.0).astype(bf16))
    out[...] = total[0 : out.shape[0]] + total[out.shape[0] :]


def octant_product(pos, octant, surf, oper):
    squared = None
    for d in range(3):
        spacing = surf[d] - pos[d : d + 1]
        squared = spacing * spacing if squared is None else squared + spacing * spacing
    value = lax.rsqrt(squared)
    round_pos = pos.astype(bf16).astype(f32)
    value = value - surf[3]
    for d in range(3):
        value = value - surf[4 + d] * round_pos[d : d + 1]
    features = [jnp.ones_like(round_pos[0:1]), round_pos]
    blank = jnp.zeros((CPAD - COEF - 2 * FEATURES, value.shape[1]), f32)
    value = [value] + features + features + [blank]
    value = jnp.concatenate([v for v in value if v.shape[0]], axis=0).astype(bf16)
    masks = [jnp.where(octant == o, 1.0, 0.0).astype(bf16) for o in range(8)]
    return dot(oper[...], jnp.concatenate([value * m for m in masks], axis=0))


TURNED = (((0,), (0,)), ((), ()))


def look_up(index, table):
    lanes, rows = table.shape[0] // 2, table.shape[1]
    width = index.shape[1]
    at_row = index // lanes
    at_lane = index - at_row * lanes
    there = at_row == lax.broadcasted_iota(jnp.int32, (rows, width), 0)
    got = dot(table, jnp.where(there, 1.0, 0.0).astype(bf16))
    mine = at_lane == lax.broadcasted_iota(jnp.int32, (lanes, width), 0)
    first = jnp.sum(jnp.where(mine, got[0:lanes], 0.0), axis=0, keepdims=True)
    return first, jnp.sum(jnp.where(mine, got[lanes:], 0.0), axis=0, keepdims=True)


def fill_surface(surf, column):
    for i, lane in enumerate((0, 1, 2, 8, 9, 10, 11)):
        surf[i] = jnp.broadcast_to(column[:, lane : lane + 1], surf.shape[1:])


def morton_place(box):
    place = jnp.zeros_like(box)
    for b in range(LEVEL):
        digit = box >> (3 * b)
        place = place + ((((digit >> 2) & 1) << (2 * LEVEL + b)))
        place = place + ((((digit >> 1) & 1) << (LEVEL + b)) + ((digit & 1) << b))
    return place


def points_kernel(n_top, box_cap, io, offsets, buf, surf, octants, outgoing):
    got, column, oper = io.ins
    out, field, place = io.outs
    sources, _, cap = got.shape
    lanes = min(cap, LANE)
    own = field.shape[1]
    wide = up(cap, LANE)
    me = io.scalars[0][0]
    buf[...] = jnp.zeros_like(buf)
    fill_surface(surf, column)
    io.wait(0)

    def put(i, offset):
        values = [got[i * STRIP + s, 0:8] for s in range(STRIP)]
        counts = [jnp.sum(v[4:5]).astype(jnp.int32) for v in values]
        for s, (value, count) in enumerate(zip(values, counts)):
            offsets[i * STRIP + s] = offset
            value = jnp.concatenate([value, jnp.zeros((8, wide + LANE - cap), f32)], axis=1)
            tile = offset // LANE
            value = pltpu.roll(value, offset - tile * LANE, 1)
            at = pl.ds(pl.multiple_of(tile * LANE, LANE), wide + LANE)
            buf[:, at] = buf[:, at] + value
            offset = offset + count
        return offset

    lax.fori_loop(0, sources // STRIP, put, jnp.int32(0))
    leaf = got[pl.ds(me * n_top, n_top), 8:, 0:lanes].reshape(own // lanes, lanes)
    leaf = leaf.astype(jnp.int32)
    first = got[me * n_top, 8:9, 0:1].astype(jnp.int32) >> 3
    offsets[sources] = jnp.sum(got[me * n_top, 8:9, 0:1]).astype(jnp.int32) >> 3
    io.wait(2)
    table = jnp.concatenate([(leaf >> 3) - first, leaf & 7], axis=1).astype(f32)
    table = jnp.transpose(table).astype(bf16)
    out_rows = out.shape[1]

    blocks_of = own // PB

    def spot(j):
        return pl.ds(pl.multiple_of(j * PB, PB), PB)

    def find(j, carry):
        to = spot(j)
        box, octant = look_up(buf[3:4, to].astype(jnp.int32), table)
        place[:, to] = box.astype(jnp.int32)
        octants[:, to] = octant
        return carry

    lax.fori_loop(0, blocks_of, find, 0, unroll=UNROLL_FIND)

    def apply(j, carry):
        to = spot(j)
        both = octant_product(buf[0:3, to], octants[:, to], surf, oper)
        outgoing[:, to] = both[0:COEF]
        field[:, to] = both[COEF : 2 * COEF]
        return carry

    lax.fori_loop(0, blocks_of, apply, 0, unroll=UNROLL_APPLY)

    def gather(j, total):
        to = spot(j)
        high, low = split(outgoing[:, to])
        rows = []
        at = lax.broadcasted_iota(jnp.int32, (box_cap, PB), 0)
        here = place[:, to] == at
        for k in range(out_rows // box_cap):
            rows.append(jnp.where(here, buf[5 + k : 6 + k, to], 0.0))
        a_high, a_low = split(jnp.concatenate(rows, axis=0))
        both = dot(jnp.concatenate([high, low], axis=0), a_high, NT)
        return total + both[0:COEF] + both[COEF : 2 * COEF] + dot(high, a_low, NT)

    total = jnp.zeros((COEF, out_rows), f32)
    total = lax.fori_loop(0, blocks_of, gather, total, unroll=UNROLL_GATHER)
    digits = jnp.concatenate([first >> 3, first & 7], axis=0).astype(f32)
    digits = jnp.broadcast_to(digits, (2, out_rows))
    blank = jnp.zeros((out.shape[0] - COEF - 2, out_rows), f32)
    out[...] = jnp.concatenate([total, digits, blank], axis=0).astype(bf16)
    io.send(0)


def box_ids(parts, dens):
    ids = []
    for part in parts:
        digits = part[COEF - 8 : COEF + 8, :].astype(f32)[8:16, 0:1].astype(jnp.int32)
        first = digits[0:1] * 8 + digits[1:2]
        at = lax.broadcasted_iota(jnp.int32, (1, part.shape[1] // dens), 1)
        ids.append(first + at)
    return jnp.concatenate(ids, axis=1)


def all_parts(parts, k, dens):
    width = parts[0].shape[1] // dens
    return jnp.concatenate([p[0:COEF, k * width : (k + 1) * width] for p in parts], axis=1)


def translate_kernel(slabs, dens, io, xs, xin, acc):
    parts = io.ins[:-6]
    first, rest = io.ins[-6:-3], io.ins[-3:]
    out = io.outs[0]
    x0 = (io.scalars[0][0] // 2 * 2) * SIDE // len(parts)
    ids = box_ids(parts, dens)
    place = morton_place(ids)
    place = (((place >> 6) - x0 + REACH) & 7) * 64 + (place & 63)
    place = jnp.where(ids < BOXES4, place, -1)
    at = lax.broadcasted_iota(jnp.int32, (BOXES4, ids.shape[1]), 0)
    there = jnp.where(at == place, 1.0, 0.0).astype(bf16)
    columns = dens * PLANE
    for k in range(dens):
        low = dot(there, all_parts(parts, k, dens), NT)
        low = low.astype(bf16).astype(f32)
        for s in range(7 + slabs - 1):
            slab = low[s * PLANE : (s + 1) * PLANE].reshape(SIDE, SIDE, COEF)
            shifted = {}
            for dz in SHIFTS:
                if dz == 0:
                    moved = slab
                else:
                    cut = dz % SIDE
                    moved = jnp.concatenate([slab[:, cut:], slab[:, :cut]], axis=1)
                shifted[dz] = moved.reshape(PLANE, COEF)
            rows = pl.ds(s * columns + k * PLANE, PLANE)
            pad = [jnp.zeros((PLANE, WFULL - 7 * COEF), f32)]
            xs[rows, :] = jnp.concatenate([shifted[z] for z in SHIFTS] + pad, axis=1).astype(bf16)
            pad = [jnp.zeros((PLANE, WIN - 4 * COEF), f32)]
            xin[rows, :] = jnp.concatenate([shifted[z] for z in OUTER] + pad, axis=1).astype(bf16)

    def rows_of(i, j):
        value = jnp.concatenate([first[i][j], rest[i][j]], axis=1)
        return value.reshape(-1, value.shape[2])

    n_out = len(OUTER) * ROWS
    n_all = len(SHIFTS) * ROWS
    for i, dx in enumerate(OUTER + INNER):
        rows = pl.ds((dx + REACH) * columns, slabs * columns)
        source = xs[rows, :]
        if dx in OUTER:
            term = dot(rows_of(0, OUTER.index(dx)), source, NT)
            if i == 0:
                acc[...] = term
            else:
                acc[...] += term
        else:
            acc[0:n_out] += dot(rows_of(1, INNER.index(dx)), source, NT)
            acc[n_out:n_all] += dot(rows_of(2, INNER.index(dx)), xin[rows, :], NT)
    lane = lax.broadcasted_iota(jnp.int32, (ROWS, LANE), 1)
    for t in range(slabs * columns // LANE):
        total = jnp.zeros((ROWS, LANE), f32)
        for i, dy in enumerate(OUTER + INNER):
            value = acc[i * ROWS : (i + 1) * ROWS, t * LANE : (t + 1) * LANE]
            by = SIDE * (dy % SIDE)
            if by:
                near = pltpu.roll(value, LANE - by, 1)
                far = pltpu.roll(value, PLANE - by, 1)
                value = jnp.where((lane & (PLANE - 1)) < PLANE - by, near, far)
            total = total + value
        out[:, t * LANE : (t + 1) * LANE] = total.astype(out.dtype)


def coarse_kernel(io):
    out = io.outs[0]
    parts = io.ins[:-1]
    opers = io.ins[-1]
    dens = out.shape[0]
    box = ids = box_ids(parts, dens)
    place = ((box & 7) << 6) + (box & 56) + (box >> 6)
    place = jnp.where(box < BOXES4, place, -1)
    at = lax.broadcasted_iota(jnp.int32, (BOXES4, ids.shape[1]), 0)
    there = jnp.where(at == place, 1.0, 0.0).astype(bf16)
    level = [dot(there, all_parts(parts, k, dens), NT) for k in range(dens)]

    io.wait(*range(len(io.ins)))

    for _ in range(LEVEL):
        count = level[0].shape[0] // 8
        total = None
        for o in range(8):
            rows = jnp.concatenate([v[o * count : (o + 1) * count] for v in level], axis=0)
            term = dot3_rows(split(rows), (opers[o], opers[8 + o]), NT)
            total = term if total is None else total + term
        level = [total[k * count : (k + 1) * count] for k in range(dens)]
    rows = jnp.concatenate(level, axis=0)
    rows = dot3(split(rows), (opers[32], opers[33]), NT)
    level = [rows[k : k + 1] for k in range(dens)]
    for _ in range(LEVEL - 1):
        count = level[0].shape[0]
        rows = split(jnp.concatenate(level, axis=0))
        children = [dot3_rows(rows, (opers[16 + o], opers[24 + o]), NT) for o in range(8)]
        level = [
            jnp.concatenate([c[k * count : (k + 1) * count] for c in children], axis=0)
            for k in range(dens)
        ]
    count = level[0].shape[0]
    rows = split(jnp.concatenate(level, axis=0))
    children = [dot3((opers[16 + o], opers[24 + o]), rows, NT) for o in range(8)]
    for k in range(dens):
        pieces = [c[:, k * count : (k + 1) * count] for c in children]
        out[k] = jnp.concatenate(pieces, axis=1)


def evaluate_kernel(slabs, step, window, io, stack, found):
    n = SIDE // slabs
    checks = io.ins[: 2 * n]
    d_hi, d_lo, lattice, place, field = io.ins[2 * n :]
    offsets = io.scalars[1]
    out = io.outs[0]
    core = io.scalars[0][0] & 1
    group = io.scalars[0][0] // step
    dens = lattice.shape[0]
    sources, cap = out.shape[0], out.shape[2] // dens
    lane = lax.broadcasted_iota(jnp.int32, (COEF, LANE), 1)
    mine = jnp.concatenate([d_hi[core], d_lo[core]], axis=0)
    other = jnp.concatenate([d_hi[1 - core], d_lo[1 - core]], axis=0)
    for m in range(n):
        value = dot(mine, checks[2 * m][...]) + dot(other, checks[2 * m + 1][...])
        value = value[0:COEF] + value[COEF : 2 * COEF]
        if slabs == 2:
            a, b = value[:, 0:LANE], value[:, LANE : 2 * LANE]
            half = LANE // 2
            pieces = [
                jnp.where(lane < half, a, pltpu.roll(b, half, 1)),
                jnp.where(lane < half, pltpu.roll(a, half, 1), b),
            ]
        else:
            pieces = [value[:, k * PLANE : (k + 1) * PLANE] for k in range(dens)]
        width = slabs * PLANE
        for k in range(dens):
            high, low = split(pieces[k])
            rows = pl.ds(k * CPAD, COEF)
            stack[rows, m * width : (m + 1) * width] = high.astype(f32)
            rows = pl.ds((dens + k) * CPAD, COEF)
            stack[rows, m * width : (m + 1) * width] = low.astype(f32)
    box = offsets[sources] + lax.broadcasted_iota(jnp.int32, (1, window), 1)
    want = morton_place(box) ^ (group * (slabs * PLANE))
    turned = BOXES4 + ((box & 7) << 6) + (box & 56) + (box >> 6)
    at = lax.broadcasted_iota(jnp.int32, (2 * BOXES4, window), 0)
    pick = ((at == want) | (at == turned)) & (box < BOXES4)
    pick = jnp.where(pick, 1.0, 0.0).astype(bf16)
    for k in range(dens):
        high, low = split(lattice[k])
        stack[pl.ds(k * CPAD, COEF), BOXES4:] = high.astype(f32)
        stack[pl.ds((dens + k) * CPAD, COEF), BOXES4:] = low.astype(f32)
    half = dens * CPAD
    local = dot(stack[...].astype(bf16), pick)
    high, low = split(local[0:half] + local[half:])
    local = jnp.concatenate([high, low], axis=1)
    found[:, place.shape[1] :] = jnp.zeros((8, found.shape[1] - place.shape[1]), f32)
    io.wait(*range(len(io.ins)))

    def block(j, carry):
        at = pl.ds(pl.multiple_of(j * PB, PB), PB)
        there = place[:, at] == lax.broadcasted_iota(jnp.int32, (window, PB), 0)
        there = jnp.where(there, 1.0, 0.0)
        there = jnp.concatenate([there, there], axis=0).astype(bf16)
        got = dot(local, there)
        mine = field[:, at]
        rows = []
        for k in range(dens):
            value = got[k * CPAD : k * CPAD + COEF]
            rows.append(jnp.sum(value * mine, axis=0, keepdims=True))
        rows.append(jnp.zeros((8 - dens, PB), f32))
        found[:, at] = jnp.concatenate(rows, axis=0)
        return carry

    lax.fori_loop(0, place.shape[1] // PB, block, 0, unroll=8)

    wide = up(cap, LANE) + LANE

    @pl.loop(0, sources // STRIP)
    def _(i):
        for s in range(STRIP):
            offset = offsets[i * STRIP + s]
            tile = offset // LANE
            value = found[:, pl.ds(pl.multiple_of(tile * LANE, LANE), wide)]
            value = pltpu.roll(value, wide - (offset - tile * LANE), 1)
            for k in range(dens):
                out[i * STRIP + s, :, k * cap : (k + 1) * cap] = value[k : k + 1, 0:cap]


def shift_by(axis, value, distance):
    size = lax.axis_size(axis)
    return lax.ppermute(value, axis, [(i, i ^ distance) for i in range(size)])


def gather_by(value, distances, beside):
    got = {m: shift_by("pts", value, m) if m else value for m in distances if m < 2 or m % 2 == 0}
    got, beside = lax.optimization_barrier((got, beside))
    got.update({m + 1: shift_by("pts", got[m], 1) for m in list(got) if m % 2 == 0 and m})
    return [got[m] for m in distances], beside


def per_device(
    local_pos, densities, morton_slot, slot_leaf, uc2e, m2m, m2l_ops, dc2e, lattice, l2l
):
    n_pts = lax.axis_size("pts")
    n_top = lax.axis_size("top")
    me = jnp.stack([lax.axis_index("pts"), lax.axis_index("top")]).astype(jnp.int32)
    points = local_pos.shape[1]
    own = points * n_top
    cap = 2 * points // n_pts
    box_cap = 2 * BOXES4 // n_pts
    dens = DENS // n_top
    slabs = max(1, 2 * SIDE // n_pts)
    coef = uc2e.shape[0]
    sources = n_pts * n_top
    lanes = min(cap, LANE)
    rows = 8 + points // lanes

    def shape(*dims, dtype=bf16):
        return jax.ShapeDtypeStruct(dims, dtype)

    outgoing, entries = run(
        functools.partial(route_kernel, own, cap, n_top),
        [],
        [
            local_pos,
            densities,
            morton_slot.reshape(1, points),
            slot_leaf.reshape(points // lanes, lanes),
        ],
        [shape(n_pts, n_top, rows, cap, dtype=f32), shape(1, points, dtype=jnp.int32)],
        1 << 27,
        stays=(1,),
        grant=GRANT_FIRST,
    )
    outgoing = outgoing.reshape(sources, rows, cap)
    incoming = lax.all_to_all(outgoing, ("pts", "top"), split_axis=0, concat_axis=0, tiled=True)

    flat = (-1, LANE)
    column = jnp.asarray(column_table())
    w_both, opers, *halves = run(
        operators_kernel,
        [],
        [m2m.reshape(flat), l2l.reshape(flat), uc2e, dc2e, lattice, column],
        [shape(2 * coef, 8 * CPAD), shape(34, coef, coef)] + [shape(2, coef, ROWS)] * 2,
        1 << 30,
        here=range(6),
        stays=range(4),
        scratch=[pltpu.VMEM((2, 8 * coef, LANE), f32)],
    )
    first = relayout(m2l_ops, me, 0, EARLY, GRANT_EARLY)
    incoming, first = lax.optimization_barrier((incoming, first))

    partial, field, place, offsets = run(
        functools.partial(points_kernel, n_top, box_cap),
        [me],
        [incoming, column, w_both],
        [
            shape(up(coef + 2, 16), dens * box_cap),
            shape(coef, own, dtype=f32),
            shape(1, own, dtype=jnp.int32),
        ],
        8 << 30,
        late=(0,),
        here=(2,),
        stays=(1, 2),
        numbers=[shape(sources + 1, dtype=jnp.int32)],
        scratch=[
            pltpu.VMEM((8, up(own + up(cap, LANE) + LANE, PB)), f32),
            pltpu.VMEM((3 + FEATURES, coef, PB), f32),
            pltpu.VMEM((1, own), f32),
            pltpu.VMEM((coef, own), f32),
        ],
    )
    later, flat_ops = lax.optimization_barrier((partial, m2l_ops))
    rest = relayout(flat_ops, me, EARLY, STEPS - EARLY, GRANT_LATER)
    parts, rest = gather_by(later, range(n_pts), rest)

    columns = dens * PLANE
    (checks,) = run(
        functools.partial(translate_kernel, slabs, dens),
        [me],
        [*parts, *first, *rest],
        [shape(ROWS, slabs * columns)],
        8 << 30,
        here=range(n_pts, n_pts + 6),
        scratch=[
            pltpu.VMEM(((7 + slabs - 1) * columns, WFULL), bf16),
            pltpu.VMEM(((7 + slabs - 1) * columns, WIN), bf16),
            pltpu.VMEM((7 * ROWS, slabs * columns), f32),
        ],
    )
    (lattice4,) = run(
        coarse_kernel,
        [],
        [*parts, opers],
        [shape(dens, coef, BOXES4, dtype=f32)],
        4 << 30,
        here=(n_pts,),
        stays=(0,),
    )
    step = n_pts // SIDE * slabs
    distances = [step * m + c for m in range(SIDE // slabs) for c in range(2)]
    gathered, lattice4 = gather_by(checks, distances, lattice4)

    (reply,) = run(
        functools.partial(evaluate_kernel, slabs, step, box_cap),
        [me, offsets],
        [*gathered, *halves, lattice4, place, field],
        [shape(sources, 1, dens * cap, dtype=f32)],
        4 << 30,
        here=range(len(gathered), len(gathered) + 5),
        scratch=[
            pltpu.VMEM((2 * dens * CPAD, 2 * BOXES4), f32),
            pltpu.VMEM((8, own + up(cap, LANE) + LANE), f32),
        ],
    )
    returned = lax.all_to_all(reply, ("pts", "top"), split_axis=0, concat_axis=0, tiled=True)
    (out,) = run(
        functools.partial(restore_kernel, n_top),
        [],
        [returned, entries],
        [shape(DENS, points, dtype=f32)],
        1 << 28,
        here=(1,),
    )
    return out


def solution(mesh):
    split_all = P(None, ("pts", "top"))
    placed = (split_all, split_all, P(("pts", "top")), P(("pts", "top"))) + (P(),) * 6
    return jax.shard_map(
        per_device, mesh=mesh, in_specs=placed, out_specs=split_all, check_vma=False
    )
```

```python
import functools
import math

import jax
import jax.numpy as jnp
import numpy as np
from jax import lax
from jax.experimental import pallas as pl
from jax.experimental.pallas import tpu as pltpu
from jax.sharding import PartitionSpec as P

LEVEL = 3
EDGE = 6
DENS = 8
SIDE = 2**LEVEL
BOXES4 = SIDE**3
PLANE = SIDE * SIDE
LANE = 128
REACH = 3
SHIFTS = list(range(-REACH, REACH + 1))
OUTER = [s for s in SHIFTS if abs(s) >= 2]
INNER = [s for s in SHIFTS if abs(s) < 2]
bf16 = jnp.bfloat16
f32 = jnp.float32
NN = (((1,), (0,)), ((), ()))
NT = (((1,), (1,)), ((), ()))


def up(value, multiple):
    return -(-value // multiple) * multiple


def surface_table():
    grid_vals = np.linspace(-1.0, 1.0, EDGE)
    points_list = []
    for a in range(EDGE):
        for b in range(EDGE):
            for c in range(EDGE):
                if min(a, b, c) == 0 or max(a, b, c) == EDGE - 1:
                    points_list.append([grid_vals[a], grid_vals[b], grid_vals[c]])
    return np.array(points_list, dtype=np.float32).T


COEF = surface_table().shape[1]
OFFSETS = (2 * REACH + 1) ** 3 - 27
FEATURES = 4
PB = 256
STRIP = 16
UNROLL_FIND, UNROLL_APPLY, UNROLL_GATHER = 16, 8, 8
GRANT = 28
GRANT_FIRST = 60
GRANT_EARLY = 52
GRANT_LATER = 49
CPAD = up(COEF, 32)


def column_table():
    surface = 1.25 * surface_table().astype(np.float64)
    grid = np.linspace(-0.9, 0.9, 10)
    points = np.stack(np.meshgrid(grid, grid, grid, indexing="ij")).reshape(3, -1)
    values = 1.0 / np.sqrt(((surface[:, :, None] - points[:, None, :]) ** 2).sum(axis=0))
    scale = (points**2).sum(axis=1)
    out = np.zeros((surface.shape[1], LANE), np.float32)
    out[:, 0:3] = (np.float32(1.25) * surface_table()).T
    out[:, 8] = values.mean(axis=1)
    out[:, 9:12] = values @ points.T / scale
    return out


def blocks():
    out, position = [], 0
    for dx in SHIFTS:
        for dy in SHIFTS:
            count = sum(max(abs(dx), abs(dy), abs(dz)) >= 2 for dz in SHIFTS)
            out.append((dx, dy, position, count))
            position += count
    return out


def dot(a, b, dims=NN):
    return lax.dot_general(a, b, dims, preferred_element_type=f32)


def split(value):
    high = value.astype(bf16)
    return high, (value - high.astype(f32)).astype(bf16)


def dot3(a, b, dims=NN):
    return dot(a[0], b[0], dims) + dot(a[1], b[0], dims) + dot(a[0], b[1], dims)


def dot3_rows(a, b, dims=NN):
    rows = a[0].shape[0]
    both = jnp.concatenate([x.astype(f32) for x in a], axis=0).astype(bf16)
    both = dot(both, b[0], dims)
    return both[0:rows] + both[rows : 2 * rows] + dot(a[0], b[1], dims)


def call(kernel, out_shape, mib, flops, bytes_accessed=1 << 20, **kw):
    return pl.pallas_call(
        kernel,
        out_shape=out_shape,
        compiler_params=pltpu.CompilerParams(vmem_limit_bytes=mib << 20),
        cost_estimate=pl.CostEstimate(
            flops=flops, bytes_accessed=bytes_accessed, transcendentals=0
        ),
        **kw,
    )


SMEM = pl.BlockSpec(memory_space=pltpu.SMEM)
VMEM = pl.BlockSpec(memory_space=pltpu.VMEM)
HBM = pl.BlockSpec(memory_space=pltpu.HBM)

class Buffers:
    def __init__(self, scalars, ins, outs, moved, sources, targets, sem_in, sem_out):
        self.scalars, self.ins, self.outs, self.targets = scalars, ins, outs, targets
        self.sem_out = sem_out
        self.coming, self.going, self.waited = {}, {}, set()
        for i in moved:
            self.coming[i] = pltpu.make_async_copy(sources[i], ins[i], sem_in.at[i])
            self.coming[i].start()

    def wait(self, *which):
        for i in which:
            if i in self.coming and i not in self.waited:
                self.waited.add(i)
                self.coming[i].wait()

    def send(self, *which):
        for i in which:
            if i not in self.going:
                copy = pltpu.make_async_copy(self.outs[i], self.targets[i], self.sem_out.at[i])
                copy.start()
                self.going[i] = copy


def run(kernel, scalars, ins, outs, flops, scratch=(), late=(), here=(), stays=(), numbers=(), grant=GRANT):
    n_s, n_i, n_o, n_n = len(scalars), len(ins), len(outs), len(numbers)
    moved_in = [i for i in range(n_i) if i not in here]
    moved_out = [i for i in range(n_o) if i not in stays]

    def body(*refs):
        refs = list(refs)
        take = lambda count: [refs.pop(0) for _ in range(count)]
        given, sources, targets, counts = take(n_s), take(n_i), take(n_o), take(n_n)
        in_refs, out_refs = list(sources), list(targets)
        for i in moved_in:
            in_refs[i] = refs.pop(0)
        for i in moved_out:
            out_refs[i] = refs.pop(0)
        io = Buffers(given, in_refs, out_refs, moved_in, sources, targets, *take(2))
        io.wait(*[i for i in moved_in if i not in late])
        kernel(io, *counts, *refs)
        io.wait(*moved_in)
        io.send(*moved_out)
        for i in moved_out:
            io.going[i].wait()

    return call(
        body,
        tuple(outs) + tuple(numbers),
        grant,
        flops,
        in_specs=[SMEM] * n_s + [VMEM if i in here else HBM for i in range(n_i)],
        out_specs=tuple(VMEM if i in stays else HBM for i in range(n_o)) + (SMEM,) * n_n,
        scratch_shapes=[pltpu.VMEM(ins[i].shape, ins[i].dtype) for i in moved_in]
        + [pltpu.VMEM(outs[i].shape, outs[i].dtype) for i in moved_out]
        + [pltpu.SemaphoreType.DMA((max(n, 1),)) for n in (n_i, n_o)]
        + list(scratch),
    )(*scalars, *ins)


HG = 4 * OFFSETS * COEF // LANE
KT = up(up(OFFSETS * COEF, LANE) // LANE, 8)
WFULL = up(7 * COEF, LANE)
WIN = up(4 * COEF, LANE)
NG = COEF // 8
STEPS = -(-NG // 4)
ROWS = 16 * STEPS
CHUNK = up(HG + 15, 16)
TAIL = 32
EARLY = 3
STRIDE = 17
PIECES = ((4, 7, WFULL), (3, 4, WFULL), (3, 3, WIN))


def relayout_kernel(nrows, step0, steps, me_ref, f_hbm, tail_ref, oa, ob, oc, inb, fbuf, tbuf, sem):
    step = pl.program_id(0)
    half = me_ref[0] & 1
    end16 = nrows // 16 * 16

    def start_row(st, g):
        return jnp.minimum(4 * (st + step0) + g, NG - 1) * (2 * HG) + half * HG

    def start(st, slot):
        for g in range(4):
            row = pl.multiple_of(start_row(st, g) // 16 * 16, 16)
            pltpu.make_async_copy(
                f_hbm.at[pl.ds(row, CHUNK - TAIL)],
                inb.at[slot, g, pl.ds(0, CHUNK - TAIL)],
                sem.at[slot, g, 0],
            ).start()
            last = row + CHUNK > end16

            @pl.when(jnp.logical_not(last))
            def _():
                pltpu.make_async_copy(
                    f_hbm.at[pl.ds(pl.multiple_of(row + CHUNK - TAIL, 16), TAIL)],
                    inb.at[slot, g, pl.ds(CHUNK - TAIL, TAIL)],
                    sem.at[slot, g, 1],
                ).start()


    def wait(st, slot):
        for g in range(4):
            row = pl.multiple_of(start_row(st, g) // 16 * 16, 16)
            pltpu.make_async_copy(
                f_hbm.at[pl.ds(row, CHUNK - TAIL)],
                inb.at[slot, g, pl.ds(0, CHUNK - TAIL)],
                sem.at[slot, g, 0],
            ).wait()
            last = row + CHUNK > end16

            @pl.when(jnp.logical_not(last))
            def _():
                pltpu.make_async_copy(
                    f_hbm.at[pl.ds(pl.multiple_of(row + CHUNK - TAIL, 16), TAIL)],
                    inb.at[slot, g, pl.ds(CHUNK - TAIL, TAIL)],
                    sem.at[slot, g, 1],
                ).wait()

            @pl.when(last)
            def _():
                row16 = lax.broadcasted_iota(jnp.int32, (16, LANE), 0)
                tail = jnp.where(row16 < nrows - end16, tail_ref[...].astype(f32), 0.0)
                inb[slot, g, CHUNK - TAIL : CHUNK - TAIL + 16] = tail.astype(bf16)

    slot = step

    @pl.when(step == 0)
    def _():
        fbuf[...] = jnp.zeros_like(fbuf)
        inb[:, :, CHUNK - 16 :] = jnp.zeros_like(inb[:, :, CHUNK - 16 :])
        for st in range(steps):
            start(st, st)

    wait(step, slot)
    lane = lax.broadcasted_iota(jnp.int32, (8, LANE), 1)
    for g in range(4):
        fbuf[g, 0:CHUNK] = inb[slot, g].astype(f32)
    for g in range(4):
        row = start_row(step, g)
        off = row - row // 16 * 16
        for e in range(4):
            first = OFFSETS * COEF * e
            phase = first % LANE

            @pl.loop(0, KT // 8, unroll=KT // 8)
            def _(n):
                base = off + first // LANE + 8 * n
                value = fbuf[g, pl.ds(base, 8), :]
                if phase:
                    after = fbuf[g, pl.ds(base + 1, 8), :]
                    value = pltpu.roll(jnp.where(lane >= phase, value, after), LANE - phase, 1)
                tbuf[pl.ds(8 * n * STRIDE + 4 * g + e, 8, stride=STRIDE), :] = value

    packed = {}

    def tile(k):
        if k not in packed:
            packed[k] = tbuf[k * STRIDE : k * STRIDE + 16, :].astype(bf16)
        return packed[k]

    lane16 = lax.broadcasted_iota(jnp.int32, (16, LANE), 1)
    here = pl.ds(pl.multiple_of(step * 16, 16), 16)
    for dx, dy, d0, count in blocks():
        tile0, phase = divmod(d0 * COEF, LANE)
        if dx in OUTER:
            ref = oa.at[OUTER.index(dx), (OUTER + INNER).index(dy)]
        elif dy in OUTER:
            ref = ob.at[INNER.index(dx), OUTER.index(dy)]
        else:
            ref = oc.at[INNER.index(dx), INNER.index(dy)]
        for t in range(up(count * COEF, LANE) // LANE):
            value = tile(tile0 + t)
            if phase:
                after = tile(min(tile0 + t + 1, KT - 1))
                value = pltpu.roll(jnp.where(lane16 >= phase, value, after), LANE - phase, 1)
            ref[here, t * LANE : (t + 1) * LANE] = value


def relayout(flat, me, step0, steps, grant):
    nrows = flat.shape[0] // LANE
    rows = flat.reshape(nrows, LANE)
    shapes = tuple((a, b, 16 * steps, c) for a, b, c in PIECES)
    return call(
        functools.partial(relayout_kernel, nrows, step0, steps),
        tuple(jax.ShapeDtypeStruct(s, bf16) for s in shapes),
        grant,
        1 << 20,
        steps << 21,
        grid_spec=pltpu.PrefetchScalarGridSpec(
            num_scalar_prefetch=1,
            grid=(steps,),
            in_specs=[HBM, pl.BlockSpec((16, LANE), lambda i, h: (nrows // 16, 0))],
            out_specs=(VMEM,) * len(shapes),
            scratch_shapes=[
                pltpu.VMEM((steps, 4, CHUNK, LANE), bf16),
                pltpu.VMEM((4, CHUNK + 16, LANE), f32),
                pltpu.VMEM((KT * STRIDE, LANE), f32),
                pltpu.SemaphoreType.DMA((steps, 4, 2)),
            ],
        ),
    )(me, rows, rows)


GROUP = 16


def square(flat, out):
    per = GROUP * COEF // LANE
    groups = flat.shape[0] // per
    lane = lax.broadcasted_iota(jnp.int32, (groups, LANE), 1)
    for r in range(GROUP):
        first, phase = divmod(r * COEF, LANE)
        got = []
        for t in range(3):
            row = min(first + t, per - 1)
            got.append(flat[pl.ds(row, groups, stride=per), :])
        for t in range(2):
            value = got[t]
            if phase:
                value = jnp.where(lane >= phase, got[t], got[t + 1])
                value = pltpu.roll(value, LANE - phase, 1)
            out[t, pl.ds(r, groups, stride=GROUP), :] = value


def operators_kernel(io, rows):
    m2m, l2l, uc2e, dc2e, lattice, column = io.ins
    w_both, coarse, d_hi, d_lo = io.outs
    scale = 1.0 / (4.0 * math.pi)
    coarse[32], coarse[33] = split(lattice[...])
    first = split(uc2e[...] * scale)

    plane = split(column[...])

    def side_by_side(pieces):
        wide = []
        for piece in pieces:
            high, low = split(dot3(split(piece), plane)[:, 8 : 8 + FEATURES])
            wide += [piece, high.astype(f32), low.astype(f32)]
            wide.append(jnp.zeros((COEF, CPAD - COEF - 2 * FEATURES), f32))
        return jnp.concatenate([w for w in wide if w.shape[1]], axis=1)

    def matrix(o):
        at = slice(o * COEF, (o + 1) * COEF)
        return jnp.concatenate([rows[0, at], rows[1, at, 0 : COEF - LANE]], axis=1)

    io.wait(0)
    square(m2m, rows)
    pieces = []
    for o in range(8):
        high, low = split(matrix(o))
        coarse[o], coarse[8 + o] = high, low
        pieces.append(dot3((high, low), first))
    upward = side_by_side(pieces)
    io.wait(1)
    square(l2l, rows)
    pieces = []
    for o in range(8):
        value = matrix(o)
        coarse[16 + o], coarse[24 + o] = split(value)
        pieces.append(jnp.transpose(value) * scale)
    w_both[...] = jnp.concatenate([upward, side_by_side(pieces)], axis=0).astype(bf16)
    high, low = split(dc2e[...])
    i = lax.broadcasted_iota(jnp.int32, (COEF, ROWS), 0)
    r = lax.broadcasted_iota(jnp.int32, (COEF, ROWS), 1)
    for h in range(2):
        here = (i == (r >> 2) * 8 + 4 * h + (r & 3)) & (r < 4 * NG)
        here = jnp.where(here, 1.0, 0.0).astype(bf16)
        d_hi[h] = dot(high, here).astype(bf16)
        d_lo[h] = dot(low, here).astype(bf16)


def route_kernel(own, cap, n_top, io):
    pos, dens, slot, leaf = io.ins
    out, entries = io.outs
    points = pos.shape[1]
    owners = out.shape[0]
    slots = slot[...]
    owner = slots // own
    inside = slots - owner * own
    hit = owner == lax.broadcasted_iota(jnp.int32, (owners, points), 0)
    hit = jnp.where(hit, 1.0, 0.0)
    hit16 = hit.astype(bf16)
    row = lax.broadcasted_iota(jnp.int32, (LANE, LANE), 0)
    col = lax.broadcasted_iota(jnp.int32, (LANE, LANE), 1)
    before = jnp.where(row < col, 1.0, 0.0).astype(bf16)
    every = jnp.ones((LANE, LANE), bf16)
    total = jnp.zeros((owners, LANE), f32)
    ranks = []
    for t in range(points // LANE):
        part = hit16[:, t * LANE : (t + 1) * LANE]
        ranks.append(total + dot(part, before))
        total = total + dot(part, every)
    rank = jnp.sum(hit * jnp.concatenate(ranks, axis=1), axis=0, keepdims=True)
    entry = owner * cap + rank.astype(jnp.int32)
    entries[...] = entry
    inside_hi = inside // 64
    value = jnp.concatenate([pos[...], dens[...]], axis=0)
    width = value.shape[0]
    high, low = split(value)
    ones = jnp.ones((1, points), f32)
    high = jnp.concatenate(
        [high.astype(f32), inside_hi.astype(f32), (inside - 64 * inside_hi).astype(f32), ones]
        + [jnp.zeros((16 - width - 3, points), f32)],
        axis=0,
    )
    low = jnp.concatenate([low.astype(f32), jnp.zeros((16 - width, points), f32)], axis=0)
    payload = jnp.concatenate([high, low], axis=0).astype(bf16)
    block = max(cap, LANE)
    per = DENS // n_top
    leaves = leaf[...].astype(f32)
    if leaves.shape[1] < cap:
        blank = jnp.zeros((leaves.shape[0], cap - leaves.shape[1]), f32)
        leaves = jnp.concatenate([leaves, blank], axis=1)
    for o in range(owners * cap // block):
        there = entry == o * block + lax.broadcasted_iota(jnp.int32, (block, points), 0)
        there = jnp.where(there, 1.0, 0.0).astype(bf16)
        got = dot(payload, there, NT)
        value = got[0:width] + got[16 : 16 + width]
        where = got[width : width + 1] * 64.0 + got[width + 1 : width + 2]
        valid = got[width + 2 : width + 3]
        for q in range(n_top):
            rows = [value[0:3], where, valid, value[3 + per * q : 3 + per * (q + 1)]]
            rows.append(jnp.zeros((8 - 5 - per, block), f32))
            packed = jnp.concatenate([r for r in rows if r.shape[0]], axis=0)
            for i in range(block // cap):
                at = o * (block // cap) + i
                out[at, q, 0:8] = packed[:, i * cap : (i + 1) * cap]
                out[at, q, 8:] = leaves


def restore_kernel(n_top, io):
    got, entries = io.ins
    out = io.outs[0]
    devices = got.shape[0]
    per = out.shape[0] // n_top
    cap = got.shape[2] // per
    points = out.shape[1]
    block = max(cap, PB)
    total = jnp.zeros((2 * out.shape[0], points), f32)
    for o in range(devices // n_top * cap // block):
        count = block // cap
        value = []
        for q in range(n_top):
            for k in range(per):
                pieces = []
                for i in range(count):
                    row = (o * count + i) * n_top + q
                    pieces.append(got[row, :, k * cap : (k + 1) * cap])
                value.append(jnp.concatenate(pieces, axis=1))
        high, low = split(jnp.concatenate(value, axis=0))
        both = jnp.concatenate([high.astype(f32), low.astype(f32)], axis=0).astype(bf16)
        at = o * block + lax.broadcasted_iota(jnp.int32, (block, points), 0)
        total = total + dot(both, jnp.where(entries[...] == at, 1.0, 0.0).astype(bf16))
    out[...] = total[0 : out.shape[0]] + total[out.shape[0] :]


def octant_product(pos, octant, surf, oper):
    squared = None
    for d in range(3):
        spacing = surf[d] - pos[d : d + 1]
        squared = spacing * spacing if squared is None else squared + spacing * spacing
    value = lax.rsqrt(squared)
    round_pos = pos.astype(bf16).astype(f32)
    value = value - surf[3]
    for d in range(3):
        value = value - surf[4 + d] * round_pos[d : d + 1]
    features = [jnp.ones_like(round_pos[0:1]), round_pos]
    blank = jnp.zeros((CPAD - COEF - 2 * FEATURES, value.shape[1]), f32)
    value = [value] + features + features + [blank]
    value = jnp.concatenate([v for v in value if v.shape[0]], axis=0).astype(bf16)
    masks = [jnp.where(octant == o, 1.0, 0.0).astype(bf16) for o in range(8)]
    return dot(oper[...], jnp.concatenate([value * m for m in masks], axis=0))


TURNED = (((0,), (0,)), ((), ()))


def look_up(index, table):
    lanes, rows = table.shape[0] // 2, table.shape[1]
    width = index.shape[1]
    at_row = index // lanes
    at_lane = index - at_row * lanes
    there = at_row == lax.broadcasted_iota(jnp.int32, (rows, width), 0)
    got = dot(table, jnp.where(there, 1.0, 0.0).astype(bf16))
    mine = at_lane == lax.broadcasted_iota(jnp.int32, (lanes, width), 0)
    first = jnp.sum(jnp.where(mine, got[0:lanes], 0.0), axis=0, keepdims=True)
    return first, jnp.sum(jnp.where(mine, got[lanes:], 0.0), axis=0, keepdims=True)


def fill_surface(surf, column):
    for i, lane in enumerate((0, 1, 2, 8, 9, 10, 11)):
        surf[i] = jnp.broadcast_to(column[:, lane : lane + 1], surf.shape[1:])


def morton_place(box):
    place = jnp.zeros_like(box)
    for b in range(LEVEL):
        digit = box >> (3 * b)
        place = place + ((((digit >> 2) & 1) << (2 * LEVEL + b)))
        place = place + ((((digit >> 1) & 1) << (LEVEL + b)) + ((digit & 1) << b))
    return place


def points_kernel(n_top, box_cap, io, offsets, buf, surf, octants, outgoing):
    got, column, oper = io.ins
    out, field, place = io.outs
    sources, _, cap = got.shape
    lanes = min(cap, LANE)
    own = field.shape[1]
    wide = up(cap, LANE)
    me = io.scalars[0][0]
    buf[...] = jnp.zeros_like(buf)
    fill_surface(surf, column)
    io.wait(0)

    def put(i, offset):
        values = [got[i * STRIP + s, 0:8] for s in range(STRIP)]
        counts = [jnp.sum(v[4:5]).astype(jnp.int32) for v in values]
        for s, (value, count) in enumerate(zip(values, counts)):
            offsets[i * STRIP + s] = offset
            value = jnp.concatenate([value, jnp.zeros((8, wide + LANE - cap), f32)], axis=1)
            tile = offset // LANE
            value = pltpu.roll(value, offset - tile * LANE, 1)
            at = pl.ds(pl.multiple_of(tile * LANE, LANE), wide + LANE)
            buf[:, at] = buf[:, at] + value
            offset = offset + count
        return offset

    lax.fori_loop(0, sources // STRIP, put, jnp.int32(0))
    leaf = got[pl.ds(me * n_top, n_top), 8:, 0:lanes].reshape(own // lanes, lanes)
    leaf = leaf.astype(jnp.int32)
    first = got[me * n_top, 8:9, 0:1].astype(jnp.int32) >> 3
    offsets[sources] = jnp.sum(got[me * n_top, 8:9, 0:1]).astype(jnp.int32) >> 3
    io.wait(2)
    table = jnp.concatenate([(leaf >> 3) - first, leaf & 7], axis=1).astype(f32)
    table = jnp.transpose(table).astype(bf16)
    out_rows = out.shape[1]

    blocks_of = own // PB

    def spot(j):
        return pl.ds(pl.multiple_of(j * PB, PB), PB)

    def find(j, carry):
        to = spot(j)
        box, octant = look_up(buf[3:4, to].astype(jnp.int32), table)
        place[:, to] = box.astype(jnp.int32)
        octants[:, to] = octant
        return carry

    lax.fori_loop(0, blocks_of, find, 0, unroll=UNROLL_FIND)

    def apply(j, carry):
        to = spot(j)
        both = octant_product(buf[0:3, to], octants[:, to], surf, oper)
        outgoing[:, to] = both[0:COEF]
        field[:, to] = both[COEF : 2 * COEF]
        return carry

    lax.fori_loop(0, blocks_of, apply, 0, unroll=UNROLL_APPLY)

    def gather(j, total):
        to = spot(j)
        high, low = split(outgoing[:, to])
        rows = []
        at = lax.broadcasted_iota(jnp.int32, (box_cap, PB), 0)
        here = place[:, to] == at
        for k in range(out_rows // box_cap):
            rows.append(jnp.where(here, buf[5 + k : 6 + k, to], 0.0))
        a_high, a_low = split(jnp.concatenate(rows, axis=0))
        both = dot(jnp.concatenate([high, low], axis=0), a_high, NT)
        return total + both[0:COEF] + both[COEF : 2 * COEF] + dot(high, a_low, NT)

    total = jnp.zeros((COEF, out_rows), f32)
    total = lax.fori_loop(0, blocks_of, gather, total, unroll=UNROLL_GATHER)
    digits = jnp.concatenate([first >> 3, first & 7], axis=0).astype(f32)
    digits = jnp.broadcast_to(digits, (2, out_rows))
    blank = jnp.zeros((out.shape[0] - COEF - 2, out_rows), f32)
    out[...] = jnp.concatenate([total, digits, blank], axis=0).astype(bf16)


def box_ids(parts, dens):
    ids = []
    for part in parts:
        digits = part[COEF - 8 : COEF + 8, :].astype(f32)[8:16, 0:1].astype(jnp.int32)
        first = digits[0:1] * 8 + digits[1:2]
        at = lax.broadcasted_iota(jnp.int32, (1, part.shape[1] // dens), 1)
        ids.append(first + at)
    return jnp.concatenate(ids, axis=1)


def all_parts(parts, k, dens):
    width = parts[0].shape[1] // dens
    return jnp.concatenate([p[0:COEF, k * width : (k + 1) * width] for p in parts], axis=1)


def translate_kernel(slabs, dens, io, xs, xin, acc):
    parts = io.ins[:-6]
    first, rest = io.ins[-6:-3], io.ins[-3:]
    out = io.outs[0]
    x0 = (io.scalars[0][0] // 2 * 2) * SIDE // len(parts)
    ids = box_ids(parts, dens)
    place = morton_place(ids)
    place = (((place >> 6) - x0 + REACH) & 7) * 64 + (place & 63)
    place = jnp.where(ids < BOXES4, place, -1)
    at = lax.broadcasted_iota(jnp.int32, (BOXES4, ids.shape[1]), 0)
    there = jnp.where(at == place, 1.0, 0.0).astype(bf16)
    columns = dens * PLANE
    for k in range(dens):
        low = dot(there, all_parts(parts, k, dens), NT)
        low = low.astype(bf16).astype(f32)
        for s in range(7 + slabs - 1):
            slab = low[s * PLANE : (s + 1) * PLANE].reshape(SIDE, SIDE, COEF)
            shifted = {}
            for dz in SHIFTS:
                if dz == 0:
                    moved = slab
                else:
                    cut = dz % SIDE
                    moved = jnp.concatenate([slab[:, cut:], slab[:, :cut]], axis=1)
                shifted[dz] = moved.reshape(PLANE, COEF)
            rows = pl.ds(s * columns + k * PLANE, PLANE)
            pad = [jnp.zeros((PLANE, WFULL - 7 * COEF), f32)]
            xs[rows, :] = jnp.concatenate([shifted[z] for z in SHIFTS] + pad, axis=1).astype(bf16)
            pad = [jnp.zeros((PLANE, WIN - 4 * COEF), f32)]
            xin[rows, :] = jnp.concatenate([shifted[z] for z in OUTER] + pad, axis=1).astype(bf16)

    def rows_of(i, j):
        value = jnp.concatenate([first[i][j], rest[i][j]], axis=1)
        return value.reshape(-1, value.shape[2])

    n_out = len(OUTER) * ROWS
    n_all = len(SHIFTS) * ROWS
    for i, dx in enumerate(OUTER + INNER):
        rows = pl.ds((dx + REACH) * columns, slabs * columns)
        source = xs[rows, :]
        if dx in OUTER:
            term = dot(rows_of(0, OUTER.index(dx)), source, NT)
            if i == 0:
                acc[...] = term
            else:
                acc[...] += term
        else:
            acc[0:n_out] += dot(rows_of(1, INNER.index(dx)), source, NT)
            acc[n_out:n_all] += dot(rows_of(2, INNER.index(dx)), xin[rows, :], NT)
    lane = lax.broadcasted_iota(jnp.int32, (ROWS, LANE), 1)
    for t in range(slabs * columns // LANE):
        total = jnp.zeros((ROWS, LANE), f32)
        for i, dy in enumerate(OUTER + INNER):
            value = acc[i * ROWS : (i + 1) * ROWS, t * LANE : (t + 1) * LANE]
            by = SIDE * (dy % SIDE)
            if by:
                near = pltpu.roll(value, LANE - by, 1)
                far = pltpu.roll(value, PLANE - by, 1)
                value = jnp.where((lane & (PLANE - 1)) < PLANE - by, near, far)
            total = total + value
        out[:, t * LANE : (t + 1) * LANE] = total.astype(out.dtype)


def coarse_kernel(io):
    out = io.outs[0]
    parts = io.ins[:-1]
    opers = io.ins[-1]
    dens = out.shape[0]
    box = ids = box_ids(parts, dens)
    place = ((box & 7) << 6) + (box & 56) + (box >> 6)
    place = jnp.where(box < BOXES4, place, -1)
    at = lax.broadcasted_iota(jnp.int32, (BOXES4, ids.shape[1]), 0)
    there = jnp.where(at == place, 1.0, 0.0).astype(bf16)
    level = [dot(there, all_parts(parts, k, dens), NT) for k in range(dens)]

    io.wait(*range(len(io.ins)))

    for _ in range(LEVEL):
        count = level[0].shape[0] // 8
        total = None
        for o in range(8):
            rows = jnp.concatenate([v[o * count : (o + 1) * count] for v in level], axis=0)
            term = dot3_rows(split(rows), (opers[o], opers[8 + o]), NT)
            total = term if total is None else total + term
        level = [total[k * count : (k + 1) * count] for k in range(dens)]
    rows = jnp.concatenate(level, axis=0)
    rows = dot3(split(rows), (opers[32], opers[33]), NT)
    level = [rows[k : k + 1] for k in range(dens)]
    for _ in range(LEVEL - 1):
        count = level[0].shape[0]
        rows = split(jnp.concatenate(level, axis=0))
        children = [dot3_rows(rows, (opers[16 + o], opers[24 + o]), NT) for o in range(8)]
        level = [
            jnp.concatenate([c[k * count : (k + 1) * count] for c in children], axis=0)
            for k in range(dens)
        ]
    count = level[0].shape[0]
    rows = split(jnp.concatenate(level, axis=0))
    children = [dot3((opers[16 + o], opers[24 + o]), rows, NT) for o in range(8)]
    for k in range(dens):
        pieces = [c[:, k * count : (k + 1) * count] for c in children]
        out[k] = jnp.concatenate(pieces, axis=1)


def evaluate_kernel(slabs, step, window, io, stack, found):
    n = SIDE // slabs
    checks = io.ins[: 2 * n]
    d_hi, d_lo, lattice, place, field = io.ins[2 * n :]
    offsets = io.scalars[1]
    out = io.outs[0]
    core = io.scalars[0][0] & 1
    group = io.scalars[0][0] // step
    dens = lattice.shape[0]
    sources, cap = out.shape[0], out.shape[2] // dens
    lane = lax.broadcasted_iota(jnp.int32, (COEF, LANE), 1)
    mine = jnp.concatenate([d_hi[core], d_lo[core]], axis=0)
    other = jnp.concatenate([d_hi[1 - core], d_lo[1 - core]], axis=0)
    for m in range(n):
        value = dot(mine, checks[2 * m][...]) + dot(other, checks[2 * m + 1][...])
        value = value[0:COEF] + value[COEF : 2 * COEF]
        if slabs == 2:
            a, b = value[:, 0:LANE], value[:, LANE : 2 * LANE]
            half = LANE // 2
            pieces = [
                jnp.where(lane < half, a, pltpu.roll(b, half, 1)),
                jnp.where(lane < half, pltpu.roll(a, half, 1), b),
            ]
        else:
            pieces = [value[:, k * PLANE : (k + 1) * PLANE] for k in range(dens)]
        width = slabs * PLANE
        for k in range(dens):
            high, low = split(pieces[k])
            rows = pl.ds(k * CPAD, COEF)
            stack[rows, m * width : (m + 1) * width] = high.astype(f32)
            rows = pl.ds((dens + k) * CPAD, COEF)
            stack[rows, m * width : (m + 1) * width] = low.astype(f32)
    box = offsets[sources] + lax.broadcasted_iota(jnp.int32, (1, window), 1)
    want = morton_place(box) ^ (group * (slabs * PLANE))
    turned = BOXES4 + ((box & 7) << 6) + (box & 56) + (box >> 6)
    at = lax.broadcasted_iota(jnp.int32, (2 * BOXES4, window), 0)
    pick = ((at == want) | (at == turned)) & (box < BOXES4)
    pick = jnp.where(pick, 1.0, 0.0).astype(bf16)
    for k in range(dens):
        high, low = split(lattice[k])
        stack[pl.ds(k * CPAD, COEF), BOXES4:] = high.astype(f32)
        stack[pl.ds((dens + k) * CPAD, COEF), BOXES4:] = low.astype(f32)
    half = dens * CPAD
    local = dot(stack[...].astype(bf16), pick)
    high, low = split(local[0:half] + local[half:])
    local = jnp.concatenate([high, low], axis=1)
    found[:, place.shape[1] :] = jnp.zeros((8, found.shape[1] - place.shape[1]), f32)
    io.wait(*range(len(io.ins)))

    def block(j, carry):
        at = pl.ds(pl.multiple_of(j * PB, PB), PB)
        there = place[:, at] == lax.broadcasted_iota(jnp.int32, (window, PB), 0)
        there = jnp.where(there, 1.0, 0.0)
        there = jnp.concatenate([there, there], axis=0).astype(bf16)
        got = dot(local, there)
        mine = field[:, at]
        rows = []
        for k in range(dens):
            value = got[k * CPAD : k * CPAD + COEF]
            rows.append(jnp.sum(value * mine, axis=0, keepdims=True))
        rows.append(jnp.zeros((8 - dens, PB), f32))
        found[:, at] = jnp.concatenate(rows, axis=0)
        return carry

    lax.fori_loop(0, place.shape[1] // PB, block, 0, unroll=8)

    wide = up(cap, LANE) + LANE

    @pl.loop(0, sources // STRIP)
    def _(i):
        for s in range(STRIP):
            offset = offsets[i * STRIP + s]
            tile = offset // LANE
            value = found[:, pl.ds(pl.multiple_of(tile * LANE, LANE), wide)]
            value = pltpu.roll(value, wide - (offset - tile * LANE), 1)
            for k in range(dens):
                out[i * STRIP + s, :, k * cap : (k + 1) * cap] = value[k : k + 1, 0:cap]


def shift_by(axis, value, distance):
    size = lax.axis_size(axis)
    return lax.ppermute(value, axis, [(i, i ^ distance) for i in range(size)])


def gather_by(value, distances, beside):
    got = {m: shift_by("pts", value, m) if m else value for m in distances if m < 2 or m % 2 == 0}
    got, beside = lax.optimization_barrier((got, beside))
    got.update({m + 1: shift_by("pts", got[m], 1) for m in list(got) if m % 2 == 0 and m})
    return [got[m] for m in distances], beside


def per_device(
    local_pos, densities, morton_slot, slot_leaf, uc2e, m2m, m2l_ops, dc2e, lattice, l2l
):
    n_pts = lax.axis_size("pts")
    n_top = lax.axis_size("top")
    me = jnp.stack([lax.axis_index("pts"), lax.axis_index("top")]).astype(jnp.int32)
    points = local_pos.shape[1]
    own = points * n_top
    cap = 2 * points // n_pts
    box_cap = 2 * BOXES4 // n_pts
    dens = DENS // n_top
    slabs = max(1, 2 * SIDE // n_pts)
    coef = uc2e.shape[0]
    sources = n_pts * n_top
    lanes = min(cap, LANE)
    rows = 8 + points // lanes

    def shape(*dims, dtype=bf16):
        return jax.ShapeDtypeStruct(dims, dtype)

    outgoing, entries = run(
        functools.partial(route_kernel, own, cap, n_top),
        [],
        [
            local_pos,
            densities,
            morton_slot.reshape(1, points),
            slot_leaf.reshape(points // lanes, lanes),
        ],
        [shape(n_pts, n_top, rows, cap, dtype=f32), shape(1, points, dtype=jnp.int32)],
        1 << 27,
        stays=(1,),
        grant=GRANT_FIRST,
    )
    outgoing = outgoing.reshape(sources, rows, cap)
    incoming = lax.all_to_all(outgoing, ("pts", "top"), split_axis=0, concat_axis=0, tiled=True)

    flat = (-1, LANE)
    column = jnp.asarray(column_table())
    w_both, opers, *halves = run(
        operators_kernel,
        [],
        [m2m.reshape(flat), l2l.reshape(flat), uc2e, dc2e, lattice, column],
        [shape(2 * coef, 8 * CPAD), shape(34, coef, coef)] + [shape(2, coef, ROWS)] * 2,
        1 << 30,
        here=range(6),
        stays=range(4),
        scratch=[pltpu.VMEM((2, 8 * coef, LANE), f32)],
    )
    first = relayout(m2l_ops, me, 0, EARLY, GRANT_EARLY)
    incoming, first = lax.optimization_barrier((incoming, first))

    partial, field, place, offsets = run(
        functools.partial(points_kernel, n_top, box_cap),
        [me],
        [incoming, column, w_both],
        [
            shape(up(coef + 2, 16), dens * box_cap),
            shape(coef, own, dtype=f32),
            shape(1, own, dtype=jnp.int32),
        ],
        8 << 30,
        here=range(3),
        stays=range(3),
        numbers=[shape(sources + 1, dtype=jnp.int32)],
        scratch=[
            pltpu.VMEM((8, up(own + up(cap, LANE) + LANE, PB)), f32),
            pltpu.VMEM((3 + FEATURES, coef, PB), f32),
            pltpu.VMEM((1, own), f32),
            pltpu.VMEM((coef, own), f32),
        ],
    )
    later, flat_ops = lax.optimization_barrier((partial, m2l_ops))
    rest = relayout(flat_ops, me, EARLY, STEPS - EARLY, GRANT_LATER)
    parts, rest = gather_by(later, range(n_pts), rest)

    columns = dens * PLANE
    (checks,) = run(
        functools.partial(translate_kernel, slabs, dens),
        [me],
        [*parts, *first, *rest],
        [shape(ROWS, slabs * columns)],
        8 << 30,
        here=range(n_pts + 6),
        stays=(0,),
        scratch=[
            pltpu.VMEM(((7 + slabs - 1) * columns, WFULL), bf16),
            pltpu.VMEM(((7 + slabs - 1) * columns, WIN), bf16),
            pltpu.VMEM((7 * ROWS, slabs * columns), f32),
        ],
    )
    (lattice4,) = run(
        coarse_kernel,
        [],
        [*parts, opers],
        [shape(dens, coef, BOXES4, dtype=f32)],
        4 << 30,
        here=range(n_pts + 1),
        stays=(0,),
    )
    step = n_pts // SIDE * slabs
    distances = [step * m + c for m in range(SIDE // slabs) for c in range(2)]
    gathered, lattice4 = gather_by(checks, distances, lattice4)

    (reply,) = run(
        functools.partial(evaluate_kernel, slabs, step, box_cap),
        [me, offsets],
        [*gathered, *halves, lattice4, place, field],
        [shape(sources, 1, dens * cap, dtype=f32)],
        4 << 30,
        here=range(len(gathered) + 5),
        stays=(0,),
        scratch=[
            pltpu.VMEM((2 * dens * CPAD, 2 * BOXES4), f32),
            pltpu.VMEM((8, own + up(cap, LANE) + LANE), f32),
        ],
    )
    returned = lax.all_to_all(reply, ("pts", "top"), split_axis=0, concat_axis=0, tiled=True)
    (out,) = run(
        functools.partial(restore_kernel, n_top),
        [],
        [returned, entries],
        [shape(DENS, points, dtype=f32)],
        1 << 28,
        here=range(2),
    )
    return out


def solution(mesh):
    split_all = P(None, ("pts", "top"))
    placed = (split_all, split_all, P(("pts", "top")), P(("pts", "top"))) + (P(),) * 6
    return jax.shard_map(
        per_device, mesh=mesh, in_specs=placed, out_specs=split_all, check_vma=False
    )
```

```python
import functools
import math

import jax
import jax.numpy as jnp
import numpy as np
from jax import lax
from jax.experimental import pallas as pl
from jax.experimental.pallas import tpu as pltpu
from jax.sharding import PartitionSpec as P

LEVEL = 3
EDGE = 6
DENS = 8
SIDE = 2**LEVEL
BOXES4 = SIDE**3
PLANE = SIDE * SIDE
LANE = 128
REACH = 3
SHIFTS = list(range(-REACH, REACH + 1))
OUTER = [s for s in SHIFTS if abs(s) >= 2]
INNER = [s for s in SHIFTS if abs(s) < 2]
bf16 = jnp.bfloat16
f32 = jnp.float32
NN = (((1,), (0,)), ((), ()))
NT = (((1,), (1,)), ((), ()))


def up(value, multiple):
    return -(-value // multiple) * multiple


def surface_table():
    grid_vals = np.linspace(-1.0, 1.0, EDGE)
    points_list = []
    for a in range(EDGE):
        for b in range(EDGE):
            for c in range(EDGE):
                if min(a, b, c) == 0 or max(a, b, c) == EDGE - 1:
                    points_list.append([grid_vals[a], grid_vals[b], grid_vals[c]])
    return np.array(points_list, dtype=np.float32).T


COEF = surface_table().shape[1]
OFFSETS = (2 * REACH + 1) ** 3 - 27
FEATURES = 4
PB = 256
STRIP = 16
UNROLL_FIND, UNROLL_APPLY, UNROLL_GATHER = 16, 8, 8
GRANT = 28
GRANT_FIRST = 60
GRANT_EARLY = 52
GRANT_LATER = 49
CPAD = up(COEF, 32)


def column_table():
    surface = 1.25 * surface_table().astype(np.float64)
    grid = np.linspace(-0.9, 0.9, 10)
    points = np.stack(np.meshgrid(grid, grid, grid, indexing="ij")).reshape(3, -1)
    values = 1.0 / np.sqrt(((surface[:, :, None] - points[:, None, :]) ** 2).sum(axis=0))
    scale = (points**2).sum(axis=1)
    out = np.zeros((surface.shape[1], LANE), np.float32)
    out[:, 0:3] = (np.float32(1.25) * surface_table()).T
    out[:, 8] = values.mean(axis=1)
    out[:, 9:12] = values @ points.T / scale
    return out


def blocks():
    out, position = [], 0
    for dx in SHIFTS:
        for dy in SHIFTS:
            count = sum(max(abs(dx), abs(dy), abs(dz)) >= 2 for dz in SHIFTS)
            out.append((dx, dy, position, count))
            position += count
    return out


def dot(a, b, dims=NN):
    return lax.dot_general(a, b, dims, preferred_element_type=f32)


def split(value):
    high = value.astype(bf16)
    return high, (value - high.astype(f32)).astype(bf16)


def dot3(a, b, dims=NN):
    return dot(a[0], b[0], dims) + dot(a[1], b[0], dims) + dot(a[0], b[1], dims)


def dot3_rows(a, b, dims=NN):
    rows = a[0].shape[0]
    both = jnp.concatenate([x.astype(f32) for x in a], axis=0).astype(bf16)
    both = dot(both, b[0], dims)
    return both[0:rows] + both[rows : 2 * rows] + dot(a[0], b[1], dims)


def call(kernel, out_shape, mib, flops, bytes_accessed=1 << 20, **kw):
    return pl.pallas_call(
        kernel,
        out_shape=out_shape,
        compiler_params=pltpu.CompilerParams(vmem_limit_bytes=mib << 20),
        cost_estimate=pl.CostEstimate(
            flops=flops, bytes_accessed=bytes_accessed, transcendentals=0
        ),
        **kw,
    )


SMEM = pl.BlockSpec(memory_space=pltpu.SMEM)
VMEM = pl.BlockSpec(memory_space=pltpu.VMEM)
HBM = pl.BlockSpec(memory_space=pltpu.HBM)

class Buffers:
    def __init__(self, scalars, ins, outs, moved, sources, targets, sem_in, sem_out):
        self.scalars, self.ins, self.outs, self.targets = scalars, ins, outs, targets
        self.sem_out = sem_out
        self.coming, self.going, self.waited = {}, {}, set()
        for i in moved:
            self.coming[i] = pltpu.make_async_copy(sources[i], ins[i], sem_in.at[i])
            self.coming[i].start()

    def wait(self, *which):
        for i in which:
            if i in self.coming and i not in self.waited:
                self.waited.add(i)
                self.coming[i].wait()

    def send(self, *which):
        for i in which:
            if i not in self.going:
                copy = pltpu.make_async_copy(self.outs[i], self.targets[i], self.sem_out.at[i])
                copy.start()
                self.going[i] = copy


def run(kernel, scalars, ins, outs, flops, scratch=(), late=(), here=(), stays=(), numbers=(), grant=GRANT):
    n_s, n_i, n_o, n_n = len(scalars), len(ins), len(outs), len(numbers)
    moved_in = [i for i in range(n_i) if i not in here]
    moved_out = [i for i in range(n_o) if i not in stays]

    def body(*refs):
        refs = list(refs)
        take = lambda count: [refs.pop(0) for _ in range(count)]
        given, sources, targets, counts = take(n_s), take(n_i), take(n_o), take(n_n)
        in_refs, out_refs = list(sources), list(targets)
        for i in moved_in:
            in_refs[i] = refs.pop(0)
        for i in moved_out:
            out_refs[i] = refs.pop(0)
        io = Buffers(given, in_refs, out_refs, moved_in, sources, targets, *take(2))
        io.wait(*[i for i in moved_in if i not in late])
        kernel(io, *counts, *refs)
        io.wait(*moved_in)
        io.send(*moved_out)
        for i in moved_out:
            io.going[i].wait()

    return call(
        body,
        tuple(outs) + tuple(numbers),
        grant,
        flops,
        in_specs=[SMEM] * n_s + [VMEM if i in here else HBM for i in range(n_i)],
        out_specs=tuple(VMEM if i in stays else HBM for i in range(n_o)) + (SMEM,) * n_n,
        scratch_shapes=[pltpu.VMEM(ins[i].shape, ins[i].dtype) for i in moved_in]
        + [pltpu.VMEM(outs[i].shape, outs[i].dtype) for i in moved_out]
        + [pltpu.SemaphoreType.DMA((max(n, 1),)) for n in (n_i, n_o)]
        + list(scratch),
    )(*scalars, *ins)


HG = 4 * OFFSETS * COEF // LANE
KT = up(up(OFFSETS * COEF, LANE) // LANE, 8)
WFULL = up(7 * COEF, LANE)
WIN = up(4 * COEF, LANE)
NG = COEF // 8
STEPS = -(-NG // 4)
ROWS = 16 * STEPS
CHUNK = up(HG + 15, 16)
TAIL = 32
EARLY = 2
STRIDE = 17
PIECES = ((4, 7, WFULL), (3, 4, WFULL), (3, 3, WIN))


def relayout_kernel(nrows, step0, steps, me_ref, f_hbm, tail_ref, oa, ob, oc, inb, fbuf, tbuf, sem):
    step = pl.program_id(0)
    half = me_ref[0] & 1
    end16 = nrows // 16 * 16

    def start_row(st, g):
        return jnp.minimum(4 * (st + step0) + g, NG - 1) * (2 * HG) + half * HG

    def start(st, slot):
        for g in range(4):
            row = pl.multiple_of(start_row(st, g) // 16 * 16, 16)
            pltpu.make_async_copy(
                f_hbm.at[pl.ds(row, CHUNK - TAIL)],
                inb.at[slot, g, pl.ds(0, CHUNK - TAIL)],
                sem.at[slot, g, 0],
            ).start()
            last = row + CHUNK > end16

            @pl.when(jnp.logical_not(last))
            def _():
                pltpu.make_async_copy(
                    f_hbm.at[pl.ds(pl.multiple_of(row + CHUNK - TAIL, 16), TAIL)],
                    inb.at[slot, g, pl.ds(CHUNK - TAIL, TAIL)],
                    sem.at[slot, g, 1],
                ).start()


    def wait(st, slot):
        for g in range(4):
            row = pl.multiple_of(start_row(st, g) // 16 * 16, 16)
            pltpu.make_async_copy(
                f_hbm.at[pl.ds(row, CHUNK - TAIL)],
                inb.at[slot, g, pl.ds(0, CHUNK - TAIL)],
                sem.at[slot, g, 0],
            ).wait()
            last = row + CHUNK > end16

            @pl.when(jnp.logical_not(last))
            def _():
                pltpu.make_async_copy(
                    f_hbm.at[pl.ds(pl.multiple_of(row + CHUNK - TAIL, 16), TAIL)],
                    inb.at[slot, g, pl.ds(CHUNK - TAIL, TAIL)],
                    sem.at[slot, g, 1],
                ).wait()

            @pl.when(last)
            def _():
                row16 = lax.broadcasted_iota(jnp.int32, (16, LANE), 0)
                tail = jnp.where(row16 < nrows - end16, tail_ref[...].astype(f32), 0.0)
                inb[slot, g, CHUNK - TAIL : CHUNK - TAIL + 16] = tail.astype(bf16)

    slot = step

    @pl.when(step == 0)
    def _():
        fbuf[...] = jnp.zeros_like(fbuf)
        inb[:, :, CHUNK - 16 :] = jnp.zeros_like(inb[:, :, CHUNK - 16 :])
        for st in range(steps):
            start(st, st)

    wait(step, slot)
    lane = lax.broadcasted_iota(jnp.int32, (8, LANE), 1)
    for g in range(4):
        fbuf[g, 0:CHUNK] = inb[slot, g].astype(f32)
    for g in range(4):
        row = start_row(step, g)
        off = row - row // 16 * 16
        for e in range(4):
            first = OFFSETS * COEF * e
            phase = first % LANE

            @pl.loop(0, KT // 8, unroll=KT // 8)
            def _(n):
                base = off + first // LANE + 8 * n
                value = fbuf[g, pl.ds(base, 8), :]
                if phase:
                    after = fbuf[g, pl.ds(base + 1, 8), :]
                    value = pltpu.roll(jnp.where(lane >= phase, value, after), LANE - phase, 1)
                tbuf[pl.ds(8 * n * STRIDE + 4 * g + e, 8, stride=STRIDE), :] = value

    packed = {}

    def tile(k):
        if k not in packed:
            packed[k] = tbuf[k * STRIDE : k * STRIDE + 16, :].astype(bf16)
        return packed[k]

    lane16 = lax.broadcasted_iota(jnp.int32, (16, LANE), 1)
    here = pl.ds(pl.multiple_of(step * 16, 16), 16)
    for dx, dy, d0, count in blocks():
        tile0, phase = divmod(d0 * COEF, LANE)
        if dx in OUTER:
            ref = oa.at[OUTER.index(dx), (OUTER + INNER).index(dy)]
        elif dy in OUTER:
            ref = ob.at[INNER.index(dx), OUTER.index(dy)]
        else:
            ref = oc.at[INNER.index(dx), INNER.index(dy)]
        for t in range(up(count * COEF, LANE) // LANE):
            value = tile(tile0 + t)
            if phase:
                after = tile(min(tile0 + t + 1, KT - 1))
                value = pltpu.roll(jnp.where(lane16 >= phase, value, after), LANE - phase, 1)
            ref[here, t * LANE : (t + 1) * LANE] = value


def relayout(flat, me, step0, steps, grant):
    nrows = flat.shape[0] // LANE
    rows = flat.reshape(nrows, LANE)
    shapes = tuple((a, b, 16 * steps, c) for a, b, c in PIECES)
    return call(
        functools.partial(relayout_kernel, nrows, step0, steps),
        tuple(jax.ShapeDtypeStruct(s, bf16) for s in shapes),
        grant,
        1 << 20,
        steps << 21,
        grid_spec=pltpu.PrefetchScalarGridSpec(
            num_scalar_prefetch=1,
            grid=(steps,),
            in_specs=[HBM, pl.BlockSpec((16, LANE), lambda i, h: (nrows // 16, 0))],
            out_specs=(VMEM,) * len(shapes),
            scratch_shapes=[
                pltpu.VMEM((steps, 4, CHUNK, LANE), bf16),
                pltpu.VMEM((4, CHUNK + 16, LANE), f32),
                pltpu.VMEM((KT * STRIDE, LANE), f32),
                pltpu.SemaphoreType.DMA((steps, 4, 2)),
            ],
        ),
    )(me, rows, rows)


GROUP = 16


def square(flat, out):
    per = GROUP * COEF // LANE
    groups = flat.shape[0] // per
    lane = lax.broadcasted_iota(jnp.int32, (groups, LANE), 1)
    for r in range(GROUP):
        first, phase = divmod(r * COEF, LANE)
        got = []
        for t in range(3):
            row = min(first + t, per - 1)
            got.append(flat[pl.ds(row, groups, stride=per), :])
        for t in range(2):
            value = got[t]
            if phase:
                value = jnp.where(lane >= phase, got[t], got[t + 1])
                value = pltpu.roll(value, LANE - phase, 1)
            out[t, pl.ds(r, groups, stride=GROUP), :] = value


def operators_kernel(io, rows):
    m2m, l2l, uc2e, dc2e, lattice, column = io.ins
    w_both, coarse, d_hi, d_lo = io.outs
    scale = 1.0 / (4.0 * math.pi)
    coarse[32], coarse[33] = split(lattice[...])
    first = split(uc2e[...] * scale)

    plane = split(column[...])

    def side_by_side(pieces):
        wide = []
        for piece in pieces:
            high, low = split(dot3(split(piece), plane)[:, 8 : 8 + FEATURES])
            wide += [piece, high.astype(f32), low.astype(f32)]
            wide.append(jnp.zeros((COEF, CPAD - COEF - 2 * FEATURES), f32))
        return jnp.concatenate([w for w in wide if w.shape[1]], axis=1)

    def matrix(o):
        at = slice(o * COEF, (o + 1) * COEF)
        return jnp.concatenate([rows[0, at], rows[1, at, 0 : COEF - LANE]], axis=1)

    io.wait(0)
    square(m2m, rows)
    pieces = []
    for o in range(8):
        high, low = split(matrix(o))
        coarse[o], coarse[8 + o] = high, low
        pieces.append(dot3((high, low), first))
    upward = side_by_side(pieces)
    io.wait(1)
    square(l2l, rows)
    pieces = []
    for o in range(8):
        value = matrix(o)
        coarse[16 + o], coarse[24 + o] = split(value)
        pieces.append(jnp.transpose(value) * scale)
    w_both[...] = jnp.concatenate([upward, side_by_side(pieces)], axis=0).astype(bf16)
    high, low = split(dc2e[...])
    i = lax.broadcasted_iota(jnp.int32, (COEF, ROWS), 0)
    r = lax.broadcasted_iota(jnp.int32, (COEF, ROWS), 1)
    for h in range(2):
        here = (i == (r >> 2) * 8 + 4 * h + (r & 3)) & (r < 4 * NG)
        here = jnp.where(here, 1.0, 0.0).astype(bf16)
        d_hi[h] = dot(high, here).astype(bf16)
        d_lo[h] = dot(low, here).astype(bf16)


def route_kernel(own, cap, n_top, io):
    pos, dens, slot, leaf = io.ins
    out, entries = io.outs
    points = pos.shape[1]
    owners = out.shape[0]
    slots = slot[...]
    owner = slots // own
    inside = slots - owner * own
    hit = owner == lax.broadcasted_iota(jnp.int32, (owners, points), 0)
    hit = jnp.where(hit, 1.0, 0.0)
    hit16 = hit.astype(bf16)
    row = lax.broadcasted_iota(jnp.int32, (LANE, LANE), 0)
    col = lax.broadcasted_iota(jnp.int32, (LANE, LANE), 1)
    before = jnp.where(row < col, 1.0, 0.0).astype(bf16)
    every = jnp.ones((LANE, LANE), bf16)
    total = jnp.zeros((owners, LANE), f32)
    ranks = []
    for t in range(points // LANE):
        part = hit16[:, t * LANE : (t + 1) * LANE]
        ranks.append(total + dot(part, before))
        total = total + dot(part, every)
    rank = jnp.sum(hit * jnp.concatenate(ranks, axis=1), axis=0, keepdims=True)
    entry = owner * cap + rank.astype(jnp.int32)
    entries[...] = entry
    inside_hi = inside // 64
    value = jnp.concatenate([pos[...], dens[...]], axis=0)
    width = value.shape[0]
    high, low = split(value)
    ones = jnp.ones((1, points), f32)
    high = jnp.concatenate(
        [high.astype(f32), inside_hi.astype(f32), (inside - 64 * inside_hi).astype(f32), ones]
        + [jnp.zeros((16 - width - 3, points), f32)],
        axis=0,
    )
    low = jnp.concatenate([low.astype(f32), jnp.zeros((16 - width, points), f32)], axis=0)
    payload = jnp.concatenate([high, low], axis=0).astype(bf16)
    block = max(cap, LANE)
    per = DENS // n_top
    leaves = leaf[...].astype(f32)
    leaves = [leaves[r : r + 1] for r in range(leaves.shape[0])]
    lanes = leaf.shape[1]
    for o in range(owners * cap // block):
        there = entry == o * block + lax.broadcasted_iota(jnp.int32, (block, points), 0)
        there = jnp.where(there, 1.0, 0.0).astype(bf16)
        got = dot(payload, there, NT)
        value = got[0:width] + got[16 : 16 + width]
        where = got[width : width + 1] * 64.0 + got[width + 1 : width + 2]
        valid = got[width + 2 : width + 3]
        for q in range(n_top):
            rows = [value[r : r + 1] for r in range(3)] + [where, valid]
            rows += [value[3 + per * q + k : 4 + per * q + k] for k in range(per)]
            for i in range(block // cap):
                at = o * (block // cap) + i
                for r, value_row in enumerate(rows):
                    out[at, q, :, r * cap : (r + 1) * cap] = value_row[:, i * cap : (i + 1) * cap]
                for r, value_row in enumerate(leaves):
                    base = len(rows) * cap + r * lanes
                    out[at, q, :, base : base + lanes] = value_row


def restore_kernel(n_top, io):
    got, entries = io.ins
    out = io.outs[0]
    devices = got.shape[0]
    per = out.shape[0] // n_top
    cap = got.shape[2] // per
    points = out.shape[1]
    block = max(cap, PB)
    total = jnp.zeros((2 * out.shape[0], points), f32)
    for o in range(devices // n_top * cap // block):
        count = block // cap
        value = []
        for q in range(n_top):
            for k in range(per):
                pieces = []
                for i in range(count):
                    row = (o * count + i) * n_top + q
                    pieces.append(got[row, :, k * cap : (k + 1) * cap])
                value.append(jnp.concatenate(pieces, axis=1))
        high, low = split(jnp.concatenate(value, axis=0))
        both = jnp.concatenate([high.astype(f32), low.astype(f32)], axis=0).astype(bf16)
        at = o * block + lax.broadcasted_iota(jnp.int32, (block, points), 0)
        total = total + dot(both, jnp.where(entries[...] == at, 1.0, 0.0).astype(bf16))
    out[...] = total[0 : out.shape[0]] + total[out.shape[0] :]


def octant_product(pos, octant, surf, oper):
    squared = None
    for d in range(3):
        spacing = surf[d] - pos[d : d + 1]
        squared = spacing * spacing if squared is None else squared + spacing * spacing
    value = lax.rsqrt(squared)
    round_pos = pos.astype(bf16).astype(f32)
    value = value - surf[3]
    for d in range(3):
        value = value - surf[4 + d] * round_pos[d : d + 1]
    features = [jnp.ones_like(round_pos[0:1]), round_pos]
    blank = jnp.zeros((CPAD - COEF - 2 * FEATURES, value.shape[1]), f32)
    value = [value] + features + features + [blank]
    value = jnp.concatenate([v for v in value if v.shape[0]], axis=0).astype(bf16)
    masks = [jnp.where(octant == o, 1.0, 0.0).astype(bf16) for o in range(8)]
    return dot(oper[...], jnp.concatenate([value * m for m in masks], axis=0))


TURNED = (((0,), (0,)), ((), ()))


def look_up(index, table):
    lanes, rows = table.shape[0] // 2, table.shape[1]
    width = index.shape[1]
    at_row = index // lanes
    at_lane = index - at_row * lanes
    there = at_row == lax.broadcasted_iota(jnp.int32, (rows, width), 0)
    got = dot(table, jnp.where(there, 1.0, 0.0).astype(bf16))
    mine = at_lane == lax.broadcasted_iota(jnp.int32, (lanes, width), 0)
    first = jnp.sum(jnp.where(mine, got[0:lanes], 0.0), axis=0, keepdims=True)
    return first, jnp.sum(jnp.where(mine, got[lanes:], 0.0), axis=0, keepdims=True)


def fill_surface(surf, column):
    for i, lane in enumerate((0, 1, 2, 8, 9, 10, 11)):
        surf[i] = jnp.broadcast_to(column[:, lane : lane + 1], surf.shape[1:])


def morton_place(box):
    place = jnp.zeros_like(box)
    for b in range(LEVEL):
        digit = box >> (3 * b)
        place = place + ((((digit >> 2) & 1) << (2 * LEVEL + b)))
        place = place + ((((digit >> 1) & 1) << (LEVEL + b)) + ((digit & 1) << b))
    return place


def points_kernel(n_top, box_cap, io, offsets, buf, surf, octants, outgoing):
    got, column, oper = io.ins[:3]
    out, field, place = io.outs
    sources = got.shape[0]
    own = field.shape[1]
    dens = out.shape[1] // box_cap
    points = own // n_top
    cap = 2 * points * n_top // sources
    leaf_at = (5 + dens) * cap
    lanes = min(cap, LANE)
    wide = up(cap, LANE)
    me = io.scalars[0][0]
    buf[...] = jnp.zeros_like(buf)
    fill_surface(surf, column)
    io.wait(0)

    def put(i, offset):
        values = []
        for s in range(STRIP):
            pieces = [got[i * STRIP + s, :, r * cap : (r + 1) * cap] for r in range(5 + dens)]
            pieces.append(jnp.zeros((3 - dens, cap), f32))
            values.append(jnp.concatenate(pieces, axis=0))
        counts = [jnp.sum(v[4:5]).astype(jnp.int32) for v in values]
        for s, (value, count) in enumerate(zip(values, counts)):
            offsets[i * STRIP + s] = offset
            value = jnp.concatenate([value, jnp.zeros((8, wide + LANE - cap), f32)], axis=1)
            tile = offset // LANE
            value = pltpu.roll(value, offset - tile * LANE, 1)
            at = pl.ds(pl.multiple_of(tile * LANE, LANE), wide + LANE)
            buf[:, at] = buf[:, at] + value
            offset = offset + count
        return offset

    lax.fori_loop(0, sources // STRIP, put, jnp.int32(0))
    leaf = []
    for t in range(n_top):
        for r in range(points // lanes):
            leaf.append(got[me * n_top + t, :, leaf_at + r * lanes : leaf_at + (r + 1) * lanes])
    leaf = jnp.concatenate(leaf, axis=0).astype(jnp.int32)
    first = leaf[0:1, 0:1] >> 3
    offsets[sources] = jnp.sum(first.astype(f32)).astype(jnp.int32)
    io.wait(2)
    table = jnp.concatenate([(leaf >> 3) - first, leaf & 7], axis=1).astype(f32)
    table = jnp.transpose(table).astype(bf16)
    out_rows = out.shape[1]

    blocks_of = own // PB

    def spot(j):
        return pl.ds(pl.multiple_of(j * PB, PB), PB)

    def find(j, carry):
        to = spot(j)
        box, octant = look_up(buf[3:4, to].astype(jnp.int32), table)
        place[:, to] = box.astype(jnp.int32)
        octants[:, to] = octant
        return carry

    lax.fori_loop(0, blocks_of, find, 0, unroll=UNROLL_FIND)

    def apply(j, carry):
        to = spot(j)
        both = octant_product(buf[0:3, to], octants[:, to], surf, oper)
        outgoing[:, to] = both[0:COEF]
        field[:, to] = both[COEF : 2 * COEF]
        return carry

    lax.fori_loop(0, blocks_of, apply, 0, unroll=UNROLL_APPLY)

    def gather(j, total):
        to = spot(j)
        high, low = split(outgoing[:, to])
        rows = []
        at = lax.broadcasted_iota(jnp.int32, (box_cap, PB), 0)
        here = place[:, to] == at
        for k in range(out_rows // box_cap):
            rows.append(jnp.where(here, buf[5 + k : 6 + k, to], 0.0))
        a_high, a_low = split(jnp.concatenate(rows, axis=0))
        both = dot(jnp.concatenate([high, low], axis=0), a_high, NT)
        return total + both[0:COEF] + both[COEF : 2 * COEF] + dot(high, a_low, NT)

    total = jnp.zeros((COEF, out_rows), f32)
    total = lax.fori_loop(0, blocks_of, gather, total, unroll=UNROLL_GATHER)
    digits = jnp.concatenate([first >> 3, first & 7], axis=0).astype(f32)
    digits = jnp.broadcast_to(digits, (2, out_rows))
    blank = jnp.zeros((out.shape[0] - COEF - 2, out_rows), f32)
    out[...] = jnp.concatenate([total, digits, blank], axis=0).astype(bf16)


def box_ids(parts, dens):
    ids = []
    for part in parts:
        digits = part[COEF - 8 : COEF + 8, :].astype(f32)[8:16, 0:1].astype(jnp.int32)
        first = digits[0:1] * 8 + digits[1:2]
        at = lax.broadcasted_iota(jnp.int32, (1, part.shape[1] // dens), 1)
        ids.append(first + at)
    return jnp.concatenate(ids, axis=1)


def all_parts(parts, k, dens):
    width = parts[0].shape[1] // dens
    return jnp.concatenate([p[0:COEF, k * width : (k + 1) * width] for p in parts], axis=1)


def translate_kernel(slabs, dens, io, xs, xin, acc):
    parts = io.ins[:-6]
    first, rest = io.ins[-6:-3], io.ins[-3:]
    out = io.outs[0]
    x0 = (io.scalars[0][0] // 2 * 2) * SIDE // len(parts)
    ids = box_ids(parts, dens)
    place = morton_place(ids)
    place = (((place >> 6) - x0 + REACH) & 7) * 64 + (place & 63)
    place = jnp.where(ids < BOXES4, place, -1)
    at = lax.broadcasted_iota(jnp.int32, (BOXES4, ids.shape[1]), 0)
    there = jnp.where(at == place, 1.0, 0.0).astype(bf16)
    columns = dens * PLANE
    for k in range(dens):
        low = dot(there, all_parts(parts, k, dens), NT)
        low = low.astype(bf16).astype(f32)
        for s in range(7 + slabs - 1):
            slab = low[s * PLANE : (s + 1) * PLANE].reshape(SIDE, SIDE, COEF)
            shifted = {}
            for dz in SHIFTS:
                if dz == 0:
                    moved = slab
                else:
                    cut = dz % SIDE
                    moved = jnp.concatenate([slab[:, cut:], slab[:, :cut]], axis=1)
                shifted[dz] = moved.reshape(PLANE, COEF)
            rows = pl.ds(s * columns + k * PLANE, PLANE)
            pad = [jnp.zeros((PLANE, WFULL - 7 * COEF), f32)]
            xs[rows, :] = jnp.concatenate([shifted[z] for z in SHIFTS] + pad, axis=1).astype(bf16)
            pad = [jnp.zeros((PLANE, WIN - 4 * COEF), f32)]
            xin[rows, :] = jnp.concatenate([shifted[z] for z in OUTER] + pad, axis=1).astype(bf16)

    def rows_of(i, j):
        value = jnp.concatenate([first[i][j], rest[i][j]], axis=1)
        return value.reshape(-1, value.shape[2])

    n_out = len(OUTER) * ROWS
    n_all = len(SHIFTS) * ROWS
    for i, dx in enumerate(OUTER + INNER):
        rows = pl.ds((dx + REACH) * columns, slabs * columns)
        source = xs[rows, :]
        if dx in OUTER:
            term = dot(rows_of(0, OUTER.index(dx)), source, NT)
            if i == 0:
                acc[...] = term
            else:
                acc[...] += term
        else:
            acc[0:n_out] += dot(rows_of(1, INNER.index(dx)), source, NT)
            acc[n_out:n_all] += dot(rows_of(2, INNER.index(dx)), xin[rows, :], NT)
    lane = lax.broadcasted_iota(jnp.int32, (ROWS, LANE), 1)
    for t in range(slabs * columns // LANE):
        total = jnp.zeros((ROWS, LANE), f32)
        for i, dy in enumerate(OUTER + INNER):
            value = acc[i * ROWS : (i + 1) * ROWS, t * LANE : (t + 1) * LANE]
            by = SIDE * (dy % SIDE)
            if by:
                near = pltpu.roll(value, LANE - by, 1)
                far = pltpu.roll(value, PLANE - by, 1)
                value = jnp.where((lane & (PLANE - 1)) < PLANE - by, near, far)
            total = total + value
        out[:, t * LANE : (t + 1) * LANE] = total.astype(out.dtype)


def coarse_kernel(io):
    out = io.outs[0]
    parts = io.ins[:-1]
    opers = io.ins[-1]
    dens = out.shape[0]
    box = ids = box_ids(parts, dens)
    place = ((box & 7) << 6) + (box & 56) + (box >> 6)
    place = jnp.where(box < BOXES4, place, -1)
    at = lax.broadcasted_iota(jnp.int32, (BOXES4, ids.shape[1]), 0)
    there = jnp.where(at == place, 1.0, 0.0).astype(bf16)
    level = [dot(there, all_parts(parts, k, dens), NT) for k in range(dens)]

    io.wait(*range(len(io.ins)))

    for _ in range(LEVEL):
        count = level[0].shape[0] // 8
        total = None
        for o in range(8):
            rows = jnp.concatenate([v[o * count : (o + 1) * count] for v in level], axis=0)
            term = dot3_rows(split(rows), (opers[o], opers[8 + o]), NT)
            total = term if total is None else total + term
        level = [total[k * count : (k + 1) * count] for k in range(dens)]
    rows = jnp.concatenate(level, axis=0)
    rows = dot3(split(rows), (opers[32], opers[33]), NT)
    level = [rows[k : k + 1] for k in range(dens)]
    for _ in range(LEVEL - 1):
        count = level[0].shape[0]
        rows = split(jnp.concatenate(level, axis=0))
        children = [dot3_rows(rows, (opers[16 + o], opers[24 + o]), NT) for o in range(8)]
        level = [
            jnp.concatenate([c[k * count : (k + 1) * count] for c in children], axis=0)
            for k in range(dens)
        ]
    count = level[0].shape[0]
    rows = split(jnp.concatenate(level, axis=0))
    children = [dot3((opers[16 + o], opers[24 + o]), rows, NT) for o in range(8)]
    for k in range(dens):
        pieces = [c[:, k * count : (k + 1) * count] for c in children]
        out[k] = jnp.concatenate(pieces, axis=1)


def evaluate_kernel(slabs, step, window, io, stack, found):
    n = SIDE // slabs
    checks = io.ins[: 2 * n]
    d_hi, d_lo, lattice, place, field = io.ins[2 * n :]
    offsets = io.scalars[1]
    out = io.outs[0]
    core = io.scalars[0][0] & 1
    group = io.scalars[0][0] // step
    dens = lattice.shape[0]
    sources, cap = out.shape[0], out.shape[2] // dens
    lane = lax.broadcasted_iota(jnp.int32, (COEF, LANE), 1)
    mine = jnp.concatenate([d_hi[core], d_lo[core]], axis=0)
    other = jnp.concatenate([d_hi[1 - core], d_lo[1 - core]], axis=0)
    for m in range(n):
        value = dot(mine, checks[2 * m][...]) + dot(other, checks[2 * m + 1][...])
        value = value[0:COEF] + value[COEF : 2 * COEF]
        if slabs == 2:
            a, b = value[:, 0:LANE], value[:, LANE : 2 * LANE]
            half = LANE // 2
            pieces = [
                jnp.where(lane < half, a, pltpu.roll(b, half, 1)),
                jnp.where(lane < half, pltpu.roll(a, half, 1), b),
            ]
        else:
            pieces = [value[:, k * PLANE : (k + 1) * PLANE] for k in range(dens)]
        width = slabs * PLANE
        for k in range(dens):
            high, low = split(pieces[k])
            rows = pl.ds(k * CPAD, COEF)
            stack[rows, m * width : (m + 1) * width] = high.astype(f32)
            rows = pl.ds((dens + k) * CPAD, COEF)
            stack[rows, m * width : (m + 1) * width] = low.astype(f32)
    box = offsets[sources] + lax.broadcasted_iota(jnp.int32, (1, window), 1)
    want = morton_place(box) ^ (group * (slabs * PLANE))
    turned = BOXES4 + ((box & 7) << 6) + (box & 56) + (box >> 6)
    at = lax.broadcasted_iota(jnp.int32, (2 * BOXES4, window), 0)
    pick = ((at == want) | (at == turned)) & (box < BOXES4)
    pick = jnp.where(pick, 1.0, 0.0).astype(bf16)
    for k in range(dens):
        high, low = split(lattice[k])
        stack[pl.ds(k * CPAD, COEF), BOXES4:] = high.astype(f32)
        stack[pl.ds((dens + k) * CPAD, COEF), BOXES4:] = low.astype(f32)
    half = dens * CPAD
    local = dot(stack[...].astype(bf16), pick)
    high, low = split(local[0:half] + local[half:])
    local = jnp.concatenate([high, low], axis=1)
    found[:, place.shape[1] :] = jnp.zeros((8, found.shape[1] - place.shape[1]), f32)
    io.wait(*range(len(io.ins)))

    def block(j, carry):
        at = pl.ds(pl.multiple_of(j * PB, PB), PB)
        there = place[:, at] == lax.broadcasted_iota(jnp.int32, (window, PB), 0)
        there = jnp.where(there, 1.0, 0.0)
        there = jnp.concatenate([there, there], axis=0).astype(bf16)
        got = dot(local, there)
        mine = field[:, at]
        rows = []
        for k in range(dens):
            value = got[k * CPAD : k * CPAD + COEF]
            rows.append(jnp.sum(value * mine, axis=0, keepdims=True))
        rows.append(jnp.zeros((8 - dens, PB), f32))
        found[:, at] = jnp.concatenate(rows, axis=0)
        return carry

    lax.fori_loop(0, place.shape[1] // PB, block, 0, unroll=8)

    wide = up(cap, LANE) + LANE

    @pl.loop(0, sources // STRIP)
    def _(i):
        for s in range(STRIP):
            offset = offsets[i * STRIP + s]
            tile = offset // LANE
            value = found[:, pl.ds(pl.multiple_of(tile * LANE, LANE), wide)]
            value = pltpu.roll(value, wide - (offset - tile * LANE), 1)
            for k in range(dens):
                out[i * STRIP + s, :, k * cap : (k + 1) * cap] = value[k : k + 1, 0:cap]


def shift_by(axis, value, distance):
    size = lax.axis_size(axis)
    return lax.ppermute(value, axis, [(i, i ^ distance) for i in range(size)])


def gather_by(value, distances, beside):
    got = {m: shift_by("pts", value, m) if m else value for m in distances if m < 2 or m % 2 == 0}
    got, beside = lax.optimization_barrier((got, beside))
    got.update({m + 1: shift_by("pts", got[m], 1) for m in list(got) if m % 2 == 0 and m})
    return [got[m] for m in distances], beside


def per_device(
    local_pos, densities, morton_slot, slot_leaf, uc2e, m2m, m2l_ops, dc2e, lattice, l2l
):
    n_pts = lax.axis_size("pts")
    n_top = lax.axis_size("top")
    me = jnp.stack([lax.axis_index("pts"), lax.axis_index("top")]).astype(jnp.int32)
    points = local_pos.shape[1]
    own = points * n_top
    cap = 2 * points // n_pts
    box_cap = 2 * BOXES4 // n_pts
    dens = DENS // n_top
    slabs = max(1, 2 * SIDE // n_pts)
    coef = uc2e.shape[0]
    sources = n_pts * n_top
    lanes = min(cap, LANE)
    width = (5 + dens) * cap + points

    def shape(*dims, dtype=bf16):
        return jax.ShapeDtypeStruct(dims, dtype)

    outgoing, entries = run(
        functools.partial(route_kernel, own, cap, n_top),
        [],
        [
            local_pos,
            densities,
            morton_slot.reshape(1, points),
            slot_leaf.reshape(points // lanes, lanes),
        ],
        [shape(n_pts, n_top, 1, width, dtype=f32), shape(1, points, dtype=jnp.int32)],
        1 << 27,
        stays=(1,),
        grant=GRANT_FIRST,
    )
    outgoing = outgoing.reshape(sources, 1, width)
    incoming = lax.all_to_all(outgoing, ("pts", "top"), split_axis=0, concat_axis=0, tiled=True)

    flat = (-1, LANE)
    column = jnp.asarray(column_table())
    w_both, opers, *halves = run(
        operators_kernel,
        [],
        [m2m.reshape(flat), l2l.reshape(flat), uc2e, dc2e, lattice, column],
        [shape(2 * coef, 8 * CPAD), shape(34, coef, coef)] + [shape(2, coef, ROWS)] * 2,
        1 << 30,
        here=range(6),
        stays=range(4),
        scratch=[pltpu.VMEM((2, 8 * coef, LANE), f32)],
    )
    first = relayout(m2l_ops, me, 0, EARLY, GRANT_EARLY)
    incoming, first = lax.optimization_barrier((incoming, first))

    partial, field, place, offsets = run(
        functools.partial(points_kernel, n_top, box_cap),
        [me],
        [incoming, column, w_both],
        [
            shape(up(coef + 2, 16), dens * box_cap),
            shape(coef, own, dtype=f32),
            shape(1, own, dtype=jnp.int32),
        ],
        8 << 30,
        here=range(3),
        stays=range(3),
        numbers=[shape(sources + 1, dtype=jnp.int32)],
        scratch=[
            pltpu.VMEM((8, up(own + up(cap, LANE) + LANE, PB)), f32),
            pltpu.VMEM((3 + FEATURES, coef, PB), f32),
            pltpu.VMEM((1, own), f32),
            pltpu.VMEM((coef, own), f32),
        ],
    )
    later, flat_ops = lax.optimization_barrier((partial, m2l_ops))
    rest = relayout(flat_ops, me, EARLY, STEPS - EARLY, GRANT_LATER)
    parts, rest = gather_by(later, range(n_pts), rest)

    columns = dens * PLANE
    (checks,) = run(
        functools.partial(translate_kernel, slabs, dens),
        [me],
        [*parts, *first, *rest],
        [shape(ROWS, slabs * columns)],
        8 << 30,
        here=range(n_pts + 6),
        stays=(0,),
        scratch=[
            pltpu.VMEM(((7 + slabs - 1) * columns, WFULL), bf16),
            pltpu.VMEM(((7 + slabs - 1) * columns, WIN), bf16),
            pltpu.VMEM((7 * ROWS, slabs * columns), f32),
        ],
    )
    (lattice4,) = run(
        coarse_kernel,
        [],
        [*parts, opers],
        [shape(dens, coef, BOXES4, dtype=f32)],
        4 << 30,
        here=range(n_pts + 1),
        stays=(0,),
    )
    step = n_pts // SIDE * slabs
    distances = [step * m + c for m in range(SIDE // slabs) for c in range(2)]
    gathered, lattice4 = gather_by(checks, distances, lattice4)

    (reply,) = run(
        functools.partial(evaluate_kernel, slabs, step, box_cap),
        [me, offsets],
        [*gathered, *halves, lattice4, place, field],
        [shape(sources, 1, dens * cap, dtype=f32)],
        4 << 30,
        here=range(len(gathered) + 5),
        stays=(0,),
        scratch=[
            pltpu.VMEM((2 * dens * CPAD, 2 * BOXES4), f32),
            pltpu.VMEM((8, own + up(cap, LANE) + LANE), f32),
        ],
    )
    returned = lax.all_to_all(reply, ("pts", "top"), split_axis=0, concat_axis=0, tiled=True)
    (out,) = run(
        functools.partial(restore_kernel, n_top),
        [],
        [returned, entries],
        [shape(DENS, points, dtype=f32)],
        1 << 28,
        here=range(2),
    )
    return out


def solution(mesh):
    split_all = P(None, ("pts", "top"))
    placed = (split_all, split_all, P(("pts", "top")), P(("pts", "top"))) + (P(),) * 6
    return jax.shard_map(
        per_device, mesh=mesh, in_specs=placed, out_specs=split_all, check_vma=False
    )
```

```python
import functools
import math

import jax
import jax.numpy as jnp
import numpy as np
from jax import lax
from jax.experimental import pallas as pl
from jax.experimental.pallas import tpu as pltpu
from jax.sharding import PartitionSpec as P

LEVEL = 3
EDGE = 6
DENS = 8
SIDE = 2**LEVEL
BOXES4 = SIDE**3
PLANE = SIDE * SIDE
LANE = 128
REACH = 3
SHIFTS = list(range(-REACH, REACH + 1))
OUTER = [s for s in SHIFTS if abs(s) >= 2]
INNER = [s for s in SHIFTS if abs(s) < 2]
bf16 = jnp.bfloat16
f32 = jnp.float32
NN = (((1,), (0,)), ((), ()))
NT = (((1,), (1,)), ((), ()))


def up(value, multiple):
    return -(-value // multiple) * multiple


def surface_table():
    grid_vals = np.linspace(-1.0, 1.0, EDGE)
    points_list = []
    for a in range(EDGE):
        for b in range(EDGE):
            for c in range(EDGE):
                if min(a, b, c) == 0 or max(a, b, c) == EDGE - 1:
                    points_list.append([grid_vals[a], grid_vals[b], grid_vals[c]])
    return np.array(points_list, dtype=np.float32).T


COEF = surface_table().shape[1]
OFFSETS = (2 * REACH + 1) ** 3 - 27
FEATURES = 4
PB = 256
STRIP = 16
UNROLL_FIND, UNROLL_APPLY, UNROLL_GATHER = 16, 16, 16
GRANT = 28
GRANT_FIRST = 60
GRANT_EARLY = 52
GRANT_LATER = 49
CPAD = up(COEF, 32)


def column_table():
    surface = 1.25 * surface_table().astype(np.float64)
    grid = np.linspace(-0.9, 0.9, 10)
    points = np.stack(np.meshgrid(grid, grid, grid, indexing="ij")).reshape(3, -1)
    values = 1.0 / np.sqrt(((surface[:, :, None] - points[:, None, :]) ** 2).sum(axis=0))
    scale = (points**2).sum(axis=1)
    out = np.zeros((surface.shape[1], LANE), np.float32)
    out[:, 0:3] = (np.float32(1.25) * surface_table()).T
    out[:, 8] = values.mean(axis=1)
    out[:, 9:12] = values @ points.T / scale
    return out


def blocks():
    out, position = [], 0
    for dx in SHIFTS:
        for dy in SHIFTS:
            count = sum(max(abs(dx), abs(dy), abs(dz)) >= 2 for dz in SHIFTS)
            out.append((dx, dy, position, count))
            position += count
    return out


def dot(a, b, dims=NN):
    return lax.dot_general(a, b, dims, preferred_element_type=f32)


def split(value):
    high = value.astype(bf16)
    return high, (value - high.astype(f32)).astype(bf16)


def dot3(a, b, dims=NN):
    return dot(a[0], b[0], dims) + dot(a[1], b[0], dims) + dot(a[0], b[1], dims)


def dot3_rows(a, b, dims=NN):
    rows = a[0].shape[0]
    both = jnp.concatenate([x.astype(f32) for x in a], axis=0).astype(bf16)
    both = dot(both, b[0], dims)
    return both[0:rows] + both[rows : 2 * rows] + dot(a[0], b[1], dims)


def call(kernel, out_shape, mib, flops, bytes_accessed=1 << 20, **kw):
    return pl.pallas_call(
        kernel,
        out_shape=out_shape,
        compiler_params=pltpu.CompilerParams(vmem_limit_bytes=mib << 20),
        cost_estimate=pl.CostEstimate(
            flops=flops, bytes_accessed=bytes_accessed, transcendentals=0
        ),
        **kw,
    )


SMEM = pl.BlockSpec(memory_space=pltpu.SMEM)
VMEM = pl.BlockSpec(memory_space=pltpu.VMEM)
HBM = pl.BlockSpec(memory_space=pltpu.HBM)

class Buffers:
    def __init__(self, scalars, ins, outs, moved, sources, targets, sem_in, sem_out):
        self.scalars, self.ins, self.outs, self.targets = scalars, ins, outs, targets
        self.sem_out = sem_out
        self.coming, self.going, self.waited = {}, {}, set()
        for i in moved:
            self.coming[i] = pltpu.make_async_copy(sources[i], ins[i], sem_in.at[i])
            self.coming[i].start()

    def wait(self, *which):
        for i in which:
            if i in self.coming and i not in self.waited:
                self.waited.add(i)
                self.coming[i].wait()

    def send(self, *which):
        for i in which:
            if i not in self.going:
                copy = pltpu.make_async_copy(self.outs[i], self.targets[i], self.sem_out.at[i])
                copy.start()
                self.going[i] = copy


def run(kernel, scalars, ins, outs, flops, scratch=(), late=(), here=(), stays=(), numbers=(), grant=GRANT):
    n_s, n_i, n_o, n_n = len(scalars), len(ins), len(outs), len(numbers)
    moved_in = [i for i in range(n_i) if i not in here]
    moved_out = [i for i in range(n_o) if i not in stays]

    def body(*refs):
        refs = list(refs)
        take = lambda count: [refs.pop(0) for _ in range(count)]
        given, sources, targets, counts = take(n_s), take(n_i), take(n_o), take(n_n)
        in_refs, out_refs = list(sources), list(targets)
        for i in moved_in:
            in_refs[i] = refs.pop(0)
        for i in moved_out:
            out_refs[i] = refs.pop(0)
        io = Buffers(given, in_refs, out_refs, moved_in, sources, targets, *take(2))
        io.wait(*[i for i in moved_in if i not in late])
        kernel(io, *counts, *refs)
        io.wait(*moved_in)
        io.send(*moved_out)
        for i in moved_out:
            io.going[i].wait()

    return call(
        body,
        tuple(outs) + tuple(numbers),
        grant,
        flops,
        in_specs=[SMEM] * n_s + [VMEM if i in here else HBM for i in range(n_i)],
        out_specs=tuple(VMEM if i in stays else HBM for i in range(n_o)) + (SMEM,) * n_n,
        scratch_shapes=[pltpu.VMEM(ins[i].shape, ins[i].dtype) for i in moved_in]
        + [pltpu.VMEM(outs[i].shape, outs[i].dtype) for i in moved_out]
        + [pltpu.SemaphoreType.DMA((max(n, 1),)) for n in (n_i, n_o)]
        + list(scratch),
    )(*scalars, *ins)


HG = 4 * OFFSETS * COEF // LANE
KT = up(up(OFFSETS * COEF, LANE) // LANE, 8)
WFULL = up(7 * COEF, LANE)
WIN = up(4 * COEF, LANE)
NG = COEF // 8
STEPS = -(-NG // 4)
ROWS = 16 * STEPS
CHUNK = up(HG + 15, 16)
TAIL = 32
EARLY = 2
STRIDE = 17
PIECES = ((4, 7, WFULL), (3, 4, WFULL), (3, 3, WIN))


def relayout_kernel(nrows, step0, steps, me_ref, f_hbm, tail_ref, oa, ob, oc, inb, fbuf, tbuf, sem):
    step = pl.program_id(0)
    half = me_ref[0] & 1
    end16 = nrows // 16 * 16

    def start_row(st, g):
        return jnp.minimum(4 * (st + step0) + g, NG - 1) * (2 * HG) + half * HG

    def start(st, slot):
        for g in range(4):
            row = pl.multiple_of(start_row(st, g) // 16 * 16, 16)
            pltpu.make_async_copy(
                f_hbm.at[pl.ds(row, CHUNK - TAIL)],
                inb.at[slot, g, pl.ds(0, CHUNK - TAIL)],
                sem.at[slot, g, 0],
            ).start()
            last = row + CHUNK > end16

            @pl.when(jnp.logical_not(last))
            def _():
                pltpu.make_async_copy(
                    f_hbm.at[pl.ds(pl.multiple_of(row + CHUNK - TAIL, 16), TAIL)],
                    inb.at[slot, g, pl.ds(CHUNK - TAIL, TAIL)],
                    sem.at[slot, g, 1],
                ).start()


    def wait(st, slot):
        for g in range(4):
            row = pl.multiple_of(start_row(st, g) // 16 * 16, 16)
            pltpu.make_async_copy(
                f_hbm.at[pl.ds(row, CHUNK - TAIL)],
                inb.at[slot, g, pl.ds(0, CHUNK - TAIL)],
                sem.at[slot, g, 0],
            ).wait()
            last = row + CHUNK > end16

            @pl.when(jnp.logical_not(last))
            def _():
                pltpu.make_async_copy(
                    f_hbm.at[pl.ds(pl.multiple_of(row + CHUNK - TAIL, 16), TAIL)],
                    inb.at[slot, g, pl.ds(CHUNK - TAIL, TAIL)],
                    sem.at[slot, g, 1],
                ).wait()

            @pl.when(last)
            def _():
                row16 = lax.broadcasted_iota(jnp.int32, (16, LANE), 0)
                tail = jnp.where(row16 < nrows - end16, tail_ref[...].astype(f32), 0.0)
                inb[slot, g, CHUNK - TAIL : CHUNK - TAIL + 16] = tail.astype(bf16)

    slot = step

    @pl.when(step == 0)
    def _():
        fbuf[...] = jnp.zeros_like(fbuf)
        inb[:, :, CHUNK - 16 :] = jnp.zeros_like(inb[:, :, CHUNK - 16 :])
        for st in range(steps):
            start(st, st)

    wait(step, slot)
    lane = lax.broadcasted_iota(jnp.int32, (8, LANE), 1)
    for g in range(4):
        fbuf[g, 0:CHUNK] = inb[slot, g].astype(f32)
    for g in range(4):
        row = start_row(step, g)
        off = row - row // 16 * 16
        for e in range(4):
            first = OFFSETS * COEF * e
            phase = first % LANE

            @pl.loop(0, KT // 8, unroll=KT // 8)
            def _(n):
                base = off + first // LANE + 8 * n
                value = fbuf[g, pl.ds(base, 8), :]
                if phase:
                    after = fbuf[g, pl.ds(base + 1, 8), :]
                    value = pltpu.roll(jnp.where(lane >= phase, value, after), LANE - phase, 1)
                tbuf[pl.ds(8 * n * STRIDE + 4 * g + e, 8, stride=STRIDE), :] = value

    packed = {}

    def tile(k):
        if k not in packed:
            packed[k] = tbuf[k * STRIDE : k * STRIDE + 16, :].astype(bf16)
        return packed[k]

    lane16 = lax.broadcasted_iota(jnp.int32, (16, LANE), 1)
    here = pl.ds(pl.multiple_of(step * 16, 16), 16)
    for dx, dy, d0, count in blocks():
        tile0, phase = divmod(d0 * COEF, LANE)
        if dx in OUTER:
            ref = oa.at[OUTER.index(dx), (OUTER + INNER).index(dy)]
        elif dy in OUTER:
            ref = ob.at[INNER.index(dx), OUTER.index(dy)]
        else:
            ref = oc.at[INNER.index(dx), INNER.index(dy)]
        for t in range(up(count * COEF, LANE) // LANE):
            value = tile(tile0 + t)
            if phase:
                after = tile(min(tile0 + t + 1, KT - 1))
                value = pltpu.roll(jnp.where(lane16 >= phase, value, after), LANE - phase, 1)
            ref[here, t * LANE : (t + 1) * LANE] = value


def relayout(flat, me, step0, steps, grant):
    nrows = flat.shape[0] // LANE
    rows = flat.reshape(nrows, LANE)
    shapes = tuple((a, b, 16 * steps, c) for a, b, c in PIECES)
    return call(
        functools.partial(relayout_kernel, nrows, step0, steps),
        tuple(jax.ShapeDtypeStruct(s, bf16) for s in shapes),
        grant,
        1 << 20,
        steps << 21,
        grid_spec=pltpu.PrefetchScalarGridSpec(
            num_scalar_prefetch=1,
            grid=(steps,),
            in_specs=[HBM, pl.BlockSpec((16, LANE), lambda i, h: (nrows // 16, 0))],
            out_specs=(VMEM,) * len(shapes),
            scratch_shapes=[
                pltpu.VMEM((steps, 4, CHUNK, LANE), bf16),
                pltpu.VMEM((4, CHUNK + 16, LANE), f32),
                pltpu.VMEM((KT * STRIDE, LANE), f32),
                pltpu.SemaphoreType.DMA((steps, 4, 2)),
            ],
        ),
    )(me, rows, rows)


GROUP = 16


def square(flat, out):
    per = GROUP * COEF // LANE
    groups = flat.shape[0] // per
    lane = lax.broadcasted_iota(jnp.int32, (groups, LANE), 1)
    for r in range(GROUP):
        first, phase = divmod(r * COEF, LANE)
        got = []
        for t in range(3):
            row = min(first + t, per - 1)
            got.append(flat[pl.ds(row, groups, stride=per), :])
        for t in range(2):
            value = got[t]
            if phase:
                value = jnp.where(lane >= phase, got[t], got[t + 1])
                value = pltpu.roll(value, LANE - phase, 1)
            out[t, pl.ds(r, groups, stride=GROUP), :] = value


def operators_kernel(io, rows):
    m2m, l2l, uc2e, dc2e, lattice, column = io.ins
    w_both, coarse, d_hi, d_lo = io.outs
    scale = 1.0 / (4.0 * math.pi)
    coarse[32], coarse[33] = split(lattice[...])
    first = split(uc2e[...] * scale)

    plane = split(column[...])

    def side_by_side(pieces):
        wide = []
        for piece in pieces:
            high, low = split(dot3(split(piece), plane)[:, 8 : 8 + FEATURES])
            wide += [piece, high.astype(f32), low.astype(f32)]
            wide.append(jnp.zeros((COEF, CPAD - COEF - 2 * FEATURES), f32))
        return jnp.concatenate([w for w in wide if w.shape[1]], axis=1)

    def matrix(o):
        at = slice(o * COEF, (o + 1) * COEF)
        return jnp.concatenate([rows[0, at], rows[1, at, 0 : COEF - LANE]], axis=1)

    io.wait(0)
    square(m2m, rows)
    pieces = []
    for o in range(8):
        high, low = split(matrix(o))
        coarse[o], coarse[8 + o] = high, low
        pieces.append(dot3((high, low), first))
    upward = side_by_side(pieces)
    io.wait(1)
    square(l2l, rows)
    pieces = []
    for o in range(8):
        value = matrix(o)
        coarse[16 + o], coarse[24 + o] = split(value)
        pieces.append(jnp.transpose(value) * scale)
    w_both[...] = jnp.concatenate([upward, side_by_side(pieces)], axis=0).astype(bf16)
    high, low = split(dc2e[...])
    i = lax.broadcasted_iota(jnp.int32, (COEF, ROWS), 0)
    r = lax.broadcasted_iota(jnp.int32, (COEF, ROWS), 1)
    for h in range(2):
        here = (i == (r >> 2) * 8 + 4 * h + (r & 3)) & (r < 4 * NG)
        here = jnp.where(here, 1.0, 0.0).astype(bf16)
        d_hi[h] = dot(high, here).astype(bf16)
        d_lo[h] = dot(low, here).astype(bf16)


def route_kernel(own, cap, n_top, io):
    pos, dens, slot, leaf = io.ins
    out, entries = io.outs
    points = pos.shape[1]
    owners = out.shape[0]
    slots = slot[...]
    owner = slots // own
    inside = slots - owner * own
    hit = owner == lax.broadcasted_iota(jnp.int32, (owners, points), 0)
    hit = jnp.where(hit, 1.0, 0.0)
    hit16 = hit.astype(bf16)
    row = lax.broadcasted_iota(jnp.int32, (LANE, LANE), 0)
    col = lax.broadcasted_iota(jnp.int32, (LANE, LANE), 1)
    before = jnp.where(row < col, 1.0, 0.0).astype(bf16)
    every = jnp.ones((LANE, LANE), bf16)
    total = jnp.zeros((owners, LANE), f32)
    ranks = []
    for t in range(points // LANE):
        part = hit16[:, t * LANE : (t + 1) * LANE]
        ranks.append(total + dot(part, before))
        total = total + dot(part, every)
    rank = jnp.sum(hit * jnp.concatenate(ranks, axis=1), axis=0, keepdims=True)
    entry = owner * cap + rank.astype(jnp.int32)
    entries[...] = entry
    inside_hi = inside // 64
    value = jnp.concatenate([pos[...], dens[...]], axis=0)
    width = value.shape[0]
    high, low = split(value)
    ones = jnp.ones((1, points), f32)
    high = jnp.concatenate(
        [high.astype(f32), inside_hi.astype(f32), (inside - 64 * inside_hi).astype(f32), ones]
        + [jnp.zeros((16 - width - 3, points), f32)],
        axis=0,
    )
    low = jnp.concatenate([low.astype(f32), jnp.zeros((16 - width, points), f32)], axis=0)
    payload = jnp.concatenate([high, low], axis=0).astype(bf16)
    block = max(cap, LANE)
    per = DENS // n_top
    leaves = leaf[...].astype(f32)
    leaves = [leaves[r : r + 1] for r in range(leaves.shape[0])]
    lanes = leaf.shape[1]
    for o in range(owners * cap // block):
        there = entry == o * block + lax.broadcasted_iota(jnp.int32, (block, points), 0)
        there = jnp.where(there, 1.0, 0.0).astype(bf16)
        got = dot(payload, there, NT)
        value = got[0:width] + got[16 : 16 + width]
        where = got[width : width + 1] * 64.0 + got[width + 1 : width + 2]
        valid = got[width + 2 : width + 3]
        for q in range(n_top):
            rows = [value[r : r + 1] for r in range(3)] + [where, valid]
            rows += [value[3 + per * q + k : 4 + per * q + k] for k in range(per)]
            for i in range(block // cap):
                at = o * (block // cap) + i
                for r, value_row in enumerate(rows):
                    out[at, q, :, r * cap : (r + 1) * cap] = value_row[:, i * cap : (i + 1) * cap]
                for r, value_row in enumerate(leaves):
                    base = len(rows) * cap + r * lanes
                    out[at, q, :, base : base + lanes] = value_row


def restore_kernel(n_top, io):
    got, entries = io.ins
    out = io.outs[0]
    devices = got.shape[0]
    per = out.shape[0] // n_top
    cap = got.shape[2] // per
    points = out.shape[1]
    block = max(cap, PB)
    total = jnp.zeros((2 * out.shape[0], points), f32)
    for o in range(devices // n_top * cap // block):
        count = block // cap
        value = []
        for q in range(n_top):
            for k in range(per):
                pieces = []
                for i in range(count):
                    row = (o * count + i) * n_top + q
                    pieces.append(got[row, :, k * cap : (k + 1) * cap])
                value.append(jnp.concatenate(pieces, axis=1))
        high, low = split(jnp.concatenate(value, axis=0))
        both = jnp.concatenate([high.astype(f32), low.astype(f32)], axis=0).astype(bf16)
        at = o * block + lax.broadcasted_iota(jnp.int32, (block, points), 0)
        total = total + dot(both, jnp.where(entries[...] == at, 1.0, 0.0).astype(bf16))
    out[...] = total[0 : out.shape[0]] + total[out.shape[0] :]


def octant_product(pos, octant, surf, oper):
    squared = None
    for d in range(3):
        spacing = surf[d] - pos[d : d + 1]
        squared = spacing * spacing if squared is None else squared + spacing * spacing
    value = lax.rsqrt(squared)
    round_pos = pos.astype(bf16).astype(f32)
    value = value - surf[3]
    for d in range(3):
        value = value - surf[4 + d] * round_pos[d : d + 1]
    features = [jnp.ones_like(round_pos[0:1]), round_pos]
    blank = jnp.zeros((CPAD - COEF - 2 * FEATURES, value.shape[1]), f32)
    value = [value] + features + features + [blank]
    value = jnp.concatenate([v for v in value if v.shape[0]], axis=0).astype(bf16)
    masks = [jnp.where(octant == o, 1.0, 0.0).astype(bf16) for o in range(8)]
    return dot(oper[...], jnp.concatenate([value * m for m in masks], axis=0))


TURNED = (((0,), (0,)), ((), ()))


def look_up(index, table):
    lanes, rows = table.shape[0] // 2, table.shape[1]
    width = index.shape[1]
    at_row = index // lanes
    at_lane = index - at_row * lanes
    there = at_row == lax.broadcasted_iota(jnp.int32, (rows, width), 0)
    got = dot(table, jnp.where(there, 1.0, 0.0).astype(bf16))
    mine = at_lane == lax.broadcasted_iota(jnp.int32, (lanes, width), 0)
    first = jnp.sum(jnp.where(mine, got[0:lanes], 0.0), axis=0, keepdims=True)
    return first, jnp.sum(jnp.where(mine, got[lanes:], 0.0), axis=0, keepdims=True)


def fill_surface(surf, column):
    for i, lane in enumerate((0, 1, 2, 8, 9, 10, 11)):
        surf[i] = jnp.broadcast_to(column[:, lane : lane + 1], surf.shape[1:])


def morton_place(box):
    place = jnp.zeros_like(box)
    for b in range(LEVEL):
        digit = box >> (3 * b)
        place = place + ((((digit >> 2) & 1) << (2 * LEVEL + b)))
        place = place + ((((digit >> 1) & 1) << (LEVEL + b)) + ((digit & 1) << b))
    return place


def points_kernel(n_top, box_cap, io, offsets, buf, surf, octants, outgoing):
    got, column, oper = io.ins[:3]
    out, field, place = io.outs
    sources = got.shape[0]
    own = field.shape[1]
    dens = out.shape[1] // box_cap
    points = own // n_top
    cap = 2 * points * n_top // sources
    leaf_at = (5 + dens) * cap
    lanes = min(cap, LANE)
    wide = up(cap, LANE)
    me = io.scalars[0][0]
    buf[...] = jnp.zeros_like(buf)
    fill_surface(surf, column)
    io.wait(0)

    def put(i, offset):
        values = []
        for s in range(STRIP):
            pieces = [got[i * STRIP + s, :, r * cap : (r + 1) * cap] for r in range(5 + dens)]
            pieces.append(jnp.zeros((3 - dens, cap), f32))
            values.append(jnp.concatenate(pieces, axis=0))
        counts = [jnp.sum(v[4:5]).astype(jnp.int32) for v in values]
        for s, (value, count) in enumerate(zip(values, counts)):
            offsets[i * STRIP + s] = offset
            value = jnp.concatenate([value, jnp.zeros((8, wide + LANE - cap), f32)], axis=1)
            tile = offset // LANE
            value = pltpu.roll(value, offset - tile * LANE, 1)
            at = pl.ds(pl.multiple_of(tile * LANE, LANE), wide + LANE)
            buf[:, at] = buf[:, at] + value
            offset = offset + count
        return offset

    lax.fori_loop(0, sources // STRIP, put, jnp.int32(0))
    leaf = []
    for t in range(n_top):
        for r in range(points // lanes):
            leaf.append(got[me * n_top + t, :, leaf_at + r * lanes : leaf_at + (r + 1) * lanes])
    leaf = jnp.concatenate(leaf, axis=0).astype(jnp.int32)
    first = leaf[0:1, 0:1] >> 3
    offsets[sources] = jnp.sum(first.astype(f32)).astype(jnp.int32)
    io.wait(2)
    table = jnp.concatenate([(leaf >> 3) - first, leaf & 7], axis=1).astype(f32)
    table = jnp.transpose(table).astype(bf16)
    out_rows = out.shape[1]

    blocks_of = own // PB

    def spot(j):
        return pl.ds(pl.multiple_of(j * PB, PB), PB)

    def find(j, carry):
        to = spot(j)
        box, octant = look_up(buf[3:4, to].astype(jnp.int32), table)
        place[:, to] = box.astype(jnp.int32)
        octants[:, to] = octant
        return carry

    lax.fori_loop(0, blocks_of, find, 0, unroll=UNROLL_FIND)

    def apply(j, carry):
        to = spot(j)
        both = octant_product(buf[0:3, to], octants[:, to], surf, oper)
        outgoing[:, to] = both[0:COEF]
        field[:, to] = both[COEF : 2 * COEF]
        return carry

    lax.fori_loop(0, blocks_of, apply, 0, unroll=UNROLL_APPLY)

    def gather(j, total):
        to = spot(j)
        high, low = split(outgoing[:, to])
        rows = []
        at = lax.broadcasted_iota(jnp.int32, (box_cap, PB), 0)
        here = place[:, to] == at
        for k in range(out_rows // box_cap):
            rows.append(jnp.where(here, buf[5 + k : 6 + k, to], 0.0))
        a_high, a_low = split(jnp.concatenate(rows, axis=0))
        both = dot(jnp.concatenate([high, low], axis=0), a_high, NT)
        return total + both[0:COEF] + both[COEF : 2 * COEF] + dot(high, a_low, NT)

    total = jnp.zeros((COEF, out_rows), f32)
    total = lax.fori_loop(0, blocks_of, gather, total, unroll=UNROLL_GATHER)
    digits = jnp.concatenate([first >> 3, first & 7], axis=0).astype(f32)
    digits = jnp.broadcast_to(digits, (2, out_rows))
    blank = jnp.zeros((out.shape[0] - COEF - 2, out_rows), f32)
    out[...] = jnp.concatenate([total, digits, blank], axis=0).astype(bf16)


def box_ids(parts, dens):
    ids = []
    for part in parts:
        digits = part[COEF - 8 : COEF + 8, :].astype(f32)[8:16, 0:1].astype(jnp.int32)
        first = digits[0:1] * 8 + digits[1:2]
        at = lax.broadcasted_iota(jnp.int32, (1, part.shape[1] // dens), 1)
        ids.append(first + at)
    return jnp.concatenate(ids, axis=1)


def all_parts(parts, k, dens):
    width = parts[0].shape[1] // dens
    return jnp.concatenate([p[0:COEF, k * width : (k + 1) * width] for p in parts], axis=1)


def translate_kernel(slabs, dens, io, xs, xin, acc):
    parts = io.ins[:-6]
    first, rest = io.ins[-6:-3], io.ins[-3:]
    out = io.outs[0]
    x0 = (io.scalars[0][0] // 2 * 2) * SIDE // len(parts)
    ids = box_ids(parts, dens)
    place = morton_place(ids)
    place = (((place >> 6) - x0 + REACH) & 7) * 64 + (place & 63)
    place = jnp.where(ids < BOXES4, place, -1)
    at = lax.broadcasted_iota(jnp.int32, (BOXES4, ids.shape[1]), 0)
    there = jnp.where(at == place, 1.0, 0.0).astype(bf16)
    columns = dens * PLANE
    for k in range(dens):
        low = dot(there, all_parts(parts, k, dens), NT)
        low = low.astype(bf16).astype(f32)
        for s in range(7 + slabs - 1):
            slab = low[s * PLANE : (s + 1) * PLANE].reshape(SIDE, SIDE, COEF)
            shifted = {}
            for dz in SHIFTS:
                if dz == 0:
                    moved = slab
                else:
                    cut = dz % SIDE
                    moved = jnp.concatenate([slab[:, cut:], slab[:, :cut]], axis=1)
                shifted[dz] = moved.reshape(PLANE, COEF)
            rows = pl.ds(s * columns + k * PLANE, PLANE)
            pad = [jnp.zeros((PLANE, WFULL - 7 * COEF), f32)]
            xs[rows, :] = jnp.concatenate([shifted[z] for z in SHIFTS] + pad, axis=1).astype(bf16)
            pad = [jnp.zeros((PLANE, WIN - 4 * COEF), f32)]
            xin[rows, :] = jnp.concatenate([shifted[z] for z in OUTER] + pad, axis=1).astype(bf16)

    def rows_of(i, j):
        value = jnp.concatenate([first[i][j], rest[i][j]], axis=1)
        return value.reshape(-1, value.shape[2])

    n_out = len(OUTER) * ROWS
    n_all = len(SHIFTS) * ROWS
    for i, dx in enumerate(OUTER + INNER):
        rows = pl.ds((dx + REACH) * columns, slabs * columns)
        source = xs[rows, :]
        if dx in OUTER:
            term = dot(rows_of(0, OUTER.index(dx)), source, NT)
            if i == 0:
                acc[...] = term
            else:
                acc[...] += term
        else:
            acc[0:n_out] += dot(rows_of(1, INNER.index(dx)), source, NT)
            acc[n_out:n_all] += dot(rows_of(2, INNER.index(dx)), xin[rows, :], NT)
    lane = lax.broadcasted_iota(jnp.int32, (ROWS, LANE), 1)
    for t in range(slabs * columns // LANE):
        total = jnp.zeros((ROWS, LANE), f32)
        for i, dy in enumerate(OUTER + INNER):
            value = acc[i * ROWS : (i + 1) * ROWS, t * LANE : (t + 1) * LANE]
            by = SIDE * (dy % SIDE)
            if by:
                near = pltpu.roll(value, LANE - by, 1)
                far = pltpu.roll(value, PLANE - by, 1)
                value = jnp.where((lane & (PLANE - 1)) < PLANE - by, near, far)
            total = total + value
        out[:, t * LANE : (t + 1) * LANE] = total.astype(out.dtype)


def coarse_kernel(io):
    out = io.outs[0]
    parts = io.ins[:-1]
    opers = io.ins[-1]
    dens = out.shape[0]
    box = ids = box_ids(parts, dens)
    place = ((box & 7) << 6) + (box & 56) + (box >> 6)
    place = jnp.where(box < BOXES4, place, -1)
    at = lax.broadcasted_iota(jnp.int32, (BOXES4, ids.shape[1]), 0)
    there = jnp.where(at == place, 1.0, 0.0).astype(bf16)
    level = [dot(there, all_parts(parts, k, dens), NT) for k in range(dens)]

    io.wait(*range(len(io.ins)))

    for _ in range(LEVEL):
        count = level[0].shape[0] // 8
        total = None
        for o in range(8):
            rows = jnp.concatenate([v[o * count : (o + 1) * count] for v in level], axis=0)
            term = dot3_rows(split(rows), (opers[o], opers[8 + o]), NT)
            total = term if total is None else total + term
        level = [total[k * count : (k + 1) * count] for k in range(dens)]
    rows = jnp.concatenate(level, axis=0)
    rows = dot3(split(rows), (opers[32], opers[33]), NT)
    level = [rows[k : k + 1] for k in range(dens)]
    for _ in range(LEVEL - 1):
        count = level[0].shape[0]
        rows = split(jnp.concatenate(level, axis=0))
        children = [dot3_rows(rows, (opers[16 + o], opers[24 + o]), NT) for o in range(8)]
        level = [
            jnp.concatenate([c[k * count : (k + 1) * count] for c in children], axis=0)
            for k in range(dens)
        ]
    count = level[0].shape[0]
    rows = split(jnp.concatenate(level, axis=0))
    children = [dot3((opers[16 + o], opers[24 + o]), rows, NT) for o in range(8)]
    for k in range(dens):
        pieces = [c[:, k * count : (k + 1) * count] for c in children]
        out[k] = jnp.concatenate(pieces, axis=1)


def evaluate_kernel(slabs, step, window, io, stack, found):
    n = SIDE // slabs
    checks = io.ins[: 2 * n]
    d_hi, d_lo, lattice, place, field = io.ins[2 * n :]
    offsets = io.scalars[1]
    out = io.outs[0]
    core = io.scalars[0][0] & 1
    group = io.scalars[0][0] // step
    dens = lattice.shape[0]
    sources, cap = out.shape[0], out.shape[2] // dens
    lane = lax.broadcasted_iota(jnp.int32, (COEF, LANE), 1)
    mine = jnp.concatenate([d_hi[core], d_lo[core]], axis=0)
    other = jnp.concatenate([d_hi[1 - core], d_lo[1 - core]], axis=0)
    for m in range(n):
        value = dot(mine, checks[2 * m][...]) + dot(other, checks[2 * m + 1][...])
        value = value[0:COEF] + value[COEF : 2 * COEF]
        if slabs == 2:
            a, b = value[:, 0:LANE], value[:, LANE : 2 * LANE]
            half = LANE // 2
            pieces = [
                jnp.where(lane < half, a, pltpu.roll(b, half, 1)),
                jnp.where(lane < half, pltpu.roll(a, half, 1), b),
            ]
        else:
            pieces = [value[:, k * PLANE : (k + 1) * PLANE] for k in range(dens)]
        width = slabs * PLANE
        for k in range(dens):
            high, low = split(pieces[k])
            rows = pl.ds(k * CPAD, COEF)
            stack[rows, m * width : (m + 1) * width] = high.astype(f32)
            rows = pl.ds((dens + k) * CPAD, COEF)
            stack[rows, m * width : (m + 1) * width] = low.astype(f32)
    box = offsets[sources] + lax.broadcasted_iota(jnp.int32, (1, window), 1)
    want = morton_place(box) ^ (group * (slabs * PLANE))
    turned = BOXES4 + ((box & 7) << 6) + (box & 56) + (box >> 6)
    at = lax.broadcasted_iota(jnp.int32, (2 * BOXES4, window), 0)
    pick = ((at == want) | (at == turned)) & (box < BOXES4)
    pick = jnp.where(pick, 1.0, 0.0).astype(bf16)
    for k in range(dens):
        high, low = split(lattice[k])
        stack[pl.ds(k * CPAD, COEF), BOXES4:] = high.astype(f32)
        stack[pl.ds((dens + k) * CPAD, COEF), BOXES4:] = low.astype(f32)
    half = dens * CPAD
    local = dot(stack[...].astype(bf16), pick)
    high, low = split(local[0:half] + local[half:])
    local = jnp.concatenate([high, low], axis=1)
    found[:, place.shape[1] :] = jnp.zeros((8, found.shape[1] - place.shape[1]), f32)
    io.wait(*range(len(io.ins)))

    def block(j, carry):
        at = pl.ds(pl.multiple_of(j * PB, PB), PB)
        there = place[:, at] == lax.broadcasted_iota(jnp.int32, (window, PB), 0)
        there = jnp.where(there, 1.0, 0.0)
        there = jnp.concatenate([there, there], axis=0).astype(bf16)
        got = dot(local, there)
        mine = field[:, at]
        rows = []
        for k in range(dens):
            value = got[k * CPAD : k * CPAD + COEF]
            rows.append(jnp.sum(value * mine, axis=0, keepdims=True))
        rows.append(jnp.zeros((8 - dens, PB), f32))
        found[:, at] = jnp.concatenate(rows, axis=0)
        return carry

    lax.fori_loop(0, place.shape[1] // PB, block, 0, unroll=8)

    wide = up(cap, LANE) + LANE

    @pl.loop(0, sources // STRIP)
    def _(i):
        for s in range(STRIP):
            offset = offsets[i * STRIP + s]
            tile = offset // LANE
            value = found[:, pl.ds(pl.multiple_of(tile * LANE, LANE), wide)]
            value = pltpu.roll(value, wide - (offset - tile * LANE), 1)
            for k in range(dens):
                out[i * STRIP + s, :, k * cap : (k + 1) * cap] = value[k : k + 1, 0:cap]


def shift_by(axis, value, distance):
    size = lax.axis_size(axis)
    return lax.ppermute(value, axis, [(i, i ^ distance) for i in range(size)])


def gather_by(value, distances, beside):
    got = {m: shift_by("pts", value, m) if m else value for m in distances if m < 2 or m % 2 == 0}
    got, beside = lax.optimization_barrier((got, beside))
    got.update({m + 1: shift_by("pts", got[m], 1) for m in list(got) if m % 2 == 0 and m})
    return [got[m] for m in distances], beside


def per_device(
    local_pos, densities, morton_slot, slot_leaf, uc2e, m2m, m2l_ops, dc2e, lattice, l2l
):
    n_pts = lax.axis_size("pts")
    n_top = lax.axis_size("top")
    me = jnp.stack([lax.axis_index("pts"), lax.axis_index("top")]).astype(jnp.int32)
    points = local_pos.shape[1]
    own = points * n_top
    cap = 2 * points // n_pts
    box_cap = 2 * BOXES4 // n_pts
    dens = DENS // n_top
    slabs = max(1, 2 * SIDE // n_pts)
    coef = uc2e.shape[0]
    sources = n_pts * n_top
    lanes = min(cap, LANE)
    width = (5 + dens) * cap + points

    def shape(*dims, dtype=bf16):
        return jax.ShapeDtypeStruct(dims, dtype)

    outgoing, entries = run(
        functools.partial(route_kernel, own, cap, n_top),
        [],
        [
            local_pos,
            densities,
            morton_slot.reshape(1, points),
            slot_leaf.reshape(points // lanes, lanes),
        ],
        [shape(n_pts, n_top, 1, width, dtype=f32), shape(1, points, dtype=jnp.int32)],
        1 << 27,
        stays=(1,),
        grant=GRANT_FIRST,
    )
    outgoing = outgoing.reshape(sources, 1, width)
    incoming = lax.all_to_all(outgoing, ("pts", "top"), split_axis=0, concat_axis=0, tiled=True)

    flat = (-1, LANE)
    column = jnp.asarray(column_table())
    w_both, opers, *halves = run(
        operators_kernel,
        [],
        [m2m.reshape(flat), l2l.reshape(flat), uc2e, dc2e, lattice, column],
        [shape(2 * coef, 8 * CPAD), shape(34, coef, coef)] + [shape(2, coef, ROWS)] * 2,
        1 << 30,
        here=range(6),
        stays=range(4),
        scratch=[pltpu.VMEM((2, 8 * coef, LANE), f32)],
    )
    first = relayout(m2l_ops, me, 0, EARLY, GRANT_EARLY)
    incoming, first = lax.optimization_barrier((incoming, first))

    partial, field, place, offsets = run(
        functools.partial(points_kernel, n_top, box_cap),
        [me],
        [incoming, column, w_both],
        [
            shape(up(coef + 2, 16), dens * box_cap),
            shape(coef, own, dtype=f32),
            shape(1, own, dtype=jnp.int32),
        ],
        8 << 30,
        here=range(3),
        stays=range(3),
        numbers=[shape(sources + 1, dtype=jnp.int32)],
        scratch=[
            pltpu.VMEM((8, up(own + up(cap, LANE) + LANE, PB)), f32),
            pltpu.VMEM((3 + FEATURES, coef, PB), f32),
            pltpu.VMEM((1, own), f32),
            pltpu.VMEM((coef, own), f32),
        ],
    )
    later, flat_ops = lax.optimization_barrier((partial, m2l_ops))
    rest = relayout(flat_ops, me, EARLY, STEPS - EARLY, GRANT_LATER)
    parts, rest = gather_by(later, range(n_pts), rest)

    columns = dens * PLANE
    (checks,) = run(
        functools.partial(translate_kernel, slabs, dens),
        [me],
        [*parts, *first, *rest],
        [shape(ROWS, slabs * columns)],
        8 << 30,
        here=range(n_pts + 6),
        stays=(0,),
        scratch=[
            pltpu.VMEM(((7 + slabs - 1) * columns, WFULL), bf16),
            pltpu.VMEM(((7 + slabs - 1) * columns, WIN), bf16),
            pltpu.VMEM((7 * ROWS, slabs * columns), f32),
        ],
    )
    (lattice4,) = run(
        coarse_kernel,
        [],
        [*parts, opers],
        [shape(dens, coef, BOXES4, dtype=f32)],
        4 << 30,
        here=range(n_pts + 1),
        stays=(0,),
    )
    step = n_pts // SIDE * slabs
    distances = [step * m + c for m in range(SIDE // slabs) for c in range(2)]
    gathered, lattice4 = gather_by(checks, distances, lattice4)

    (reply,) = run(
        functools.partial(evaluate_kernel, slabs, step, box_cap),
        [me, offsets],
        [*gathered, *halves, lattice4, place, field],
        [shape(sources, 1, dens * cap, dtype=f32)],
        4 << 30,
        here=range(len(gathered) + 5),
        stays=(0,),
        scratch=[
            pltpu.VMEM((2 * dens * CPAD, 2 * BOXES4), f32),
            pltpu.VMEM((8, own + up(cap, LANE) + LANE), f32),
        ],
    )
    returned = lax.all_to_all(reply, ("pts", "top"), split_axis=0, concat_axis=0, tiled=True)
    (out,) = run(
        functools.partial(restore_kernel, n_top),
        [],
        [returned, entries],
        [shape(DENS, points, dtype=f32)],
        1 << 28,
        here=range(2),
    )
    return out


def solution(mesh):
    split_all = P(None, ("pts", "top"))
    placed = (split_all, split_all, P(("pts", "top")), P(("pts", "top"))) + (P(),) * 6
    return jax.shard_map(
        per_device, mesh=mesh, in_specs=placed, out_specs=split_all, check_vma=False
    )
```

```python
import functools
import math

import jax
import jax.numpy as jnp
import numpy as np
from jax import lax
from jax.experimental import pallas as pl
from jax.experimental.pallas import tpu as pltpu
from jax.sharding import PartitionSpec as P

LEVEL = 3
EDGE = 6
DENS = 8
SIDE = 2**LEVEL
BOXES4 = SIDE**3
PLANE = SIDE * SIDE
LANE = 128
REACH = 3
SHIFTS = list(range(-REACH, REACH + 1))
OUTER = [s for s in SHIFTS if abs(s) >= 2]
INNER = [s for s in SHIFTS if abs(s) < 2]
bf16 = jnp.bfloat16
f32 = jnp.float32
NN = (((1,), (0,)), ((), ()))
NT = (((1,), (1,)), ((), ()))


def up(value, multiple):
    return -(-value // multiple) * multiple


def surface_table():
    grid_vals = np.linspace(-1.0, 1.0, EDGE)
    points_list = []
    for a in range(EDGE):
        for b in range(EDGE):
            for c in range(EDGE):
                if min(a, b, c) == 0 or max(a, b, c) == EDGE - 1:
                    points_list.append([grid_vals[a], grid_vals[b], grid_vals[c]])
    return np.array(points_list, dtype=np.float32).T


COEF = surface_table().shape[1]
OFFSETS = (2 * REACH + 1) ** 3 - 27
FEATURES = 4
PB = 256
STRIP = 32
UNROLL_FIND, UNROLL_APPLY, UNROLL_GATHER = 16, 16, 16
GRANT = 28
GRANT_FIRST = 60
GRANT_EARLY = 52
GRANT_LATER = 49
CPAD = up(COEF, 32)


def column_table():
    surface = 1.25 * surface_table().astype(np.float64)
    grid = np.linspace(-0.9, 0.9, 10)
    points = np.stack(np.meshgrid(grid, grid, grid, indexing="ij")).reshape(3, -1)
    values = 1.0 / np.sqrt(((surface[:, :, None] - points[:, None, :]) ** 2).sum(axis=0))
    scale = (points**2).sum(axis=1)
    out = np.zeros((surface.shape[1], LANE), np.float32)
    out[:, 0:3] = (np.float32(1.25) * surface_table()).T
    out[:, 8] = values.mean(axis=1)
    out[:, 9:12] = values @ points.T / scale
    return out


def blocks():
    out, position = [], 0
    for dx in SHIFTS:
        for dy in SHIFTS:
            count = sum(max(abs(dx), abs(dy), abs(dz)) >= 2 for dz in SHIFTS)
            out.append((dx, dy, position, count))
            position += count
    return out


def dot(a, b, dims=NN):
    return lax.dot_general(a, b, dims, preferred_element_type=f32)


def split(value):
    high = value.astype(bf16)
    return high, (value - high.astype(f32)).astype(bf16)


def dot3(a, b, dims=NN):
    return dot(a[0], b[0], dims) + dot(a[1], b[0], dims) + dot(a[0], b[1], dims)


def dot3_rows(a, b, dims=NN):
    rows = a[0].shape[0]
    both = jnp.concatenate([x.astype(f32) for x in a], axis=0).astype(bf16)
    both = dot(both, b[0], dims)
    return both[0:rows] + both[rows : 2 * rows] + dot(a[0], b[1], dims)


def call(kernel, out_shape, mib, flops, bytes_accessed=1 << 20, **kw):
    return pl.pallas_call(
        kernel,
        out_shape=out_shape,
        compiler_params=pltpu.CompilerParams(vmem_limit_bytes=mib << 20),
        cost_estimate=pl.CostEstimate(
            flops=flops, bytes_accessed=bytes_accessed, transcendentals=0
        ),
        **kw,
    )


SMEM = pl.BlockSpec(memory_space=pltpu.SMEM)
VMEM = pl.BlockSpec(memory_space=pltpu.VMEM)
HBM = pl.BlockSpec(memory_space=pltpu.HBM)

class Buffers:
    def __init__(self, scalars, ins, outs, moved, sources, targets, sem_in, sem_out):
        self.scalars, self.ins, self.outs, self.targets = scalars, ins, outs, targets
        self.sem_out = sem_out
        self.coming, self.going, self.waited = {}, {}, set()
        for i in moved:
            self.coming[i] = pltpu.make_async_copy(sources[i], ins[i], sem_in.at[i])
            self.coming[i].start()

    def wait(self, *which):
        for i in which:
            if i in self.coming and i not in self.waited:
                self.waited.add(i)
                self.coming[i].wait()

    def send(self, *which):
        for i in which:
            if i not in self.going:
                copy = pltpu.make_async_copy(self.outs[i], self.targets[i], self.sem_out.at[i])
                copy.start()
                self.going[i] = copy


def run(kernel, scalars, ins, outs, flops, scratch=(), late=(), here=(), stays=(), numbers=(), grant=GRANT,
        by_kernel=()):
    n_s, n_i, n_o, n_n = len(scalars), len(ins), len(outs), len(numbers)
    moved_in = [i for i in range(n_i) if i not in here]
    moved_out = [i for i in range(n_o) if i not in stays]

    def body(*refs):
        refs = list(refs)
        take = lambda count: [refs.pop(0) for _ in range(count)]
        given, sources, targets, counts = take(n_s), take(n_i), take(n_o), take(n_n)
        in_refs, out_refs = list(sources), list(targets)
        for i in moved_in:
            in_refs[i] = refs.pop(0)
        for i in moved_out:
            out_refs[i] = refs.pop(0)
        io = Buffers(given, in_refs, out_refs, moved_in, sources, targets, *take(2))
        io.wait(*[i for i in moved_in if i not in late])
        kernel(io, *counts, *refs)
        io.wait(*moved_in)
        mine = [i for i in moved_out if i not in by_kernel]
        io.send(*mine)
        for i in mine:
            io.going[i].wait()

    return call(
        body,
        tuple(outs) + tuple(numbers),
        grant,
        flops,
        in_specs=[SMEM] * n_s + [VMEM if i in here else HBM for i in range(n_i)],
        out_specs=tuple(VMEM if i in stays else HBM for i in range(n_o)) + (SMEM,) * n_n,
        scratch_shapes=[pltpu.VMEM(ins[i].shape, ins[i].dtype) for i in moved_in]
        + [pltpu.VMEM(outs[i].shape, outs[i].dtype) for i in moved_out]
        + [pltpu.SemaphoreType.DMA((max(n, 1),)) for n in (n_i, n_o)]
        + list(scratch),
    )(*scalars, *ins)


HG = 4 * OFFSETS * COEF // LANE
KT = up(up(OFFSETS * COEF, LANE) // LANE, 8)
WFULL = up(7 * COEF, LANE)
WIN = up(4 * COEF, LANE)
NG = COEF // 8
STEPS = -(-NG // 4)
ROWS = 16 * STEPS
CHUNK = up(HG + 15, 16)
TAIL = 32
EARLY = 2
STRIDE = 17
PIECES = ((4, 7, WFULL), (3, 4, WFULL), (3, 3, WIN))


def relayout_kernel(nrows, step0, steps, me_ref, f_hbm, tail_ref, oa, ob, oc, inb, fbuf, tbuf, sem):
    step = pl.program_id(0)
    half = me_ref[0] & 1
    end16 = nrows // 16 * 16

    def start_row(st, g):
        return jnp.minimum(4 * (st + step0) + g, NG - 1) * (2 * HG) + half * HG

    def start(st, slot):
        for g in range(4):
            row = pl.multiple_of(start_row(st, g) // 16 * 16, 16)
            pltpu.make_async_copy(
                f_hbm.at[pl.ds(row, CHUNK - TAIL)],
                inb.at[slot, g, pl.ds(0, CHUNK - TAIL)],
                sem.at[slot, g, 0],
            ).start()
            last = row + CHUNK > end16

            @pl.when(jnp.logical_not(last))
            def _():
                pltpu.make_async_copy(
                    f_hbm.at[pl.ds(pl.multiple_of(row + CHUNK - TAIL, 16), TAIL)],
                    inb.at[slot, g, pl.ds(CHUNK - TAIL, TAIL)],
                    sem.at[slot, g, 1],
                ).start()


    def wait(st, slot):
        for g in range(4):
            row = pl.multiple_of(start_row(st, g) // 16 * 16, 16)
            pltpu.make_async_copy(
                f_hbm.at[pl.ds(row, CHUNK - TAIL)],
                inb.at[slot, g, pl.ds(0, CHUNK - TAIL)],
                sem.at[slot, g, 0],
            ).wait()
            last = row + CHUNK > end16

            @pl.when(jnp.logical_not(last))
            def _():
                pltpu.make_async_copy(
                    f_hbm.at[pl.ds(pl.multiple_of(row + CHUNK - TAIL, 16), TAIL)],
                    inb.at[slot, g, pl.ds(CHUNK - TAIL, TAIL)],
                    sem.at[slot, g, 1],
                ).wait()

            @pl.when(last)
            def _():
                row16 = lax.broadcasted_iota(jnp.int32, (16, LANE), 0)
                tail = jnp.where(row16 < nrows - end16, tail_ref[...].astype(f32), 0.0)
                inb[slot, g, CHUNK - TAIL : CHUNK - TAIL + 16] = tail.astype(bf16)

    slot = step

    @pl.when(step == 0)
    def _():
        fbuf[...] = jnp.zeros_like(fbuf)
        inb[:, :, CHUNK - 16 :] = jnp.zeros_like(inb[:, :, CHUNK - 16 :])
        for st in range(steps):
            start(st, st)

    wait(step, slot)
    lane = lax.broadcasted_iota(jnp.int32, (8, LANE), 1)
    for g in range(4):
        fbuf[g, 0:CHUNK] = inb[slot, g].astype(f32)
    for g in range(4):
        row = start_row(step, g)
        off = row - row // 16 * 16
        for e in range(4):
            first = OFFSETS * COEF * e
            phase = first % LANE

            @pl.loop(0, KT // 8, unroll=KT // 8)
            def _(n):
                base = off + first // LANE + 8 * n
                value = fbuf[g, pl.ds(base, 8), :]
                if phase:
                    after = fbuf[g, pl.ds(base + 1, 8), :]
                    value = pltpu.roll(jnp.where(lane >= phase, value, after), LANE - phase, 1)
                tbuf[pl.ds(8 * n * STRIDE + 4 * g + e, 8, stride=STRIDE), :] = value

    packed = {}

    def tile(k):
        if k not in packed:
            packed[k] = tbuf[k * STRIDE : k * STRIDE + 16, :].astype(bf16)
        return packed[k]

    lane16 = lax.broadcasted_iota(jnp.int32, (16, LANE), 1)
    here = pl.ds(pl.multiple_of(step * 16, 16), 16)
    for dx, dy, d0, count in blocks():
        tile0, phase = divmod(d0 * COEF, LANE)
        if dx in OUTER:
            ref = oa.at[OUTER.index(dx), (OUTER + INNER).index(dy)]
        elif dy in OUTER:
            ref = ob.at[INNER.index(dx), OUTER.index(dy)]
        else:
            ref = oc.at[INNER.index(dx), INNER.index(dy)]
        for t in range(up(count * COEF, LANE) // LANE):
            value = tile(tile0 + t)
            if phase:
                after = tile(min(tile0 + t + 1, KT - 1))
                value = pltpu.roll(jnp.where(lane16 >= phase, value, after), LANE - phase, 1)
            ref[here, t * LANE : (t + 1) * LANE] = value


def relayout(flat, me, step0, steps, grant):
    nrows = flat.shape[0] // LANE
    rows = flat.reshape(nrows, LANE)
    shapes = tuple((a, b, 16 * steps, c) for a, b, c in PIECES)
    return call(
        functools.partial(relayout_kernel, nrows, step0, steps),
        tuple(jax.ShapeDtypeStruct(s, bf16) for s in shapes),
        grant,
        1 << 20,
        steps << 21,
        grid_spec=pltpu.PrefetchScalarGridSpec(
            num_scalar_prefetch=1,
            grid=(steps,),
            in_specs=[HBM, pl.BlockSpec((16, LANE), lambda i, h: (nrows // 16, 0))],
            out_specs=(VMEM,) * len(shapes),
            scratch_shapes=[
                pltpu.VMEM((steps, 4, CHUNK, LANE), bf16),
                pltpu.VMEM((4, CHUNK + 16, LANE), f32),
                pltpu.VMEM((KT * STRIDE, LANE), f32),
                pltpu.SemaphoreType.DMA((steps, 4, 2)),
            ],
        ),
    )(me, rows, rows)


GROUP = 16


def square(flat, out):
    per = GROUP * COEF // LANE
    groups = flat.shape[0] // per
    lane = lax.broadcasted_iota(jnp.int32, (groups, LANE), 1)
    for r in range(GROUP):
        first, phase = divmod(r * COEF, LANE)
        got = []
        for t in range(3):
            row = min(first + t, per - 1)
            got.append(flat[pl.ds(row, groups, stride=per), :])
        for t in range(2):
            value = got[t]
            if phase:
                value = jnp.where(lane >= phase, got[t], got[t + 1])
                value = pltpu.roll(value, LANE - phase, 1)
            out[t, pl.ds(r, groups, stride=GROUP), :] = value


def operators_kernel(io, rows):
    m2m, l2l, uc2e, dc2e, lattice, column = io.ins
    w_both, coarse, d_hi, d_lo = io.outs
    scale = 1.0 / (4.0 * math.pi)
    coarse[32], coarse[33] = split(lattice[...])
    first = split(uc2e[...] * scale)

    plane = split(column[...])

    def side_by_side(pieces):
        wide = []
        for piece in pieces:
            high, low = split(dot3(split(piece), plane)[:, 8 : 8 + FEATURES])
            wide += [piece, high.astype(f32), low.astype(f32)]
            wide.append(jnp.zeros((COEF, CPAD - COEF - 2 * FEATURES), f32))
        return jnp.concatenate([w for w in wide if w.shape[1]], axis=1)

    def matrix(o):
        at = slice(o * COEF, (o + 1) * COEF)
        return jnp.concatenate([rows[0, at], rows[1, at, 0 : COEF - LANE]], axis=1)

    io.wait(0)
    square(m2m, rows)
    pieces = []
    for o in range(8):
        high, low = split(matrix(o))
        coarse[o], coarse[8 + o] = high, low
        pieces.append(dot3((high, low), first))
    upward = side_by_side(pieces)
    io.wait(1)
    square(l2l, rows)
    pieces = []
    for o in range(8):
        value = matrix(o)
        coarse[16 + o], coarse[24 + o] = split(value)
        pieces.append(jnp.transpose(value) * scale)
    w_both[...] = jnp.concatenate([upward, side_by_side(pieces)], axis=0).astype(bf16)
    high, low = split(dc2e[...])
    i = lax.broadcasted_iota(jnp.int32, (COEF, ROWS), 0)
    r = lax.broadcasted_iota(jnp.int32, (COEF, ROWS), 1)
    for h in range(2):
        here = (i == (r >> 2) * 8 + 4 * h + (r & 3)) & (r < 4 * NG)
        here = jnp.where(here, 1.0, 0.0).astype(bf16)
        d_hi[h] = dot(high, here).astype(bf16)
        d_lo[h] = dot(low, here).astype(bf16)


def route_kernel(own, cap, n_top, io, sem):
    pos, dens, slot, leaf = io.ins
    out, entries = io.outs
    points = pos.shape[1]
    owners = out.shape[0]
    slots = slot[...]
    owner = slots // own
    inside = slots - owner * own
    hit = owner == lax.broadcasted_iota(jnp.int32, (owners, points), 0)
    hit = jnp.where(hit, 1.0, 0.0)
    hit16 = hit.astype(bf16)
    row = lax.broadcasted_iota(jnp.int32, (LANE, LANE), 0)
    col = lax.broadcasted_iota(jnp.int32, (LANE, LANE), 1)
    before = jnp.where(row < col, 1.0, 0.0).astype(bf16)
    every = jnp.ones((LANE, LANE), bf16)
    total = jnp.zeros((owners, LANE), f32)
    ranks = []
    for t in range(points // LANE):
        part = hit16[:, t * LANE : (t + 1) * LANE]
        ranks.append(total + dot(part, before))
        total = total + dot(part, every)
    rank = jnp.sum(hit * jnp.concatenate(ranks, axis=1), axis=0, keepdims=True)
    entry = owner * cap + rank.astype(jnp.int32)
    entries[...] = entry
    inside_hi = inside // 64
    io.wait(0, 1, 3)
    value = jnp.concatenate([pos[...], dens[...]], axis=0)
    width = value.shape[0]
    high, low = split(value)
    ones = jnp.ones((1, points), f32)
    high = jnp.concatenate(
        [high.astype(f32), inside_hi.astype(f32), (inside - 64 * inside_hi).astype(f32), ones]
        + [jnp.zeros((16 - width - 3, points), f32)],
        axis=0,
    )
    low = jnp.concatenate([low.astype(f32), jnp.zeros((16 - width, points), f32)], axis=0)
    payload = jnp.concatenate([high, low], axis=0).astype(bf16)
    block = max(cap, LANE)
    per = DENS // n_top
    leaves = leaf[...].astype(f32)
    leaves = [leaves[r : r + 1] for r in range(leaves.shape[0])]
    lanes = leaf.shape[1]
    going = []
    for o in range(owners * cap // block):
        there = entry == o * block + lax.broadcasted_iota(jnp.int32, (block, points), 0)
        there = jnp.where(there, 1.0, 0.0).astype(bf16)
        got = dot(payload, there, NT)
        value = got[0:width] + got[16 : 16 + width]
        where = got[width : width + 1] * 64.0 + got[width + 1 : width + 2]
        valid = got[width + 2 : width + 3]
        for q in range(n_top):
            rows = [value[r : r + 1] for r in range(3)] + [where, valid]
            rows += [value[3 + per * q + k : 4 + per * q + k] for k in range(per)]
            for i in range(block // cap):
                at = o * (block // cap) + i
                for r, value_row in enumerate(rows):
                    out[at, q, :, r * cap : (r + 1) * cap] = value_row[:, i * cap : (i + 1) * cap]
                for r, value_row in enumerate(leaves):
                    base = len(rows) * cap + r * lanes
                    out[at, q, :, base : base + lanes] = value_row
        here = pl.ds(o * (block // cap), block // cap)
        going.append(pltpu.make_async_copy(out.at[here], io.targets[0].at[here], sem.at[o]))
        going[-1].start()
    for copy in going:
        copy.wait()


def restore_kernel(n_top, io):
    got, entries = io.ins
    out = io.outs[0]
    devices = got.shape[0]
    per = out.shape[0] // n_top
    cap = got.shape[2] // per
    points = out.shape[1]
    block = max(cap, PB)
    total = jnp.zeros((2 * out.shape[0], points), f32)
    for o in range(devices // n_top * cap // block):
        count = block // cap
        value = []
        for q in range(n_top):
            for k in range(per):
                pieces = []
                for i in range(count):
                    row = (o * count + i) * n_top + q
                    pieces.append(got[row, :, k * cap : (k + 1) * cap])
                value.append(jnp.concatenate(pieces, axis=1))
        high, low = split(jnp.concatenate(value, axis=0))
        both = jnp.concatenate([high.astype(f32), low.astype(f32)], axis=0).astype(bf16)
        at = o * block + lax.broadcasted_iota(jnp.int32, (block, points), 0)
        total = total + dot(both, jnp.where(entries[...] == at, 1.0, 0.0).astype(bf16))
    out[...] = total[0 : out.shape[0]] + total[out.shape[0] :]


def octant_product(pos, octant, surf, oper):
    squared = None
    for d in range(3):
        spacing = surf[d] - pos[d : d + 1]
        squared = spacing * spacing if squared is None else squared + spacing * spacing
    value = lax.rsqrt(squared)
    round_pos = pos.astype(bf16).astype(f32)
    value = value - surf[3]
    for d in range(3):
        value = value - surf[4 + d] * round_pos[d : d + 1]
    features = [jnp.ones_like(round_pos[0:1]), round_pos]
    blank = jnp.zeros((CPAD - COEF - 2 * FEATURES, value.shape[1]), f32)
    value = [value] + features + features + [blank]
    value = jnp.concatenate([v for v in value if v.shape[0]], axis=0).astype(bf16)
    masks = [jnp.where(octant == o, 1.0, 0.0).astype(bf16) for o in range(8)]
    return dot(oper[...], jnp.concatenate([value * m for m in masks], axis=0))


TURNED = (((0,), (0,)), ((), ()))


def look_up(index, table):
    lanes, rows = table.shape[0] // 2, table.shape[1]
    width = index.shape[1]
    at_row = index // lanes
    at_lane = index - at_row * lanes
    there = at_row == lax.broadcasted_iota(jnp.int32, (rows, width), 0)
    got = dot(table, jnp.where(there, 1.0, 0.0).astype(bf16))
    mine = at_lane == lax.broadcasted_iota(jnp.int32, (lanes, width), 0)
    first = jnp.sum(jnp.where(mine, got[0:lanes], 0.0), axis=0, keepdims=True)
    return first, jnp.sum(jnp.where(mine, got[lanes:], 0.0), axis=0, keepdims=True)


def fill_surface(surf, column):
    for i, lane in enumerate((0, 1, 2, 8, 9, 10, 11)):
        surf[i] = jnp.broadcast_to(column[:, lane : lane + 1], surf.shape[1:])


def morton_place(box):
    place = jnp.zeros_like(box)
    for b in range(LEVEL):
        digit = box >> (3 * b)
        place = place + ((((digit >> 2) & 1) << (2 * LEVEL + b)))
        place = place + ((((digit >> 1) & 1) << (LEVEL + b)) + ((digit & 1) << b))
    return place


def points_kernel(n_top, box_cap, io, offsets, buf, surf, octants, outgoing):
    got, column, oper = io.ins[:3]
    out, field, place = io.outs
    sources = got.shape[0]
    own = field.shape[1]
    dens = out.shape[1] // box_cap
    points = own // n_top
    cap = 2 * points * n_top // sources
    leaf_at = (5 + dens) * cap
    lanes = min(cap, LANE)
    wide = up(cap, LANE)
    me = io.scalars[0][0]
    buf[...] = jnp.zeros_like(buf)
    fill_surface(surf, column)
    io.wait(0)

    def put(i, offset):
        values = []
        for s in range(STRIP):
            pieces = [got[i * STRIP + s, :, r * cap : (r + 1) * cap] for r in range(5 + dens)]
            pieces.append(jnp.zeros((3 - dens, cap), f32))
            values.append(jnp.concatenate(pieces, axis=0))
        counts = [jnp.sum(v[4:5]).astype(jnp.int32) for v in values]
        for s, (value, count) in enumerate(zip(values, counts)):
            offsets[i * STRIP + s] = offset
            value = jnp.concatenate([value, jnp.zeros((8, wide + LANE - cap), f32)], axis=1)
            tile = offset // LANE
            value = pltpu.roll(value, offset - tile * LANE, 1)
            at = pl.ds(pl.multiple_of(tile * LANE, LANE), wide + LANE)
            buf[:, at] = buf[:, at] + value
            offset = offset + count
        return offset

    lax.fori_loop(0, sources // STRIP, put, jnp.int32(0))
    leaf = []
    for t in range(n_top):
        for r in range(points // lanes):
            leaf.append(got[me * n_top + t, :, leaf_at + r * lanes : leaf_at + (r + 1) * lanes])
    leaf = jnp.concatenate(leaf, axis=0).astype(jnp.int32)
    first = leaf[0:1, 0:1] >> 3
    offsets[sources] = jnp.sum(first.astype(f32)).astype(jnp.int32)
    io.wait(2)
    table = jnp.concatenate([(leaf >> 3) - first, leaf & 7], axis=1).astype(f32)
    table = jnp.transpose(table).astype(bf16)
    out_rows = out.shape[1]

    blocks_of = own // PB

    def spot(j):
        return pl.ds(pl.multiple_of(j * PB, PB), PB)

    def find(j, carry):
        to = spot(j)
        box, octant = look_up(buf[3:4, to].astype(jnp.int32), table)
        place[:, to] = box.astype(jnp.int32)
        octants[:, to] = octant
        return carry

    lax.fori_loop(0, blocks_of, find, 0, unroll=UNROLL_FIND)

    def apply(j, carry):
        to = spot(j)
        both = octant_product(buf[0:3, to], octants[:, to], surf, oper)
        outgoing[:, to] = both[0:COEF]
        field[:, to] = both[COEF : 2 * COEF]
        return carry

    lax.fori_loop(0, blocks_of, apply, 0, unroll=UNROLL_APPLY)

    def gather(j, total):
        to = spot(j)
        high, low = split(outgoing[:, to])
        rows = []
        at = lax.broadcasted_iota(jnp.int32, (box_cap, PB), 0)
        here = place[:, to] == at
        for k in range(out_rows // box_cap):
            rows.append(jnp.where(here, buf[5 + k : 6 + k, to], 0.0))
        a_high, a_low = split(jnp.concatenate(rows, axis=0))
        both = dot(jnp.concatenate([high, low], axis=0), a_high, NT)
        return total + both[0:COEF] + both[COEF : 2 * COEF] + dot(high, a_low, NT)

    total = jnp.zeros((COEF, out_rows), f32)
    total = lax.fori_loop(0, blocks_of, gather, total, unroll=UNROLL_GATHER)
    digits = jnp.concatenate([first >> 3, first & 7], axis=0).astype(f32)
    digits = jnp.broadcast_to(digits, (2, out_rows))
    blank = jnp.zeros((out.shape[0] - COEF - 2, out_rows), f32)
    out[...] = jnp.concatenate([total, digits, blank], axis=0).astype(bf16)


def box_ids(parts, dens):
    ids = []
    for part in parts:
        digits = part[COEF - 8 : COEF + 8, :].astype(f32)[8:16, 0:1].astype(jnp.int32)
        first = digits[0:1] * 8 + digits[1:2]
        at = lax.broadcasted_iota(jnp.int32, (1, part.shape[1] // dens), 1)
        ids.append(first + at)
    return jnp.concatenate(ids, axis=1)


def all_parts(parts, k, dens):
    width = parts[0].shape[1] // dens
    return jnp.concatenate([p[0:COEF, k * width : (k + 1) * width] for p in parts], axis=1)


def translate_kernel(slabs, dens, io, xs, xin, acc):
    parts = io.ins[:-6]
    first, rest = io.ins[-6:-3], io.ins[-3:]
    out = io.outs[0]
    x0 = (io.scalars[0][0] // 2 * 2) * SIDE // len(parts)
    ids = box_ids(parts, dens)
    place = morton_place(ids)
    place = (((place >> 6) - x0 + REACH) & 7) * 64 + (place & 63)
    place = jnp.where(ids < BOXES4, place, -1)
    at = lax.broadcasted_iota(jnp.int32, (BOXES4, ids.shape[1]), 0)
    there = jnp.where(at == place, 1.0, 0.0).astype(bf16)
    columns = dens * PLANE
    for k in range(dens):
        low = dot(there, all_parts(parts, k, dens), NT)
        low = low.astype(bf16).astype(f32)
        for s in range(7 + slabs - 1):
            slab = low[s * PLANE : (s + 1) * PLANE].reshape(SIDE, SIDE, COEF)
            shifted = {}
            for dz in SHIFTS:
                if dz == 0:
                    moved = slab
                else:
                    cut = dz % SIDE
                    moved = jnp.concatenate([slab[:, cut:], slab[:, :cut]], axis=1)
                shifted[dz] = moved.reshape(PLANE, COEF)
            rows = pl.ds(s * columns + k * PLANE, PLANE)
            pad = [jnp.zeros((PLANE, WFULL - 7 * COEF), f32)]
            xs[rows, :] = jnp.concatenate([shifted[z] for z in SHIFTS] + pad, axis=1).astype(bf16)
            pad = [jnp.zeros((PLANE, WIN - 4 * COEF), f32)]
            xin[rows, :] = jnp.concatenate([shifted[z] for z in OUTER] + pad, axis=1).astype(bf16)

    def rows_of(i, j):
        value = jnp.concatenate([first[i][j], rest[i][j]], axis=1)
        return value.reshape(-1, value.shape[2])

    n_out = len(OUTER) * ROWS
    n_all = len(SHIFTS) * ROWS
    for i, dx in enumerate(OUTER + INNER):
        rows = pl.ds((dx + REACH) * columns, slabs * columns)
        source = xs[rows, :]
        if dx in OUTER:
            term = dot(rows_of(0, OUTER.index(dx)), source, NT)
            if i == 0:
                acc[...] = term
            else:
                acc[...] += term
        else:
            acc[0:n_out] += dot(rows_of(1, INNER.index(dx)), source, NT)
            acc[n_out:n_all] += dot(rows_of(2, INNER.index(dx)), xin[rows, :], NT)
    lane = lax.broadcasted_iota(jnp.int32, (ROWS, LANE), 1)
    for t in range(slabs * columns // LANE):
        total = jnp.zeros((ROWS, LANE), f32)
        for i, dy in enumerate(OUTER + INNER):
            value = acc[i * ROWS : (i + 1) * ROWS, t * LANE : (t + 1) * LANE]
            by = SIDE * (dy % SIDE)
            if by:
                near = pltpu.roll(value, LANE - by, 1)
                far = pltpu.roll(value, PLANE - by, 1)
                value = jnp.where((lane & (PLANE - 1)) < PLANE - by, near, far)
            total = total + value
        out[:, t * LANE : (t + 1) * LANE] = total.astype(out.dtype)


def coarse_kernel(io):
    out = io.outs[0]
    parts = io.ins[:-1]
    opers = io.ins[-1]
    dens = out.shape[0]
    box = ids = box_ids(parts, dens)
    place = ((box & 7) << 6) + (box & 56) + (box >> 6)
    place = jnp.where(box < BOXES4, place, -1)
    at = lax.broadcasted_iota(jnp.int32, (BOXES4, ids.shape[1]), 0)
    there = jnp.where(at == place, 1.0, 0.0).astype(bf16)
    level = [dot(there, all_parts(parts, k, dens), NT) for k in range(dens)]

    io.wait(*range(len(io.ins)))

    for _ in range(LEVEL):
        count = level[0].shape[0] // 8
        total = None
        for o in range(8):
            rows = jnp.concatenate([v[o * count : (o + 1) * count] for v in level], axis=0)
            term = dot3_rows(split(rows), (opers[o], opers[8 + o]), NT)
            total = term if total is None else total + term
        level = [total[k * count : (k + 1) * count] for k in range(dens)]
    rows = jnp.concatenate(level, axis=0)
    rows = dot3(split(rows), (opers[32], opers[33]), NT)
    level = [rows[k : k + 1] for k in range(dens)]
    for _ in range(LEVEL - 1):
        count = level[0].shape[0]
        rows = split(jnp.concatenate(level, axis=0))
        children = [dot3_rows(rows, (opers[16 + o], opers[24 + o]), NT) for o in range(8)]
        level = [
            jnp.concatenate([c[k * count : (k + 1) * count] for c in children], axis=0)
            for k in range(dens)
        ]
    count = level[0].shape[0]
    rows = split(jnp.concatenate(level, axis=0))
    children = [dot3((opers[16 + o], opers[24 + o]), rows, NT) for o in range(8)]
    for k in range(dens):
        pieces = [c[:, k * count : (k + 1) * count] for c in children]
        out[k] = jnp.concatenate(pieces, axis=1)


def evaluate_kernel(slabs, step, window, io, stack, found):
    n = SIDE // slabs
    checks = io.ins[: 2 * n]
    d_hi, d_lo, lattice, place, field = io.ins[2 * n :]
    offsets = io.scalars[1]
    out = io.outs[0]
    core = io.scalars[0][0] & 1
    group = io.scalars[0][0] // step
    dens = lattice.shape[0]
    sources, cap = out.shape[0], out.shape[2] // dens
    lane = lax.broadcasted_iota(jnp.int32, (COEF, LANE), 1)
    mine = jnp.concatenate([d_hi[core], d_lo[core]], axis=0)
    other = jnp.concatenate([d_hi[1 - core], d_lo[1 - core]], axis=0)
    for m in range(n):
        value = dot(mine, checks[2 * m][...]) + dot(other, checks[2 * m + 1][...])
        value = value[0:COEF] + value[COEF : 2 * COEF]
        if slabs == 2:
            a, b = value[:, 0:LANE], value[:, LANE : 2 * LANE]
            half = LANE // 2
            pieces = [
                jnp.where(lane < half, a, pltpu.roll(b, half, 1)),
                jnp.where(lane < half, pltpu.roll(a, half, 1), b),
            ]
        else:
            pieces = [value[:, k * PLANE : (k + 1) * PLANE] for k in range(dens)]
        width = slabs * PLANE
        for k in range(dens):
            high, low = split(pieces[k])
            rows = pl.ds(k * CPAD, COEF)
            stack[rows, m * width : (m + 1) * width] = high.astype(f32)
            rows = pl.ds((dens + k) * CPAD, COEF)
            stack[rows, m * width : (m + 1) * width] = low.astype(f32)
    box = offsets[sources] + lax.broadcasted_iota(jnp.int32, (1, window), 1)
    want = morton_place(box) ^ (group * (slabs * PLANE))
    turned = BOXES4 + ((box & 7) << 6) + (box & 56) + (box >> 6)
    at = lax.broadcasted_iota(jnp.int32, (2 * BOXES4, window), 0)
    pick = ((at == want) | (at == turned)) & (box < BOXES4)
    pick = jnp.where(pick, 1.0, 0.0).astype(bf16)
    for k in range(dens):
        high, low = split(lattice[k])
        stack[pl.ds(k * CPAD, COEF), BOXES4:] = high.astype(f32)
        stack[pl.ds((dens + k) * CPAD, COEF), BOXES4:] = low.astype(f32)
    half = dens * CPAD
    local = dot(stack[...].astype(bf16), pick)
    high, low = split(local[0:half] + local[half:])
    local = jnp.concatenate([high, low], axis=1)
    found[:, place.shape[1] :] = jnp.zeros((8, found.shape[1] - place.shape[1]), f32)
    io.wait(*range(len(io.ins)))

    def block(j, carry):
        at = pl.ds(pl.multiple_of(j * PB, PB), PB)
        there = place[:, at] == lax.broadcasted_iota(jnp.int32, (window, PB), 0)
        there = jnp.where(there, 1.0, 0.0)
        there = jnp.concatenate([there, there], axis=0).astype(bf16)
        got = dot(local, there)
        mine = field[:, at]
        rows = []
        for k in range(dens):
            value = got[k * CPAD : k * CPAD + COEF]
            rows.append(jnp.sum(value * mine, axis=0, keepdims=True))
        rows.append(jnp.zeros((8 - dens, PB), f32))
        found[:, at] = jnp.concatenate(rows, axis=0)
        return carry

    lax.fori_loop(0, place.shape[1] // PB, block, 0, unroll=8)

    wide = up(cap, LANE) + LANE

    @pl.loop(0, sources // STRIP)
    def _(i):
        for s in range(STRIP):
            offset = offsets[i * STRIP + s]
            tile = offset // LANE
            value = found[:, pl.ds(pl.multiple_of(tile * LANE, LANE), wide)]
            value = pltpu.roll(value, wide - (offset - tile * LANE), 1)
            for k in range(dens):
                out[i * STRIP + s, :, k * cap : (k + 1) * cap] = value[k : k + 1, 0:cap]


def shift_by(axis, value, distance):
    size = lax.axis_size(axis)
    return lax.ppermute(value, axis, [(i, i ^ distance) for i in range(size)])


def gather_by(value, distances, beside):
    got = {m: shift_by("pts", value, m) if m else value for m in distances if m < 2 or m % 2 == 0}
    got, beside = lax.optimization_barrier((got, beside))
    got.update({m + 1: shift_by("pts", got[m], 1) for m in list(got) if m % 2 == 0 and m})
    return [got[m] for m in distances], beside


def per_device(
    local_pos, densities, morton_slot, slot_leaf, uc2e, m2m, m2l_ops, dc2e, lattice, l2l
):
    n_pts = lax.axis_size("pts")
    n_top = lax.axis_size("top")
    me = jnp.stack([lax.axis_index("pts"), lax.axis_index("top")]).astype(jnp.int32)
    points = local_pos.shape[1]
    own = points * n_top
    cap = 2 * points // n_pts
    box_cap = 2 * BOXES4 // n_pts
    dens = DENS // n_top
    slabs = max(1, 2 * SIDE // n_pts)
    coef = uc2e.shape[0]
    sources = n_pts * n_top
    lanes = min(cap, LANE)
    width = (5 + dens) * cap + points

    def shape(*dims, dtype=bf16):
        return jax.ShapeDtypeStruct(dims, dtype)

    outgoing, entries = run(
        functools.partial(route_kernel, own, cap, n_top),
        [],
        [
            local_pos,
            densities,
            morton_slot.reshape(1, points),
            slot_leaf.reshape(points // lanes, lanes),
        ],
        [shape(n_pts, n_top, 1, width, dtype=f32), shape(1, points, dtype=jnp.int32)],
        1 << 27,
        late=(0, 1, 3),
        stays=(1,),
        by_kernel=(0,),
        scratch=[pltpu.SemaphoreType.DMA((2 * points // max(cap, LANE),))],
        grant=GRANT_FIRST,
    )
    outgoing = outgoing.reshape(sources, 1, width)
    incoming = lax.all_to_all(outgoing, ("pts", "top"), split_axis=0, concat_axis=0, tiled=True)

    flat = (-1, LANE)
    column = jnp.asarray(column_table())
    w_both, opers, *halves = run(
        operators_kernel,
        [],
        [m2m.reshape(flat), l2l.reshape(flat), uc2e, dc2e, lattice, column],
        [shape(2 * coef, 8 * CPAD), shape(34, coef, coef)] + [shape(2, coef, ROWS)] * 2,
        1 << 30,
        here=range(6),
        stays=range(4),
        scratch=[pltpu.VMEM((2, 8 * coef, LANE), f32)],
    )
    first = relayout(m2l_ops, me, 0, EARLY, GRANT_EARLY)
    incoming, first = lax.optimization_barrier((incoming, first))

    partial, field, place, offsets = run(
        functools.partial(points_kernel, n_top, box_cap),
        [me],
        [incoming, column, w_both],
        [
            shape(up(coef + 2, 16), dens * box_cap),
            shape(coef, own, dtype=f32),
            shape(1, own, dtype=jnp.int32),
        ],
        8 << 30,
        here=range(3),
        stays=range(3),
        numbers=[shape(sources + 1, dtype=jnp.int32)],
        scratch=[
            pltpu.VMEM((8, up(own + up(cap, LANE) + LANE, PB)), f32),
            pltpu.VMEM((3 + FEATURES, coef, PB), f32),
            pltpu.VMEM((1, own), f32),
            pltpu.VMEM((coef, own), f32),
        ],
    )
    later, flat_ops = lax.optimization_barrier((partial, m2l_ops))
    rest = relayout(flat_ops, me, EARLY, STEPS - EARLY, GRANT_LATER)
    parts, rest = gather_by(later, range(n_pts), rest)

    columns = dens * PLANE
    (checks,) = run(
        functools.partial(translate_kernel, slabs, dens),
        [me],
        [*parts, *first, *rest],
        [shape(ROWS, slabs * columns)],
        8 << 30,
        here=range(n_pts + 6),
        stays=(0,),
        scratch=[
            pltpu.VMEM(((7 + slabs - 1) * columns, WFULL), bf16),
            pltpu.VMEM(((7 + slabs - 1) * columns, WIN), bf16),
            pltpu.VMEM((7 * ROWS, slabs * columns), f32),
        ],
    )
    (lattice4,) = run(
        coarse_kernel,
        [],
        [*parts, opers],
        [shape(dens, coef, BOXES4, dtype=f32)],
        4 << 30,
        here=range(n_pts + 1),
        stays=(0,),
    )
    step = n_pts // SIDE * slabs
    distances = [step * m + c for m in range(SIDE // slabs) for c in range(2)]
    gathered, lattice4 = gather_by(checks, distances, lattice4)

    (reply,) = run(
        functools.partial(evaluate_kernel, slabs, step, box_cap),
        [me, offsets],
        [*gathered, *halves, lattice4, place, field],
        [shape(sources, 1, dens * cap, dtype=f32)],
        4 << 30,
        here=range(len(gathered) + 5),
        stays=(0,),
        scratch=[
            pltpu.VMEM((2 * dens * CPAD, 2 * BOXES4), f32),
            pltpu.VMEM((8, own + up(cap, LANE) + LANE), f32),
        ],
    )
    returned = lax.all_to_all(reply, ("pts", "top"), split_axis=0, concat_axis=0, tiled=True)
    (out,) = run(
        functools.partial(restore_kernel, n_top),
        [],
        [returned, entries],
        [shape(DENS, points, dtype=f32)],
        1 << 28,
        here=range(2),
    )
    return out


def solution(mesh):
    split_all = P(None, ("pts", "top"))
    placed = (split_all, split_all, P(("pts", "top")), P(("pts", "top"))) + (P(),) * 6
    return jax.shard_map(
        per_device, mesh=mesh, in_specs=placed, out_specs=split_all, check_vma=False
    )
```
